32 devices in a mesh: seg: 4 (over z), sec: 8 (over y, x, core).
Axes of the slice: x: 2, y: 2, z: 4, core: 2. Of those that a mesh axis runs over, the one named last changes fastest.
Arguments:
- left_env: bfloat16 [4, 8, 34, 128, 128], P('seg', 'sec'), as said below
- right_env: bfloat16 [4, 8, 34, 128, 128], P('seg', 'sec')
- site_tensors: bfloat16 [4, 1, 4, 8, 128, 128], P('seg', None, None, 'sec'), may hold values from -0.5 to 0.5
- mpo: float32 [4, 1, 34, 34, 4], P('seg'), may hold values from -0.5 to 0.5
- boundary_mpo: float32 [4, 34, 34, 4], P('seg'), may hold values from -1 to 1
- guess: float32 [4, 4, 8, 128, 128], P('seg', None, 'sec'), may hold values from -6 to 6
- sector_dims: int32 [8], replicated, may hold values from 16 to 128, as said below
Outputs:
- new_env: bfloat16 [4, 8, 34, 128, 128], P('seg', 'sec')
- lanczos_vector: float32 [4, 4, 8, 128, 128], P('seg', None, 'sec')
- coefficients: float32 [4, 4, 2], P('seg')
The draws below stay inside these ranges and needn't reach their ends.
Inputs may be any that keep to these rules, and one draw needn't show every extreme that they name: sector_dims[q] counts the live rows and columns of sector q within its 128 padded ones; some sector has exactly 128. Every block of left_env and right_env is symmetric.
All inputs are finite; a program needn't handle non-finite values.
Results may differ from the reference program's by a relative error of at most 0.01.
Values may be sent and summed in bfloat16 or wider, within the bound.
No kernel may reach another device: no remote copies, remote signals or barrier semaphores. Data moves between devices by JAX's collectives and lax.ppermute only.
A program may use at most 128 MiB of HBM per device.

```python
import jax
import jax.numpy as jnp
from jax import lax

TILE = 128
W = 34
PHYS = 4
SITES = 1
LANCZOS = 4
SECTORS = 8
SEGMENTS = 4


def symmetric_blocks(key, scale):
    shape = (SEGMENTS, SECTORS, W, TILE, TILE)
    values = jax.random.normal(key, shape, jnp.float32)
    return (values + jnp.swapaxes(values, -1, -2)) * (scale * 0.7071067811865476)


def draw_left_env(key, part):
    key = jax.random.fold_in(key, 1)
    return symmetric_blocks(key, 1.0).astype(jnp.bfloat16)


def draw_right_env(key, part):
    key = jax.random.fold_in(key, 2)
    return symmetric_blocks(key, 1.0 / TILE).astype(jnp.bfloat16)


def draw_sector_dims(key, part):
    key = jax.random.fold_in(key, 3)
    first, second = jax.random.split(key)
    drawn = jax.random.randint(first, (SECTORS,), TILE // 8, TILE + 1, jnp.int32)
    chosen = jax.random.randint(second, (), 0, SECTORS, jnp.int32)
    places = jnp.arange(SECTORS, dtype=jnp.int32)
    return jnp.where(places == chosen, TILE, drawn).astype(jnp.int32)


def block_scale(own_key, dims, cuts, low, high):
    def one(position, parts):
        draws = jax.random.uniform(jax.random.fold_in(jax.random.fold_in(own_key, 6), position), (parts,), jnp.float32, low / len(cuts), high / len(cuts))
        return jnp.repeat(jnp.exp(draws), dims[position] // parts).reshape((-1,) + (1,) * (len(dims) - position - 1))

    gain = one(*cuts[0])
    for cut in cuts[1:]:
        gain = gain * one(*cut)
    return gain


def normal_values(rng, shape, spread, bound, cuts=(), kind=jnp.bfloat16):
    values = spread * jax.random.normal(rng, shape, jnp.float32)
    if cuts:
        values = values * block_scale(rng, shape, cuts, -0.22, 0.18)
    return jnp.clip(values, -bound, bound).astype(kind)


def setup_inputs(seed: int = 0) -> dict:
    key_of = jax.random.split(jax.random.key(seed), 8)
    return {
        "left_env": draw_left_env(jax.random.fold_in(key_of[7], 71), 0),
        "right_env": draw_right_env(jax.random.fold_in(key_of[7], 71), 0),
        "site_tensors": normal_values(key_of[2], (SEGMENTS, SITES, PHYS, SECTORS, TILE, TILE), TILE ** -0.5, 0.5, ((0, 4), (3, 8))),
        "mpo": normal_values(key_of[3], (SEGMENTS, SITES, W, W, PHYS), (4 * W) ** -0.5, 0.5, ((0, 4),), jnp.float32),
        "boundary_mpo": normal_values(key_of[4], (SEGMENTS, W, W, PHYS), W ** -0.5, 1.0, ((0, 4),), jnp.float32),
        "guess": normal_values(key_of[5], (SEGMENTS, PHYS, SECTORS, TILE, TILE), 1.0, 6.0, ((0, 4), (2, 8)), jnp.float32),
        "sector_dims": draw_sector_dims(jax.random.fold_in(key_of[7], 71), 0),
    }


def live_masks(sector_dims):
    charges = jnp.array([0, 1, 1, 2], jnp.int32)
    sectors = jnp.arange(SECTORS, dtype=jnp.int32)
    targets = sectors[None, :] + charges[:, None]
    hits = sectors[None, None, :] == targets[:, :, None]
    dim_next = lax.optimization_barrier(jnp.sum(jnp.where(hits, sector_dims[None, None, :], 0), axis=2))
    places = jnp.arange(TILE, dtype=jnp.int32)
    rows = places[None, :] < sector_dims[:, None]
    columns = places[None, None, :] < dim_next[:, :, None]
    return (rows[None, :, :, None] & columns[:, :, None, :]).astype(jnp.float32)

def move_sectors(tensor, offset):
    if offset > 0:
        return jnp.concatenate([jnp.zeros_like(tensor[:offset]), tensor[:-offset]], axis=0)
    return jnp.concatenate([tensor[-offset:], jnp.zeros_like(tensor[:-offset])], axis=0)

def rounded(tensor):
    return lax.optimization_barrier(tensor.astype(jnp.bfloat16)).astype(jnp.float32)

def advance(environ, tensors, weights, live_mask):
    blocks = tensors.astype(jnp.float32) * live_mask
    half = jnp.einsum('swab,psbc->pswac', environ.astype(jnp.float32), blocks)
    half = rounded(half)
    turned = jnp.einsum('psad,pswac->pswdc', blocks, half)
    folded = jnp.einsum('wvp,pswdc->psvdc', weights, turned, precision=lax.Precision.HIGHEST)
    charge_one = rounded(folded[1] + folded[2])
    charge_two = rounded(folded[3])
    total = folded[0] + move_sectors(charge_one, 1) + move_sectors(charge_two, 2)
    return total.astype(jnp.bfloat16)

def hamiltonian(field, boundary, selected, weights, live_mask):
    field_low = rounded(field)
    first = jnp.einsum('swab,psbc->pswac', boundary.astype(jnp.float32), field_low)
    inner = rounded(jnp.einsum('wvp,pswac->psvac', weights, first, precision=lax.Precision.HIGHEST))
    return jnp.einsum('psvac,psvcd->psad', inner, selected) * live_mask

def lanczos(boundary, right_block, weights, start, live_mask):
    selected = jnp.stack([right_block, move_sectors(right_block, -1), move_sectors(right_block, -1), move_sectors(right_block, -2)]).astype(jnp.float32)
    entries = float(PHYS * SECTORS * TILE * TILE)
    vector = start * live_mask
    vector = vector / jnp.sqrt(jnp.sum(vector * vector) / entries + 1e-06)
    previous = jnp.zeros_like(vector)
    beta_prev = jnp.float32(0.0)
    coefficient_list = []
    for iteration in range(LANCZOS):
        image_now = hamiltonian(vector, boundary, selected, weights, live_mask)
        alpha_now = jnp.sum(vector * image_now) / entries
        image_now = image_now - alpha_now * vector - beta_prev * previous
        beta_now = jnp.sqrt(jnp.sum(image_now * image_now) / entries + 1e-06)
        previous = vector
        vector = image_now / beta_now
        beta_prev = beta_now
        coefficient_list.append(jnp.stack([alpha_now, beta_now]))
    return (vector, jnp.stack(coefficient_list))

def reference(left_env, right_env, site_tensors, mpo, boundary_mpo, guess, sector_dims):
    live_mask = live_masks(sector_dims)
    carried = []
    for segment in range(SEGMENTS):
        environ = left_env[segment]
        for site in range(SITES):
            environ = advance(environ, site_tensors[segment, site], mpo[segment, site], live_mask)
        carried.append(environ)
    new_env = jnp.stack(carried)
    boundaries = jnp.concatenate([left_env[:1], new_env[:-1]], axis=0)
    vectors = []
    tables = []
    for segment in range(SEGMENTS):
        vector, table = lanczos(boundaries[segment], right_env[segment], boundary_mpo[segment], guess[segment], live_mask)
        vectors.append(vector)
        tables.append(table)
    return (new_env, jnp.stack(vectors), jnp.stack(tables))
```

```python
import functools

import jax
import jax.numpy as jnp
from jax import lax
from jax.experimental import pallas as pl
from jax.experimental.pallas import tpu as pltpu
from jax.sharding import PartitionSpec as P

LANCZOS = 4
CHARGES = (0, 1, 1, 2)
F32 = jnp.float32
BF16 = jnp.bfloat16
VMEM_LIMIT = 56 * 1024 * 1024


def params():
    return pltpu.CompilerParams(vmem_limit_bytes=VMEM_LIMIT)


def padded(count):
    return -(-count // 8) * 8


def packed_rows(width, tile):
    return -(-(width * tile // 2 + padded(width)) // 16) * 16


def iotas(shape):
    return lax.broadcasted_iota(jnp.int32, shape, 0), lax.broadcasted_iota(jnp.int32, shape, 1)


def pack_block(block):
    tile = block.shape[0]
    half = tile // 2
    top, low = block[:half], block[half:]
    row, lane = iotas((half, tile))
    turned = pltpu.roll(low, half, 1)
    folded = jnp.where((lane < half) & (row > lane), turned, top)
    diagonal = jnp.sum(jnp.where(lane == row + half, low, 0.0), axis=0, keepdims=True)
    return folded, diagonal


def unpack_block(folded, diagonal):
    half, tile = folded.shape
    row, lane = iotas((half, tile))
    rolled = pltpu.roll(folded, half, 1)
    turned = jnp.transpose(jnp.concatenate([folded, rolled], axis=0))
    top = jnp.where((lane < half) & (row > lane), turned[:half], folded)
    low = jnp.where((lane >= half) & (row > lane - half), rolled, turned[half:])
    low = jnp.where(lane == row + half, diagonal, low)
    return jnp.concatenate([top, low], axis=0)


def live_limits(dims_ref, sector):
    count = dims_ref.shape[0]
    rows = dims_ref[sector]
    columns = []
    for charge in CHARGES:
        target = sector + charge
        columns.append(jnp.where(target < count, dims_ref[jnp.minimum(target, count - 1)], 0))
    return rows, columns


def pack_kernel(width, tile, source_ref, out_ref, diag):
    half = tile // 2
    diag[...] = jnp.zeros_like(diag)

    def one(w, carry):
        block = source_ref[pl.ds(pl.multiple_of(w * tile, tile), tile), :].astype(F32)
        folded, diagonal = pack_block(block)
        out_ref[pl.ds(pl.multiple_of(w * half, half), half), :] = folded.astype(BF16)
        diag[pl.ds(w, 1), :] = diagonal
        return carry

    lax.fori_loop(0, width, one, 0, unroll=2)
    out_ref[width * half :, :] = diag[...].astype(BF16)


def unpack_kernel(width, tile, source_ref, out_ref, diag):
    half = tile // 2
    diag[...] = source_ref[width * half :, :].astype(F32)

    def one(w, carry):
        folded = source_ref[pl.ds(pl.multiple_of(w * half, half), half), :].astype(F32)
        block = unpack_block(folded, diag[pl.ds(w, 1), :])
        out_ref[pl.ds(pl.multiple_of(w * tile, tile), tile), :] = block.astype(BF16)
        return carry

    lax.fori_loop(0, width, one, 0, unroll=2)


def fold_kernel(
    width, tile, place_ref, dims_ref, environ_ref, site_ref, weight_ref,
    own_ref, one_ref, two_ref, half_s, turned_s, diag_s, sums_s, diag_sums_s,
):
    half = tile // 2
    wide = padded(width)
    states = len(CHARGES)
    rows, columns = live_limits(dims_ref, place_ref[0])
    row, lane = iotas((tile, tile))
    blocks = []
    for p in range(states):
        live = (row < rows) & (lane < columns[p])
        blocks.append(jnp.where(live, site_ref[p].astype(F32), 0.0))
    turned_blocks = [jnp.transpose(block).astype(BF16) for block in blocks]
    joined = jnp.concatenate(blocks, axis=1).astype(BF16)

    def first(w, carry):
        at = pl.ds(pl.multiple_of(w * tile, tile), tile)
        half_s[at, :] = jnp.dot(environ_ref[at, :], joined, preferred_element_type=F32).astype(BF16)
        return carry

    lax.fori_loop(0, width, first, 0, unroll=2)
    for p in range(states):
        turned_s[p, width * half :, :] = jnp.zeros(((wide - width) * half, tile), F32)
        diag_s[p] = jnp.zeros_like(diag_s[p])

    def second(w, carry):
        at = pl.ds(pl.multiple_of(w * tile, tile), tile)
        for p in range(states):
            block = jnp.dot(
                turned_blocks[p], half_s[at, p * tile : (p + 1) * tile], preferred_element_type=F32
            )
            folded, diagonal = pack_block(block)
            turned_s[p, pl.ds(pl.multiple_of(w * half, half), half), :] = folded
            diag_s[p, pl.ds(w, 1), :] = diagonal
        return carry

    lax.fori_loop(0, width, second, 0, unroll=2)

    def mixed(inputs):
        products = []
        for p in range(states):
            value = inputs[p]
            value = jnp.concatenate([value, value], axis=0).astype(BF16)
            products.append(jnp.dot(weight_ref[p], value, preferred_element_type=F32)[:wide])
        return products[0], products[1] + products[2], products[3]

    def mix(step, carry):
        at = step * 2
        inputs = [
            jnp.concatenate(
                [turned_s[p, pl.ds(at + k, wide, stride=half), :] for k in range(2)], axis=1
            )
            for p in range(states)
        ]
        for index, value in enumerate(mixed(inputs)):
            for k in range(2):
                sums_s[index, pl.ds(at + k, wide, stride=half), :] = value[:, k * tile : (k + 1) * tile]
        return carry

    lax.fori_loop(0, half // 2, mix, 0, unroll=2)
    diag_sums_s[...] = jnp.zeros_like(diag_sums_s)
    for index, value in enumerate(mixed([diag_s[p, :wide] for p in range(states)])):
        diag_sums_s[index, :wide, :] = value
    for index, ref in enumerate((own_ref, one_ref, two_ref)):
        ref[: width * half, :] = sums_s[index, : width * half, :].astype(ref.dtype)
        ref[width * half :, :] = diag_sums_s[index].astype(ref.dtype)


def mix_into(width, tile, weight, wide_s, sums_s, out_ref, base):
    wide = padded(width)

    def mix(step, carry):
        at = step * 2
        value = jnp.concatenate(
            [wide_s[pl.ds(at + k, wide, stride=tile), :] for k in range(2)], axis=1
        )
        value = jnp.concatenate([value, value], axis=0).astype(BF16)
        value = jnp.dot(weight, value, preferred_element_type=F32)[:wide]
        for k in range(2):
            sums_s[pl.ds(at + k, wide, stride=tile), :] = value[:, k * tile : (k + 1) * tile]
        return carry

    lax.fori_loop(0, tile // 2, mix, 0, unroll=4)
    out_ref[pl.ds(base * tile, width * tile), :] = sums_s[: width * tile, :].astype(BF16)


def mix_own_kernel(width, tile, source_ref, weight_ref, out_ref, wide_s, sums_s):
    wide_s[: width * tile, :] = source_ref[...].astype(F32)
    wide_s[width * tile :, :] = jnp.zeros_like(wide_s[width * tile :, :])
    mix_into(width, tile, weight_ref[0], wide_s, sums_s, out_ref, 0)


def mix_far_kernel(
    width, tile, near_ref, relay_ref, far_ref, weight_ref, out_ref, diag, wide_s, sums_s
):
    half = tile // 2
    wide_s[width * tile :, :] = jnp.zeros_like(wide_s[width * tile :, :])

    def unpacked(read):
        diag[...] = read(pl.ds(width * half, diag.shape[0]))

        def one(w, carry):
            folded = read(pl.ds(pl.multiple_of(w * half, half), half))
            wide_s[pl.ds(pl.multiple_of(w * tile, tile), tile), :] = unpack_block(
                folded, diag[pl.ds(w, 1), :]
            )
            return carry

        lax.fori_loop(0, width, one, 0, unroll=2)

    unpacked(lambda at: near_ref[at, :].astype(F32) + relay_ref[at, :].astype(F32))
    mix_into(width, tile, weight_ref[1], wide_s, sums_s, out_ref, 0)
    mix_into(width, tile, weight_ref[2], wide_s, sums_s, out_ref, width)
    unpacked(lambda at: far_ref[at, :].astype(F32))
    mix_into(width, tile, weight_ref[3], wide_s, sums_s, out_ref, 2 * width)


def total(value):
    return jnp.sum(jnp.sum(value, axis=0, keepdims=True), axis=1, keepdims=True)


def lanczos_kernel(
    width, tile, place_ref, dims_ref, packed_ref, environ_ref, own_ref, far_ref, guess_ref,
    basis_ref, stats_ref, bound_s, first_s, diag,
):
    half = tile // 2
    states = len(CHARGES)
    sector = place_ref[0]

    @pl.when(place_ref[1] == 0)
    def _():
        bound_s[...] = environ_ref[...]

    @pl.when(place_ref[1] != 0)
    def _():
        diag[...] = packed_ref[width * half :, :].astype(F32)

        def one(w, carry):
            folded = packed_ref[pl.ds(pl.multiple_of(w * half, half), half), :].astype(F32)
            bound_s[pl.ds(pl.multiple_of(w * tile, tile), tile), :] = unpack_block(
                folded, diag[pl.ds(w, 1), :]
            ).astype(BF16)
            return carry

        lax.fori_loop(0, width, one, 0, unroll=2)

    rows, columns = live_limits(dims_ref, sector)
    row, lane = iotas((tile, tile))
    stat_row, stat_lane = iotas(stats_ref.shape)
    stats = jnp.zeros(stats_ref.shape, F32)

    def put(stats, kind, p, value):
        here = (stat_row == kind) & (stat_lane == sector * states + p)
        return jnp.where(here, value, stats)

    def scaled(value):
        square = total(value * value)
        inverse = jnp.where(square > 0.0, lax.rsqrt(square), 0.0)
        return value * inverse, square * inverse

    for p in range(states):
        live = (row < rows) & (lane < columns[p])
        vector, norm = scaled(jnp.where(live, guess_ref[p], 0.0))
        basis_ref[0, p] = vector
        stats = put(stats, 0, p, norm)

    betas = [jnp.zeros((1, 1), F32)] * states
    for j in range(LANCZOS):
        field = jnp.concatenate([basis_ref[j, p] for p in range(states)], axis=1).astype(BF16)
        for w in range(width):
            first = jnp.dot(
                bound_s[w * tile : (w + 1) * tile, :], field, preferred_element_type=F32
            ).astype(BF16)
            for p in range(states):
                first_s[p, :, w * tile : (w + 1) * tile] = first[:, p * tile : (p + 1) * tile]
        for p in range(states):
            live = (row < rows) & (lane < columns[p])
            if p == 0:
                right = own_ref[...]
            else:
                right = far_ref[(p - 1) * width * tile : p * width * tile, :]
            image = jnp.dot(first_s[p], right, preferred_element_type=F32)
            image = jnp.where(live, image, 0.0)
            vector = basis_ref[j, p]
            alpha = total(vector * image)
            image = image - alpha * vector
            if j > 0:
                image = image - betas[p] * basis_ref[j - 1, p]
            following, beta = scaled(image)
            basis_ref[j + 1, p] = following
            betas[p] = beta
            stats = put(stats, 1 + 2 * j, p, alpha)
            stats = put(stats, 2 + 2 * j, p, beta)
    stats_ref[...] = stats


def finish_kernel(entries, place_ref, stats_ref, basis_ref, vector_ref, table_ref):
    states = len(CHARGES)
    sector = place_ref[0]
    stats = stats_ref[...]
    alphas = [stats[1 + 2 * j : 2 + 2 * j, :] for j in range(LANCZOS)]
    betas = [stats[2 + 2 * j : 3 + 2 * j, :] for j in range(LANCZOS)]

    def mean(left, right):
        products = left[0] * right[0]
        for x, y in zip(left[1:], right[1:]):
            products = products + x * y
        return jnp.sum(products, axis=1, keepdims=True) / entries

    start = [stats[0:1, :]]
    vector = [start[0] / jnp.sqrt(mean(start, start) + 1e-06)]
    previous = []
    beta = jnp.zeros((1, 1), F32)
    table_row, table_column = iotas(table_ref.shape)
    table = jnp.zeros(table_ref.shape, F32)
    for j in range(LANCZOS):
        image = []
        for k in range(j + 2):
            term = None
            if k > 0:
                term = betas[k - 1] * vector[k - 1]
            if k <= j:
                more = alphas[k] * vector[k]
                term = more if term is None else term + more
            if k + 1 <= j:
                term = term + betas[k] * vector[k + 1]
            image.append(term)
        alpha = mean(vector, image[: j + 1])
        for k in range(j + 1):
            image[k] = image[k] - alpha * vector[k]
        for k in range(j):
            image[k] = image[k] - beta * previous[k]
        beta = jnp.sqrt(mean(image, image) + 1e-06)
        previous = vector
        vector = [value / beta for value in image]
        table = jnp.where((table_row == j) & (table_column == 0), alpha, table)
        table = jnp.where((table_row == j) & (table_column == 1), beta, table)
    table_ref[...] = table
    lane = lax.broadcasted_iota(jnp.int32, (1, stats.shape[1]), 1)
    for p in range(states):
        value = None
        here = lane == sector * states + p
        for k in range(LANCZOS + 1):
            weight = jnp.sum(jnp.where(here, vector[k], 0.0), axis=1, keepdims=True)
            term = weight * basis_ref[k, p]
            value = term if value is None else value + term
        vector_ref[p] = value


def smem():
    return pl.BlockSpec(memory_space=pltpu.SMEM)


def vmem():
    return pl.BlockSpec(memory_space=pltpu.VMEM)


def call(kernel, scalars, arrays, outs, scratch, flops=0, name=None):
    many = isinstance(outs, (tuple, list))
    return pl.pallas_call(
        kernel,
        out_shape=outs,
        in_specs=[smem()] * len(scalars) + [vmem()] * len(arrays),
        out_specs=[vmem()] * len(outs) if many else vmem(),
        scratch_shapes=scratch,
        compiler_params=params(),
        name=name,
        cost_estimate=pl.CostEstimate(flops=flops, bytes_accessed=4 * 1024 * 1024, transcendentals=0),
    )(*scalars, *arrays)


def split_weights(weights, rows):
    states, out_count, in_count = weights.shape
    wide = padded(in_count)
    high = weights.astype(BF16)
    low = (weights - high.astype(F32)).astype(BF16)
    gap = ((0, 0), (0, rows - out_count), (0, wide - in_count))
    return jnp.concatenate([jnp.pad(high, gap), jnp.pad(low, gap)], axis=2)


def pairs_of(count, pick):
    return [(source, target) for source in range(count) for target in pick(source) if 0 <= target < count]


def on_device(left_env, right_env, site_tensors, mpo, boundary_mpo, guess, sector_dims):
    width, tile = left_env.shape[2], left_env.shape[-1]
    half = tile // 2
    wide = padded(width)
    states = len(CHARGES)
    sector_count = sector_dims.shape[0]
    sectors = lax.axis_size("sec")
    segments = lax.axis_size("seg")
    prows = packed_rows(width, tile)
    drows = prows - width * half
    sector = lax.axis_index("sec")
    place = jnp.stack([sector, lax.axis_index("seg")]).astype(jnp.int32)
    odd = lax.rem(sector, 2) == 1
    packed = jax.ShapeDtypeStruct((prows, tile), BF16)
    packed32 = jax.ShapeDtypeStruct((prows, tile), F32)
    product = 2 * width * tile**3

    environ = left_env.reshape(width * tile, tile)
    right = right_env.reshape(width * tile, tile)
    site = site_tensors[0, 0, :, 0]
    mrows = -(-width // 16) * 16
    site_weights = split_weights(jnp.transpose(mpo[0, 0], (2, 1, 0)), mrows)
    bound_weights = split_weights(jnp.transpose(boundary_mpo[0], (2, 0, 1)), mrows)

    swap = pairs_of(sectors, lambda q: [q ^ 1])
    down = pairs_of(sectors, lambda q: [q - 1] if q % 2 else [])
    across = pairs_of(sectors, lambda q: [q + 1] if q % 2 == 0 else [])
    up_two = pairs_of(sectors, lambda q: [q + 2])
    down_two = pairs_of(sectors, lambda q: [q - 2])
    onward = pairs_of(segments, lambda s: [s + 1])

    right_packed = call(
        functools.partial(pack_kernel, width, tile), [], [right], packed,
        [pltpu.VMEM((drows, tile), F32)], name="pack_right",
    )
    right_far = lax.ppermute(right_packed, "sec", down_two)
    right_near = lax.ppermute(right_packed, "sec", down)

    own, one, two = call(
        functools.partial(fold_kernel, width, tile),
        [place, sector_dims], [environ, site, site_weights],
        (packed32, packed, packed32),
        [
            pltpu.VMEM((width * tile, states * tile), BF16),
            pltpu.VMEM((states, wide * half, tile), F32),
            pltpu.VMEM((states, drows, tile), F32),
            pltpu.VMEM((3, wide * half, tile), F32),
            pltpu.VMEM((3, drows, tile), F32),
        ],
        flops=2 * states * product, name="fold",
    )
    partner = lax.ppermute(one, "sec", swap)
    outgoing = jnp.where(odd, two, two + partner.astype(F32)).astype(BF16)
    arrived = lax.ppermute(outgoing, "sec", up_two)
    own_mixed = call(
        functools.partial(mix_own_kernel, width, tile), [], [right, bound_weights],
        jax.ShapeDtypeStruct((width * tile, tile), BF16),
        [pltpu.VMEM((wide * tile, tile), F32)] * 2,
        flops=product, name="mix_own",
    )
    right_relay = lax.ppermute(right_far, "sec", across)
    fresh = own + arrived.astype(F32) + jnp.where(odd, partner.astype(F32), 0.0)
    fresh = fresh.astype(BF16)
    received = lax.ppermute(fresh, "seg", onward)
    far_mixed = call(
        functools.partial(mix_far_kernel, width, tile), [],
        [right_near, right_relay, right_far, bound_weights],
        jax.ShapeDtypeStruct((3 * width * tile, tile), BF16),
        [pltpu.VMEM((drows, tile), F32)] + [pltpu.VMEM((wide * tile, tile), F32)] * 2,
        flops=3 * product, name="mix_far",
    )
    new_env = call(
        functools.partial(unpack_kernel, width, tile), [], [fresh],
        jax.ShapeDtypeStruct((width * tile, tile), BF16),
        [pltpu.VMEM((drows, tile), F32)], name="unpack_env",
    )
    basis, stats = call(
        functools.partial(lanczos_kernel, width, tile),
        [place, sector_dims], [received, environ, own_mixed, far_mixed, guess[0, :, 0]],
        (
            jax.ShapeDtypeStruct((LANCZOS + 1, states, tile, tile), F32),
            jax.ShapeDtypeStruct((16, 128), F32),
        ),
        [
            pltpu.VMEM((width * tile, tile), BF16),
            pltpu.VMEM((states, tile, width * tile), BF16),
            pltpu.VMEM((drows, tile), F32),
        ],
        flops=8 * states * product, name="lanczos",
    )
    stats = lax.psum(stats, "sec")
    entries = float(states * sector_count * tile * tile)
    vector, table = call(
        functools.partial(finish_kernel, entries), [place], [stats, basis],
        (
            jax.ShapeDtypeStruct((states, tile, tile), F32),
            jax.ShapeDtypeStruct((LANCZOS, 2), F32),
        ),
        [], name="finish",
    )
    return new_env.reshape(left_env.shape), vector[None, :, None], table[None]


def solution(mesh):
    placed = (
        P("seg", "sec", None, None, None),
        P("seg", "sec", None, None, None),
        P("seg", None, None, "sec", None, None),
        P("seg", None, None, None, None),
        P("seg", None, None, None),
        P("seg", None, "sec", None, None),
        P(),
    )
    return jax.shard_map(
        on_device,
        mesh=mesh,
        in_specs=placed,
        out_specs=(
            P("seg", "sec", None, None, None),
            P("seg", None, "sec", None, None),
            P("seg", None, None),
        ),
        check_vma=False,
    )
```

```python
import functools

import jax
import jax.numpy as jnp
from jax import lax
from jax.experimental import pallas as pl
from jax.experimental.pallas import tpu as pltpu
from jax.sharding import PartitionSpec as P

LANCZOS = 4
CHARGES = (0, 1, 1, 2)
F32 = jnp.float32
BF16 = jnp.bfloat16
MIB = 1024 * 1024


def padded(count):
    return -(-count // 8) * 8


def packed_height(count):
    return -(-count // 16) * 16


def packed_rows(width, tile):
    return -(-(width * tile // 2 + padded(width)) // 16) * 16


def iotas(shape):
    return lax.broadcasted_iota(jnp.int32, shape, 0), lax.broadcasted_iota(jnp.int32, shape, 1)


def pack_block(block):
    tile = block.shape[0]
    half = tile // 2
    top, low = block[:half], block[half:]
    row, lane = iotas((half, tile))
    turned = pltpu.roll(low, half, 1)
    folded = jnp.where((lane < half) & (row > lane), turned, top)
    diagonal = jnp.sum(jnp.where(lane == row + half, low, 0.0), axis=0, keepdims=True)
    return folded, diagonal


def unpack_block(folded, diagonal):
    half, tile = folded.shape
    row, lane = iotas((half, tile))
    rolled = pltpu.roll(folded, half, 1)
    turned = jnp.transpose(jnp.concatenate([folded, rolled], axis=0))
    top = jnp.where((lane < half) & (row > lane), turned[:half], folded)
    low = jnp.where((lane >= half) & (row > lane - half), rolled, turned[half:])
    low = jnp.where(lane == row + half, diagonal, low)
    return jnp.concatenate([top, low], axis=0)


def live_limits(dims_ref):
    sector = lax.axis_index("sec")
    count = dims_ref.shape[0]
    rows = dims_ref[sector]
    columns = []
    for charge in CHARGES:
        target = sector + charge
        columns.append(jnp.where(target < count, dims_ref[jnp.minimum(target, count - 1)], 0))
    return rows, columns


def aligned(index, size):
    return pl.ds(pl.multiple_of(index * size, size), size)


def weight_rows(weight_ref, width, p, square, turned):
    wide = padded(width)
    square[...] = jnp.zeros_like(square)
    square[:width, :width] = weight_ref[pl.ds(p, width, stride=len(CHARGES)), :]
    value = square[...]
    if turned:
        value = jnp.transpose(value)
    high = value.astype(BF16).astype(F32)
    joined = (high + pltpu.roll(value - high, wide, 1)).astype(BF16)
    return joined[: packed_height(width), : 2 * wide]


def doubled(value):
    return jnp.concatenate([value, value], axis=0).astype(BF16)


def pack_kernel(width, tile, source_ref, out_ref, diag):
    half = tile // 2
    diag[...] = jnp.zeros_like(diag)
    for w in range(width):
        folded, diagonal = pack_block(source_ref[w * tile : (w + 1) * tile, :].astype(F32))
        out_ref[w * half : (w + 1) * half, :] = folded.astype(BF16)
        diag[w : w + 1, :] = diagonal
    out_ref[width * half :, :] = diag[...].astype(BF16)


def unpack_into(width, tile, pitch, read, out_ref, diag):
    half = tile // 2
    diag[...] = read(width * half, diag.shape[0])
    for w in range(width):
        block = unpack_block(read(w * half, half), diag[w : w + 1, :])
        out_ref[w * pitch : w * pitch + tile, :] = block.astype(out_ref.dtype)


def unpack_kernel(width, tile, source_ref, out_ref, diag):
    unpack_into(
        width, tile, tile, lambda at, size: source_ref[at : at + size, :].astype(F32), out_ref, diag
    )


def fold_kernel(
    width, tile, dims_ref, environ_ref, site_ref, weight_ref, own_ref, one_ref, two_ref,
    joined_s, turned_s, square_s, weight_s, half_s, packed_s, diag_s, sums_s, diag_sums_s,
):
    half = tile // 2
    pitch = half + 8
    wide = padded(width)
    states = len(CHARGES)
    rows, columns = live_limits(dims_ref)
    row, lane = iotas((tile, tile))
    for p in range(states):
        live = (row < rows) & (lane < columns[p])
        block = jnp.where(live, site_ref[p].astype(F32), 0.0)
        joined_s[:, p * tile : (p + 1) * tile] = block.astype(BF16)
        turned_s[p] = jnp.transpose(block).astype(BF16)
        weight_s[p] = weight_rows(weight_ref, width, p, square_s, True)
        packed_s[p, width * pitch :, :] = jnp.zeros(((wide - width) * pitch, tile), F32)
        diag_s[p] = jnp.zeros_like(diag_s[p])

    def first(pair, carry):
        for k in range(2):
            block = environ_ref[aligned(pair * 2 + k, tile), :]
            block = jnp.dot(block, joined_s[...], preferred_element_type=F32).astype(BF16)
            for p in range(states):
                half_s[p, aligned(pair, tile), k * tile : (k + 1) * tile] = block[
                    :, p * tile : (p + 1) * tile
                ]
        return carry

    lax.fori_loop(0, width // 2, first, 0, unroll=2)

    def second(pair, carry):
        for p in range(states):
            both = jnp.dot(turned_s[p], half_s[p, aligned(pair, tile), :], preferred_element_type=F32)
            for k in range(2):
                folded, diagonal = pack_block(both[:, k * tile : (k + 1) * tile])
                at = pl.multiple_of((pair * 2 + k) * pitch, 8)
                packed_s[p, pl.ds(at, half), :] = folded
                diag_s[p, pl.ds(pair * 2 + k, 1), :] = diagonal
        return carry

    lax.fori_loop(0, width // 2, second, 0, unroll=2)

    def mixed(inputs):
        products = [
            jnp.dot(weight_s[p], doubled(inputs[p]), preferred_element_type=F32)[:wide]
            for p in range(states)
        ]
        return products[0], products[1] + products[2], products[3]

    def mix(step, carry):
        at = step * 2
        inputs = [
            jnp.concatenate(
                [packed_s[p, pl.ds(at + k, wide, stride=pitch), :] for k in range(2)], axis=1
            )
            for p in range(states)
        ]
        for index, value in enumerate(mixed(inputs)):
            for k in range(2):
                sums_s[index, pl.ds(at + k, wide, stride=pitch), :] = value[:, k * tile : (k + 1) * tile]
        return carry

    lax.fori_loop(0, half // 2, mix, 0, unroll=4)
    diag_sums_s[...] = jnp.zeros_like(diag_sums_s)
    for index, value in enumerate(mixed([diag_s[p, :wide] for p in range(states)])):
        diag_sums_s[index, :wide, :] = value
    for index, ref in enumerate((own_ref, one_ref, two_ref)):
        for w in range(width):
            ref[w * half : (w + 1) * half, :] = sums_s[index, w * pitch : w * pitch + half, :].astype(
                ref.dtype
            )
        ref[width * half :, :] = diag_sums_s[index].astype(ref.dtype)


def mix_into(width, tile, weights, wide_s, sums_s, out_ref):
    wide = padded(width)
    pitch = tile + 8
    wide_s[width * pitch :, :] = jnp.zeros_like(wide_s[width * pitch :, :])

    def mix(step, carry):
        at = step * 2
        value = doubled(
            jnp.concatenate(
                [wide_s[pl.ds(at + k, wide, stride=pitch), :] for k in range(2)], axis=1
            )
        )
        for index, weight in enumerate(weights):
            mixed = jnp.dot(weight[...], value, preferred_element_type=F32)[:wide]
            for k in range(2):
                sums_s[index, pl.ds(at + k, wide, stride=pitch), :] = mixed[:, k * tile : (k + 1) * tile]
        return carry

    lax.fori_loop(0, tile // 2, mix, 0, unroll=4)
    for index in range(len(weights)):
        for w in range(width):
            out = (index * width + w) * tile
            out_ref[out : out + tile, :] = sums_s[index, w * pitch : w * pitch + tile, :].astype(BF16)


def mix_own_kernel(width, tile, source_ref, weight_ref, out_ref, square_s, weight_s, wide_s, sums_s):
    pitch = tile + 8
    weight_s[0] = weight_rows(weight_ref, width, 0, square_s, False)
    for w in range(width):
        wide_s[w * pitch : w * pitch + tile, :] = source_ref[w * tile : (w + 1) * tile, :].astype(F32)
    mix_into(width, tile, [weight_s.at[0]], wide_s, sums_s, out_ref)


def mix_next_kernel(
    width, tile, near_ref, relay_ref, weight_ref, out_ref, square_s, weight_s, wide_s, sums_s, diag
):
    for k in range(2):
        weight_s[k] = weight_rows(weight_ref, width, k + 1, square_s, False)

    def read(at, size):
        return near_ref[at : at + size, :].astype(F32) + relay_ref[at : at + size, :].astype(F32)

    unpack_into(width, tile, tile + 8, read, wide_s, diag)
    mix_into(width, tile, [weight_s.at[k] for k in range(2)], wide_s, sums_s, out_ref)


def mix_after_kernel(
    width, tile, far_ref, weight_ref, out_ref, square_s, weight_s, wide_s, sums_s, diag
):
    weight_s[0] = weight_rows(weight_ref, width, 3, square_s, False)

    def read(at, size):
        return far_ref[at : at + size, :].astype(F32)

    unpack_into(width, tile, tile + 8, read, wide_s, diag)
    mix_into(width, tile, [weight_s.at[0]], wide_s, sums_s, out_ref)


def total(value):
    return jnp.sum(jnp.sum(value, axis=0, keepdims=True), axis=1, keepdims=True)


def lanczos_kernel(
    width, tile, dims_ref, packed_ref, environ_ref, own_ref, next_ref, after_ref, guess_ref,
    basis_ref, stats_ref, bound_s, first_s, diag,
):
    states = len(CHARGES)
    sector = lax.axis_index("sec")
    segment = lax.axis_index("seg")

    @pl.when(segment == 0)
    def _():
        bound_s[...] = environ_ref[...]

    @pl.when(segment != 0)
    def _():
        unpack_into(
            width, tile, tile, lambda at, size: packed_ref[at : at + size, :].astype(F32), bound_s, diag
        )

    rows, columns = live_limits(dims_ref)
    row, lane = iotas((tile, tile))
    stat_row, stat_lane = iotas(stats_ref.shape)
    stats = jnp.zeros(stats_ref.shape, F32)

    def put(stats, kind, p, value):
        here = (stat_row == kind) & (stat_lane == sector * states + p)
        return jnp.where(here, value, stats)

    def scaled(value):
        square = total(value * value)
        inverse = jnp.where(square > 0.0, lax.rsqrt(square), 0.0)
        return value * inverse, square * inverse

    for p in range(states):
        live = (row < rows) & (lane < columns[p])
        vector, norm = scaled(jnp.where(live, guess_ref[p], 0.0))
        basis_ref[0, p] = vector
        stats = put(stats, 0, p, norm)

    size = width * tile
    rights = [own_ref, next_ref.at[:size, :], next_ref.at[size:, :], after_ref]
    betas = [jnp.zeros((1, 1), F32)] * states
    for j in range(LANCZOS):
        field = jnp.concatenate([basis_ref[j, p] for p in range(states)], axis=1).astype(BF16)
        for w in range(width):
            first = jnp.dot(
                bound_s[w * tile : (w + 1) * tile, :], field, preferred_element_type=F32
            ).astype(BF16)
            for p in range(states):
                first_s[p, :, w * tile : (w + 1) * tile] = first[:, p * tile : (p + 1) * tile]
        for p in range(states):
            live = (row < rows) & (lane < columns[p])
            right = rights[p][...]
            image = jnp.dot(first_s[p], right, preferred_element_type=F32)
            image = jnp.where(live, image, 0.0)
            vector = basis_ref[j, p]
            alpha = total(vector * image)
            image = image - alpha * vector
            if j > 0:
                image = image - betas[p] * basis_ref[j - 1, p]
            following, beta = scaled(image)
            basis_ref[j + 1, p] = following
            betas[p] = beta
            stats = put(stats, 1 + 2 * j, p, alpha)
            stats = put(stats, 2 + 2 * j, p, beta)
    stats_ref[...] = stats


def finish_kernel(entries, stats_ref, basis_ref, vector_ref, table_ref):
    states = len(CHARGES)
    sector = lax.axis_index("sec")
    stats = stats_ref[...]
    alphas = [stats[1 + 2 * j : 2 + 2 * j, :] for j in range(LANCZOS)]
    betas = [stats[2 + 2 * j : 3 + 2 * j, :] for j in range(LANCZOS)]

    def mean(left, right):
        products = left[0] * right[0]
        for x, y in zip(left[1:], right[1:]):
            products = products + x * y
        return jnp.sum(products, axis=1, keepdims=True) / entries

    start = [stats[0:1, :]]
    vector = [start[0] / jnp.sqrt(mean(start, start) + 1e-06)]
    previous = []
    beta = jnp.zeros((1, 1), F32)
    table_row, table_column = iotas(table_ref.shape)
    table = jnp.zeros(table_ref.shape, F32)
    for j in range(LANCZOS):
        image = []
        for k in range(j + 2):
            term = None
            if k > 0:
                term = betas[k - 1] * vector[k - 1]
            if k <= j:
                more = alphas[k] * vector[k]
                term = more if term is None else term + more
            if k + 1 <= j:
                term = term + betas[k] * vector[k + 1]
            image.append(term)
        alpha = mean(vector, image[: j + 1])
        for k in range(j + 1):
            image[k] = image[k] - alpha * vector[k]
        for k in range(j):
            image[k] = image[k] - beta * previous[k]
        beta = jnp.sqrt(mean(image, image) + 1e-06)
        previous = vector
        vector = [value / beta for value in image]
        table = jnp.where((table_row == 0) & (table_column == j), alpha, table)
        table = jnp.where((table_row == 1) & (table_column == j), beta, table)
    table_ref[...] = table
    lane = lax.broadcasted_iota(jnp.int32, (1, stats.shape[1]), 1)
    for p in range(states):
        value = None
        here = lane == sector * states + p
        for k in range(LANCZOS + 1):
            weight = jnp.sum(jnp.where(here, vector[k], 0.0), axis=1, keepdims=True)
            term = weight * basis_ref[k, p]
            value = term if value is None else value + term
        vector_ref[p] = value


def smem():
    return pl.BlockSpec(memory_space=pltpu.SMEM)


def vmem():
    return pl.BlockSpec(memory_space=pltpu.VMEM)


def call(name, kernel, scalars, arrays, outs, scratch, limit, micros):
    many = isinstance(outs, (tuple, list))
    return pl.pallas_call(
        kernel,
        out_shape=outs,
        in_specs=[smem()] * len(scalars) + [vmem()] * len(arrays),
        out_specs=[vmem()] * len(outs) if many else vmem(),
        scratch_shapes=scratch,
        compiler_params=pltpu.CompilerParams(vmem_limit_bytes=limit * MIB),
        name=name,
        cost_estimate=pl.CostEstimate(
            flops=int(micros * 1.1e9), bytes_accessed=0, transcendentals=0
        ),
    )(*scalars, *arrays)


def pairs_of(count, pick):
    return [(source, target) for source in range(count) for target in pick(source) if 0 <= target < count]


def on_device(left_env, right_env, site_tensors, mpo, boundary_mpo, guess, sector_dims):
    width, tile = left_env.shape[2], left_env.shape[-1]
    half = tile // 2
    wide = padded(width)
    states = len(CHARGES)
    sector_count = sector_dims.shape[0]
    sectors = lax.axis_size("sec")
    segments = lax.axis_size("seg")
    prows = packed_rows(width, tile)
    drows = prows - width * half
    odd = lax.rem(lax.axis_index("sec"), 2) == 1
    packed = jax.ShapeDtypeStruct((prows, tile), BF16)
    packed32 = jax.ShapeDtypeStruct((prows, tile), F32)

    def blocks(count):
        return jax.ShapeDtypeStruct((count * width * tile, tile), BF16)

    environ = left_env.reshape(width * tile, tile)
    right = right_env.reshape(width * tile, tile)
    site = site_tensors[0, 0, :, 0]
    site_weights = jnp.transpose(mpo[0, 0], (0, 2, 1)).reshape(width * states, width)
    bound_weights = jnp.transpose(boundary_mpo[0], (0, 2, 1)).reshape(width * states, width)

    swap = pairs_of(sectors, lambda q: [q ^ 1])
    down = pairs_of(sectors, lambda q: [q - 1] if q % 2 else [])
    across = pairs_of(sectors, lambda q: [q + 1] if q % 2 == 0 else [])
    up_two = pairs_of(sectors, lambda q: [q + 2])
    down_two = pairs_of(sectors, lambda q: [q - 2])
    onward = pairs_of(segments, lambda s: [s + 1])
    diag = pltpu.VMEM((drows, tile), F32)

    def mix_scratch(count):
        return [
            pltpu.VMEM((tile, tile), F32),
            pltpu.VMEM((count, packed_height(width), 2 * wide), BF16),
            pltpu.VMEM((wide * (tile + 8), tile), F32),
            pltpu.VMEM((count, wide * (tile + 8), tile), F32),
        ]

    right_packed = call(
        "pack_right", functools.partial(pack_kernel, width, tile), [], [right], packed, [diag], 6, 2
    )
    right_far = lax.ppermute(right_packed, "sec", down_two)
    right_near = lax.ppermute(right_packed, "sec", down)
    environ, right_packed = lax.optimization_barrier((environ, right_packed))
    own, one, two = call(
        "fold", functools.partial(fold_kernel, width, tile),
        [sector_dims], [environ, site, site_weights], (packed32, packed, packed32),
        [
            pltpu.VMEM((tile, states * tile), BF16),
            pltpu.VMEM((states, tile, tile), BF16),
            pltpu.VMEM((tile, tile), F32),
            pltpu.VMEM((states, packed_height(width), 2 * wide), BF16),
            pltpu.VMEM((states, width // 2 * tile, 2 * tile), BF16),
            pltpu.VMEM((states, wide * (half + 8), tile), F32),
            pltpu.VMEM((states, drows, tile), F32),
            pltpu.VMEM((3, wide * (half + 8), tile), F32),
            pltpu.VMEM((3, drows, tile), F32),
        ],
        26, 12,
    )
    one, right_far = lax.optimization_barrier((one, right_far))
    partner = lax.ppermute(one, "sec", swap)
    outgoing = jnp.where(odd, two, two + partner.astype(F32)).astype(BF16)
    right, outgoing = lax.optimization_barrier((right, outgoing))
    arrived = lax.ppermute(outgoing, "sec", up_two)
    right_relay = lax.ppermute(right_far, "sec", across)
    own_mixed = call(
        "mix_own", functools.partial(mix_own_kernel, width, tile), [], [right, bound_weights],
        blocks(1), mix_scratch(1), 12, 5,
    )
    after_mixed = call(
        "mix_after", functools.partial(mix_after_kernel, width, tile), [],
        [right_far, bound_weights], blocks(1), mix_scratch(1) + [diag], 12, 6,
    )
    arrived, own_mixed, after_mixed = lax.optimization_barrier((arrived, own_mixed, after_mixed))
    fresh = own + arrived.astype(F32) + jnp.where(odd, partner.astype(F32), 0.0)
    fresh = fresh.astype(BF16)
    received = lax.ppermute(fresh, "seg", onward)
    next_mixed = call(
        "mix_next", functools.partial(mix_next_kernel, width, tile), [],
        [right_near, right_relay, bound_weights], blocks(2), mix_scratch(2) + [diag], 16, 7,
    )
    new_env = call(
        "unpack_env", functools.partial(unpack_kernel, width, tile), [], [fresh], blocks(1), [diag],
        6, 3,
    )
    received, next_mixed, new_env = lax.optimization_barrier((received, next_mixed, new_env))
    basis, stats = call(
        "lanczos", functools.partial(lanczos_kernel, width, tile),
        [sector_dims], [received, environ, own_mixed, next_mixed, after_mixed, guess[0, :, 0]],
        (
            jax.ShapeDtypeStruct((LANCZOS + 1, states, tile, tile), F32),
            jax.ShapeDtypeStruct((16, 128), F32),
        ),
        [
            pltpu.VMEM((width * tile, tile), BF16),
            pltpu.VMEM((states, tile, width * tile), BF16),
            diag,
        ],
        18, 15,
    )
    stats = lax.psum(stats, "sec")
    entries = float(states * sector_count * tile * tile)
    vector, table = call(
        "finish", functools.partial(finish_kernel, entries), [], [stats, basis],
        (
            jax.ShapeDtypeStruct((states, tile, tile), F32),
            jax.ShapeDtypeStruct((2, LANCZOS), F32),
        ),
        [], 6, 2,
    )
    return new_env.reshape(left_env.shape), vector[None, :, None], jnp.transpose(table)[None]


def solution(mesh):
    placed = (
        P("seg", "sec", None, None, None),
        P("seg", "sec", None, None, None),
        P("seg", None, None, "sec", None, None),
        P("seg", None, None, None, None),
        P("seg", None, None, None),
        P("seg", None, "sec", None, None),
        P(),
    )
    return jax.shard_map(
        on_device,
        mesh=mesh,
        in_specs=placed,
        out_specs=(
            P("seg", "sec", None, None, None),
            P("seg", None, "sec", None, None),
            P("seg", None, None),
        ),
        check_vma=False,
    )
```

```python
import functools

import jax
import jax.numpy as jnp
from jax import lax
from jax.experimental import pallas as pl
from jax.experimental.pallas import tpu as pltpu
from jax.sharding import PartitionSpec as P

LANCZOS = 4
CHARGES = (0, 1, 1, 2)
F32 = jnp.float32
BF16 = jnp.bfloat16
MIB = 1024 * 1024


def padded(count):
    return -(-count // 8) * 8


def packed_height(count):
    return -(-count // 16) * 16


def packed_rows(width, tile):
    return -(-(width * tile // 2 + padded(width)) // 16) * 16


def iotas(shape):
    return lax.broadcasted_iota(jnp.int32, shape, 0), lax.broadcasted_iota(jnp.int32, shape, 1)


def pack_block(block):
    tile = block.shape[0]
    half = tile // 2
    top, low = block[:half], block[half:]
    row, lane = iotas((half, tile))
    turned = pltpu.roll(low, half, 1)
    folded = jnp.where((lane < half) & (row > lane), turned, top)
    diagonal = jnp.sum(jnp.where(lane == row + half, low, 0.0), axis=0, keepdims=True)
    return folded, diagonal


def unpack_block(folded, diagonal):
    half, tile = folded.shape
    row, lane = iotas((half, tile))
    rolled = pltpu.roll(folded, half, 1)
    turned = jnp.transpose(jnp.concatenate([folded, rolled], axis=0))
    top = jnp.where((lane < half) & (row > lane), turned[:half], folded)
    low = jnp.where((lane >= half) & (row > lane - half), rolled, turned[half:])
    low = jnp.where(lane == row + half, diagonal, low)
    return jnp.concatenate([top, low], axis=0)


def partner_of(sector):
    return sector + 1 - 2 * lax.rem(sector, 2)


def live_limits(dims_ref, sector):
    count = dims_ref.shape[0]
    rows = dims_ref[sector]
    columns = []
    for charge in CHARGES:
        target = sector + charge
        columns.append(jnp.where(target < count, dims_ref[jnp.minimum(target, count - 1)], 0))
    return rows, columns


def aligned(index, size):
    return pl.ds(pl.multiple_of(index * size, size), size)


def weight_rows(weight_ref, width, p, square, turned):
    wide = padded(width)
    square[...] = jnp.zeros_like(square)
    square[:width, :width] = weight_ref[pl.ds(p, width, stride=len(CHARGES)), :]
    value = square[...]
    if turned:
        value = jnp.transpose(value)
    high = value.astype(BF16).astype(F32)
    joined = (high + pltpu.roll(value - high, wide, 1)).astype(BF16)
    return joined[: packed_height(width), : 2 * wide]


def doubled(value):
    return jnp.concatenate([value, value], axis=0).astype(BF16)


def prepare_kernel(width, tile, right_ref, environ_ref, site_ref, packed_ref, bundle_ref, diag):
    half = tile // 2
    size = width * tile
    diag[...] = jnp.zeros_like(diag)
    bundle_ref[:size, :] = environ_ref[...]
    for k in range(2):
        bundle_ref[size + k * tile : size + (k + 1) * tile, :] = site_ref[k + 1]
    base = size + 2 * tile
    for w in range(width):
        folded, diagonal = pack_block(right_ref[w * tile : (w + 1) * tile, :].astype(F32))
        folded = folded.astype(BF16)
        packed_ref[w * half : (w + 1) * half, :] = folded
        bundle_ref[base + w * half : base + (w + 1) * half, :] = folded
        diag[w : w + 1, :] = diagonal
    rows = diag[...].astype(BF16)
    packed_ref[width * half :, :] = rows
    bundle_ref[base + width * half :, :] = rows


def unpack_into(width, tile, pitch, read, out_ref, diag):
    half = tile // 2
    diag[...] = read(width * half, diag.shape[0])
    for w in range(width):
        block = unpack_block(read(w * half, half), diag[w : w + 1, :])
        out_ref[w * pitch : w * pitch + tile, :] = block.astype(out_ref.dtype)


def unpack_kernel(width, tile, source_ref, out_ref, diag):
    unpack_into(
        width, tile, tile, lambda at, size: source_ref[at : at + size, :].astype(F32), out_ref, diag
    )


def fold_kernel(
    width, tile, travels, dims_ref, environ_ref, site_ref, bundle_ref, weight_ref, out_ref,
    joined_s, turned_s, square_s, weight_s, half_s, packed_s, diag_s, sums_s, diag_sums_s,
):
    half = tile // 2
    pitch = half + 8
    wide = padded(width)
    size = width * tile
    sector = lax.axis_index("sec")
    partner = partner_of(sector)
    row, lane = iotas((tile, tile))

    def run(own_state, with_partner):
        rows, columns = live_limits(dims_ref, sector)
        live = (row < rows) & (lane < columns[own_state])
        sites = [jnp.where(live, site_ref[own_state].astype(F32), 0.0)]
        states = [own_state]
        if with_partner:
            rows, columns = live_limits(dims_ref, partner)
            for k in range(2):
                live = (row < rows) & (lane < columns[k + 1])
                block = bundle_ref[size + k * tile : size + (k + 1) * tile, :].astype(F32)
                sites.append(jnp.where(live, block, 0.0))
                states.append(k + 1)
        parts = len(states)
        for n in range(parts):
            joined_s[:, n * tile : (n + 1) * tile] = sites[n].astype(BF16)
            turned_s[n] = jnp.transpose(sites[n]).astype(BF16)
            weight_s[n] = weight_rows(weight_ref, width, states[n], square_s, True)
            packed_s[n, width * pitch :, :] = jnp.zeros(((wide - width) * pitch, tile), F32)
            diag_s[n] = jnp.zeros_like(diag_s[n])

        def first(pair, carry):
            for k in range(2):
                at = aligned(pair * 2 + k, tile)
                blocks = [
                    jnp.dot(environ_ref[at, :], joined_s[:, :tile], preferred_element_type=F32)
                ]
                if with_partner:
                    both = jnp.dot(
                        bundle_ref[at, :], joined_s[:, tile:], preferred_element_type=F32
                    )
                    blocks += [both[:, :tile], both[:, tile:]]
                for n in range(parts):
                    half_s[n, aligned(pair, tile), k * tile : (k + 1) * tile] = blocks[n].astype(BF16)
            return carry

        lax.fori_loop(0, width // 2, first, 0, unroll=2)

        def second(pair, carry):
            for n in range(parts):
                both = jnp.dot(
                    turned_s[n], half_s[n, aligned(pair, tile), :], preferred_element_type=F32
                )
                for k in range(2):
                    folded, diagonal = pack_block(both[:, k * tile : (k + 1) * tile])
                    at = pl.multiple_of((pair * 2 + k) * pitch, 8)
                    packed_s[n, pl.ds(at, half), :] = folded
                    diag_s[n, pl.ds(pair * 2 + k, 1), :] = diagonal
            return carry

        lax.fori_loop(0, width // 2, second, 0, unroll=2)

        def mixed(inputs):
            value = None
            for n in range(parts):
                term = jnp.dot(weight_s[n], doubled(inputs[n]), preferred_element_type=F32)
                value = term if value is None else value + term
            return value[:wide]

        def mix(step, carry):
            at = step * 2
            value = mixed([
                jnp.concatenate(
                    [packed_s[n, pl.ds(at + k, wide, stride=pitch), :] for k in range(2)], axis=1
                )
                for n in range(parts)
            ])
            for k in range(2):
                sums_s[pl.ds(at + k, wide, stride=pitch), :] = value[:, k * tile : (k + 1) * tile]
            return carry

        lax.fori_loop(0, half // 2, mix, 0, unroll=4)
        diag_sums_s[...] = jnp.zeros_like(diag_sums_s)
        diag_sums_s[:wide, :] = mixed([diag_s[n, :wide] for n in range(parts)])
        for w in range(width):
            out_ref[w * half : (w + 1) * half, :] = sums_s[w * pitch : w * pitch + half, :].astype(
                out_ref.dtype
            )
        out_ref[width * half :, :] = diag_sums_s[...].astype(out_ref.dtype)

    even = lax.rem(sector, 2) == 0
    own_state = len(CHARGES) - 1 if travels else 0

    @pl.when(even)
    def _():
        run(own_state, travels)

    @pl.when(jnp.logical_not(even))
    def _():
        run(own_state, not travels)


def mix_into(width, tile, weights, wide_s, sums_s, out_ref):
    wide = padded(width)
    pitch = tile + 8
    wide_s[width * pitch :, :] = jnp.zeros_like(wide_s[width * pitch :, :])

    def mix(step, carry):
        at = step * 2
        value = doubled(
            jnp.concatenate(
                [wide_s[pl.ds(at + k, wide, stride=pitch), :] for k in range(2)], axis=1
            )
        )
        for index, weight in enumerate(weights):
            mixed = jnp.dot(weight[...], value, preferred_element_type=F32)[:wide]
            for k in range(2):
                sums_s[index, pl.ds(at + k, wide, stride=pitch), :] = mixed[:, k * tile : (k + 1) * tile]
        return carry

    lax.fori_loop(0, tile // 2, mix, 0, unroll=4)
    for index in range(len(weights)):
        for w in range(width):
            out = (index * width + w) * tile
            out_ref[out : out + tile, :] = sums_s[index, w * pitch : w * pitch + tile, :].astype(BF16)


def mix_own_kernel(width, tile, source_ref, weight_ref, out_ref, square_s, weight_s, wide_s, sums_s):
    pitch = tile + 8
    weight_s[0] = weight_rows(weight_ref, width, 0, square_s, False)
    for w in range(width):
        wide_s[w * pitch : w * pitch + tile, :] = source_ref[w * tile : (w + 1) * tile, :].astype(F32)
    mix_into(width, tile, [weight_s.at[0]], wide_s, sums_s, out_ref)


def mix_next_kernel(
    width, tile, bundle_ref, relay_ref, weight_ref, out_ref, square_s, weight_s, wide_s, sums_s, diag
):
    base = (width + 2) * tile
    even = lax.rem(lax.axis_index("sec"), 2) == 0
    for k in range(2):
        weight_s[k] = weight_rows(weight_ref, width, k + 1, square_s, False)

    def read(at, size):
        near = bundle_ref[base + at : base + at + size, :].astype(F32)
        return jnp.where(even, near, relay_ref[at : at + size, :].astype(F32))

    unpack_into(width, tile, tile + 8, read, wide_s, diag)
    mix_into(width, tile, [weight_s.at[k] for k in range(2)], wide_s, sums_s, out_ref)


def mix_after_kernel(
    width, tile, far_ref, weight_ref, out_ref, square_s, weight_s, wide_s, sums_s, diag
):
    weight_s[0] = weight_rows(weight_ref, width, 3, square_s, False)

    def read(at, size):
        return far_ref[at : at + size, :].astype(F32)

    unpack_into(width, tile, tile + 8, read, wide_s, diag)
    mix_into(width, tile, [weight_s.at[0]], wide_s, sums_s, out_ref)


def total(value):
    return jnp.sum(jnp.sum(value, axis=0, keepdims=True), axis=1, keepdims=True)


def lanczos_kernel(
    width, tile, dims_ref, packed_ref, environ_ref, own_ref, next_ref, after_ref, guess_ref,
    basis_ref, stats_ref, bound_s, first_s, diag,
):
    states = len(CHARGES)
    sector = lax.axis_index("sec")
    segment = lax.axis_index("seg")

    @pl.when(segment == 0)
    def _():
        bound_s[...] = environ_ref[...]

    @pl.when(segment != 0)
    def _():
        unpack_into(
            width, tile, tile, lambda at, size: packed_ref[at : at + size, :].astype(F32), bound_s, diag
        )

    rows, columns = live_limits(dims_ref, sector)
    row, lane = iotas((tile, tile))
    stat_row, stat_lane = iotas(stats_ref.shape)
    stats = jnp.zeros(stats_ref.shape, F32)

    def put(stats, kind, p, value):
        here = (stat_row == kind) & (stat_lane == sector * states + p)
        return jnp.where(here, value, stats)

    def scaled(value):
        square = total(value * value)
        inverse = jnp.where(square > 0.0, lax.rsqrt(square), 0.0)
        return value * inverse, square * inverse

    for p in range(states):
        live = (row < rows) & (lane < columns[p])
        vector, norm = scaled(jnp.where(live, guess_ref[p], 0.0))
        basis_ref[0, p] = vector
        stats = put(stats, 0, p, norm)

    size = width * tile
    rights = [own_ref, next_ref.at[:size, :], next_ref.at[size:, :], after_ref]
    betas = [jnp.zeros((1, 1), F32)] * states
    for j in range(LANCZOS):
        field = jnp.concatenate([basis_ref[j, p] for p in range(states)], axis=1).astype(BF16)
        for w in range(width):
            first = jnp.dot(
                bound_s[w * tile : (w + 1) * tile, :], field, preferred_element_type=F32
            ).astype(BF16)
            for p in range(states):
                first_s[p, :, w * tile : (w + 1) * tile] = first[:, p * tile : (p + 1) * tile]
        for p in range(states):
            live = (row < rows) & (lane < columns[p])
            right = rights[p][...]
            image = jnp.dot(first_s[p], right, preferred_element_type=F32)
            image = jnp.where(live, image, 0.0)
            vector = basis_ref[j, p]
            alpha = total(vector * image)
            image = image - alpha * vector
            if j > 0:
                image = image - betas[p] * basis_ref[j - 1, p]
            following, beta = scaled(image)
            basis_ref[j + 1, p] = following
            betas[p] = beta
            stats = put(stats, 1 + 2 * j, p, alpha)
            stats = put(stats, 2 + 2 * j, p, beta)
    stats_ref[...] = stats


def finish_kernel(entries, stats_ref, basis_ref, vector_ref, table_ref):
    states = len(CHARGES)
    sector = lax.axis_index("sec")
    stats = stats_ref[...]
    alphas = [stats[1 + 2 * j : 2 + 2 * j, :] for j in range(LANCZOS)]
    betas = [stats[2 + 2 * j : 3 + 2 * j, :] for j in range(LANCZOS)]

    def mean(left, right):
        products = left[0] * right[0]
        for x, y in zip(left[1:], right[1:]):
            products = products + x * y
        return jnp.sum(products, axis=1, keepdims=True) / entries

    start = [stats[0:1, :]]
    vector = [start[0] / jnp.sqrt(mean(start, start) + 1e-06)]
    previous = []
    beta = jnp.zeros((1, 1), F32)
    table_row, table_column = iotas(table_ref.shape)
    table = jnp.zeros(table_ref.shape, F32)
    for j in range(LANCZOS):
        image = []
        for k in range(j + 2):
            term = None
            if k > 0:
                term = betas[k - 1] * vector[k - 1]
            if k <= j:
                more = alphas[k] * vector[k]
                term = more if term is None else term + more
            if k + 1 <= j:
                term = term + betas[k] * vector[k + 1]
            image.append(term)
        alpha = mean(vector, image[: j + 1])
        for k in range(j + 1):
            image[k] = image[k] - alpha * vector[k]
        for k in range(j):
            image[k] = image[k] - beta * previous[k]
        beta = jnp.sqrt(mean(image, image) + 1e-06)
        previous = vector
        vector = [value / beta for value in image]
        table = jnp.where((table_row == 0) & (table_column == j), alpha, table)
        table = jnp.where((table_row == 1) & (table_column == j), beta, table)
    table_ref[...] = table
    lane = lax.broadcasted_iota(jnp.int32, (1, stats.shape[1]), 1)
    for p in range(states):
        value = None
        here = lane == sector * states + p
        for k in range(LANCZOS + 1):
            weight = jnp.sum(jnp.where(here, vector[k], 0.0), axis=1, keepdims=True)
            term = weight * basis_ref[k, p]
            value = term if value is None else value + term
        vector_ref[p] = value


def smem():
    return pl.BlockSpec(memory_space=pltpu.SMEM)


def vmem():
    return pl.BlockSpec(memory_space=pltpu.VMEM)


def call(name, kernel, scalars, arrays, outs, scratch, limit, micros):
    many = isinstance(outs, (tuple, list))
    return pl.pallas_call(
        kernel,
        out_shape=outs,
        in_specs=[smem()] * len(scalars) + [vmem()] * len(arrays),
        out_specs=[vmem()] * len(outs) if many else vmem(),
        scratch_shapes=scratch,
        compiler_params=pltpu.CompilerParams(vmem_limit_bytes=limit * MIB),
        name=name,
        cost_estimate=pl.CostEstimate(
            flops=int(micros * 1.1e9), bytes_accessed=0, transcendentals=0
        ),
    )(*scalars, *arrays)


def pairs_of(count, pick):
    return [(source, target) for source in range(count) for target in pick(source) if 0 <= target < count]


def sum_over(value, axis):
    count = lax.axis_size(axis)
    if count & (count - 1):
        return lax.psum(value, axis)
    step = 1
    while step < count:
        value = value + lax.ppermute(value, axis, [(q, q ^ step) for q in range(count)])
        step *= 2
    return value


def on_device(left_env, right_env, site_tensors, mpo, boundary_mpo, guess, sector_dims):
    width, tile = left_env.shape[2], left_env.shape[-1]
    half = tile // 2
    wide = padded(width)
    states = len(CHARGES)
    sector_count = sector_dims.shape[0]
    sectors = lax.axis_size("sec")
    segments = lax.axis_size("seg")
    prows = packed_rows(width, tile)
    drows = prows - width * half
    packed = jax.ShapeDtypeStruct((prows, tile), BF16)
    packed32 = jax.ShapeDtypeStruct((prows, tile), F32)

    def blocks(count):
        return jax.ShapeDtypeStruct((count * width * tile, tile), BF16)

    environ = left_env.reshape(width * tile, tile)
    right = right_env.reshape(width * tile, tile)
    site = site_tensors[0, 0, :, 0]
    site_weights = jnp.transpose(mpo[0, 0], (0, 2, 1)).reshape(width * states, width)
    bound_weights = jnp.transpose(boundary_mpo[0], (0, 2, 1)).reshape(width * states, width)

    swap = pairs_of(sectors, lambda q: [q ^ 1])
    across = pairs_of(sectors, lambda q: [q + 1] if q % 2 == 0 else [])
    up_two = pairs_of(sectors, lambda q: [q + 2])
    down_two = pairs_of(sectors, lambda q: [q - 2])
    onward = pairs_of(segments, lambda s: [s + 1])
    diag = pltpu.VMEM((drows, tile), F32)

    def mix_scratch(count):
        return [
            pltpu.VMEM((tile, tile), F32),
            pltpu.VMEM((count, packed_height(width), 2 * wide), BF16),
            pltpu.VMEM((wide * (tile + 8), tile), F32),
            pltpu.VMEM((count, wide * (tile + 8), tile), F32),
        ]

    right_packed, bundle = call(
        "prepare", functools.partial(prepare_kernel, width, tile), [], [right, environ, site],
        (packed, jax.ShapeDtypeStruct((width * tile + 2 * tile + prows, tile), BF16)), [diag], 10, 2,
    )
    bundle = lax.ppermute(bundle, "sec", swap)
    right_far = lax.ppermute(right_packed, "sec", down_two)
    fold_scratch = [
        pltpu.VMEM((tile, 3 * tile), BF16),
        pltpu.VMEM((3, tile, tile), BF16),
        pltpu.VMEM((tile, tile), F32),
        pltpu.VMEM((3, packed_height(width), 2 * wide), BF16),
        pltpu.VMEM((3, width // 2 * tile, 2 * tile), BF16),
        pltpu.VMEM((3, wide * (half + 8), tile), F32),
        pltpu.VMEM((3, drows, tile), F32),
        pltpu.VMEM((wide * (half + 8), tile), F32),
        pltpu.VMEM((drows, tile), F32),
    ]
    outgoing = call(
        "fold_up", functools.partial(fold_kernel, width, tile, True),
        [sector_dims], [environ, site, bundle, site_weights], packed, fold_scratch, 20, 12,
    )
    outgoing, right_far, right = lax.optimization_barrier((outgoing, right_far, right))
    arrived = lax.ppermute(outgoing, "sec", up_two)
    kept = call(
        "fold_own", functools.partial(fold_kernel, width, tile, False),
        [sector_dims], [environ, site, bundle, site_weights], packed32, fold_scratch, 20, 8,
    )
    kept, right_far, right = lax.optimization_barrier((kept, right_far, right))
    right_relay = lax.ppermute(right_far, "sec", across)
    own_mixed = call(
        "mix_own", functools.partial(mix_own_kernel, width, tile), [], [right, bound_weights],
        blocks(1), mix_scratch(1), 12, 5,
    )
    after_mixed = call(
        "mix_after", functools.partial(mix_after_kernel, width, tile), [],
        [right_far, bound_weights], blocks(1), mix_scratch(1) + [diag], 12, 6,
    )
    arrived, own_mixed, after_mixed = lax.optimization_barrier((arrived, own_mixed, after_mixed))
    fresh = (kept + arrived.astype(F32)).astype(BF16)
    received = lax.ppermute(fresh, "seg", onward)
    next_mixed = call(
        "mix_next", functools.partial(mix_next_kernel, width, tile), [],
        [bundle, right_relay, bound_weights], blocks(2), mix_scratch(2) + [diag], 16, 7,
    )
    new_env = call(
        "unpack_env", functools.partial(unpack_kernel, width, tile), [], [fresh], blocks(1), [diag],
        6, 3,
    )
    received, next_mixed, new_env = lax.optimization_barrier((received, next_mixed, new_env))
    basis, stats = call(
        "lanczos", functools.partial(lanczos_kernel, width, tile),
        [sector_dims], [received, environ, own_mixed, next_mixed, after_mixed, guess[0, :, 0]],
        (
            jax.ShapeDtypeStruct((LANCZOS + 1, states, tile, tile), F32),
            jax.ShapeDtypeStruct((16, 128), F32),
        ),
        [
            pltpu.VMEM((width * tile, tile), BF16),
            pltpu.VMEM((states, tile, width * tile), BF16),
            diag,
        ],
        18, 15,
    )
    stats = sum_over(stats, "sec")
    entries = float(states * sector_count * tile * tile)
    vector, table = call(
        "finish", functools.partial(finish_kernel, entries), [], [stats, basis],
        (
            jax.ShapeDtypeStruct((states, tile, tile), F32),
            jax.ShapeDtypeStruct((2, LANCZOS), F32),
        ),
        [], 6, 2,
    )
    return new_env.reshape(left_env.shape), vector[None, :, None], jnp.transpose(table)[None]


def solution(mesh):
    placed = (
        P("seg", "sec", None, None, None),
        P("seg", "sec", None, None, None),
        P("seg", None, None, "sec", None, None),
        P("seg", None, None, None, None),
        P("seg", None, None, None),
        P("seg", None, "sec", None, None),
        P(),
    )
    return jax.shard_map(
        on_device,
        mesh=mesh,
        in_specs=placed,
        out_specs=(
            P("seg", "sec", None, None, None),
            P("seg", None, "sec", None, None),
            P("seg", None, None),
        ),
        check_vma=False,
    )
```

```python
import functools

import jax
import jax.numpy as jnp
from jax import lax
from jax.experimental import pallas as pl
from jax.experimental.pallas import tpu as pltpu
from jax.sharding import PartitionSpec as P

LANCZOS = 4
CHARGES = (0, 1, 1, 2)
F32 = jnp.float32
BF16 = jnp.bfloat16
MIB = 1024 * 1024


def padded(count):
    return -(-count // 8) * 8


def packed_height(count):
    return -(-count // 16) * 16


def packed_rows(width, tile):
    return -(-(width * tile // 2 + padded(width)) // 16) * 16


def iotas(shape):
    return lax.broadcasted_iota(jnp.int32, shape, 0), lax.broadcasted_iota(jnp.int32, shape, 1)


def pack_block(block):
    tile = block.shape[0]
    half = tile // 2
    top, low = block[:half], block[half:]
    row, lane = iotas((half, tile))
    turned = pltpu.roll(low, half, 1)
    folded = jnp.where((lane < half) & (row > lane), turned, top)
    diagonal = jnp.sum(jnp.where(lane == row + half, low, 0.0), axis=0, keepdims=True)
    return folded, diagonal


def unpack_block(folded, diagonal):
    half, tile = folded.shape
    row, lane = iotas((half, tile))
    rolled = pltpu.roll(folded, half, 1)
    turned = jnp.transpose(jnp.concatenate([folded, rolled], axis=0))
    top = jnp.where((lane < half) & (row > lane), turned[:half], folded)
    low = jnp.where((lane >= half) & (row > lane - half), rolled, turned[half:])
    low = jnp.where(lane == row + half, diagonal, low)
    return jnp.concatenate([top, low], axis=0)


def partner_of(sector):
    return sector + 1 - 2 * lax.rem(sector, 2)


def live_limits(dims_ref, sector):
    count = dims_ref.shape[0]
    rows = dims_ref[sector]
    columns = []
    for charge in CHARGES:
        target = sector + charge
        columns.append(jnp.where(target < count, dims_ref[jnp.minimum(target, count - 1)], 0))
    return rows, columns


def weight_rows(weight_ref, width, p, square, turned):
    wide = padded(width)
    square[...] = jnp.zeros_like(square)
    square[:width, :width] = weight_ref[pl.ds(p, width, stride=len(CHARGES)), :]
    value = square[...]
    if turned:
        value = jnp.transpose(value)
    high = value.astype(BF16).astype(F32)
    joined = (high + pltpu.roll(value - high, wide, 1)).astype(BF16)
    return joined[: packed_height(width), : 2 * wide]


def doubled(value):
    return jnp.concatenate([value, value], axis=0).astype(BF16)


def pack_kernel(width, tile, source_ref, out_ref, diag):
    half = tile // 2
    diag[...] = jnp.zeros_like(diag)
    for w in range(width):
        folded, diagonal = pack_block(source_ref[w * tile : (w + 1) * tile, :].astype(F32))
        out_ref[w * half : (w + 1) * half, :] = folded.astype(BF16)
        diag[w : w + 1, :] = diagonal
    out_ref[width * half :, :] = diag[...].astype(BF16)


def unpack_into(width, tile, pitch, read, out_ref, diag):
    half = tile // 2
    diag[...] = read(width * half, diag.shape[0])
    for w in range(width):
        block = unpack_block(read(w * half, half), diag[w : w + 1, :])
        out_ref[w * pitch : w * pitch + tile, :] = block.astype(out_ref.dtype)


def unpack_kernel(width, tile, source_ref, out_ref, diag):
    unpack_into(
        width, tile, tile, lambda at, size: source_ref[at : at + size, :].astype(F32), out_ref, diag
    )


def fold_kernel(
    width, tile, travels, dims_ref, environ_ref, site_ref, far_environ_ref, far_site_ref, weight_ref, out_ref,
    joined_s, turned_s, square_s, weight_s, half_s, packed_s, diag_s, sums_s, diag_sums_s,
):
    half = tile // 2
    pitch = half + 8
    wide = padded(width)
    sector = lax.axis_index("sec")
    partner = partner_of(sector)
    row, lane = iotas((tile, tile))

    def run(own_state, with_partner):
        rows, columns = live_limits(dims_ref, sector)
        live = (row < rows) & (lane < columns[own_state])
        sites = [jnp.where(live, site_ref[own_state].astype(F32), 0.0)]
        states = [own_state]
        if with_partner:
            rows, columns = live_limits(dims_ref, partner)
            for k in range(2):
                live = (row < rows) & (lane < columns[k + 1])
                sites.append(jnp.where(live, far_site_ref[k + 1].astype(F32), 0.0))
                states.append(k + 1)
        parts = len(states)
        for n in range(parts):
            joined_s[:, n * tile : (n + 1) * tile] = sites[n].astype(BF16)
            turned_s[n] = jnp.transpose(sites[n]).astype(BF16)
            weight_s[n] = weight_rows(weight_ref, width, states[n], square_s, True)
            packed_s[n, width * pitch :, :] = jnp.zeros(((wide - width) * pitch, tile), F32)
            diag_s[n] = jnp.zeros_like(diag_s[n])

        for pair in range(width // 2):
            at = slice(pair * tile, (pair + 1) * tile)
            for k in range(2):
                here = slice((pair * 2 + k) * tile, (pair * 2 + k + 1) * tile)
                blocks = [
                    jnp.dot(environ_ref[here, :], joined_s[:, :tile], preferred_element_type=F32)
                ]
                if with_partner:
                    both = jnp.dot(
                        far_environ_ref[here, :], joined_s[:, tile:], preferred_element_type=F32
                    )
                    blocks += [both[:, :tile], both[:, tile:]]
                for n in range(parts):
                    half_s[n, at, k * tile : (k + 1) * tile] = blocks[n].astype(BF16)
            for n in range(parts):
                both = jnp.dot(turned_s[n], half_s[n, at, :], preferred_element_type=F32)
                for k in range(2):
                    w = pair * 2 + k
                    folded, diagonal = pack_block(both[:, k * tile : (k + 1) * tile])
                    packed_s[n, w * pitch : w * pitch + half, :] = folded
                    diag_s[n, w : w + 1, :] = diagonal

        def mixed(inputs):
            value = None
            for n in range(parts):
                term = jnp.dot(weight_s[n], doubled(inputs[n]), preferred_element_type=F32)
                value = term if value is None else value + term
            return value[:wide]

        for at in range(0, half, 2):
            value = mixed([
                jnp.concatenate(
                    [packed_s[n, pl.ds(at + k, wide, stride=pitch), :] for k in range(2)], axis=1
                )
                for n in range(parts)
            ])
            for k in range(2):
                sums_s[pl.ds(at + k, wide, stride=pitch), :] = value[:, k * tile : (k + 1) * tile]
        diag_sums_s[...] = jnp.zeros_like(diag_sums_s)
        diag_sums_s[:wide, :] = mixed([diag_s[n, :wide] for n in range(parts)])
        for w in range(width):
            out_ref[w * half : (w + 1) * half, :] = sums_s[w * pitch : w * pitch + half, :].astype(
                out_ref.dtype
            )
        out_ref[width * half :, :] = diag_sums_s[...].astype(out_ref.dtype)

    even = lax.rem(sector, 2) == 0
    own_state = len(CHARGES) - 1 if travels else 0

    @pl.when(even)
    def _():
        run(own_state, travels)

    @pl.when(jnp.logical_not(even))
    def _():
        run(own_state, not travels)


def mix_into(width, tile, weights, wide_s, sums_s, out_ref):
    wide = padded(width)
    pitch = tile + 8
    wide_s[width * pitch :, :] = jnp.zeros_like(wide_s[width * pitch :, :])

    for at in range(0, tile, 2):
        value = doubled(
            jnp.concatenate(
                [wide_s[pl.ds(at + k, wide, stride=pitch), :] for k in range(2)], axis=1
            )
        )
        for index, weight in enumerate(weights):
            mixed = jnp.dot(weight[...], value, preferred_element_type=F32)[:wide]
            for k in range(2):
                sums_s[index, pl.ds(at + k, wide, stride=pitch), :] = mixed[:, k * tile : (k + 1) * tile]
    for index in range(len(weights)):
        for w in range(width):
            out = (index * width + w) * tile
            out_ref[out : out + tile, :] = sums_s[index, w * pitch : w * pitch + tile, :].astype(BF16)


def mix_own_kernel(width, tile, source_ref, weight_ref, out_ref, square_s, weight_s, wide_s, sums_s):
    pitch = tile + 8
    weight_s[0] = weight_rows(weight_ref, width, 0, square_s, False)
    for w in range(width):
        wide_s[w * pitch : w * pitch + tile, :] = source_ref[w * tile : (w + 1) * tile, :].astype(F32)
    mix_into(width, tile, [weight_s.at[0]], wide_s, sums_s, out_ref)


def mix_next_kernel(
    width, tile, near_ref, relay_ref, weight_ref, out_ref, square_s, weight_s, wide_s, sums_s, diag
):
    even = lax.rem(lax.axis_index("sec"), 2) == 0
    for k in range(2):
        weight_s[k] = weight_rows(weight_ref, width, k + 1, square_s, False)

    def read(at, size):
        near = near_ref[at : at + size, :].astype(F32)
        return jnp.where(even, near, relay_ref[at : at + size, :].astype(F32))

    unpack_into(width, tile, tile + 8, read, wide_s, diag)
    mix_into(width, tile, [weight_s.at[k] for k in range(2)], wide_s, sums_s, out_ref)


def mix_after_kernel(
    width, tile, far_ref, weight_ref, out_ref, square_s, weight_s, wide_s, sums_s, diag
):
    weight_s[0] = weight_rows(weight_ref, width, 3, square_s, False)

    def read(at, size):
        return far_ref[at : at + size, :].astype(F32)

    unpack_into(width, tile, tile + 8, read, wide_s, diag)
    mix_into(width, tile, [weight_s.at[0]], wide_s, sums_s, out_ref)


def total(value):
    return jnp.sum(jnp.sum(value, axis=0, keepdims=True), axis=1, keepdims=True)


def lanczos_kernel(
    width, tile, dims_ref, packed_ref, environ_ref, own_ref, next_ref, after_ref, guess_ref,
    basis_ref, stats_ref, bound_s, first_s, diag,
):
    states = len(CHARGES)
    sector = lax.axis_index("sec")
    segment = lax.axis_index("seg")

    @pl.when(segment == 0)
    def _():
        bound_s[...] = environ_ref[...]

    @pl.when(segment != 0)
    def _():
        unpack_into(
            width, tile, tile, lambda at, size: packed_ref[at : at + size, :].astype(F32), bound_s, diag
        )

    rows, columns = live_limits(dims_ref, sector)
    row, lane = iotas((tile, tile))
    stat_row, stat_lane = iotas(stats_ref.shape)
    stats = jnp.zeros(stats_ref.shape, F32)

    def put(stats, kind, p, value):
        here = (stat_row == kind) & (stat_lane == sector * states + p)
        return jnp.where(here, value, stats)

    def scaled(value):
        square = total(value * value)
        inverse = jnp.where(square > 0.0, lax.rsqrt(square), 0.0)
        return value * inverse, square * inverse

    for p in range(states):
        live = (row < rows) & (lane < columns[p])
        vector, norm = scaled(jnp.where(live, guess_ref[p], 0.0))
        basis_ref[0, p] = vector
        stats = put(stats, 0, p, norm)

    size = width * tile
    rights = [own_ref, next_ref.at[:size, :], next_ref.at[size:, :], after_ref]
    betas = [jnp.zeros((1, 1), F32)] * states
    for j in range(LANCZOS):
        field = jnp.concatenate([basis_ref[j, p] for p in range(states)], axis=1).astype(BF16)
        for w in range(width):
            first = jnp.dot(
                bound_s[w * tile : (w + 1) * tile, :], field, preferred_element_type=F32
            ).astype(BF16)
            for p in range(states):
                first_s[p, :, w * tile : (w + 1) * tile] = first[:, p * tile : (p + 1) * tile]
        for p in range(states):
            live = (row < rows) & (lane < columns[p])
            right = rights[p][...]
            image = jnp.dot(first_s[p], right, preferred_element_type=F32)
            image = jnp.where(live, image, 0.0)
            vector = basis_ref[j, p]
            alpha = total(vector * image)
            image = image - alpha * vector
            if j > 0:
                image = image - betas[p] * basis_ref[j - 1, p]
            following, beta = scaled(image)
            basis_ref[j + 1, p] = following
            betas[p] = beta
            stats = put(stats, 1 + 2 * j, p, alpha)
            stats = put(stats, 2 + 2 * j, p, beta)
    stats_ref[...] = stats


def finish_kernel(entries, stats_ref, basis_ref, vector_ref, table_ref):
    states = len(CHARGES)
    sector = lax.axis_index("sec")
    stats = stats_ref[0]
    for q in range(1, stats_ref.shape[0]):
        stats = stats + stats_ref[q]
    alphas = [stats[1 + 2 * j : 2 + 2 * j, :] for j in range(LANCZOS)]
    betas = [stats[2 + 2 * j : 3 + 2 * j, :] for j in range(LANCZOS)]

    def mean(left, right):
        products = left[0] * right[0]
        for x, y in zip(left[1:], right[1:]):
            products = products + x * y
        return jnp.sum(products, axis=1, keepdims=True) / entries

    start = [stats[0:1, :]]
    vector = [start[0] / jnp.sqrt(mean(start, start) + 1e-06)]
    previous = []
    beta = jnp.zeros((1, 1), F32)
    table_row, table_column = iotas(table_ref.shape)
    table = jnp.zeros(table_ref.shape, F32)
    for j in range(LANCZOS):
        image = []
        for k in range(j + 2):
            term = None
            if k > 0:
                term = betas[k - 1] * vector[k - 1]
            if k <= j:
                more = alphas[k] * vector[k]
                term = more if term is None else term + more
            if k + 1 <= j:
                term = term + betas[k] * vector[k + 1]
            image.append(term)
        alpha = mean(vector, image[: j + 1])
        for k in range(j + 1):
            image[k] = image[k] - alpha * vector[k]
        for k in range(j):
            image[k] = image[k] - beta * previous[k]
        beta = jnp.sqrt(mean(image, image) + 1e-06)
        previous = vector
        vector = [value / beta for value in image]
        table = jnp.where((table_row == 0) & (table_column == j), alpha, table)
        table = jnp.where((table_row == 1) & (table_column == j), beta, table)
    table_ref[...] = table
    lane = lax.broadcasted_iota(jnp.int32, (1, stats.shape[1]), 1)
    for p in range(states):
        value = None
        here = lane == sector * states + p
        for k in range(LANCZOS + 1):
            weight = jnp.sum(jnp.where(here, vector[k], 0.0), axis=1, keepdims=True)
            term = weight * basis_ref[k, p]
            value = term if value is None else value + term
        vector_ref[p] = value


def smem():
    return pl.BlockSpec(memory_space=pltpu.SMEM)


def vmem():
    return pl.BlockSpec(memory_space=pltpu.VMEM)


def call(name, kernel, scalars, arrays, outs, scratch, limit, micros):
    many = isinstance(outs, (tuple, list))
    return pl.pallas_call(
        kernel,
        out_shape=outs,
        in_specs=[smem()] * len(scalars) + [vmem()] * len(arrays),
        out_specs=[vmem()] * len(outs) if many else vmem(),
        scratch_shapes=scratch,
        compiler_params=pltpu.CompilerParams(vmem_limit_bytes=limit * MIB),
        name=name,
        cost_estimate=pl.CostEstimate(
            flops=int(micros * 1.1e9), bytes_accessed=0, transcendentals=0
        ),
    )(*scalars, *arrays)


def pairs_of(count, pick):
    return [(source, target) for source in range(count) for target in pick(source) if 0 <= target < count]


def gathered(value, axis):
    count = lax.axis_size(axis)
    return lax.all_to_all(jnp.broadcast_to(value, (count,) + value.shape), axis, 0, 0)


def on_device(left_env, right_env, site_tensors, mpo, boundary_mpo, guess, sector_dims):
    width, tile = left_env.shape[2], left_env.shape[-1]
    half = tile // 2
    wide = padded(width)
    states = len(CHARGES)
    sector_count = sector_dims.shape[0]
    sectors = lax.axis_size("sec")
    segments = lax.axis_size("seg")
    prows = packed_rows(width, tile)
    drows = prows - width * half
    packed = jax.ShapeDtypeStruct((prows, tile), BF16)
    packed32 = jax.ShapeDtypeStruct((prows, tile), F32)

    def blocks(count):
        return jax.ShapeDtypeStruct((count * width * tile, tile), BF16)

    environ = left_env.reshape(width * tile, tile)
    right = right_env.reshape(width * tile, tile)
    site = site_tensors[0, 0, :, 0]
    site_weights = jnp.transpose(mpo[0, 0], (0, 2, 1)).reshape(width * states, width)
    bound_weights = jnp.transpose(boundary_mpo[0], (0, 2, 1)).reshape(width * states, width)

    swap = pairs_of(sectors, lambda q: [q ^ 1])
    across = pairs_of(sectors, lambda q: [q + 1] if q % 2 == 0 else [])
    up_two = pairs_of(sectors, lambda q: [q + 2])
    down_two = pairs_of(sectors, lambda q: [q - 2])
    onward = pairs_of(segments, lambda s: [s + 1])
    diag = pltpu.VMEM((drows, tile), F32)

    def mix_scratch(count):
        return [
            pltpu.VMEM((tile, tile), F32),
            pltpu.VMEM((count, packed_height(width), 2 * wide), BF16),
            pltpu.VMEM((wide * (tile + 8), tile), F32),
            pltpu.VMEM((count, wide * (tile + 8), tile), F32),
        ]

    far_environ = lax.ppermute(environ, "sec", swap)
    far_site = lax.ppermute(site, "sec", swap)
    right_packed = call(
        "pack_right", functools.partial(pack_kernel, width, tile), [], [right], packed, [diag], 6, 1
    )
    right_far = lax.ppermute(right_packed, "sec", down_two)
    fold_scratch = [
        pltpu.VMEM((tile, 3 * tile), BF16),
        pltpu.VMEM((3, tile, tile), BF16),
        pltpu.VMEM((tile, tile), F32),
        pltpu.VMEM((3, packed_height(width), 2 * wide), BF16),
        pltpu.VMEM((3, width // 2 * tile, 2 * tile), BF16),
        pltpu.VMEM((3, wide * (half + 8), tile), F32),
        pltpu.VMEM((3, drows, tile), F32),
        pltpu.VMEM((wide * (half + 8), tile), F32),
        pltpu.VMEM((drows, tile), F32),
    ]
    outgoing = call(
        "fold_up", functools.partial(fold_kernel, width, tile, True),
        [sector_dims], [environ, site, far_environ, far_site, site_weights], packed, fold_scratch, 20, 12,
    )
    arrived = lax.ppermute(outgoing, "sec", up_two)
    outgoing, right_far, far_environ = lax.optimization_barrier((outgoing, right_far, far_environ))
    kept = call(
        "fold_own", functools.partial(fold_kernel, width, tile, False),
        [sector_dims], [environ, site, far_environ, far_site, site_weights], packed32, fold_scratch, 20, 8,
    )
    kept, right_far, right, right_packed = lax.optimization_barrier(
        (kept, right_far, right, right_packed)
    )
    right_near = lax.ppermute(right_packed, "sec", swap)
    right_relay = lax.ppermute(right_far, "sec", across)
    own_mixed = call(
        "mix_own", functools.partial(mix_own_kernel, width, tile), [], [right, bound_weights],
        blocks(1), mix_scratch(1), 12, 5,
    )
    after_mixed = call(
        "mix_after", functools.partial(mix_after_kernel, width, tile), [],
        [right_far, bound_weights], blocks(1), mix_scratch(1) + [diag], 12, 6,
    )
    arrived, own_mixed, after_mixed = lax.optimization_barrier((arrived, own_mixed, after_mixed))
    fresh = (kept + arrived.astype(F32)).astype(BF16)
    received = lax.ppermute(fresh, "seg", onward)
    next_mixed = call(
        "mix_next", functools.partial(mix_next_kernel, width, tile), [],
        [right_near, right_relay, bound_weights], blocks(2), mix_scratch(2) + [diag], 16, 7,
    )
    new_env = call(
        "unpack_env", functools.partial(unpack_kernel, width, tile), [], [fresh], blocks(1), [diag],
        6, 3,
    )
    received, next_mixed, new_env = lax.optimization_barrier((received, next_mixed, new_env))
    basis, stats = call(
        "lanczos", functools.partial(lanczos_kernel, width, tile),
        [sector_dims], [received, environ, own_mixed, next_mixed, after_mixed, guess[0, :, 0]],
        (
            jax.ShapeDtypeStruct((LANCZOS + 1, states, tile, tile), F32),
            jax.ShapeDtypeStruct((16, 128), F32),
        ),
        [
            pltpu.VMEM((width * tile, tile), BF16),
            pltpu.VMEM((states, tile, width * tile), BF16),
            diag,
        ],
        18, 15,
    )
    stats = gathered(stats, "sec")
    entries = float(states * sector_count * tile * tile)
    vector, table = call(
        "finish", functools.partial(finish_kernel, entries), [], [stats, basis],
        (
            jax.ShapeDtypeStruct((states, tile, tile), F32),
            jax.ShapeDtypeStruct((2, LANCZOS), F32),
        ),
        [], 6, 2,
    )
    return new_env.reshape(left_env.shape), vector[None, :, None], jnp.transpose(table)[None]


def solution(mesh):
    placed = (
        P("seg", "sec", None, None, None),
        P("seg", "sec", None, None, None),
        P("seg", None, None, "sec", None, None),
        P("seg", None, None, None, None),
        P("seg", None, None, None),
        P("seg", None, "sec", None, None),
        P(),
    )
    return jax.shard_map(
        on_device,
        mesh=mesh,
        in_specs=placed,
        out_specs=(
            P("seg", "sec", None, None, None),
            P("seg", None, "sec", None, None),
            P("seg", None, None),
        ),
        check_vma=False,
    )
```

```python
import functools

import jax
import jax.numpy as jnp
from jax import lax
from jax.experimental import pallas as pl
from jax.experimental.pallas import tpu as pltpu
from jax.sharding import PartitionSpec as P

LANCZOS = 4
CHARGES = (0, 1, 1, 2)
F32 = jnp.float32
BF16 = jnp.bfloat16
MIB = 1024 * 1024


def padded(count):
    return -(-count // 8) * 8


def packed_height(count):
    return -(-count // 16) * 16


def packed_rows(count, tile):
    return count * tile // 2 + packed_height(count)


def chunks_of(width):
    first = -(-width // 4) * 2
    return (0, first), (first, width - first)


def iotas(shape):
    return lax.broadcasted_iota(jnp.int32, shape, 0), lax.broadcasted_iota(jnp.int32, shape, 1)


def pack_block(block):
    tile = block.shape[0]
    half = tile // 2
    top, low = block[:half], block[half:]
    row, lane = iotas((half, tile))
    turned = pltpu.roll(low, half, 1)
    folded = jnp.where((lane < half) & (row > lane), turned, top)
    diagonal = jnp.sum(jnp.where(lane == row + half, low, 0.0), axis=0, keepdims=True)
    return folded, diagonal


def unpack_block(folded, diagonal):
    half, tile = folded.shape
    row, lane = iotas((half, tile))
    rolled = pltpu.roll(folded, half, 1)
    turned = jnp.transpose(jnp.concatenate([folded, rolled], axis=0))
    top = jnp.where((lane < half) & (row > lane), turned[:half], folded)
    low = jnp.where((lane >= half) & (row > lane - half), rolled, turned[half:])
    low = jnp.where(lane == row + half, diagonal, low)
    return jnp.concatenate([top, low], axis=0)


def partner_of(sector):
    return sector + 1 - 2 * lax.rem(sector, 2)


def live_limits(dims_ref, sector):
    count = dims_ref.shape[0]
    rows = dims_ref[sector]
    columns = []
    for charge in CHARGES:
        target = sector + charge
        columns.append(jnp.where(target < count, dims_ref[jnp.minimum(target, count - 1)], 0))
    return rows, columns


def weight_rows(weight_ref, width, p, square, turned):
    wide = padded(width)
    square[...] = jnp.zeros_like(square)
    square[:width, :width] = weight_ref[pl.ds(p, width, stride=len(CHARGES)), :]
    value = square[...]
    if turned:
        value = jnp.transpose(value)
    high = value.astype(BF16).astype(F32)
    joined = (high + pltpu.roll(value - high, wide, 1)).astype(BF16)
    return joined[: packed_height(width), : 2 * wide]


def doubled(value):
    return jnp.concatenate([value, value], axis=0).astype(BF16)


def pack_kernel(width, tile, source_ref, out_ref, diag):
    half = tile // 2
    diag[...] = jnp.zeros_like(diag)
    for w in range(width):
        folded, diagonal = pack_block(source_ref[w * tile : (w + 1) * tile, :].astype(F32))
        out_ref[w * half : (w + 1) * half, :] = folded.astype(BF16)
        diag[w : w + 1, :] = diagonal
    out_ref[width * half :, :] = diag[...].astype(BF16)


def unpack_into(count, tile, read, write, diag):
    half = tile // 2
    size = packed_height(count)
    diag[:size, :] = read(count * half, size)
    for w in range(count):
        write(w, unpack_block(read(w * half, half), diag[w : w + 1, :]))


def reader(ref):
    return lambda at, size: ref[at : at + size, :].astype(F32)


def unpack_kernel(width, tile, early_ref, late_ref, out_ref, diag):
    for (first, count), ref in zip(chunks_of(width), (early_ref, late_ref)):

        def write(w, block, first=first):
            out_ref[(first + w) * tile : (first + w + 1) * tile, :] = block.astype(BF16)

        unpack_into(count, tile, reader(ref), write, diag)


def fold_kernel(
    width, tile, travels, dims_ref, environ_ref, site_ref, far_environ_ref, far_site_ref, weight_ref, early_ref, late_ref,
    joined_s, turned_s, square_s, weight_s, half_s, packed_s, diag_s, sums_s, diag_sums_s,
):
    half = tile // 2
    pitch = half + 8
    wide = padded(width)
    sector = lax.axis_index("sec")
    partner = partner_of(sector)
    row, lane = iotas((tile, tile))

    def run(own_state, with_partner):
        rows, columns = live_limits(dims_ref, sector)
        live = (row < rows) & (lane < columns[own_state])
        sites = [jnp.where(live, site_ref[own_state].astype(F32), 0.0)]
        states = [own_state]
        if with_partner:
            rows, columns = live_limits(dims_ref, partner)
            for k in range(2):
                live = (row < rows) & (lane < columns[k + 1])
                sites.append(jnp.where(live, far_site_ref[k + 1].astype(F32), 0.0))
                states.append(k + 1)
        parts = len(states)
        for n in range(parts):
            joined_s[:, n * tile : (n + 1) * tile] = sites[n].astype(BF16)
            turned_s[n] = jnp.transpose(sites[n]).astype(BF16)
            weight_s[n] = weight_rows(weight_ref, width, states[n], square_s, True)
            packed_s[n, width * pitch :, :] = jnp.zeros(((wide - width) * pitch, tile), F32)
            diag_s[n] = jnp.zeros_like(diag_s[n])

        for pair in range(width // 2):
            at = slice(pair * tile, (pair + 1) * tile)
            for k in range(2):
                here = slice((pair * 2 + k) * tile, (pair * 2 + k + 1) * tile)
                blocks = [
                    jnp.dot(environ_ref[here, :], joined_s[:, :tile], preferred_element_type=F32)
                ]
                if with_partner:
                    both = jnp.dot(
                        far_environ_ref[here, :], joined_s[:, tile:], preferred_element_type=F32
                    )
                    blocks += [both[:, :tile], both[:, tile:]]
                for n in range(parts):
                    half_s[n, at, k * tile : (k + 1) * tile] = blocks[n].astype(BF16)
            for n in range(parts):
                both = jnp.dot(turned_s[n], half_s[n, at, :], preferred_element_type=F32)
                for k in range(2):
                    w = pair * 2 + k
                    folded, diagonal = pack_block(both[:, k * tile : (k + 1) * tile])
                    packed_s[n, w * pitch : w * pitch + half, :] = folded
                    diag_s[n, w : w + 1, :] = diagonal

        def mixed(inputs):
            value = None
            for n in range(parts):
                term = jnp.dot(weight_s[n], doubled(inputs[n]), preferred_element_type=F32)
                value = term if value is None else value + term
            return value[:wide]

        for at in range(0, half, 2):
            value = mixed([
                jnp.concatenate(
                    [packed_s[n, pl.ds(at + k, wide, stride=pitch), :] for k in range(2)], axis=1
                )
                for n in range(parts)
            ])
            for k in range(2):
                sums_s[pl.ds(at + k, wide, stride=pitch), :] = value[:, k * tile : (k + 1) * tile]
        diag_sums_s[...] = jnp.zeros_like(diag_sums_s)
        diag_sums_s[:wide, :] = mixed([diag_s[n, :wide] for n in range(parts)])
        for (first, count), ref in zip(chunks_of(width), (early_ref, late_ref)):
            for w in range(count):
                at = (first + w) * pitch
                ref[w * half : (w + 1) * half, :] = sums_s[at : at + half, :].astype(ref.dtype)
            rows = packed_height(count)
            ref[count * half :, :] = diag_sums_s[first : first + rows, :].astype(ref.dtype)

    even = lax.rem(sector, 2) == 0
    own_state = len(CHARGES) - 1 if travels else 0

    @pl.when(even)
    def _():
        run(own_state, travels)

    @pl.when(jnp.logical_not(even))
    def _():
        run(own_state, not travels)


def mix_into(width, tile, weights, wide_s, sums_s, out_ref):
    wide = padded(width)
    pitch = tile + 8
    wide_s[width * pitch :, :] = jnp.zeros_like(wide_s[width * pitch :, :])

    for at in range(0, tile, 2):
        value = doubled(
            jnp.concatenate(
                [wide_s[pl.ds(at + k, wide, stride=pitch), :] for k in range(2)], axis=1
            )
        )
        for index, weight in enumerate(weights):
            mixed = jnp.dot(weight[...], value, preferred_element_type=F32)[:wide]
            for k in range(2):
                sums_s[index, pl.ds(at + k, wide, stride=pitch), :] = mixed[:, k * tile : (k + 1) * tile]
    for index in range(len(weights)):
        for w in range(width):
            out_ref[index, :, w * tile : (w + 1) * tile] = sums_s[
                index, w * pitch : w * pitch + tile, :
            ].astype(BF16)


def unpack_wide(width, tile, read, wide_s, diag):
    def write(w, block):
        wide_s[w * (tile + 8) : w * (tile + 8) + tile, :] = block

    unpack_into(width, tile, read, write, diag)


def mix_own_kernel(width, tile, source_ref, weight_ref, out_ref, square_s, weight_s, wide_s, sums_s):
    pitch = tile + 8
    weight_s[0] = weight_rows(weight_ref, width, 0, square_s, False)
    for w in range(width):
        wide_s[w * pitch : w * pitch + tile, :] = source_ref[w * tile : (w + 1) * tile, :].astype(F32)
    mix_into(width, tile, [weight_s.at[0]], wide_s, sums_s, out_ref)


def mix_next_kernel(
    width, tile, near_ref, relay_ref, weight_ref, out_ref, square_s, weight_s, wide_s, sums_s, diag
):
    even = lax.rem(lax.axis_index("sec"), 2) == 0
    for k in range(2):
        weight_s[k] = weight_rows(weight_ref, width, k + 1, square_s, False)

    def read(at, size):
        near = near_ref[at : at + size, :].astype(F32)
        return jnp.where(even, near, relay_ref[at : at + size, :].astype(F32))

    unpack_wide(width, tile, read, wide_s, diag)
    mix_into(width, tile, [weight_s.at[k] for k in range(2)], wide_s, sums_s, out_ref)


def mix_after_kernel(
    width, tile, far_ref, weight_ref, out_ref, square_s, weight_s, wide_s, sums_s, diag
):
    weight_s[0] = weight_rows(weight_ref, width, 3, square_s, False)
    unpack_wide(width, tile, reader(far_ref), wide_s, diag)
    mix_into(width, tile, [weight_s.at[0]], wide_s, sums_s, out_ref)


def total(value):
    return jnp.sum(jnp.sum(value, axis=0, keepdims=True), axis=1, keepdims=True)


def put(stats, kind, lane_at, value):
    row, lane = iotas(stats.shape)
    return jnp.where((row == kind) & (lane == lane_at), value, stats)


def scaled(value):
    square = total(value * value)
    inverse = jnp.where(square > 0.0, lax.rsqrt(square), 0.0)
    return value * inverse, square * inverse


def right_products(width, tile, field, right_ref, out_ref, p):
    group, lanes = p // 2, slice(p % 2 * tile, (p % 2 + 1) * tile)
    for pair in range(width // 2):
        at = pair * 2 * tile
        both = jnp.dot(field, right_ref[:, at : at + 2 * tile], preferred_element_type=F32).astype(BF16)
        for k in range(2):
            out_ref[group, at + k * tile : at + (k + 1) * tile, lanes] = both[:, k * tile : (k + 1) * tile]


def head_kernel(
    width, tile, dims_ref, guess_ref, own_ref, next_ref, after_ref, vector_ref, stats_ref, product_ref
):
    states = len(CHARGES)
    sector = lax.axis_index("sec")
    rows, columns = live_limits(dims_ref, sector)
    row, lane = iotas((tile, tile))
    rights = [own_ref.at[0], next_ref.at[0], next_ref.at[1], after_ref.at[0]]
    stats = jnp.zeros(stats_ref.shape, F32)
    for p in range(states):
        live = (row < rows) & (lane < columns[p])
        vector, norm = scaled(jnp.where(live, guess_ref[p], 0.0))
        vector_ref[p] = vector
        stats = put(stats, 0, sector * states + p, norm)
        right_products(width, tile, vector.astype(BF16), rights[p], product_ref, p)
    stats_ref[...] = stats


def bound_blocks(first, count, tile, packed_ref, environ_ref, out_ref, diag):
    segment = lax.axis_index("seg")

    @pl.when(segment == 0)
    def _():
        for w in range(count):
            out_ref[:, w * tile : (w + 1) * tile] = environ_ref[
                (first + w) * tile : (first + w + 1) * tile, :
            ]

    @pl.when(segment != 0)
    def _():
        def write(w, block):
            out_ref[:, w * tile : (w + 1) * tile] = block.astype(BF16)

        unpack_into(count, tile, reader(packed_ref), write, diag)


def open_kernel(width, tile, packed_ref, environ_ref, product_ref, bound_ref, image_ref, diag):
    first, count = chunks_of(width)[0]
    bound_blocks(first, count, tile, packed_ref, environ_ref, bound_ref, diag)
    for group in range(len(CHARGES) // 2):
        image_ref[group] = jnp.dot(
            bound_ref[...], product_ref[group, : count * tile, :], preferred_element_type=F32
        )


def lanczos_kernel(
    width, tile, dims_ref, packed_ref, environ_ref, early_ref, image_ref, own_ref, next_ref, after_ref,
    start_ref, norm_ref, product_ref, basis_ref, stats_ref, late_s, product_s, diag,
):
    states = len(CHARGES)
    sector = lax.axis_index("sec")
    first, count = chunks_of(width)[1]
    bound_blocks(first, count, tile, packed_ref, environ_ref, late_s, diag)
    rows, columns = live_limits(dims_ref, sector)
    row, lane = iotas((tile, tile))
    rights = [own_ref.at[0], next_ref.at[0], next_ref.at[1], after_ref.at[0]]
    stats = norm_ref[...]
    split = first * tile
    betas = [None] * states
    for j in range(LANCZOS):
        source = product_ref if j == 0 else product_s
        for group in range(states // 2):
            members = (2 * group, 2 * group + 1)
            if j == 0:
                images = image_ref[group]
            else:
                for p in members:
                    field = basis_ref[j - 1, p].astype(BF16)
                    right_products(width, tile, field, rights[p], product_s, p)
                images = jnp.dot(early_ref[...], source[group, :split, :], preferred_element_type=F32)
            images = images + jnp.dot(
                late_s[...], source[group, split:, :], preferred_element_type=F32
            )
            for p in members:
                live = (row < rows) & (lane < columns[p])
                image = jnp.where(live, images[:, p % 2 * tile : (p % 2 + 1) * tile], 0.0)
                vector = start_ref[p] if j == 0 else basis_ref[j - 1, p]
                alpha = total(vector * image)
                image = image - alpha * vector
                if j > 0:
                    before = start_ref[p] if j == 1 else basis_ref[j - 2, p]
                    image = image - betas[p] * before
                following, beta = scaled(image)
                basis_ref[j, p] = following
                betas[p] = beta
                stats = put(stats, 1 + 2 * j, sector * states + p, alpha)
                stats = put(stats, 2 + 2 * j, sector * states + p, beta)
    stats_ref[...] = stats


def finish_kernel(entries, stats_ref, start_ref, basis_ref, vector_ref, table_ref):
    states = len(CHARGES)
    sector = lax.axis_index("sec")
    stats = stats_ref[0]
    for q in range(1, stats_ref.shape[0]):
        stats = stats + stats_ref[q]
    alphas = [stats[1 + 2 * j : 2 + 2 * j, :] for j in range(LANCZOS)]
    betas = [stats[2 + 2 * j : 3 + 2 * j, :] for j in range(LANCZOS)]

    def mean(left, right):
        products = left[0] * right[0]
        for x, y in zip(left[1:], right[1:]):
            products = products + x * y
        return jnp.sum(products, axis=1, keepdims=True) / entries

    start = [stats[0:1, :]]
    vector = [start[0] / jnp.sqrt(mean(start, start) + 1e-06)]
    previous = []
    beta = jnp.zeros((1, 1), F32)
    table_row, table_column = iotas(table_ref.shape)
    table = jnp.zeros(table_ref.shape, F32)
    for j in range(LANCZOS):
        image = []
        for k in range(j + 2):
            term = None
            if k > 0:
                term = betas[k - 1] * vector[k - 1]
            if k <= j:
                more = alphas[k] * vector[k]
                term = more if term is None else term + more
            if k + 1 <= j:
                term = term + betas[k] * vector[k + 1]
            image.append(term)
        alpha = mean(vector, image[: j + 1])
        for k in range(j + 1):
            image[k] = image[k] - alpha * vector[k]
        for k in range(j):
            image[k] = image[k] - beta * previous[k]
        beta = jnp.sqrt(mean(image, image) + 1e-06)
        previous = vector
        vector = [value / beta for value in image]
        table = jnp.where((table_row == 0) & (table_column == j), alpha, table)
        table = jnp.where((table_row == 1) & (table_column == j), beta, table)
    table_ref[...] = table
    lane = lax.broadcasted_iota(jnp.int32, (1, stats.shape[1]), 1)
    for p in range(states):
        value = None
        here = lane == sector * states + p
        for k in range(LANCZOS + 1):
            weight = jnp.sum(jnp.where(here, vector[k], 0.0), axis=1, keepdims=True)
            term = weight * (start_ref[p] if k == 0 else basis_ref[k - 1, p])
            value = term if value is None else value + term
        vector_ref[p] = value


def smem():
    return pl.BlockSpec(memory_space=pltpu.SMEM)


def vmem():
    return pl.BlockSpec(memory_space=pltpu.VMEM)


def call(name, kernel, scalars, arrays, outs, scratch, limit, micros):
    many = isinstance(outs, (tuple, list))
    return pl.pallas_call(
        kernel,
        out_shape=outs,
        in_specs=[smem()] * len(scalars) + [vmem()] * len(arrays),
        out_specs=[vmem()] * len(outs) if many else vmem(),
        scratch_shapes=scratch,
        compiler_params=pltpu.CompilerParams(vmem_limit_bytes=limit * MIB),
        name=name,
        cost_estimate=pl.CostEstimate(
            flops=int(micros * 1.1e9), bytes_accessed=0, transcendentals=0
        ),
    )(*scalars, *arrays)


def pairs_of(count, pick):
    return [(source, target) for source in range(count) for target in pick(source) if 0 <= target < count]


def gathered(value, axis):
    count = lax.axis_size(axis)
    return lax.all_to_all(jnp.broadcast_to(value, (count,) + value.shape), axis, 0, 0)


def on_device(left_env, right_env, site_tensors, mpo, boundary_mpo, guess, sector_dims):
    width, tile = left_env.shape[2], left_env.shape[-1]
    half = tile // 2
    wide = padded(width)
    states = len(CHARGES)
    sector_count = sector_dims.shape[0]
    sectors = lax.axis_size("sec")
    segments = lax.axis_size("seg")
    prows = packed_rows(width, tile)
    drows = prows - width * half
    packed = jax.ShapeDtypeStruct((prows, tile), BF16)
    parts = chunks_of(width)

    def packed_parts(dtype):
        return [jax.ShapeDtypeStruct((packed_rows(count, tile), tile), dtype) for _, count in parts]

    def mixed(count):
        return jax.ShapeDtypeStruct((count, tile, width * tile), BF16)

    environ = left_env.reshape(width * tile, tile)
    right = right_env.reshape(width * tile, tile)
    site = site_tensors[0, 0, :, 0]
    site_weights = jnp.transpose(mpo[0, 0], (0, 2, 1)).reshape(width * states, width)
    bound_weights = jnp.transpose(boundary_mpo[0], (0, 2, 1)).reshape(width * states, width)

    swap = pairs_of(sectors, lambda q: [q ^ 1])
    across = pairs_of(sectors, lambda q: [q + 1] if q % 2 == 0 else [])
    up_two = pairs_of(sectors, lambda q: [q + 2])
    down_two = pairs_of(sectors, lambda q: [q - 2])
    onward = pairs_of(segments, lambda s: [s + 1])
    diag = pltpu.VMEM((drows, tile), F32)

    def mix_scratch(count):
        return [
            pltpu.VMEM((tile, tile), F32),
            pltpu.VMEM((count, packed_height(width), 2 * wide), BF16),
            pltpu.VMEM((wide * (tile + 8), tile), F32),
            pltpu.VMEM((count, wide * (tile + 8), tile), F32),
        ]

    far_environ = lax.ppermute(environ, "sec", swap)
    far_site = lax.ppermute(site, "sec", swap)
    right_packed = call(
        "pack_right", functools.partial(pack_kernel, width, tile), [], [right], packed, [diag], 6, 1
    )
    right_far = lax.ppermute(right_packed, "sec", down_two)
    fold_scratch = [
        pltpu.VMEM((tile, 3 * tile), BF16),
        pltpu.VMEM((3, tile, tile), BF16),
        pltpu.VMEM((tile, tile), F32),
        pltpu.VMEM((3, packed_height(width), 2 * wide), BF16),
        pltpu.VMEM((3, width // 2 * tile, 2 * tile), BF16),
        pltpu.VMEM((3, wide * (half + 8), tile), F32),
        pltpu.VMEM((3, drows, tile), F32),
        pltpu.VMEM((wide * (half + 8), tile), F32),
        pltpu.VMEM((drows, tile), F32),
    ]
    outgoing = call(
        "fold_up", functools.partial(fold_kernel, width, tile, True),
        [sector_dims], [environ, site, far_environ, far_site, site_weights], packed_parts(BF16),
        fold_scratch, 20, 12,
    )
    arrived = [lax.ppermute(part, "sec", up_two) for part in outgoing]
    kept = call(
        "fold_own", functools.partial(fold_kernel, width, tile, False),
        [sector_dims], [environ, site, far_environ, far_site, site_weights], packed_parts(F32),
        fold_scratch, 20, 0.1,
    )
    kept, right_far = lax.optimization_barrier((kept, right_far))
    early = (kept[0] + arrived[0].astype(F32)).astype(BF16)
    early_bound = lax.ppermute(early, "seg", onward)
    early, right_far, right, right_packed = lax.optimization_barrier(
        (early, right_far, right, right_packed)
    )
    right_near = lax.ppermute(right_packed, "sec", swap)
    right_relay = lax.ppermute(right_far, "sec", across)
    own_mixed = call(
        "mix_own", functools.partial(mix_own_kernel, width, tile), [], [right, bound_weights],
        mixed(1), mix_scratch(1), 12, 1,
    )
    after_mixed = call(
        "mix_after", functools.partial(mix_after_kernel, width, tile), [],
        [right_far, bound_weights], mixed(1), mix_scratch(1) + [diag], 12, 2,
    )
    late_arrived, own_mixed, after_mixed = lax.optimization_barrier(
        (arrived[1], own_mixed, after_mixed)
    )
    late = (kept[1] + late_arrived.astype(F32)).astype(BF16)
    late_bound = lax.ppermute(late, "seg", onward)
    late, right_near, right_relay = lax.optimization_barrier((late, right_near, right_relay))
    next_mixed = call(
        "mix_next", functools.partial(mix_next_kernel, width, tile), [],
        [right_near, right_relay, bound_weights], mixed(2), mix_scratch(2) + [diag], 16, 3,
    )
    start, norms, products = call(
        "head", functools.partial(head_kernel, width, tile),
        [sector_dims], [guess[0, :, 0], own_mixed, next_mixed, after_mixed],
        (
            jax.ShapeDtypeStruct((states, tile, tile), F32),
            jax.ShapeDtypeStruct((16, 128), F32),
            jax.ShapeDtypeStruct((states // 2, width * tile, 2 * tile), BF16),
        ),
        [], 14, 2,
    )
    new_env = call(
        "unpack_env", functools.partial(unpack_kernel, width, tile), [], [early, late],
        jax.ShapeDtypeStruct((width * tile, tile), BF16), [diag], 6, 2,
    )
    early_bound, products, new_env = lax.optimization_barrier((early_bound, products, new_env))
    bound, image = call(
        "open", functools.partial(open_kernel, width, tile), [], [early_bound, environ, products],
        (
            jax.ShapeDtypeStruct((tile, parts[0][1] * tile), BF16),
            jax.ShapeDtypeStruct((states // 2, tile, 2 * tile), F32),
        ),
        [diag], 12, 1,
    )
    late_bound, bound = lax.optimization_barrier((late_bound, bound))
    basis, stats = call(
        "lanczos", functools.partial(lanczos_kernel, width, tile),
        [sector_dims],
        [late_bound, environ, bound, image, own_mixed, next_mixed, after_mixed, start, norms, products],
        (
            jax.ShapeDtypeStruct((LANCZOS, states, tile, tile), F32),
            jax.ShapeDtypeStruct((16, 128), F32),
        ),
        [
            pltpu.VMEM((tile, parts[1][1] * tile), BF16),
            pltpu.VMEM((states // 2, width * tile, 2 * tile), BF16),
            diag,
        ],
        22, 12,
    )
    stats = gathered(stats, "sec")
    entries = float(states * sector_count * tile * tile)
    vector, table = call(
        "finish", functools.partial(finish_kernel, entries), [], [stats, start, basis],
        (
            jax.ShapeDtypeStruct((states, tile, tile), F32),
            jax.ShapeDtypeStruct((2, LANCZOS), F32),
        ),
        [], 6, 2,
    )
    return new_env.reshape(left_env.shape), vector[None, :, None], jnp.transpose(table)[None]


def solution(mesh):
    placed = (
        P("seg", "sec", None, None, None),
        P("seg", "sec", None, None, None),
        P("seg", None, None, "sec", None, None),
        P("seg", None, None, None, None),
        P("seg", None, None, None),
        P("seg", None, "sec", None, None),
        P(),
    )
    return jax.shard_map(
        on_device,
        mesh=mesh,
        in_specs=placed,
        out_specs=(
            P("seg", "sec", None, None, None),
            P("seg", None, "sec", None, None),
            P("seg", None, None),
        ),
        check_vma=False,
    )
```

```python
import functools

import jax
import jax.numpy as jnp
from jax import lax
from jax.experimental import pallas as pl
from jax.experimental.pallas import tpu as pltpu
from jax.sharding import PartitionSpec as P

LANCZOS = 4
CHARGES = (0, 1, 1, 2)
F32 = jnp.float32
BF16 = jnp.bfloat16
MIB = 1024 * 1024


def padded(count):
    return -(-count // 8) * 8


def packed_height(count):
    return -(-count // 16) * 16


def packed_rows(count, tile):
    return count * tile // 2 + packed_height(count)


def chunks_of(width):
    first = -(-width // 4) * 2
    return (0, first), (first, width - first)


def iotas(shape):
    return lax.broadcasted_iota(jnp.int32, shape, 0), lax.broadcasted_iota(jnp.int32, shape, 1)


def pack_block(block):
    tile = block.shape[0]
    half = tile // 2
    top, low = block[:half], block[half:]
    row, lane = iotas((half, tile))
    turned = pltpu.roll(low, half, 1)
    folded = jnp.where((lane < half) & (row > lane), turned, top)
    diagonal = jnp.sum(jnp.where(lane == row + half, low, 0.0), axis=0, keepdims=True)
    return folded, diagonal


def unpack_block(folded, diagonal):
    half, tile = folded.shape
    row, lane = iotas((half, tile))
    rolled = pltpu.roll(folded, half, 1)
    turned = jnp.transpose(jnp.concatenate([folded, rolled], axis=0))
    top = jnp.where((lane < half) & (row > lane), turned[:half], folded)
    low = jnp.where((lane >= half) & (row > lane - half), rolled, turned[half:])
    low = jnp.where(lane == row + half, diagonal, low)
    return jnp.concatenate([top, low], axis=0)


def partner_of(sector):
    return sector + 1 - 2 * lax.rem(sector, 2)


def live_limits(dims_ref, sector):
    count = dims_ref.shape[0]
    rows = dims_ref[sector]
    columns = []
    for charge in CHARGES:
        target = sector + charge
        columns.append(jnp.where(target < count, dims_ref[jnp.minimum(target, count - 1)], 0))
    return rows, columns


def weight_rows(weight_ref, width, p, square, turned):
    wide = padded(width)
    square[...] = jnp.zeros_like(square)
    square[:width, :width] = weight_ref[pl.ds(p, width, stride=len(CHARGES)), :]
    value = square[...]
    if turned:
        value = jnp.transpose(value)
    high = value.astype(BF16).astype(F32)
    joined = (high + pltpu.roll(value - high, wide, 1)).astype(BF16)
    return joined[: packed_height(width), : 2 * wide]


def doubled(value):
    return jnp.concatenate([value, value], axis=0).astype(BF16)


def pack_kernel(width, tile, source_ref, out_ref, diag):
    half = tile // 2
    diag[...] = jnp.zeros_like(diag)
    for w in range(width):
        folded, diagonal = pack_block(source_ref[w * tile : (w + 1) * tile, :].astype(F32))
        out_ref[w * half : (w + 1) * half, :] = folded.astype(BF16)
        diag[w : w + 1, :] = diagonal
    out_ref[width * half :, :] = diag[...].astype(BF16)


def unpack_into(count, tile, read, write, diag):
    half = tile // 2
    size = packed_height(count)
    diag[:size, :] = read(count * half, size)
    for w in range(count):
        write(w, unpack_block(read(w * half, half), diag[w : w + 1, :]))


def reader(ref):
    return lambda at, size: ref[at : at + size, :].astype(F32)


def unpack_kernel(width, tile, early_ref, late_ref, out_ref, diag):
    for (first, count), ref in zip(chunks_of(width), (early_ref, late_ref)):

        def write(w, block, first=first):
            out_ref[(first + w) * tile : (first + w + 1) * tile, :] = block.astype(BF16)

        unpack_into(count, tile, reader(ref), write, diag)


def fold_kernel(
    width, tile, travels, dims_ref, environ_ref, site_ref, far_environ_ref, far_site_ref, weight_ref, early_ref, late_ref,
    joined_s, turned_s, square_s, weight_s, half_s, packed_s, diag_s, sums_s, diag_sums_s,
):
    half = tile // 2
    pitch = half + 8
    wide = padded(width)
    sector = lax.axis_index("sec")
    partner = partner_of(sector)
    row, lane = iotas((tile, tile))

    def run(own_state, with_partner):
        rows, columns = live_limits(dims_ref, sector)
        live = (row < rows) & (lane < columns[own_state])
        sites = [jnp.where(live, site_ref[own_state].astype(F32), 0.0)]
        states = [own_state]
        if with_partner:
            rows, columns = live_limits(dims_ref, partner)
            for k in range(2):
                live = (row < rows) & (lane < columns[k + 1])
                sites.append(jnp.where(live, far_site_ref[k + 1].astype(F32), 0.0))
                states.append(k + 1)
        parts = len(states)
        for n in range(parts):
            joined_s[:, n * tile : (n + 1) * tile] = sites[n].astype(BF16)
            turned_s[n] = jnp.transpose(sites[n]).astype(BF16)
            weight_s[n] = weight_rows(weight_ref, width, states[n], square_s, True)
            packed_s[n, width * pitch :, :] = jnp.zeros(((wide - width) * pitch, tile), F32)
            diag_s[n] = jnp.zeros_like(diag_s[n])

        for pair in range(width // 2):
            at = slice(pair * tile, (pair + 1) * tile)
            for k in range(2):
                here = slice((pair * 2 + k) * tile, (pair * 2 + k + 1) * tile)
                blocks = [
                    jnp.dot(environ_ref[here, :], joined_s[:, :tile], preferred_element_type=F32)
                ]
                if with_partner:
                    both = jnp.dot(
                        far_environ_ref[here, :], joined_s[:, tile:], preferred_element_type=F32
                    )
                    blocks += [both[:, :tile], both[:, tile:]]
                for n in range(parts):
                    half_s[n, at, k * tile : (k + 1) * tile] = blocks[n].astype(BF16)
            for n in range(parts):
                both = jnp.dot(turned_s[n], half_s[n, at, :], preferred_element_type=F32)
                for k in range(2):
                    w = pair * 2 + k
                    folded, diagonal = pack_block(both[:, k * tile : (k + 1) * tile])
                    packed_s[n, w * pitch : w * pitch + half, :] = folded
                    diag_s[n, w : w + 1, :] = diagonal

        def mixed(inputs):
            value = None
            for n in range(parts):
                term = jnp.dot(weight_s[n], doubled(inputs[n]), preferred_element_type=F32)
                value = term if value is None else value + term
            return value[:wide]

        for at in range(0, half, 2):
            value = mixed([
                jnp.concatenate(
                    [packed_s[n, pl.ds(at + k, wide, stride=pitch), :] for k in range(2)], axis=1
                )
                for n in range(parts)
            ])
            for k in range(2):
                sums_s[pl.ds(at + k, wide, stride=pitch), :] = value[:, k * tile : (k + 1) * tile]
        diag_sums_s[...] = jnp.zeros_like(diag_sums_s)
        diag_sums_s[:wide, :] = mixed([diag_s[n, :wide] for n in range(parts)])
        for (first, count), ref in zip(chunks_of(width), (early_ref, late_ref)):
            for w in range(count):
                at = (first + w) * pitch
                ref[w * half : (w + 1) * half, :] = sums_s[at : at + half, :].astype(ref.dtype)
            rows = packed_height(count)
            ref[count * half :, :] = diag_sums_s[first : first + rows, :].astype(ref.dtype)

    even = lax.rem(sector, 2) == 0
    own_state = len(CHARGES) - 1 if travels else 0

    @pl.when(even)
    def _():
        run(own_state, travels)

    @pl.when(jnp.logical_not(even))
    def _():
        run(own_state, not travels)


def mix_into(width, tile, weights, wide_s, sums_s, out_ref):
    wide = padded(width)
    pitch = tile + 8
    wide_s[width * pitch :, :] = jnp.zeros_like(wide_s[width * pitch :, :])

    for at in range(0, tile, 2):
        value = doubled(
            jnp.concatenate(
                [wide_s[pl.ds(at + k, wide, stride=pitch), :] for k in range(2)], axis=1
            )
        )
        for index, weight in enumerate(weights):
            mixed = jnp.dot(weight[...], value, preferred_element_type=F32)[:wide]
            for k in range(2):
                sums_s[index, pl.ds(at + k, wide, stride=pitch), :] = mixed[:, k * tile : (k + 1) * tile]
    for index in range(len(weights)):
        for w in range(width):
            out_ref[index, :, w * tile : (w + 1) * tile] = sums_s[
                index, w * pitch : w * pitch + tile, :
            ].astype(BF16)


def unpack_wide(width, tile, read, wide_s, diag):
    def write(w, block):
        wide_s[w * (tile + 8) : w * (tile + 8) + tile, :] = block

    unpack_into(width, tile, read, write, diag)


def copy_wide(width, tile, source_ref, wide_s):
    for w in range(width):
        at = w * (tile + 8)
        wide_s[at : at + tile, :] = source_ref[w * tile : (w + 1) * tile, :].astype(F32)


def mix_own_kernel(width, tile, source_ref, weight_ref, out_ref, square_s, weight_s, wide_s, sums_s):
    weight_s[0] = weight_rows(weight_ref, width, 0, square_s, False)
    copy_wide(width, tile, source_ref, wide_s)
    mix_into(width, tile, [weight_s.at[0]], wide_s, sums_s, out_ref)


def mix_next_kernel(
    width, tile, near_ref, relay_ref, weight_ref, out_ref, square_s, weight_s, wide_s, sums_s, diag
):
    even = lax.rem(lax.axis_index("sec"), 2) == 0
    for k in range(2):
        weight_s[k] = weight_rows(weight_ref, width, k + 1, square_s, False)

    @pl.when(even)
    def _():
        copy_wide(width, tile, near_ref, wide_s)

    @pl.when(jnp.logical_not(even))
    def _():
        unpack_wide(width, tile, reader(relay_ref), wide_s, diag)

    mix_into(width, tile, [weight_s.at[k] for k in range(2)], wide_s, sums_s, out_ref)


def mix_after_kernel(
    width, tile, far_ref, weight_ref, out_ref, square_s, weight_s, wide_s, sums_s, diag
):
    weight_s[0] = weight_rows(weight_ref, width, 3, square_s, False)
    unpack_wide(width, tile, reader(far_ref), wide_s, diag)
    mix_into(width, tile, [weight_s.at[0]], wide_s, sums_s, out_ref)


def total(value):
    return jnp.sum(jnp.sum(value, axis=0, keepdims=True), axis=1, keepdims=True)


def put(stats, kind, lane_at, value):
    row, lane = iotas(stats.shape)
    return jnp.where((row == kind) & (lane == lane_at), value, stats)


def scaled(value):
    square = total(value * value)
    inverse = jnp.where(square > 0.0, lax.rsqrt(square), 0.0)
    return value * inverse, square * inverse


def right_products(width, tile, field, right_ref, out_ref, p):
    group, lanes = p // 2, slice(p % 2 * tile, (p % 2 + 1) * tile)
    for pair in range(width // 2):
        at = pair * 2 * tile
        both = jnp.dot(field, right_ref[:, at : at + 2 * tile], preferred_element_type=F32).astype(BF16)
        for k in range(2):
            out_ref[group, at + k * tile : at + (k + 1) * tile, lanes] = both[:, k * tile : (k + 1) * tile]


def head_kernel(
    width, tile, dims_ref, guess_ref, own_ref, next_ref, after_ref, vector_ref, stats_ref, product_ref
):
    states = len(CHARGES)
    sector = lax.axis_index("sec")
    rows, columns = live_limits(dims_ref, sector)
    row, lane = iotas((tile, tile))
    rights = [own_ref.at[0], next_ref.at[0], next_ref.at[1], after_ref.at[0]]
    stats = jnp.zeros(stats_ref.shape, F32)
    for p in range(states):
        live = (row < rows) & (lane < columns[p])
        vector, norm = scaled(jnp.where(live, guess_ref[p], 0.0))
        vector_ref[p] = vector
        stats = put(stats, 0, sector * states + p, norm)
        right_products(width, tile, vector.astype(BF16), rights[p], product_ref, p)
    stats_ref[...] = stats


def bound_blocks(first, count, tile, packed_ref, environ_ref, out_ref, diag):
    segment = lax.axis_index("seg")

    @pl.when(segment == 0)
    def _():
        for w in range(count):
            out_ref[:, w * tile : (w + 1) * tile] = environ_ref[
                (first + w) * tile : (first + w + 1) * tile, :
            ]

    @pl.when(segment != 0)
    def _():
        def write(w, block):
            out_ref[:, w * tile : (w + 1) * tile] = block.astype(BF16)

        unpack_into(count, tile, reader(packed_ref), write, diag)


def open_kernel(width, tile, packed_ref, environ_ref, product_ref, bound_ref, image_ref, diag):
    first, count = chunks_of(width)[0]
    bound_blocks(first, count, tile, packed_ref, environ_ref, bound_ref, diag)
    for group in range(len(CHARGES) // 2):
        image_ref[group] = jnp.dot(
            bound_ref[...], product_ref[group, : count * tile, :], preferred_element_type=F32
        )


def lanczos_kernel(
    width, tile, dims_ref, packed_ref, environ_ref, early_ref, image_ref, own_ref, next_ref, after_ref,
    start_ref, norm_ref, product_ref, basis_ref, stats_ref, late_s, product_s, diag,
):
    states = len(CHARGES)
    sector = lax.axis_index("sec")
    first, count = chunks_of(width)[1]
    bound_blocks(first, count, tile, packed_ref, environ_ref, late_s, diag)
    rows, columns = live_limits(dims_ref, sector)
    row, lane = iotas((tile, tile))
    rights = [own_ref.at[0], next_ref.at[0], next_ref.at[1], after_ref.at[0]]
    stats = norm_ref[...]
    split = first * tile
    betas = [None] * states
    for j in range(LANCZOS):
        source = product_ref if j == 0 else product_s
        for group in range(states // 2):
            members = (2 * group, 2 * group + 1)
            if j == 0:
                images = image_ref[group]
            else:
                for p in members:
                    field = basis_ref[j - 1, p].astype(BF16)
                    right_products(width, tile, field, rights[p], product_s, p)
                images = jnp.dot(early_ref[...], source[group, :split, :], preferred_element_type=F32)
            images = images + jnp.dot(
                late_s[...], source[group, split:, :], preferred_element_type=F32
            )
            for p in members:
                live = (row < rows) & (lane < columns[p])
                image = jnp.where(live, images[:, p % 2 * tile : (p % 2 + 1) * tile], 0.0)
                vector = start_ref[p] if j == 0 else basis_ref[j - 1, p]
                alpha = total(vector * image)
                image = image - alpha * vector
                if j > 0:
                    before = start_ref[p] if j == 1 else basis_ref[j - 2, p]
                    image = image - betas[p] * before
                following, beta = scaled(image)
                basis_ref[j, p] = following
                betas[p] = beta
                stats = put(stats, 1 + 2 * j, sector * states + p, alpha)
                stats = put(stats, 2 + 2 * j, sector * states + p, beta)
    stats_ref[...] = stats


def finish_kernel(entries, stats_ref, start_ref, basis_ref, vector_ref, table_ref):
    states = len(CHARGES)
    sector = lax.axis_index("sec")
    stats = stats_ref[0]
    for q in range(1, stats_ref.shape[0]):
        stats = stats + stats_ref[q]
    alphas = [stats[1 + 2 * j : 2 + 2 * j, :] for j in range(LANCZOS)]
    betas = [stats[2 + 2 * j : 3 + 2 * j, :] for j in range(LANCZOS)]

    def mean(left, right):
        products = left[0] * right[0]
        for x, y in zip(left[1:], right[1:]):
            products = products + x * y
        return jnp.sum(products, axis=1, keepdims=True) / entries

    start = [stats[0:1, :]]
    vector = [start[0] / jnp.sqrt(mean(start, start) + 1e-06)]
    previous = []
    beta = jnp.zeros((1, 1), F32)
    table_row, table_column = iotas(table_ref.shape)
    table = jnp.zeros(table_ref.shape, F32)
    for j in range(LANCZOS):
        image = []
        for k in range(j + 2):
            term = None
            if k > 0:
                term = betas[k - 1] * vector[k - 1]
            if k <= j:
                more = alphas[k] * vector[k]
                term = more if term is None else term + more
            if k + 1 <= j:
                term = term + betas[k] * vector[k + 1]
            image.append(term)
        alpha = mean(vector, image[: j + 1])
        for k in range(j + 1):
            image[k] = image[k] - alpha * vector[k]
        for k in range(j):
            image[k] = image[k] - beta * previous[k]
        beta = jnp.sqrt(mean(image, image) + 1e-06)
        previous = vector
        vector = [value / beta for value in image]
        table = jnp.where((table_row == 0) & (table_column == j), alpha, table)
        table = jnp.where((table_row == 1) & (table_column == j), beta, table)
    table_ref[...] = table
    lane = lax.broadcasted_iota(jnp.int32, (1, stats.shape[1]), 1)
    for p in range(states):
        value = None
        here = lane == sector * states + p
        for k in range(LANCZOS + 1):
            weight = jnp.sum(jnp.where(here, vector[k], 0.0), axis=1, keepdims=True)
            term = weight * (start_ref[p] if k == 0 else basis_ref[k - 1, p])
            value = term if value is None else value + term
        vector_ref[p] = value


def smem():
    return pl.BlockSpec(memory_space=pltpu.SMEM)


def vmem():
    return pl.BlockSpec(memory_space=pltpu.VMEM)


def call(name, kernel, scalars, arrays, outs, scratch, limit, micros):
    many = isinstance(outs, (tuple, list))
    return pl.pallas_call(
        kernel,
        out_shape=outs,
        in_specs=[smem()] * len(scalars) + [vmem()] * len(arrays),
        out_specs=[vmem()] * len(outs) if many else vmem(),
        scratch_shapes=scratch,
        compiler_params=pltpu.CompilerParams(vmem_limit_bytes=limit * MIB),
        name=name,
        cost_estimate=pl.CostEstimate(
            flops=int(micros * 1.1e9), bytes_accessed=0, transcendentals=0
        ),
    )(*scalars, *arrays)


def pairs_of(count, pick):
    return [(source, target) for source in range(count) for target in pick(source) if 0 <= target < count]


def gathered(value, axis):
    count = lax.axis_size(axis)
    return lax.all_to_all(jnp.broadcast_to(value, (count,) + value.shape), axis, 0, 0)


def on_device(left_env, right_env, site_tensors, mpo, boundary_mpo, guess, sector_dims):
    width, tile = left_env.shape[2], left_env.shape[-1]
    half = tile // 2
    wide = padded(width)
    states = len(CHARGES)
    sector_count = sector_dims.shape[0]
    sectors = lax.axis_size("sec")
    segments = lax.axis_size("seg")
    prows = packed_rows(width, tile)
    drows = prows - width * half
    packed = jax.ShapeDtypeStruct((prows, tile), BF16)
    parts = chunks_of(width)

    def packed_parts(dtype):
        return [jax.ShapeDtypeStruct((packed_rows(count, tile), tile), dtype) for _, count in parts]

    def mixed(count):
        return jax.ShapeDtypeStruct((count, tile, width * tile), BF16)

    environ = left_env.reshape(width * tile, tile)
    right = right_env.reshape(width * tile, tile)
    site = site_tensors[0, 0, :, 0]
    site_weights = jnp.transpose(mpo[0, 0], (0, 2, 1)).reshape(width * states, width)
    bound_weights = jnp.transpose(boundary_mpo[0], (0, 2, 1)).reshape(width * states, width)

    swap = pairs_of(sectors, lambda q: [q ^ 1])
    across = pairs_of(sectors, lambda q: [q + 1] if q % 2 == 0 else [])
    down = pairs_of(sectors, lambda q: [q - 1] if q % 2 else [])
    up_two = pairs_of(sectors, lambda q: [q + 2])
    down_two = pairs_of(sectors, lambda q: [q - 2])
    onward = pairs_of(segments, lambda s: [s + 1])
    diag = pltpu.VMEM((drows, tile), F32)

    def mix_scratch(count):
        return [
            pltpu.VMEM((tile, tile), F32),
            pltpu.VMEM((count, packed_height(width), 2 * wide), BF16),
            pltpu.VMEM((wide * (tile + 8), tile), F32),
            pltpu.VMEM((count, wide * (tile + 8), tile), F32),
        ]

    far_environ = lax.ppermute(environ, "sec", swap)
    far_site = lax.ppermute(site, "sec", swap)
    right_near = lax.ppermute(right, "sec", down)
    right_packed = call(
        "pack_right", functools.partial(pack_kernel, width, tile), [], [right], packed, [diag], 6, 1
    )
    right_far = lax.ppermute(right_packed, "sec", down_two)
    fold_scratch = [
        pltpu.VMEM((tile, 3 * tile), BF16),
        pltpu.VMEM((3, tile, tile), BF16),
        pltpu.VMEM((tile, tile), F32),
        pltpu.VMEM((3, packed_height(width), 2 * wide), BF16),
        pltpu.VMEM((3, width // 2 * tile, 2 * tile), BF16),
        pltpu.VMEM((3, wide * (half + 8), tile), F32),
        pltpu.VMEM((3, drows, tile), F32),
        pltpu.VMEM((wide * (half + 8), tile), F32),
        pltpu.VMEM((drows, tile), F32),
    ]
    outgoing = call(
        "fold_up", functools.partial(fold_kernel, width, tile, True),
        [sector_dims], [environ, site, far_environ, far_site, site_weights], packed_parts(BF16),
        fold_scratch, 20, 12,
    )
    early_arrived = lax.ppermute(outgoing[0], "sec", up_two)
    far_environ, outgoing = lax.optimization_barrier((far_environ, outgoing))
    kept = call(
        "fold_own", functools.partial(fold_kernel, width, tile, False),
        [sector_dims], [environ, site, far_environ, far_site, site_weights], packed_parts(F32),
        fold_scratch, 20, 0.1,
    )
    kept, late_outgoing = lax.optimization_barrier((kept, outgoing[1]))
    late_arrived = lax.ppermute(late_outgoing, "sec", up_two)
    kept, right_far, right = lax.optimization_barrier((kept, right_far, right))
    right_relay = lax.ppermute(right_far, "sec", across)
    own_mixed = call(
        "mix_own", functools.partial(mix_own_kernel, width, tile), [], [right, bound_weights],
        mixed(1), mix_scratch(1), 12, 1,
    )
    after_mixed = call(
        "mix_after", functools.partial(mix_after_kernel, width, tile), [],
        [right_far, bound_weights], mixed(1), mix_scratch(1) + [diag], 12, 2,
    )
    early_arrived, own_mixed, after_mixed = lax.optimization_barrier(
        (early_arrived, own_mixed, after_mixed)
    )
    early = (kept[0] + early_arrived.astype(F32)).astype(BF16)
    early_bound = lax.ppermute(early, "seg", onward)
    early, late_arrived = lax.optimization_barrier((early, late_arrived))
    late = (kept[1] + late_arrived.astype(F32)).astype(BF16)
    late_bound = lax.ppermute(late, "seg", onward)
    late, right_near, right_relay = lax.optimization_barrier((late, right_near, right_relay))
    next_mixed = call(
        "mix_next", functools.partial(mix_next_kernel, width, tile), [],
        [right_near, right_relay, bound_weights], mixed(2), mix_scratch(2) + [diag], 16, 3,
    )
    start, norms, products = call(
        "head", functools.partial(head_kernel, width, tile),
        [sector_dims], [guess[0, :, 0], own_mixed, next_mixed, after_mixed],
        (
            jax.ShapeDtypeStruct((states, tile, tile), F32),
            jax.ShapeDtypeStruct((16, 128), F32),
            jax.ShapeDtypeStruct((states // 2, width * tile, 2 * tile), BF16),
        ),
        [], 14, 2,
    )
    new_env = call(
        "unpack_env", functools.partial(unpack_kernel, width, tile), [], [early, late],
        jax.ShapeDtypeStruct((width * tile, tile), BF16), [diag], 6, 2,
    )
    early_bound, products, new_env = lax.optimization_barrier((early_bound, products, new_env))
    bound, image = call(
        "open", functools.partial(open_kernel, width, tile), [], [early_bound, environ, products],
        (
            jax.ShapeDtypeStruct((tile, parts[0][1] * tile), BF16),
            jax.ShapeDtypeStruct((states // 2, tile, 2 * tile), F32),
        ),
        [diag], 12, 1,
    )
    late_bound, bound = lax.optimization_barrier((late_bound, bound))
    basis, stats = call(
        "lanczos", functools.partial(lanczos_kernel, width, tile),
        [sector_dims],
        [late_bound, environ, bound, image, own_mixed, next_mixed, after_mixed, start, norms, products],
        (
            jax.ShapeDtypeStruct((LANCZOS, states, tile, tile), F32),
            jax.ShapeDtypeStruct((16, 128), F32),
        ),
        [
            pltpu.VMEM((tile, parts[1][1] * tile), BF16),
            pltpu.VMEM((states // 2, width * tile, 2 * tile), BF16),
            diag,
        ],
        22, 12,
    )
    stats = gathered(stats, "sec")
    entries = float(states * sector_count * tile * tile)
    vector, table = call(
        "finish", functools.partial(finish_kernel, entries), [], [stats, start, basis],
        (
            jax.ShapeDtypeStruct((states, tile, tile), F32),
            jax.ShapeDtypeStruct((2, LANCZOS), F32),
        ),
        [], 6, 2,
    )
    return new_env.reshape(left_env.shape), vector[None, :, None], jnp.transpose(table)[None]


def solution(mesh):
    placed = (
        P("seg", "sec", None, None, None),
        P("seg", "sec", None, None, None),
        P("seg", None, None, "sec", None, None),
        P("seg", None, None, None, None),
        P("seg", None, None, None),
        P("seg", None, "sec", None, None),
        P(),
    )
    return jax.shard_map(
        on_device,
        mesh=mesh,
        in_specs=placed,
        out_specs=(
            P("seg", "sec", None, None, None),
            P("seg", None, "sec", None, None),
            P("seg", None, None),
        ),
        check_vma=False,
    )
```

```python
import functools

import jax
import jax.numpy as jnp
from jax import lax
from jax.experimental import pallas as pl
from jax.experimental.pallas import tpu as pltpu
from jax.sharding import PartitionSpec as P

LANCZOS = 4
CHARGES = (0, 1, 1, 2)
F32 = jnp.float32
BF16 = jnp.bfloat16
MIB = 1024 * 1024


def padded(count):
    return -(-count // 8) * 8


def packed_height(count):
    return -(-count // 16) * 16


def packed_rows(count, tile):
    return count * tile // 2 + packed_height(count)


def chunks_of(width):
    first = -(-width // 4) * 2
    return (0, first), (first, width - first)


def iotas(shape):
    return lax.broadcasted_iota(jnp.int32, shape, 0), lax.broadcasted_iota(jnp.int32, shape, 1)


def pack_block(block):
    tile = block.shape[0]
    half = tile // 2
    top, low = block[:half], block[half:]
    row, lane = iotas((half, tile))
    turned = pltpu.roll(low, half, 1)
    folded = jnp.where((lane < half) & (row > lane), turned, top)
    diagonal = jnp.sum(jnp.where(lane == row + half, low, 0.0), axis=0, keepdims=True)
    return folded, diagonal


def unpack_block(folded, diagonal):
    half, tile = folded.shape
    row, lane = iotas((half, tile))
    rolled = pltpu.roll(folded, half, 1)
    turned = jnp.transpose(jnp.concatenate([folded, rolled], axis=0))
    top = jnp.where((lane < half) & (row > lane), turned[:half], folded)
    low = jnp.where((lane >= half) & (row > lane - half), rolled, turned[half:])
    low = jnp.where(lane == row + half, diagonal, low)
    return jnp.concatenate([top, low], axis=0)


def partner_of(sector):
    return sector + 1 - 2 * lax.rem(sector, 2)


def live_limits(dims_ref, sector):
    count = dims_ref.shape[0]
    rows = dims_ref[sector]
    columns = []
    for charge in CHARGES:
        target = sector + charge
        columns.append(jnp.where(target < count, dims_ref[jnp.minimum(target, count - 1)], 0))
    return rows, columns


def weight_rows(weight_ref, width, p, square, turned):
    wide = padded(width)
    square[...] = jnp.zeros_like(square)
    square[:width, :width] = weight_ref[pl.ds(p, width, stride=len(CHARGES)), :]
    value = square[...]
    if turned:
        value = jnp.transpose(value)
    high = value.astype(BF16).astype(F32)
    joined = (high + pltpu.roll(value - high, wide, 1)).astype(BF16)
    return joined[: packed_height(width), : 2 * wide]


def doubled(value):
    return jnp.concatenate([value, value], axis=0).astype(BF16)


def pack_kernel(width, tile, source_ref, out_ref, held, diag, sems):
    half = tile // 2
    copies = sems.shape[0]
    edges = [width * k // copies for k in range(copies + 1)]
    pending = []
    for k in range(copies):
        at = pl.ds(edges[k] * tile, (edges[k + 1] - edges[k]) * tile)
        pending.append(pltpu.make_async_copy(source_ref.at[at, :], held.at[at, :], sems.at[k]))
        pending[-1].start()
    diag[...] = jnp.zeros_like(diag)
    for k in range(copies):
        pending[k].wait()
        for w in range(edges[k], edges[k + 1]):
            folded, diagonal = pack_block(held[w * tile : (w + 1) * tile, :].astype(F32))
            out_ref[w * half : (w + 1) * half, :] = folded.astype(BF16)
            diag[w : w + 1, :] = diagonal
    out_ref[width * half :, :] = diag[...].astype(BF16)


def unpack_into(count, tile, read, write, diag):
    half = tile // 2
    size = packed_height(count)
    diag[:size, :] = read(count * half, size)
    for w in range(count):
        write(w, unpack_block(read(w * half, half), diag[w : w + 1, :]))


def reader(ref):
    return lambda at, size: ref[at : at + size, :].astype(F32)


def unpack_kernel(width, tile, early_ref, late_ref, out_ref, diag):
    for (first, count), ref in zip(chunks_of(width), (early_ref, late_ref)):

        def write(w, block, first=first):
            out_ref[(first + w) * tile : (first + w + 1) * tile, :] = block.astype(BF16)

        unpack_into(count, tile, reader(ref), write, diag)


def fold_kernel(
    width, tile, travels, dims_ref, environ_ref, site_ref, far_environ_ref, far_site_ref, weight_ref, early_ref, late_ref,
    joined_s, turned_s, square_s, weight_s, half_s, packed_s, diag_s, sums_s, diag_sums_s,
):
    half = tile // 2
    pitch = half + 8
    wide = padded(width)
    sector = lax.axis_index("sec")
    partner = partner_of(sector)
    row, lane = iotas((tile, tile))

    def run(own_state, with_partner):
        rows, columns = live_limits(dims_ref, sector)
        live = (row < rows) & (lane < columns[own_state])
        sites = [jnp.where(live, site_ref[own_state].astype(F32), 0.0)]
        states = [own_state]
        if with_partner:
            rows, columns = live_limits(dims_ref, partner)
            for k in range(2):
                live = (row < rows) & (lane < columns[k + 1])
                sites.append(jnp.where(live, far_site_ref[k + 1].astype(F32), 0.0))
                states.append(k + 1)
        parts = len(states)
        for n in range(parts):
            joined_s[:, n * tile : (n + 1) * tile] = sites[n].astype(BF16)
            turned_s[n] = jnp.transpose(sites[n]).astype(BF16)
            weight_s[n] = weight_rows(weight_ref, width, states[n], square_s, True)
            packed_s[n, width * pitch :, :] = jnp.zeros(((wide - width) * pitch, tile), F32)
            diag_s[n] = jnp.zeros_like(diag_s[n])

        for pair in range(width // 2):
            at = slice(pair * tile, (pair + 1) * tile)
            for k in range(2):
                here = slice((pair * 2 + k) * tile, (pair * 2 + k + 1) * tile)
                blocks = [
                    jnp.dot(environ_ref[here, :], joined_s[:, :tile], preferred_element_type=F32)
                ]
                if with_partner:
                    both = jnp.dot(
                        far_environ_ref[here, :], joined_s[:, tile:], preferred_element_type=F32
                    )
                    blocks += [both[:, :tile], both[:, tile:]]
                for n in range(parts):
                    half_s[n, at, k * tile : (k + 1) * tile] = blocks[n].astype(BF16)
            for n in range(parts):
                both = jnp.dot(turned_s[n], half_s[n, at, :], preferred_element_type=F32)
                for k in range(2):
                    w = pair * 2 + k
                    folded, diagonal = pack_block(both[:, k * tile : (k + 1) * tile])
                    packed_s[n, w * pitch : w * pitch + half, :] = folded
                    diag_s[n, w : w + 1, :] = diagonal

        def mixed(inputs):
            value = None
            for n in range(parts):
                term = jnp.dot(weight_s[n], doubled(inputs[n]), preferred_element_type=F32)
                value = term if value is None else value + term
            return value[:wide]

        for at in range(0, half, 2):
            value = mixed([
                jnp.concatenate(
                    [packed_s[n, pl.ds(at + k, wide, stride=pitch), :] for k in range(2)], axis=1
                )
                for n in range(parts)
            ])
            for k in range(2):
                sums_s[pl.ds(at + k, wide, stride=pitch), :] = value[:, k * tile : (k + 1) * tile]
        diag_sums_s[...] = jnp.zeros_like(diag_sums_s)
        diag_sums_s[:wide, :] = mixed([diag_s[n, :wide] for n in range(parts)])
        for (first, count), ref in zip(chunks_of(width), (early_ref, late_ref)):
            for w in range(count):
                at = (first + w) * pitch
                ref[w * half : (w + 1) * half, :] = sums_s[at : at + half, :].astype(ref.dtype)
            rows = packed_height(count)
            ref[count * half :, :] = diag_sums_s[first : first + rows, :].astype(ref.dtype)

    even = lax.rem(sector, 2) == 0
    own_state = len(CHARGES) - 1 if travels else 0

    @pl.when(even)
    def _():
        run(own_state, travels)

    @pl.when(jnp.logical_not(even))
    def _():
        run(own_state, not travels)


def mix_into(width, tile, weights, wide_s, sums_s, out_ref):
    wide = padded(width)
    pitch = tile + 8
    wide_s[width * pitch :, :] = jnp.zeros_like(wide_s[width * pitch :, :])

    for at in range(0, tile, 2):
        value = doubled(
            jnp.concatenate(
                [wide_s[pl.ds(at + k, wide, stride=pitch), :] for k in range(2)], axis=1
            )
        )
        for index, weight in enumerate(weights):
            mixed = jnp.dot(weight[...], value, preferred_element_type=F32)[:wide]
            for k in range(2):
                sums_s[index, pl.ds(at + k, wide, stride=pitch), :] = mixed[:, k * tile : (k + 1) * tile]
    for index in range(len(weights)):
        for w in range(width):
            out_ref[index, :, w * tile : (w + 1) * tile] = sums_s[
                index, w * pitch : w * pitch + tile, :
            ].astype(BF16)


def unpack_wide(width, tile, read, wide_s, diag):
    def write(w, block):
        wide_s[w * (tile + 8) : w * (tile + 8) + tile, :] = block

    unpack_into(width, tile, read, write, diag)


def copy_wide(width, tile, source_ref, wide_s):
    for w in range(width):
        at = w * (tile + 8)
        wide_s[at : at + tile, :] = source_ref[w * tile : (w + 1) * tile, :].astype(F32)


def mix_own_kernel(width, tile, source_ref, weight_ref, out_ref, square_s, weight_s, wide_s, sums_s):
    weight_s[0] = weight_rows(weight_ref, width, 0, square_s, False)
    copy_wide(width, tile, source_ref, wide_s)
    mix_into(width, tile, [weight_s.at[0]], wide_s, sums_s, out_ref)


def mix_next_kernel(
    width, tile, near_ref, relay_ref, weight_ref, out_ref, square_s, weight_s, wide_s, sums_s, diag
):
    even = lax.rem(lax.axis_index("sec"), 2) == 0
    for k in range(2):
        weight_s[k] = weight_rows(weight_ref, width, k + 1, square_s, False)

    @pl.when(even)
    def _():
        copy_wide(width, tile, near_ref, wide_s)

    @pl.when(jnp.logical_not(even))
    def _():
        unpack_wide(width, tile, reader(relay_ref), wide_s, diag)

    mix_into(width, tile, [weight_s.at[k] for k in range(2)], wide_s, sums_s, out_ref)


def mix_after_kernel(
    width, tile, far_ref, weight_ref, out_ref, square_s, weight_s, wide_s, sums_s, diag
):
    weight_s[0] = weight_rows(weight_ref, width, 3, square_s, False)
    unpack_wide(width, tile, reader(far_ref), wide_s, diag)
    mix_into(width, tile, [weight_s.at[0]], wide_s, sums_s, out_ref)


def total(value):
    return jnp.sum(jnp.sum(value, axis=0, keepdims=True), axis=1, keepdims=True)


def put(stats, kind, lane_at, value):
    row, lane = iotas(stats.shape)
    return jnp.where((row == kind) & (lane == lane_at), value, stats)


def scaled(value):
    square = total(value * value)
    inverse = jnp.where(square > 0.0, lax.rsqrt(square), 0.0)
    return value * inverse, square * inverse


def right_products(width, tile, field, right_ref, out_ref, p):
    group, lanes = p // 2, slice(p % 2 * tile, (p % 2 + 1) * tile)
    for pair in range(width // 2):
        at = pair * 2 * tile
        both = jnp.dot(field, right_ref[:, at : at + 2 * tile], preferred_element_type=F32).astype(BF16)
        for k in range(2):
            out_ref[group, at + k * tile : at + (k + 1) * tile, lanes] = both[:, k * tile : (k + 1) * tile]


def head_kernel(
    width, tile, dims_ref, guess_ref, own_ref, next_ref, after_ref, vector_ref, stats_ref, product_ref
):
    states = len(CHARGES)
    sector = lax.axis_index("sec")
    rows, columns = live_limits(dims_ref, sector)
    row, lane = iotas((tile, tile))
    rights = [own_ref.at[0], next_ref.at[0], next_ref.at[1], after_ref.at[0]]
    stats = jnp.zeros(stats_ref.shape, F32)
    for p in range(states):
        live = (row < rows) & (lane < columns[p])
        vector, norm = scaled(jnp.where(live, guess_ref[p], 0.0))
        vector_ref[p] = vector
        stats = put(stats, 0, sector * states + p, norm)
        right_products(width, tile, vector.astype(BF16), rights[p], product_ref, p)
    stats_ref[...] = stats


def bound_blocks(first, count, tile, packed_ref, environ_ref, out_ref, diag):
    segment = lax.axis_index("seg")

    @pl.when(segment == 0)
    def _():
        for w in range(count):
            out_ref[:, w * tile : (w + 1) * tile] = environ_ref[
                (first + w) * tile : (first + w + 1) * tile, :
            ]

    @pl.when(segment != 0)
    def _():
        def write(w, block):
            out_ref[:, w * tile : (w + 1) * tile] = block.astype(BF16)

        unpack_into(count, tile, reader(packed_ref), write, diag)


def open_kernel(width, tile, packed_ref, environ_ref, product_ref, bound_ref, image_ref, diag):
    first, count = chunks_of(width)[0]
    bound_blocks(first, count, tile, packed_ref, environ_ref, bound_ref, diag)
    for group in range(len(CHARGES) // 2):
        image_ref[group] = jnp.dot(
            bound_ref[...], product_ref[group, : count * tile, :], preferred_element_type=F32
        )


def lanczos_kernel(
    width, tile, dims_ref, packed_ref, environ_ref, early_ref, image_ref, own_ref, next_ref, after_ref,
    start_ref, norm_ref, product_ref, basis_ref, stats_ref, late_s, product_s, diag,
):
    states = len(CHARGES)
    sector = lax.axis_index("sec")
    first, count = chunks_of(width)[1]
    bound_blocks(first, count, tile, packed_ref, environ_ref, late_s, diag)
    rows, columns = live_limits(dims_ref, sector)
    row, lane = iotas((tile, tile))
    rights = [own_ref.at[0], next_ref.at[0], next_ref.at[1], after_ref.at[0]]
    stats = norm_ref[...]
    split = first * tile
    betas = [None] * states
    for j in range(LANCZOS):
        source = product_ref if j == 0 else product_s
        for group in range(states // 2):
            members = (2 * group, 2 * group + 1)
            if j == 0:
                images = image_ref[group]
            else:
                for p in members:
                    field = basis_ref[j - 1, p].astype(BF16)
                    right_products(width, tile, field, rights[p], product_s, p)
                images = jnp.dot(early_ref[...], source[group, :split, :], preferred_element_type=F32)
            images = images + jnp.dot(
                late_s[...], source[group, split:, :], preferred_element_type=F32
            )
            for p in members:
                live = (row < rows) & (lane < columns[p])
                image = jnp.where(live, images[:, p % 2 * tile : (p % 2 + 1) * tile], 0.0)
                vector = start_ref[p] if j == 0 else basis_ref[j - 1, p]
                alpha = total(vector * image)
                image = image - alpha * vector
                if j > 0:
                    before = start_ref[p] if j == 1 else basis_ref[j - 2, p]
                    image = image - betas[p] * before
                following, beta = scaled(image)
                basis_ref[j, p] = following
                betas[p] = beta
                stats = put(stats, 1 + 2 * j, sector * states + p, alpha)
                stats = put(stats, 2 + 2 * j, sector * states + p, beta)
    stats_ref[...] = stats


def finish_kernel(entries, stats_ref, start_ref, basis_ref, vector_ref, table_ref):
    states = len(CHARGES)
    sector = lax.axis_index("sec")
    stats = stats_ref[0]
    for q in range(1, stats_ref.shape[0]):
        stats = stats + stats_ref[q]
    alphas = [stats[1 + 2 * j : 2 + 2 * j, :] for j in range(LANCZOS)]
    betas = [stats[2 + 2 * j : 3 + 2 * j, :] for j in range(LANCZOS)]

    def mean(left, right):
        products = left[0] * right[0]
        for x, y in zip(left[1:], right[1:]):
            products = products + x * y
        return jnp.sum(products, axis=1, keepdims=True) / entries

    start = [stats[0:1, :]]
    vector = [start[0] / jnp.sqrt(mean(start, start) + 1e-06)]
    previous = []
    beta = jnp.zeros((1, 1), F32)
    table_row, table_column = iotas(table_ref.shape)
    table = jnp.zeros(table_ref.shape, F32)
    for j in range(LANCZOS):
        image = []
        for k in range(j + 2):
            term = None
            if k > 0:
                term = betas[k - 1] * vector[k - 1]
            if k <= j:
                more = alphas[k] * vector[k]
                term = more if term is None else term + more
            if k + 1 <= j:
                term = term + betas[k] * vector[k + 1]
            image.append(term)
        alpha = mean(vector, image[: j + 1])
        for k in range(j + 1):
            image[k] = image[k] - alpha * vector[k]
        for k in range(j):
            image[k] = image[k] - beta * previous[k]
        beta = jnp.sqrt(mean(image, image) + 1e-06)
        previous = vector
        vector = [value / beta for value in image]
        table = jnp.where((table_row == 0) & (table_column == j), alpha, table)
        table = jnp.where((table_row == 1) & (table_column == j), beta, table)
    table_ref[...] = table
    lane = lax.broadcasted_iota(jnp.int32, (1, stats.shape[1]), 1)
    for p in range(states):
        value = None
        here = lane == sector * states + p
        for k in range(LANCZOS + 1):
            weight = jnp.sum(jnp.where(here, vector[k], 0.0), axis=1, keepdims=True)
            term = weight * (start_ref[p] if k == 0 else basis_ref[k - 1, p])
            value = term if value is None else value + term
        vector_ref[p] = value


def smem():
    return pl.BlockSpec(memory_space=pltpu.SMEM)


def vmem():
    return pl.BlockSpec(memory_space=pltpu.VMEM)


def call(name, kernel, scalars, arrays, outs, scratch, limit, micros, space=pltpu.VMEM):
    many = isinstance(outs, (tuple, list))
    return pl.pallas_call(
        kernel,
        out_shape=outs,
        in_specs=[smem()] * len(scalars)
        + [pl.BlockSpec(memory_space=space)] * len(arrays),
        out_specs=[vmem()] * len(outs) if many else vmem(),
        scratch_shapes=scratch,
        compiler_params=pltpu.CompilerParams(vmem_limit_bytes=limit * MIB),
        name=name,
        cost_estimate=pl.CostEstimate(
            flops=int(micros * 1.1e9), bytes_accessed=0, transcendentals=0
        ),
    )(*scalars, *arrays)


def pairs_of(count, pick):
    return [(source, target) for source in range(count) for target in pick(source) if 0 <= target < count]


def gathered(value, axis):
    count = lax.axis_size(axis)
    return lax.all_to_all(jnp.broadcast_to(value, (count,) + value.shape), axis, 0, 0)


def on_device(left_env, right_env, site_tensors, mpo, boundary_mpo, guess, sector_dims):
    width, tile = left_env.shape[2], left_env.shape[-1]
    half = tile // 2
    wide = padded(width)
    states = len(CHARGES)
    sector_count = sector_dims.shape[0]
    sectors = lax.axis_size("sec")
    segments = lax.axis_size("seg")
    prows = packed_rows(width, tile)
    drows = prows - width * half
    packed = jax.ShapeDtypeStruct((prows, tile), BF16)
    parts = chunks_of(width)

    def packed_parts(dtype):
        return [jax.ShapeDtypeStruct((packed_rows(count, tile), tile), dtype) for _, count in parts]

    def mixed(count):
        return jax.ShapeDtypeStruct((count, tile, width * tile), BF16)

    environ = left_env.reshape(width * tile, tile)
    right = right_env.reshape(width * tile, tile)
    site = site_tensors[0, 0, :, 0]
    site_weights = jnp.transpose(mpo[0, 0], (0, 2, 1)).reshape(width * states, width)
    bound_weights = jnp.transpose(boundary_mpo[0], (0, 2, 1)).reshape(width * states, width)

    swap = pairs_of(sectors, lambda q: [q ^ 1])
    across = pairs_of(sectors, lambda q: [q + 1] if q % 2 == 0 else [])
    down = pairs_of(sectors, lambda q: [q - 1] if q % 2 else [])
    up_two = pairs_of(sectors, lambda q: [q + 2])
    down_two = pairs_of(sectors, lambda q: [q - 2])
    onward = pairs_of(segments, lambda s: [s + 1])
    diag = pltpu.VMEM((drows, tile), F32)

    def mix_scratch(count):
        return [
            pltpu.VMEM((tile, tile), F32),
            pltpu.VMEM((count, packed_height(width), 2 * wide), BF16),
            pltpu.VMEM((wide * (tile + 8), tile), F32),
            pltpu.VMEM((count, wide * (tile + 8), tile), F32),
        ]

    right_packed = call(
        "pack_right", functools.partial(pack_kernel, width, tile), [], [right], packed,
        [pltpu.VMEM((width * tile, tile), BF16), diag, pltpu.SemaphoreType.DMA((4,))], 6, 1, pltpu.HBM,
    )
    right_far = lax.ppermute(right_packed, "sec", down_two)
    far_environ = lax.ppermute(environ, "sec", swap)
    far_site = lax.ppermute(site, "sec", swap)
    fold_scratch = [
        pltpu.VMEM((tile, 3 * tile), BF16),
        pltpu.VMEM((3, tile, tile), BF16),
        pltpu.VMEM((tile, tile), F32),
        pltpu.VMEM((3, packed_height(width), 2 * wide), BF16),
        pltpu.VMEM((3, width // 2 * tile, 2 * tile), BF16),
        pltpu.VMEM((3, wide * (half + 8), tile), F32),
        pltpu.VMEM((3, drows, tile), F32),
        pltpu.VMEM((wide * (half + 8), tile), F32),
        pltpu.VMEM((drows, tile), F32),
    ]
    outgoing = call(
        "fold_up", functools.partial(fold_kernel, width, tile, True),
        [sector_dims], [environ, site, far_environ, far_site, site_weights], packed_parts(BF16),
        fold_scratch, 20, 12,
    )
    early_arrived = lax.ppermute(outgoing[0], "sec", up_two)
    far_environ, outgoing = lax.optimization_barrier((far_environ, outgoing))
    kept = call(
        "fold_own", functools.partial(fold_kernel, width, tile, False),
        [sector_dims], [environ, site, far_environ, far_site, site_weights], packed_parts(F32),
        fold_scratch, 20, 0.1,
    )
    kept, late_outgoing = lax.optimization_barrier((kept, outgoing[1]))
    late_arrived = lax.ppermute(late_outgoing, "sec", up_two)
    kept, right = lax.optimization_barrier((kept, right))
    right_near = lax.ppermute(right, "sec", down)
    own_mixed = call(
        "mix_own", functools.partial(mix_own_kernel, width, tile), [], [right, bound_weights],
        mixed(1), mix_scratch(1), 12, 1,
    )
    own_mixed, right_far = lax.optimization_barrier((own_mixed, right_far))
    right_relay = lax.ppermute(right_far, "sec", across)
    after_mixed = call(
        "mix_after", functools.partial(mix_after_kernel, width, tile), [],
        [right_far, bound_weights], mixed(1), mix_scratch(1) + [diag], 12, 2,
    )
    early_arrived, own_mixed, after_mixed = lax.optimization_barrier(
        (early_arrived, own_mixed, after_mixed)
    )
    early = (kept[0] + early_arrived.astype(F32)).astype(BF16)
    early_bound = lax.ppermute(early, "seg", onward)
    early, late_arrived = lax.optimization_barrier((early, late_arrived))
    late = (kept[1] + late_arrived.astype(F32)).astype(BF16)
    late_bound = lax.ppermute(late, "seg", onward)
    late, right_near, right_relay = lax.optimization_barrier((late, right_near, right_relay))
    next_mixed = call(
        "mix_next", functools.partial(mix_next_kernel, width, tile), [],
        [right_near, right_relay, bound_weights], mixed(2), mix_scratch(2) + [diag], 16, 3,
    )
    start, norms, products = call(
        "head", functools.partial(head_kernel, width, tile),
        [sector_dims], [guess[0, :, 0], own_mixed, next_mixed, after_mixed],
        (
            jax.ShapeDtypeStruct((states, tile, tile), F32),
            jax.ShapeDtypeStruct((16, 128), F32),
            jax.ShapeDtypeStruct((states // 2, width * tile, 2 * tile), BF16),
        ),
        [], 14, 2,
    )
    new_env = call(
        "unpack_env", functools.partial(unpack_kernel, width, tile), [], [early, late],
        jax.ShapeDtypeStruct((width * tile, tile), BF16), [diag], 6, 2,
    )
    early_bound, products, new_env = lax.optimization_barrier((early_bound, products, new_env))
    bound, image = call(
        "open", functools.partial(open_kernel, width, tile), [], [early_bound, environ, products],
        (
            jax.ShapeDtypeStruct((tile, parts[0][1] * tile), BF16),
            jax.ShapeDtypeStruct((states // 2, tile, 2 * tile), F32),
        ),
        [diag], 12, 1,
    )
    late_bound, bound = lax.optimization_barrier((late_bound, bound))
    basis, stats = call(
        "lanczos", functools.partial(lanczos_kernel, width, tile),
        [sector_dims],
        [late_bound, environ, bound, image, own_mixed, next_mixed, after_mixed, start, norms, products],
        (
            jax.ShapeDtypeStruct((LANCZOS, states, tile, tile), F32),
            jax.ShapeDtypeStruct((16, 128), F32),
        ),
        [
            pltpu.VMEM((tile, parts[1][1] * tile), BF16),
            pltpu.VMEM((states // 2, width * tile, 2 * tile), BF16),
            diag,
        ],
        22, 12,
    )
    stats = gathered(stats, "sec")
    entries = float(states * sector_count * tile * tile)
    vector, table = call(
        "finish", functools.partial(finish_kernel, entries), [], [stats, start, basis],
        (
            jax.ShapeDtypeStruct((states, tile, tile), F32),
            jax.ShapeDtypeStruct((2, LANCZOS), F32),
        ),
        [], 6, 2,
    )
    return new_env.reshape(left_env.shape), vector[None, :, None], jnp.transpose(table)[None]


def solution(mesh):
    placed = (
        P("seg", "sec", None, None, None),
        P("seg", "sec", None, None, None),
        P("seg", None, None, "sec", None, None),
        P("seg", None, None, None, None),
        P("seg", None, None, None),
        P("seg", None, "sec", None, None),
        P(),
    )
    return jax.shard_map(
        on_device,
        mesh=mesh,
        in_specs=placed,
        out_specs=(
            P("seg", "sec", None, None, None),
            P("seg", None, "sec", None, None),
            P("seg", None, None),
        ),
        check_vma=False,
    )
```

```python
import functools

import jax
import jax.numpy as jnp
from jax import lax
from jax.experimental import pallas as pl
from jax.experimental.pallas import tpu as pltpu
from jax.sharding import PartitionSpec as P

LANCZOS = 4
CHARGES = (0, 1, 1, 2)
F32 = jnp.float32
BF16 = jnp.bfloat16
MIB = 1024 * 1024


def padded(count):
    return -(-count // 8) * 8


def packed_height(count):
    return -(-count // 16) * 16


def packed_rows(count, tile):
    return count * tile // 2 + packed_height(count)


def chunks_of(width):
    first = -(-width // 4) * 2
    return (0, first), (first, width - first)


def iotas(shape):
    return lax.broadcasted_iota(jnp.int32, shape, 0), lax.broadcasted_iota(jnp.int32, shape, 1)


def pack_block(block):
    tile = block.shape[0]
    half = tile // 2
    top, low = block[:half], block[half:]
    row, lane = iotas((half, tile))
    turned = pltpu.roll(low, half, 1)
    folded = jnp.where((lane < half) & (row > lane), turned, top)
    diagonal = jnp.sum(jnp.where(lane == row + half, low, 0.0), axis=0, keepdims=True)
    return folded, diagonal


def unpack_block(folded, diagonal):
    half, tile = folded.shape
    row, lane = iotas((half, tile))
    rolled = pltpu.roll(folded, half, 1)
    turned = jnp.transpose(jnp.concatenate([folded, rolled], axis=0))
    top = jnp.where((lane < half) & (row > lane), turned[:half], folded)
    low = jnp.where((lane >= half) & (row > lane - half), rolled, turned[half:])
    low = jnp.where(lane == row + half, diagonal, low)
    return jnp.concatenate([top, low], axis=0)


def partner_of(sector):
    return sector + 1 - 2 * lax.rem(sector, 2)


def live_limits(dims_ref, sector):
    count = dims_ref.shape[0]
    rows = dims_ref[sector]
    columns = []
    for charge in CHARGES:
        target = sector + charge
        columns.append(jnp.where(target < count, dims_ref[jnp.minimum(target, count - 1)], 0))
    return rows, columns


def weight_rows(weight_ref, width, p, square, turned):
    wide = padded(width)
    square[...] = jnp.zeros_like(square)
    square[:width, :width] = weight_ref[pl.ds(p, width, stride=len(CHARGES)), :]
    value = square[...]
    if turned:
        value = jnp.transpose(value)
    high = value.astype(BF16).astype(F32)
    joined = (high + pltpu.roll(value - high, wide, 1)).astype(BF16)
    return joined[: packed_height(width), : 2 * wide]


def doubled(value):
    return jnp.concatenate([value, value], axis=0).astype(BF16)


def joined_weights(weight_ref, width, states, square, turned):
    wide = padded(width)
    tile = square.shape[0]
    highs = lows = None
    for n, p in enumerate(states):
        square[...] = jnp.zeros_like(square)
        square[:width, :width] = weight_ref[pl.ds(p, width, stride=len(CHARGES)), :]
        value = square[...]
        if turned:
            value = jnp.transpose(value)
        high = value.astype(BF16).astype(F32)
        low = value - high
        if n:
            high, low = pltpu.roll(high, n * wide, 1), pltpu.roll(low, n * wide, 1)
        highs = high if highs is None else highs + high
        lows = low if lows is None else lows + low
    used = len(states) * wide
    assert used <= tile
    if 2 * used <= tile:
        joined = highs + pltpu.roll(lows, used, 1)
    else:
        joined = jnp.concatenate([highs, lows], axis=1)
    return joined.astype(BF16)[: packed_height(width)]


def joined_rows(values, tile):
    used = sum(value.shape[0] for value in values)
    if 2 * used <= tile:
        gap = jnp.zeros((tile - 2 * used, values[0].shape[1]), F32)
        return jnp.concatenate(list(values) * 2 + [gap], axis=0).astype(BF16)
    gap = jnp.zeros((tile - used, values[0].shape[1]), F32)
    value = jnp.concatenate(list(values) + [gap], axis=0).astype(BF16)
    return jnp.concatenate([value, value], axis=0)


def pack_kernel(width, tile, source_ref, out_ref, diag):
    half = tile // 2
    diag[...] = jnp.zeros_like(diag)
    for w in range(width):
        folded, diagonal = pack_block(source_ref[w * tile : (w + 1) * tile, :].astype(F32))
        out_ref[w * half : (w + 1) * half, :] = folded.astype(BF16)
        diag[w : w + 1, :] = diagonal
    out_ref[width * half :, :] = diag[...].astype(BF16)


def unpack_into(count, tile, read, write, diag):
    half = tile // 2
    size = packed_height(count)
    diag[:size, :] = read(count * half, size)
    for w in range(count):
        write(w, unpack_block(read(w * half, half), diag[w : w + 1, :]))


def reader(ref):
    return lambda at, size: ref[at : at + size, :].astype(F32)


def fold_kernel(
    width, tile, travels, dims_ref, environ_ref, site_ref, far_environ_ref, far_site_ref, weight_ref, early_ref, late_ref,
    joined_s, turned_s, square_s, weight_s, half_s, packed_s, diag_s, sums_s, diag_sums_s,
):
    half = tile // 2
    pitch = half + 8
    wide = padded(width)
    sector = lax.axis_index("sec")
    partner = partner_of(sector)
    row, lane = iotas((tile, tile))

    def run(own_state, with_partner):
        rows, columns = live_limits(dims_ref, sector)
        live = (row < rows) & (lane < columns[own_state])
        sites = [jnp.where(live, site_ref[own_state].astype(F32), 0.0)]
        states = [own_state]
        if with_partner:
            rows, columns = live_limits(dims_ref, partner)
            for k in range(2):
                live = (row < rows) & (lane < columns[k + 1])
                sites.append(jnp.where(live, far_site_ref[k + 1].astype(F32), 0.0))
                states.append(k + 1)
        parts = len(states)
        for n in range(parts):
            joined_s[:, n * tile : (n + 1) * tile] = sites[n].astype(BF16)
            turned_s[n] = jnp.transpose(sites[n]).astype(BF16)
            packed_s[n, width * pitch :, :] = jnp.zeros(((wide - width) * pitch, tile), F32)
            diag_s[n] = jnp.zeros_like(diag_s[n])
        weights = joined_weights(weight_ref, width, states, square_s, True)
        weight_s[:, : weights.shape[1]] = weights

        for pair in range(width // 2):
            at = slice(pair * tile, (pair + 1) * tile)
            here = slice(pair * 2 * tile, (pair + 1) * 2 * tile)
            blocks = [jnp.dot(environ_ref[here, :], joined_s[:, :tile], preferred_element_type=F32)]
            if with_partner:
                both = jnp.dot(far_environ_ref[here, :], joined_s[:, tile:], preferred_element_type=F32)
                blocks += [both[:, :tile], both[:, tile:]]
            for n in range(parts):
                block = blocks[n].astype(BF16)
                for k in range(2):
                    half_s[n, at, k * tile : (k + 1) * tile] = block[k * tile : (k + 1) * tile]
            for n in range(parts):
                both = jnp.dot(turned_s[n], half_s[n, at, :], preferred_element_type=F32)
                for k in range(2):
                    w = pair * 2 + k
                    folded, diagonal = pack_block(both[:, k * tile : (k + 1) * tile])
                    packed_s[n, w * pitch : w * pitch + half, :] = folded
                    diag_s[n, w : w + 1, :] = diagonal

        def mixed(inputs):
            value = joined_rows(inputs, tile)
            return jnp.dot(weight_s[:, : value.shape[0]], value, preferred_element_type=F32)[:wide]

        for at in range(0, half, 2):
            value = mixed([
                jnp.concatenate(
                    [packed_s[n, pl.ds(at + k, wide, stride=pitch), :] for k in range(2)], axis=1
                )
                for n in range(parts)
            ])
            for k in range(2):
                sums_s[pl.ds(at + k, wide, stride=pitch), :] = value[:, k * tile : (k + 1) * tile]
        diag_sums_s[...] = jnp.zeros_like(diag_sums_s)
        diag_sums_s[:wide, :] = mixed([diag_s[n, :wide] for n in range(parts)])
        for (first, count), ref in zip(chunks_of(width), (early_ref, late_ref)):
            for w in range(count):
                at = (first + w) * pitch
                ref[w * half : (w + 1) * half, :] = sums_s[at : at + half, :].astype(ref.dtype)
            rows = packed_height(count)
            ref[count * half :, :] = diag_sums_s[first : first + rows, :].astype(ref.dtype)

    even = lax.rem(sector, 2) == 0
    own_state = len(CHARGES) - 1 if travels else 0

    @pl.when(even)
    def _():
        run(own_state, travels)

    @pl.when(jnp.logical_not(even))
    def _():
        run(own_state, not travels)


def mix_into(width, tile, weights, wide_s, sums_s, out_ref):
    wide = padded(width)
    pitch = tile + 8
    wide_s[width * pitch :, :] = jnp.zeros_like(wide_s[width * pitch :, :])

    for at in range(0, tile, 2):
        value = doubled(
            jnp.concatenate(
                [wide_s[pl.ds(at + k, wide, stride=pitch), :] for k in range(2)], axis=1
            )
        )
        for index, weight in enumerate(weights):
            mixed = jnp.dot(weight[...], value, preferred_element_type=F32)[:wide]
            for k in range(2):
                sums_s[index, pl.ds(at + k, wide, stride=pitch), :] = mixed[:, k * tile : (k + 1) * tile]
    for index in range(len(weights)):
        for w in range(width):
            out_ref[index, :, w * tile : (w + 1) * tile] = sums_s[
                index, w * pitch : w * pitch + tile, :
            ].astype(BF16)


def unpack_wide(width, tile, read, wide_s, diag):
    def write(w, block):
        wide_s[w * (tile + 8) : w * (tile + 8) + tile, :] = block

    unpack_into(width, tile, read, write, diag)


def copy_wide(width, tile, source_ref, wide_s):
    for w in range(width):
        at = w * (tile + 8)
        wide_s[at : at + tile, :] = source_ref[w * tile : (w + 1) * tile, :].astype(F32)


def mix_own_kernel(width, tile, source_ref, weight_ref, out_ref, square_s, weight_s, wide_s, sums_s):
    weight_s[0] = weight_rows(weight_ref, width, 0, square_s, False)
    copy_wide(width, tile, source_ref, wide_s)
    mix_into(width, tile, [weight_s.at[0]], wide_s, sums_s, out_ref)


def mix_next_kernel(
    width, tile, near_ref, weight_ref, out_ref, square_s, weight_s, wide_s, sums_s, diag
):
    for k in range(2):
        weight_s[k] = weight_rows(weight_ref, width, k + 1, square_s, False)
    unpack_wide(width, tile, reader(near_ref), wide_s, diag)
    mix_into(width, tile, [weight_s.at[k] for k in range(2)], wide_s, sums_s, out_ref)


def mix_after_kernel(
    width, tile, far_ref, weight_ref, out_ref, square_s, weight_s, wide_s, sums_s, diag
):
    weight_s[0] = weight_rows(weight_ref, width, 3, square_s, False)
    unpack_wide(width, tile, reader(far_ref), wide_s, diag)
    mix_into(width, tile, [weight_s.at[0]], wide_s, sums_s, out_ref)


def total(value):
    return jnp.sum(jnp.sum(value, axis=0, keepdims=True), axis=1, keepdims=True)


def put(stats, kind, lane_at, value):
    row, lane = iotas(stats.shape)
    return jnp.where((row == kind) & (lane == lane_at), value, stats)


def scaled(value):
    square = total(value * value)
    inverse = jnp.where(square > 0.0, lax.rsqrt(square), 0.0)
    return value * inverse, square * inverse


def right_products(width, tile, field, right_ref, out_ref, p):
    group, lanes = p // 2, slice(p % 2 * tile, (p % 2 + 1) * tile)
    for pair in range(width // 2):
        at = pair * 2 * tile
        both = jnp.dot(field, right_ref[:, at : at + 2 * tile], preferred_element_type=F32).astype(BF16)
        for k in range(2):
            out_ref[group, at + k * tile : at + (k + 1) * tile, lanes] = both[:, k * tile : (k + 1) * tile]


def head_kernel(
    width, tile, dims_ref, guess_ref, own_ref, next_ref, after_ref, vector_ref, stats_ref, product_ref
):
    states = len(CHARGES)
    sector = lax.axis_index("sec")
    rows, columns = live_limits(dims_ref, sector)
    row, lane = iotas((tile, tile))
    rights = [own_ref.at[0], next_ref.at[0], next_ref.at[1], after_ref.at[0]]
    stats = jnp.zeros(stats_ref.shape, F32)
    for p in range(states):
        live = (row < rows) & (lane < columns[p])
        vector, norm = scaled(jnp.where(live, guess_ref[p], 0.0))
        vector_ref[p] = vector
        stats = put(stats, 0, sector * states + p, norm)
        right_products(width, tile, vector.astype(BF16), rights[p], product_ref, p)
    stats_ref[...] = stats


def bound_blocks(first, count, tile, packed_ref, environ_ref, out_ref, diag):
    segment = lax.axis_index("seg")

    @pl.when(segment == 0)
    def _():
        for w in range(count):
            out_ref[:, w * tile : (w + 1) * tile] = environ_ref[
                (first + w) * tile : (first + w + 1) * tile, :
            ]

    @pl.when(segment != 0)
    def _():
        def write(w, block):
            out_ref[:, w * tile : (w + 1) * tile] = block.astype(BF16)

        unpack_into(count, tile, reader(packed_ref), write, diag)


def open_kernel(width, tile, packed_ref, environ_ref, product_ref, bound_ref, image_ref, diag):
    first, count = chunks_of(width)[0]
    bound_blocks(first, count, tile, packed_ref, environ_ref, bound_ref, diag)
    for group in range(len(CHARGES) // 2):
        image_ref[group] = jnp.dot(
            bound_ref[...], product_ref[group, : count * tile, :], preferred_element_type=F32
        )


def lanczos_kernel(
    width, tile, dims_ref, packed_ref, environ_ref, early_ref, image_ref, own_ref, next_ref, after_ref,
    start_ref, norm_ref, product_ref, fresh_early_ref, fresh_late_ref, basis_ref, stats_ref, env_ref,
    late_s, product_s, env_s, diag, sem,
):
    states = len(CHARGES)
    sector = lax.axis_index("sec")
    first, count = chunks_of(width)[1]
    bound_blocks(first, count, tile, packed_ref, environ_ref, late_s, diag)
    rows, columns = live_limits(dims_ref, sector)
    row, lane = iotas((tile, tile))
    rights = [own_ref.at[0], next_ref.at[0], next_ref.at[1], after_ref.at[0]]
    stats = norm_ref[...]
    split = first * tile
    betas = [None] * states
    copy = pltpu.make_async_copy(env_s, env_ref, sem)
    for j in range(LANCZOS):
        if j == 1:
            for (begin, size), ref in zip(chunks_of(width), (fresh_early_ref, fresh_late_ref)):

                def write(w, block, begin=begin):
                    at = (begin + w) * tile
                    env_s[at : at + tile, :] = block.astype(BF16)

                unpack_into(size, tile, reader(ref), write, diag)
            copy.start()
        source = product_ref if j == 0 else product_s
        for group in range(states // 2):
            members = (2 * group, 2 * group + 1)
            if j == 0:
                images = image_ref[group]
            else:
                for p in members:
                    field = basis_ref[j - 1, p].astype(BF16)
                    right_products(width, tile, field, rights[p], product_s, p)
                images = jnp.dot(early_ref[...], source[group, :split, :], preferred_element_type=F32)
            images = images + jnp.dot(
                late_s[...], source[group, split:, :], preferred_element_type=F32
            )
            for p in members:
                live = (row < rows) & (lane < columns[p])
                image = jnp.where(live, images[:, p % 2 * tile : (p % 2 + 1) * tile], 0.0)
                vector = start_ref[p] if j == 0 else basis_ref[j - 1, p]
                alpha = total(vector * image)
                image = image - alpha * vector
                if j > 0:
                    before = start_ref[p] if j == 1 else basis_ref[j - 2, p]
                    image = image - betas[p] * before
                following, beta = scaled(image)
                basis_ref[j, p] = following
                betas[p] = beta
                stats = put(stats, 1 + 2 * j, sector * states + p, alpha)
                stats = put(stats, 2 + 2 * j, sector * states + p, beta)
    stats_ref[...] = stats
    copy.wait()


def finish_kernel(entries, stats_ref, start_ref, basis_ref, vector_ref, table_ref):
    states = len(CHARGES)
    sector = lax.axis_index("sec")
    stats = stats_ref[0]
    for q in range(1, stats_ref.shape[0]):
        stats = stats + stats_ref[q]
    alphas = [stats[1 + 2 * j : 2 + 2 * j, :] for j in range(LANCZOS)]
    betas = [stats[2 + 2 * j : 3 + 2 * j, :] for j in range(LANCZOS)]

    def mean(left, right):
        products = left[0] * right[0]
        for x, y in zip(left[1:], right[1:]):
            products = products + x * y
        return jnp.sum(products, axis=1, keepdims=True) / entries

    start = [stats[0:1, :]]
    vector = [start[0] / jnp.sqrt(mean(start, start) + 1e-06)]
    previous = []
    beta = jnp.zeros((1, 1), F32)
    table_row, table_column = iotas(table_ref.shape)
    table = jnp.zeros(table_ref.shape, F32)
    for j in range(LANCZOS):
        image = []
        for k in range(j + 2):
            term = None
            if k > 0:
                term = betas[k - 1] * vector[k - 1]
            if k <= j:
                more = alphas[k] * vector[k]
                term = more if term is None else term + more
            if k + 1 <= j:
                term = term + betas[k] * vector[k + 1]
            image.append(term)
        alpha = mean(vector, image[: j + 1])
        for k in range(j + 1):
            image[k] = image[k] - alpha * vector[k]
        for k in range(j):
            image[k] = image[k] - beta * previous[k]
        beta = jnp.sqrt(mean(image, image) + 1e-06)
        previous = vector
        vector = [value / beta for value in image]
        table = jnp.where((table_row == 0) & (table_column == j), alpha, table)
        table = jnp.where((table_row == 1) & (table_column == j), beta, table)
    table_ref[...] = table
    lane = lax.broadcasted_iota(jnp.int32, (1, stats.shape[1]), 1)
    for p in range(states):
        value = None
        here = lane == sector * states + p
        for k in range(LANCZOS + 1):
            weight = jnp.sum(jnp.where(here, vector[k], 0.0), axis=1, keepdims=True)
            term = weight * (start_ref[p] if k == 0 else basis_ref[k - 1, p])
            value = term if value is None else value + term
        vector_ref[p] = value


def smem():
    return pl.BlockSpec(memory_space=pltpu.SMEM)


def vmem():
    return pl.BlockSpec(memory_space=pltpu.VMEM)


def call(name, kernel, scalars, arrays, outs, scratch, limit, micros, out_specs=None):
    many = isinstance(outs, (tuple, list))
    return pl.pallas_call(
        kernel,
        out_shape=outs,
        in_specs=[smem()] * len(scalars) + [vmem()] * len(arrays),
        out_specs=out_specs or ([vmem()] * len(outs) if many else vmem()),
        scratch_shapes=scratch,
        compiler_params=pltpu.CompilerParams(vmem_limit_bytes=limit * MIB),
        name=name,
        cost_estimate=pl.CostEstimate(
            flops=int(micros * 1.1e9), bytes_accessed=0, transcendentals=0
        ),
    )(*scalars, *arrays)


def pairs_of(count, pick):
    return [(source, target) for source in range(count) for target in pick(source) if 0 <= target < count]


def on_device(left_env, right_env, site_tensors, mpo, boundary_mpo, guess, sector_dims):
    width, tile = left_env.shape[2], left_env.shape[-1]
    half = tile // 2
    wide = padded(width)
    states = len(CHARGES)
    sector_count = sector_dims.shape[0]
    sectors = lax.axis_size("sec")
    segments = lax.axis_size("seg")
    prows = packed_rows(width, tile)
    drows = prows - width * half
    packed = jax.ShapeDtypeStruct((prows, tile), BF16)
    parts = chunks_of(width)

    def packed_parts(dtype):
        return [jax.ShapeDtypeStruct((packed_rows(count, tile), tile), dtype) for _, count in parts]

    def mixed(count):
        return jax.ShapeDtypeStruct((count, tile, width * tile), BF16)

    environ = left_env.reshape(width * tile, tile)
    right = right_env.reshape(width * tile, tile)
    site = site_tensors[0, 0, :, 0]
    site_weights = jnp.transpose(mpo[0, 0], (0, 2, 1)).reshape(width * states, width)
    bound_weights = jnp.transpose(boundary_mpo[0], (0, 2, 1)).reshape(width * states, width)

    swap = pairs_of(sectors, lambda q: [q ^ 1])
    up_two = pairs_of(sectors, lambda q: [q + 2])
    down_two = pairs_of(sectors, lambda q: [q - 2])
    onward = pairs_of(segments, lambda s: [s + 1])
    diag = pltpu.VMEM((drows, tile), F32)

    def mix_scratch(count):
        return [
            pltpu.VMEM((tile, tile), F32),
            pltpu.VMEM((count, packed_height(width), 2 * wide), BF16),
            pltpu.VMEM((wide * (tile + 8), tile), F32),
            pltpu.VMEM((count, wide * (tile + 8), tile), F32),
        ]

    right_packed = call(
        "pack_right", functools.partial(pack_kernel, width, tile), [], [right], packed,
        [diag], 6, 1,
    )
    right_far = lax.ppermute(right_packed, "sec", down_two)
    far_environ = lax.ppermute(environ, "sec", swap)
    far_site = lax.ppermute(site, "sec", swap)
    fold_scratch = [
        pltpu.VMEM((tile, 3 * tile), BF16),
        pltpu.VMEM((3, tile, tile), BF16),
        pltpu.VMEM((tile, tile), F32),
        pltpu.VMEM((packed_height(width), 2 * tile), BF16),
        pltpu.VMEM((3, width // 2 * tile, 2 * tile), BF16),
        pltpu.VMEM((3, wide * (half + 8), tile), F32),
        pltpu.VMEM((3, drows, tile), F32),
        pltpu.VMEM((wide * (half + 8), tile), F32),
        pltpu.VMEM((drows, tile), F32),
    ]
    outgoing = call(
        "fold_up", functools.partial(fold_kernel, width, tile, True),
        [sector_dims], [environ, site, far_environ, far_site, site_weights], packed_parts(BF16),
        fold_scratch, 20, 12,
    )
    early_arrived = lax.ppermute(outgoing[0], "sec", up_two)
    far_environ, outgoing = lax.optimization_barrier((far_environ, outgoing))
    kept = call(
        "fold_own", functools.partial(fold_kernel, width, tile, False),
        [sector_dims], [environ, site, far_environ, far_site, site_weights], packed_parts(F32),
        fold_scratch, 20, 0.1,
    )
    kept, late_outgoing = lax.optimization_barrier((kept, outgoing[1]))
    late_arrived = lax.ppermute(late_outgoing, "sec", up_two)
    kept, right = lax.optimization_barrier((kept, right))
    own_mixed = call(
        "mix_own", functools.partial(mix_own_kernel, width, tile), [], [right, bound_weights],
        mixed(1), mix_scratch(1), 12, 1,
    )
    own_mixed, right_far = lax.optimization_barrier((own_mixed, right_far))
    even = lax.rem(lax.axis_index("sec"), 2) == 0
    right_near = lax.ppermute(jnp.where(even, right_far, right_packed), "sec", swap)
    after_mixed = call(
        "mix_after", functools.partial(mix_after_kernel, width, tile), [],
        [right_far, bound_weights], mixed(1), mix_scratch(1) + [diag], 12, 2,
    )
    early_arrived, own_mixed, after_mixed = lax.optimization_barrier(
        (early_arrived, own_mixed, after_mixed)
    )
    early = (kept[0] + early_arrived.astype(F32)).astype(BF16)
    early_bound = lax.ppermute(early, "seg", onward)
    early, late_arrived = lax.optimization_barrier((early, late_arrived))
    late = (kept[1] + late_arrived.astype(F32)).astype(BF16)
    late_bound = lax.ppermute(late, "seg", onward)
    late, right_near = lax.optimization_barrier((late, right_near))
    next_mixed = call(
        "mix_next", functools.partial(mix_next_kernel, width, tile), [],
        [right_near, bound_weights], mixed(2), mix_scratch(2) + [diag], 16, 3,
    )
    start, norms, products = call(
        "head", functools.partial(head_kernel, width, tile),
        [sector_dims], [guess[0, :, 0], own_mixed, next_mixed, after_mixed],
        (
            jax.ShapeDtypeStruct((states, tile, tile), F32),
            jax.ShapeDtypeStruct((16, 128), F32),
            jax.ShapeDtypeStruct((states // 2, width * tile, 2 * tile), BF16),
        ),
        [], 14, 2,
    )
    early_bound, products = lax.optimization_barrier((early_bound, products))
    bound, image = call(
        "open", functools.partial(open_kernel, width, tile), [], [early_bound, environ, products],
        (
            jax.ShapeDtypeStruct((tile, parts[0][1] * tile), BF16),
            jax.ShapeDtypeStruct((states // 2, tile, 2 * tile), F32),
        ),
        [diag], 12, 1,
    )
    late_bound, bound = lax.optimization_barrier((late_bound, bound))
    basis, stats, new_env = call(
        "lanczos", functools.partial(lanczos_kernel, width, tile),
        [sector_dims],
        [late_bound, environ, bound, image, own_mixed, next_mixed, after_mixed, start, norms, products,
         early, late],
        (
            jax.ShapeDtypeStruct((LANCZOS, states, tile, tile), F32),
            jax.ShapeDtypeStruct((16, 128), F32),
            jax.ShapeDtypeStruct((width * tile, tile), BF16),
        ),
        [
            pltpu.VMEM((tile, parts[1][1] * tile), BF16),
            pltpu.VMEM((states // 2, width * tile, 2 * tile), BF16),
            pltpu.VMEM((width * tile, tile), BF16),
            diag,
            pltpu.SemaphoreType.DMA,
        ],
        24, 12, [vmem(), vmem(), pl.BlockSpec(memory_space=pltpu.HBM)],
    )
    stats = lax.all_gather(stats, "sec")
    entries = float(states * sector_count * tile * tile)
    vector, table = call(
        "finish", functools.partial(finish_kernel, entries), [], [stats, start, basis],
        (
            jax.ShapeDtypeStruct((states, tile, tile), F32),
            jax.ShapeDtypeStruct((2, LANCZOS), F32),
        ),
        [], 6, 2,
    )
    return new_env.reshape(left_env.shape), vector[None, :, None], jnp.transpose(table)[None]


def solution(mesh):
    placed = (
        P("seg", "sec", None, None, None),
        P("seg", "sec", None, None, None),
        P("seg", None, None, "sec", None, None),
        P("seg", None, None, None, None),
        P("seg", None, None, None),
        P("seg", None, "sec", None, None),
        P(),
    )
    return jax.shard_map(
        on_device,
        mesh=mesh,
        in_specs=placed,
        out_specs=(
            P("seg", "sec", None, None, None),
            P("seg", None, "sec", None, None),
            P("seg", None, None),
        ),
        check_vma=False,
    )
```

```python
import functools

import jax
import jax.numpy as jnp
from jax import lax
from jax.experimental import pallas as pl
from jax.experimental.pallas import tpu as pltpu
from jax.sharding import PartitionSpec as P

LANCZOS = 4
CHARGES = (0, 1, 1, 2)
GROUPS = ((0, 3), (1, 2))
F32 = jnp.float32
BF16 = jnp.bfloat16
MIB = 1024 * 1024


def padded(count):
    return -(-count // 8) * 8


def packed_height(count):
    return -(-count // 16) * 16


def packed_rows(count, tile):
    return count * tile // 2 + packed_height(count)


def chunks_of(width):
    first = -(-width // 4) * 2
    return (0, first), (first, width - first)


def iotas(shape):
    return lax.broadcasted_iota(jnp.int32, shape, 0), lax.broadcasted_iota(jnp.int32, shape, 1)


def pack_block(block):
    tile = block.shape[0]
    half = tile // 2
    top, low = block[:half], block[half:]
    row, lane = iotas((half, tile))
    turned = pltpu.roll(low, half, 1)
    folded = jnp.where((lane < half) & (row > lane), turned, top)
    diagonal = jnp.sum(jnp.where(lane == row + half, low, 0.0), axis=0, keepdims=True)
    return folded, diagonal


def unpack_block(folded, diagonal):
    half, tile = folded.shape
    row, lane = iotas((half, tile))
    rolled = pltpu.roll(folded, half, 1)
    turned = jnp.transpose(jnp.concatenate([folded, rolled], axis=0))
    top = jnp.where((lane < half) & (row > lane), turned[:half], folded)
    low = jnp.where((lane >= half) & (row > lane - half), rolled, turned[half:])
    low = jnp.where(lane == row + half, diagonal, low)
    return jnp.concatenate([top, low], axis=0)


def partner_of(sector):
    return sector + 1 - 2 * lax.rem(sector, 2)


def live_limits(dims_ref, sector):
    count = dims_ref.shape[0]
    rows = dims_ref[sector]
    columns = []
    for charge in CHARGES:
        target = sector + charge
        columns.append(jnp.where(target < count, dims_ref[jnp.minimum(target, count - 1)], 0))
    return rows, columns


def weight_rows(weight_ref, width, p, square, turned):
    wide = padded(width)
    square[...] = jnp.zeros_like(square)
    square[:width, :width] = weight_ref[pl.ds(p, width, stride=len(CHARGES)), :]
    value = square[...]
    if turned:
        value = jnp.transpose(value)
    high = value.astype(BF16).astype(F32)
    joined = (high + pltpu.roll(value - high, wide, 1)).astype(BF16)
    return joined[: packed_height(width), : 2 * wide]


def doubled(value):
    return jnp.concatenate([value, value], axis=0).astype(BF16)


def pack_kernel(width, tile, source_ref, out_ref, diag):
    half = tile // 2
    diag[...] = jnp.zeros_like(diag)
    for w in range(width):
        folded, diagonal = pack_block(source_ref[w * tile : (w + 1) * tile, :].astype(F32))
        out_ref[w * half : (w + 1) * half, :] = folded.astype(BF16)
        diag[w : w + 1, :] = diagonal
    out_ref[width * half :, :] = diag[...].astype(BF16)


def unpack_into(count, tile, read, write, diag):
    half = tile // 2
    size = packed_height(count)
    diag[:size, :] = read(count * half, size)
    for w in range(count):
        write(w, unpack_block(read(w * half, half), diag[w : w + 1, :]))


def reader(ref):
    return lambda at, size: ref[at : at + size, :].astype(F32)


def unpack_kernel(width, tile, early_ref, late_ref, out_ref, diag):
    for (first, count), ref in zip(chunks_of(width), (early_ref, late_ref)):

        def write(w, block, first=first):
            out_ref[(first + w) * tile : (first + w + 1) * tile, :] = block.astype(BF16)

        unpack_into(count, tile, reader(ref), write, diag)


def fold_kernel(
    width, tile, travels, dims_ref, environ_ref, site_ref, far_environ_ref, far_site_ref, weight_ref, early_ref, late_ref,
    joined_s, turned_s, square_s, weight_s, half_s, packed_s, diag_s, sums_s, diag_sums_s,
):
    half = tile // 2
    pitch = half + 8
    wide = padded(width)
    sector = lax.axis_index("sec")
    partner = partner_of(sector)
    row, lane = iotas((tile, tile))

    def run(own_state, with_partner):
        rows, columns = live_limits(dims_ref, sector)
        live = (row < rows) & (lane < columns[own_state])
        sites = [jnp.where(live, site_ref[own_state].astype(F32), 0.0)]
        states = [own_state]
        if with_partner:
            rows, columns = live_limits(dims_ref, partner)
            for k in range(2):
                live = (row < rows) & (lane < columns[k + 1])
                sites.append(jnp.where(live, far_site_ref[k + 1].astype(F32), 0.0))
                states.append(k + 1)
        parts = len(states)
        for n in range(parts):
            joined_s[:, n * tile : (n + 1) * tile] = sites[n].astype(BF16)
            turned_s[n] = jnp.transpose(sites[n]).astype(BF16)
            weight_s[n] = weight_rows(weight_ref, width, states[n], square_s, True)
            packed_s[n, width * pitch :, :] = jnp.zeros(((wide - width) * pitch, tile), F32)
            diag_s[n] = jnp.zeros_like(diag_s[n])

        for pair in range(width // 2):
            at = slice(pair * tile, (pair + 1) * tile)
            for k in range(2):
                here = slice((pair * 2 + k) * tile, (pair * 2 + k + 1) * tile)
                blocks = [
                    jnp.dot(environ_ref[here, :], joined_s[:, :tile], preferred_element_type=F32)
                ]
                if with_partner:
                    both = jnp.dot(
                        far_environ_ref[here, :], joined_s[:, tile:], preferred_element_type=F32
                    )
                    blocks += [both[:, :tile], both[:, tile:]]
                for n in range(parts):
                    half_s[n, at, k * tile : (k + 1) * tile] = blocks[n].astype(BF16)
            for n in range(parts):
                both = jnp.dot(turned_s[n], half_s[n, at, :], preferred_element_type=F32)
                for k in range(2):
                    w = pair * 2 + k
                    folded, diagonal = pack_block(both[:, k * tile : (k + 1) * tile])
                    packed_s[n, w * pitch : w * pitch + half, :] = folded
                    diag_s[n, w : w + 1, :] = diagonal

        def mixed(inputs):
            value = None
            for n in range(parts):
                term = jnp.dot(weight_s[n], doubled(inputs[n]), preferred_element_type=F32)
                value = term if value is None else value + term
            return value[:wide]

        for at in range(0, half, 2):
            value = mixed([
                jnp.concatenate(
                    [packed_s[n, pl.ds(at + k, wide, stride=pitch), :] for k in range(2)], axis=1
                )
                for n in range(parts)
            ])
            for k in range(2):
                sums_s[pl.ds(at + k, wide, stride=pitch), :] = value[:, k * tile : (k + 1) * tile]
        diag_sums_s[...] = jnp.zeros_like(diag_sums_s)
        diag_sums_s[:wide, :] = mixed([diag_s[n, :wide] for n in range(parts)])
        for (first, count), ref in zip(chunks_of(width), (early_ref, late_ref)):
            for w in range(count):
                at = (first + w) * pitch
                ref[w * half : (w + 1) * half, :] = sums_s[at : at + half, :].astype(ref.dtype)
            rows = packed_height(count)
            ref[count * half :, :] = diag_sums_s[first : first + rows, :].astype(ref.dtype)

    even = lax.rem(sector, 2) == 0
    own_state = len(CHARGES) - 1 if travels else 0

    @pl.when(even)
    def _():
        run(own_state, travels)

    @pl.when(jnp.logical_not(even))
    def _():
        run(own_state, not travels)


def mix_into(width, tile, weights, wide_s, sums_s, out_ref):
    wide = padded(width)
    pitch = tile + 8
    wide_s[width * pitch :, :] = jnp.zeros_like(wide_s[width * pitch :, :])

    for at in range(0, tile, 2):
        value = doubled(
            jnp.concatenate(
                [wide_s[pl.ds(at + k, wide, stride=pitch), :] for k in range(2)], axis=1
            )
        )
        for index, weight in enumerate(weights):
            mixed = jnp.dot(weight[...], value, preferred_element_type=F32)[:wide]
            for k in range(2):
                sums_s[index, pl.ds(at + k, wide, stride=pitch), :] = mixed[:, k * tile : (k + 1) * tile]
    for index in range(len(weights)):
        for w in range(width):
            out_ref[index, :, w * tile : (w + 1) * tile] = sums_s[
                index, w * pitch : w * pitch + tile, :
            ].astype(BF16)


def unpack_wide(width, tile, read, wide_s, diag):
    def write(w, block):
        wide_s[w * (tile + 8) : w * (tile + 8) + tile, :] = block

    unpack_into(width, tile, read, write, diag)


def copy_wide(width, tile, source_ref, wide_s):
    for w in range(width):
        at = w * (tile + 8)
        wide_s[at : at + tile, :] = source_ref[w * tile : (w + 1) * tile, :].astype(F32)


def mix_own_kernel(width, tile, source_ref, weight_ref, out_ref, square_s, weight_s, wide_s, sums_s):
    weight_s[0] = weight_rows(weight_ref, width, 0, square_s, False)
    copy_wide(width, tile, source_ref, wide_s)
    mix_into(width, tile, [weight_s.at[0]], wide_s, sums_s, out_ref)


def mix_next_kernel(
    width, tile, near_ref, weight_ref, out_ref, square_s, weight_s, wide_s, sums_s, diag
):
    for k in range(2):
        weight_s[k] = weight_rows(weight_ref, width, k + 1, square_s, False)
    unpack_wide(width, tile, reader(near_ref), wide_s, diag)
    mix_into(width, tile, [weight_s.at[k] for k in range(2)], wide_s, sums_s, out_ref)


def mix_after_kernel(
    width, tile, far_ref, weight_ref, out_ref, square_s, weight_s, wide_s, sums_s, diag
):
    weight_s[0] = weight_rows(weight_ref, width, 3, square_s, False)
    inside = lax.axis_index("sec") + 2 < lax.axis_size("sec")

    def read(at, size):
        return jnp.where(inside, far_ref[at : at + size, :].astype(F32), 0.0)

    unpack_wide(width, tile, read, wide_s, diag)
    mix_into(width, tile, [weight_s.at[0]], wide_s, sums_s, out_ref)


def total(value):
    return jnp.sum(jnp.sum(value, axis=0, keepdims=True), axis=1, keepdims=True)


def put(stats, kind, lane_at, value):
    row, lane = iotas(stats.shape)
    return jnp.where((row == kind) & (lane == lane_at), value, stats)


def scaled(value):
    square = total(value * value)
    inverse = jnp.where(square > 0.0, lax.rsqrt(square), 0.0)
    return value * inverse, square * inverse


def right_products(width, tile, field, right_ref, out_ref, k):
    lanes = slice(k * tile, (k + 1) * tile)
    for pair in range(width // 2):
        at = pair * 2 * tile
        both = jnp.dot(field, right_ref[:, at : at + 2 * tile], preferred_element_type=F32).astype(BF16)
        for n in range(2):
            out_ref[at + n * tile : at + (n + 1) * tile, lanes] = both[:, n * tile : (n + 1) * tile]


def head_kernel(members, width, tile, dims_ref, guess_ref, *refs):
    *right_refs, vector_ref, stats_ref, product_ref = refs
    rights = [ref.at[n] for ref in right_refs for n in range(ref.shape[0])]
    sector = lax.axis_index("sec")
    rows, columns = live_limits(dims_ref, sector)
    row, lane = iotas((tile, tile))
    stats = jnp.zeros(stats_ref.shape, F32)
    for k, p in enumerate(members):
        live = (row < rows) & (lane < columns[p])
        vector, norm = scaled(jnp.where(live, guess_ref[p], 0.0))
        vector_ref[k] = vector
        stats = put(stats, 0, sector * len(CHARGES) + p, norm)
        right_products(width, tile, vector.astype(BF16), rights[k], product_ref, k)
    stats_ref[...] = stats


def bound_blocks(first, count, tile, packed_ref, environ_ref, out_ref, diag):
    segment = lax.axis_index("seg")

    @pl.when(segment == 0)
    def _():
        for w in range(count):
            out_ref[:, w * tile : (w + 1) * tile] = environ_ref[
                (first + w) * tile : (first + w + 1) * tile, :
            ]

    @pl.when(segment != 0)
    def _():
        def write(w, block):
            out_ref[:, w * tile : (w + 1) * tile] = block.astype(BF16)

        unpack_into(count, tile, reader(packed_ref), write, diag)


def open_kernel(width, tile, packed_ref, environ_ref, *refs):
    *product_refs, bound_ref, image_ref, diag = refs
    first, count = chunks_of(width)[0]
    bound_blocks(first, count, tile, packed_ref, environ_ref, bound_ref, diag)
    for group, product_ref in enumerate(product_refs):
        image_ref[group] = jnp.dot(
            bound_ref[...], product_ref[: count * tile, :], preferred_element_type=F32
        )


def lanczos_kernel(
    width, tile, dims_ref, packed_ref, environ_ref, early_ref, image_ref, own_ref, next_ref, after_ref,
    start_a, start_b, norm_a, norm_b, product_a, product_b, basis_ref, stats_ref,
    late_s, product_s, diag,
):
    states = len(CHARGES)
    sector = lax.axis_index("sec")
    first, count = chunks_of(width)[1]
    bound_blocks(first, count, tile, packed_ref, environ_ref, late_s, diag)
    rows, columns = live_limits(dims_ref, sector)
    row, lane = iotas((tile, tile))
    rights = [own_ref.at[0], next_ref.at[0], next_ref.at[1], after_ref.at[0]]
    stats = norm_a[...] + norm_b[...]
    starts = (start_a, start_b)
    split = first * tile
    betas = [None] * states
    for j in range(LANCZOS):
        for group, members in enumerate(GROUPS):
            if j == 0:
                source = (product_a, product_b)[group]
                images = image_ref[group]
            else:
                source = product_s.at[group]
                for k, p in enumerate(members):
                    field = basis_ref[j - 1, p].astype(BF16)
                    right_products(width, tile, field, rights[p], source, k)
                images = jnp.dot(early_ref[...], source[:split, :], preferred_element_type=F32)
            images = images + jnp.dot(late_s[...], source[split:, :], preferred_element_type=F32)
            for k, p in enumerate(members):
                live = (row < rows) & (lane < columns[p])
                image = jnp.where(live, images[:, k * tile : (k + 1) * tile], 0.0)
                vector = starts[group][k] if j == 0 else basis_ref[j - 1, p]
                alpha = total(vector * image)
                image = image - alpha * vector
                if j > 0:
                    before = starts[group][k] if j == 1 else basis_ref[j - 2, p]
                    image = image - betas[p] * before
                following, beta = scaled(image)
                basis_ref[j, p] = following
                betas[p] = beta
                stats = put(stats, 1 + 2 * j, sector * states + p, alpha)
                stats = put(stats, 2 + 2 * j, sector * states + p, beta)
    stats_ref[...] = stats


def finish_kernel(entries, stats_ref, start_a, start_b, basis_ref, vector_ref, table_ref):
    states = len(CHARGES)
    sector = lax.axis_index("sec")
    stats = stats_ref[0]
    for q in range(1, stats_ref.shape[0]):
        stats = stats + stats_ref[q]
    alphas = [stats[1 + 2 * j : 2 + 2 * j, :] for j in range(LANCZOS)]
    betas = [stats[2 + 2 * j : 3 + 2 * j, :] for j in range(LANCZOS)]

    def mean(left, right):
        products = left[0] * right[0]
        for x, y in zip(left[1:], right[1:]):
            products = products + x * y
        return jnp.sum(products, axis=1, keepdims=True) / entries

    start = [stats[0:1, :]]
    vector = [start[0] / jnp.sqrt(mean(start, start) + 1e-06)]
    previous = []
    beta = jnp.zeros((1, 1), F32)
    table_row, table_column = iotas(table_ref.shape)
    table = jnp.zeros(table_ref.shape, F32)
    for j in range(LANCZOS):
        image = []
        for k in range(j + 2):
            term = None
            if k > 0:
                term = betas[k - 1] * vector[k - 1]
            if k <= j:
                more = alphas[k] * vector[k]
                term = more if term is None else term + more
            if k + 1 <= j:
                term = term + betas[k] * vector[k + 1]
            image.append(term)
        alpha = mean(vector, image[: j + 1])
        for k in range(j + 1):
            image[k] = image[k] - alpha * vector[k]
        for k in range(j):
            image[k] = image[k] - beta * previous[k]
        beta = jnp.sqrt(mean(image, image) + 1e-06)
        previous = vector
        vector = [value / beta for value in image]
        table = jnp.where((table_row == 0) & (table_column == j), alpha, table)
        table = jnp.where((table_row == 1) & (table_column == j), beta, table)
    table_ref[...] = table
    lane = lax.broadcasted_iota(jnp.int32, (1, stats.shape[1]), 1)
    starts = {p: ref[k] for members, ref in zip(GROUPS, (start_a, start_b)) for k, p in enumerate(members)}
    for p in range(states):
        value = None
        here = lane == sector * states + p
        for k in range(LANCZOS + 1):
            weight = jnp.sum(jnp.where(here, vector[k], 0.0), axis=1, keepdims=True)
            term = weight * (starts[p] if k == 0 else basis_ref[k - 1, p])
            value = term if value is None else value + term
        vector_ref[p] = value


def smem():
    return pl.BlockSpec(memory_space=pltpu.SMEM)


def vmem():
    return pl.BlockSpec(memory_space=pltpu.VMEM)


def call(name, kernel, scalars, arrays, outs, scratch, limit, micros):
    many = isinstance(outs, (tuple, list))
    return pl.pallas_call(
        kernel,
        out_shape=outs,
        in_specs=[smem()] * len(scalars) + [vmem()] * len(arrays),
        out_specs=[vmem()] * len(outs) if many else vmem(),
        scratch_shapes=scratch,
        compiler_params=pltpu.CompilerParams(vmem_limit_bytes=limit * MIB),
        name=name,
        cost_estimate=pl.CostEstimate(
            flops=int(micros * 1.1e9), bytes_accessed=0, transcendentals=0
        ),
    )(*scalars, *arrays)


def shift_by(count, steps):
    return [(source, (source + steps) % count) for source in range(count)]


def gathered(value, axis):
    count = lax.axis_size(axis)
    return lax.all_to_all(jnp.broadcast_to(value, (count,) + value.shape), axis, 0, 0)


def on_device(left_env, right_env, site_tensors, mpo, boundary_mpo, guess, sector_dims):
    width, tile = left_env.shape[2], left_env.shape[-1]
    half = tile // 2
    wide = padded(width)
    states = len(CHARGES)
    sector_count = sector_dims.shape[0]
    sectors = lax.axis_size("sec")
    segments = lax.axis_size("seg")
    prows = packed_rows(width, tile)
    drows = prows - width * half
    packed = jax.ShapeDtypeStruct((prows, tile), BF16)
    parts = chunks_of(width)

    def packed_parts(dtype):
        return [jax.ShapeDtypeStruct((packed_rows(count, tile), tile), dtype) for _, count in parts]

    def mixed(count):
        return jax.ShapeDtypeStruct((count, tile, width * tile), BF16)

    environ = left_env.reshape(width * tile, tile)
    right = right_env.reshape(width * tile, tile)
    site = site_tensors[0, 0, :, 0]
    site_weights = jnp.transpose(mpo[0, 0], (0, 2, 1)).reshape(width * states, width)
    bound_weights = jnp.transpose(boundary_mpo[0], (0, 2, 1)).reshape(width * states, width)

    sector = lax.axis_index("sec")
    swap = [(q, q ^ 1) for q in range(sectors)]
    up_two = shift_by(sectors, 2)
    down_two = shift_by(sectors, -2)
    onward = shift_by(segments, 1)
    diag = pltpu.VMEM((drows, tile), F32)

    def mix_scratch(count):
        return [
            pltpu.VMEM((tile, tile), F32),
            pltpu.VMEM((count, packed_height(width), 2 * wide), BF16),
            pltpu.VMEM((wide * (tile + 8), tile), F32),
            pltpu.VMEM((count, wide * (tile + 8), tile), F32),
        ]

    right_packed = call(
        "pack_right", functools.partial(pack_kernel, width, tile), [], [right], packed,
        [diag], 6, 1,
    )
    right_far = lax.ppermute(right_packed, "sec", down_two)
    far_environ = lax.ppermute(environ, "sec", swap)
    far_site = lax.ppermute(site, "sec", swap)
    fold_scratch = [
        pltpu.VMEM((tile, 3 * tile), BF16),
        pltpu.VMEM((3, tile, tile), BF16),
        pltpu.VMEM((tile, tile), F32),
        pltpu.VMEM((3, packed_height(width), 2 * wide), BF16),
        pltpu.VMEM((3, width // 2 * tile, 2 * tile), BF16),
        pltpu.VMEM((3, wide * (half + 8), tile), F32),
        pltpu.VMEM((3, drows, tile), F32),
        pltpu.VMEM((wide * (half + 8), tile), F32),
        pltpu.VMEM((drows, tile), F32),
    ]
    outgoing = call(
        "fold_up", functools.partial(fold_kernel, width, tile, True),
        [sector_dims], [environ, site, far_environ, far_site, site_weights], packed_parts(BF16),
        fold_scratch, 20, 12,
    )
    early_arrived = lax.ppermute(outgoing[0], "sec", up_two)
    far_environ, outgoing = lax.optimization_barrier((far_environ, outgoing))
    kept = call(
        "fold_own", functools.partial(fold_kernel, width, tile, False),
        [sector_dims], [environ, site, far_environ, far_site, site_weights], packed_parts(F32),
        fold_scratch, 20, 0.1,
    )
    kept, late_outgoing = lax.optimization_barrier((kept, outgoing[1]))
    late_arrived = lax.ppermute(late_outgoing, "sec", up_two)
    kept, right = lax.optimization_barrier((kept, right))
    own_mixed = call(
        "mix_own", functools.partial(mix_own_kernel, width, tile), [], [right, bound_weights],
        mixed(1), mix_scratch(1), 12, 1,
    )
    own_mixed, right_far = lax.optimization_barrier((own_mixed, right_far))
    passed_on = jnp.where(sector + 2 < sectors, right_far, jnp.zeros_like(right_far))
    passed_on = jnp.where(lax.rem(sector, 2) == 0, passed_on, right_packed)
    right_near = lax.ppermute(passed_on, "sec", swap)
    after_mixed = call(
        "mix_after", functools.partial(mix_after_kernel, width, tile), [],
        [right_far, bound_weights], mixed(1), mix_scratch(1) + [diag], 12, 2,
    )
    def head(members, rights):
        return call(
            "head", functools.partial(head_kernel, members, width, tile),
            [sector_dims], [guess[0, :, 0]] + rights,
            (
                jax.ShapeDtypeStruct((2, tile, tile), F32),
                jax.ShapeDtypeStruct((16, 128), F32),
                jax.ShapeDtypeStruct((width * tile, 2 * tile), BF16),
            ),
            [], 9, 0.5,
        )

    start_a, norms_a, products_a = head(GROUPS[0], [own_mixed, after_mixed])
    early_arrived, products_a = lax.optimization_barrier((early_arrived, products_a))

    def carried(stays, comes):
        return (stays + jnp.where(sector >= 2, comes.astype(F32), 0.0)).astype(BF16)

    early = carried(kept[0], early_arrived)
    early_bound = lax.ppermute(early, "seg", onward)
    early, late_arrived = lax.optimization_barrier((early, late_arrived))
    late = carried(kept[1], late_arrived)
    late_bound = lax.ppermute(late, "seg", onward)
    late, right_near = lax.optimization_barrier((late, right_near))
    next_mixed = call(
        "mix_next", functools.partial(mix_next_kernel, width, tile), [],
        [right_near, bound_weights], mixed(2), mix_scratch(2) + [diag], 16, 3,
    )
    start_b, norms_b, products_b = head(GROUPS[1], [next_mixed])
    new_env = call(
        "unpack_env", functools.partial(unpack_kernel, width, tile), [], [early, late],
        jax.ShapeDtypeStruct((width * tile, tile), BF16), [diag], 6, 2,
    )
    early_bound, products_b, new_env = lax.optimization_barrier((early_bound, products_b, new_env))
    bound, image = call(
        "open", functools.partial(open_kernel, width, tile), [], [early_bound, environ, products_a, products_b],
        (
            jax.ShapeDtypeStruct((tile, parts[0][1] * tile), BF16),
            jax.ShapeDtypeStruct((len(GROUPS), tile, 2 * tile), F32),
        ),
        [diag], 12, 1,
    )
    late_bound, bound = lax.optimization_barrier((late_bound, bound))
    basis, stats = call(
        "lanczos", functools.partial(lanczos_kernel, width, tile),
        [sector_dims],
        [late_bound, environ, bound, image, own_mixed, next_mixed, after_mixed, start_a, start_b,
         norms_a, norms_b, products_a, products_b],
        (
            jax.ShapeDtypeStruct((LANCZOS, states, tile, tile), F32),
            jax.ShapeDtypeStruct((16, 128), F32),
        ),
        [
            pltpu.VMEM((tile, parts[1][1] * tile), BF16),
            pltpu.VMEM((len(GROUPS), width * tile, 2 * tile), BF16),
            diag,
        ],
        22, 12,
    )
    stats = gathered(stats, "sec")
    entries = float(states * sector_count * tile * tile)
    vector, table = call(
        "finish", functools.partial(finish_kernel, entries), [], [stats, start_a, start_b, basis],
        (
            jax.ShapeDtypeStruct((states, tile, tile), F32),
            jax.ShapeDtypeStruct((2, LANCZOS), F32),
        ),
        [], 6, 2,
    )
    return new_env.reshape(left_env.shape), vector[None, :, None], jnp.transpose(table)[None]


def solution(mesh):
    placed = (
        P("seg", "sec", None, None, None),
        P("seg", "sec", None, None, None),
        P("seg", None, None, "sec", None, None),
        P("seg", None, None, None, None),
        P("seg", None, None, None),
        P("seg", None, "sec", None, None),
        P(),
    )
    return jax.shard_map(
        on_device,
        mesh=mesh,
        in_specs=placed,
        out_specs=(
            P("seg", "sec", None, None, None),
            P("seg", None, "sec", None, None),
            P("seg", None, None),
        ),
        check_vma=False,
    )
```

```python
import functools

import jax
import jax.numpy as jnp
from jax import lax
from jax.experimental import pallas as pl
from jax.experimental.pallas import tpu as pltpu
from jax.sharding import PartitionSpec as P

LANCZOS = 4
CHARGES = (0, 1, 1, 2)
GROUPS = ((0, 3), (1, 2))
F32 = jnp.float32
BF16 = jnp.bfloat16
MIB = 1024 * 1024


def padded(count):
    return -(-count // 8) * 8


def packed_height(count):
    return -(-count // 16) * 16


def packed_rows(count, tile):
    return count * tile // 2 + packed_height(count)


def chunks_of(width):
    one = width // 6 * 2
    two = (width - one) // 4 * 2
    return (0, one), (one, two), (one + two, width - one - two)


def iotas(shape):
    return lax.broadcasted_iota(jnp.int32, shape, 0), lax.broadcasted_iota(jnp.int32, shape, 1)


def pack_block(block):
    tile = block.shape[0]
    half = tile // 2
    top, low = block[:half], block[half:]
    row, lane = iotas((half, tile))
    turned = pltpu.roll(low, half, 1)
    folded = jnp.where((lane < half) & (row > lane), turned, top)
    diagonal = jnp.sum(jnp.where(lane == row + half, low, 0.0), axis=0, keepdims=True)
    return folded, diagonal


def unpack_block(folded, diagonal):
    half, tile = folded.shape
    row, lane = iotas((half, tile))
    rolled = pltpu.roll(folded, half, 1)
    turned = jnp.transpose(jnp.concatenate([folded, rolled], axis=0))
    top = jnp.where((lane < half) & (row > lane), turned[:half], folded)
    low = jnp.where((lane >= half) & (row > lane - half), rolled, turned[half:])
    low = jnp.where(lane == row + half, diagonal, low)
    return jnp.concatenate([top, low], axis=0)


def partner_of(sector):
    return sector + 1 - 2 * lax.rem(sector, 2)


def live_limits(dims_ref, sector):
    count = dims_ref.shape[0]
    rows = dims_ref[sector]
    columns = []
    for charge in CHARGES:
        target = sector + charge
        columns.append(jnp.where(target < count, dims_ref[jnp.minimum(target, count - 1)], 0))
    return rows, columns


def weight_rows(weight_ref, width, p, square, turned):
    wide = padded(width)
    square[...] = jnp.zeros_like(square)
    square[:width, :width] = weight_ref[pl.ds(p, width, stride=len(CHARGES)), :]
    value = square[...]
    if turned:
        value = jnp.transpose(value)
    high = value.astype(BF16).astype(F32)
    joined = (high + pltpu.roll(value - high, wide, 1)).astype(BF16)
    return joined[: packed_height(width), : 2 * wide]


def doubled(value):
    return jnp.concatenate([value, value], axis=0).astype(BF16)


def pack_kernel(width, tile, source_ref, out_ref, diag):
    half = tile // 2
    diag[...] = jnp.zeros_like(diag)
    for w in range(width):
        folded, diagonal = pack_block(source_ref[w * tile : (w + 1) * tile, :].astype(F32))
        out_ref[w * half : (w + 1) * half, :] = folded.astype(BF16)
        diag[w : w + 1, :] = diagonal
    out_ref[width * half :, :] = diag[...].astype(BF16)


def unpack_into(count, tile, read, write, diag):
    half = tile // 2
    size = packed_height(count)
    diag[:size, :] = read(count * half, size)
    for w in range(count):
        write(w, unpack_block(read(w * half, half), diag[w : w + 1, :]))


def reader(ref):
    return lambda at, size: ref[at : at + size, :].astype(F32)


def unpack_kernel(width, tile, *refs):
    *part_refs, out_ref, diag = refs
    for (first, count), ref in zip(chunks_of(width), part_refs):

        def write(w, block, first=first):
            out_ref[(first + w) * tile : (first + w + 1) * tile, :] = block.astype(BF16)

        unpack_into(count, tile, reader(ref), write, diag)


def fold_kernel(
    width, tile, travels, dims_ref, environ_ref, site_ref, far_environ_ref, far_site_ref, weight_ref, *refs
):
    part_refs = refs[: len(chunks_of(width))]
    joined_s, turned_s, square_s, weight_s, half_s, packed_s, diag_s, sums_s, diag_sums_s = refs[
        len(part_refs) :
    ]
    half = tile // 2
    pitch = half + 8
    wide = padded(width)
    sector = lax.axis_index("sec")
    partner = partner_of(sector)
    row, lane = iotas((tile, tile))

    def run(own_state, with_partner):
        rows, columns = live_limits(dims_ref, sector)
        live = (row < rows) & (lane < columns[own_state])
        sites = [jnp.where(live, site_ref[own_state].astype(F32), 0.0)]
        states = [own_state]
        if with_partner:
            rows, columns = live_limits(dims_ref, partner)
            for k in range(2):
                live = (row < rows) & (lane < columns[k + 1])
                sites.append(jnp.where(live, far_site_ref[k + 1].astype(F32), 0.0))
                states.append(k + 1)
        parts = len(states)
        for n in range(parts):
            joined_s[:, n * tile : (n + 1) * tile] = sites[n].astype(BF16)
            turned_s[n] = jnp.transpose(sites[n]).astype(BF16)
            weight_s[n] = weight_rows(weight_ref, width, states[n], square_s, True)
            packed_s[n, width * pitch :, :] = jnp.zeros(((wide - width) * pitch, tile), F32)
            diag_s[n] = jnp.zeros_like(diag_s[n])

        for pair in range(width // 2):
            at = slice(pair * tile, (pair + 1) * tile)
            for k in range(2):
                here = slice((pair * 2 + k) * tile, (pair * 2 + k + 1) * tile)
                blocks = [
                    jnp.dot(environ_ref[here, :], joined_s[:, :tile], preferred_element_type=F32)
                ]
                if with_partner:
                    both = jnp.dot(
                        far_environ_ref[here, :], joined_s[:, tile:], preferred_element_type=F32
                    )
                    blocks += [both[:, :tile], both[:, tile:]]
                for n in range(parts):
                    half_s[n, at, k * tile : (k + 1) * tile] = blocks[n].astype(BF16)
            for n in range(parts):
                both = jnp.dot(turned_s[n], half_s[n, at, :], preferred_element_type=F32)
                for k in range(2):
                    w = pair * 2 + k
                    folded, diagonal = pack_block(both[:, k * tile : (k + 1) * tile])
                    packed_s[n, w * pitch : w * pitch + half, :] = folded
                    diag_s[n, w : w + 1, :] = diagonal

        def mixed(inputs):
            value = None
            for n in range(parts):
                term = jnp.dot(weight_s[n], doubled(inputs[n]), preferred_element_type=F32)
                value = term if value is None else value + term
            return value[:wide]

        for at in range(0, half, 2):
            value = mixed([
                jnp.concatenate(
                    [packed_s[n, pl.ds(at + k, wide, stride=pitch), :] for k in range(2)], axis=1
                )
                for n in range(parts)
            ])
            for k in range(2):
                sums_s[pl.ds(at + k, wide, stride=pitch), :] = value[:, k * tile : (k + 1) * tile]
        diag_sums_s[...] = jnp.zeros_like(diag_sums_s)
        diag_sums_s[:wide, :] = mixed([diag_s[n, :wide] for n in range(parts)])
        for (first, count), ref in zip(chunks_of(width), part_refs):
            for w in range(count):
                at = (first + w) * pitch
                ref[w * half : (w + 1) * half, :] = sums_s[at : at + half, :].astype(ref.dtype)
            rows = packed_height(count)
            ref[count * half :, :] = diag_sums_s[first : first + rows, :].astype(ref.dtype)

    even = lax.rem(sector, 2) == 0
    own_state = len(CHARGES) - 1 if travels else 0

    @pl.when(even)
    def _():
        run(own_state, travels)

    @pl.when(jnp.logical_not(even))
    def _():
        run(own_state, not travels)


def mix_into(width, tile, weights, wide_s, sums_s, out_ref):
    wide = padded(width)
    pitch = tile + 8
    wide_s[width * pitch :, :] = jnp.zeros_like(wide_s[width * pitch :, :])

    for at in range(0, tile, 2):
        value = doubled(
            jnp.concatenate(
                [wide_s[pl.ds(at + k, wide, stride=pitch), :] for k in range(2)], axis=1
            )
        )
        for index, weight in enumerate(weights):
            mixed = jnp.dot(weight[...], value, preferred_element_type=F32)[:wide]
            for k in range(2):
                sums_s[index, pl.ds(at + k, wide, stride=pitch), :] = mixed[:, k * tile : (k + 1) * tile]
    for index in range(len(weights)):
        for w in range(width):
            out_ref[index, :, w * tile : (w + 1) * tile] = sums_s[
                index, w * pitch : w * pitch + tile, :
            ].astype(BF16)


def unpack_wide(width, tile, read, wide_s, diag):
    def write(w, block):
        wide_s[w * (tile + 8) : w * (tile + 8) + tile, :] = block

    unpack_into(width, tile, read, write, diag)


def copy_wide(width, tile, source_ref, wide_s):
    for w in range(width):
        at = w * (tile + 8)
        wide_s[at : at + tile, :] = source_ref[w * tile : (w + 1) * tile, :].astype(F32)


def mix_own_kernel(width, tile, source_ref, weight_ref, out_ref, square_s, weight_s, wide_s, sums_s):
    weight_s[0] = weight_rows(weight_ref, width, 0, square_s, False)
    copy_wide(width, tile, source_ref, wide_s)
    mix_into(width, tile, [weight_s.at[0]], wide_s, sums_s, out_ref)


def mix_next_kernel(
    width, tile, near_ref, weight_ref, out_ref, square_s, weight_s, wide_s, sums_s, diag
):
    for k in range(2):
        weight_s[k] = weight_rows(weight_ref, width, k + 1, square_s, False)
    unpack_wide(width, tile, reader(near_ref), wide_s, diag)
    mix_into(width, tile, [weight_s.at[k] for k in range(2)], wide_s, sums_s, out_ref)


def mix_after_kernel(
    width, tile, far_ref, weight_ref, out_ref, square_s, weight_s, wide_s, sums_s, diag
):
    weight_s[0] = weight_rows(weight_ref, width, 3, square_s, False)
    inside = lax.axis_index("sec") + 2 < lax.axis_size("sec")

    def read(at, size):
        return jnp.where(inside, far_ref[at : at + size, :].astype(F32), 0.0)

    unpack_wide(width, tile, read, wide_s, diag)
    mix_into(width, tile, [weight_s.at[0]], wide_s, sums_s, out_ref)


def total(value):
    return jnp.sum(jnp.sum(value, axis=0, keepdims=True), axis=1, keepdims=True)


def put(stats, kind, lane_at, value):
    row, lane = iotas(stats.shape)
    return jnp.where((row == kind) & (lane == lane_at), value, stats)


def scaled(value):
    square = total(value * value)
    inverse = jnp.where(square > 0.0, lax.rsqrt(square), 0.0)
    return value * inverse, square * inverse


def right_products(width, tile, field, right_ref, out_ref, k):
    lanes = slice(k * tile, (k + 1) * tile)
    for pair in range(width // 2):
        at = pair * 2 * tile
        both = jnp.dot(field, right_ref[:, at : at + 2 * tile], preferred_element_type=F32).astype(BF16)
        for n in range(2):
            out_ref[at + n * tile : at + (n + 1) * tile, lanes] = both[:, n * tile : (n + 1) * tile]


def head_kernel(members, width, tile, dims_ref, guess_ref, *refs):
    *right_refs, vector_ref, stats_ref, product_ref = refs
    rights = [ref.at[n] for ref in right_refs for n in range(ref.shape[0])]
    sector = lax.axis_index("sec")
    rows, columns = live_limits(dims_ref, sector)
    row, lane = iotas((tile, tile))
    stats = jnp.zeros(stats_ref.shape, F32)
    for k, p in enumerate(members):
        live = (row < rows) & (lane < columns[p])
        vector, norm = scaled(jnp.where(live, guess_ref[p], 0.0))
        vector_ref[k] = vector
        stats = put(stats, 0, sector * len(CHARGES) + p, norm)
        right_products(width, tile, vector.astype(BF16), rights[k], product_ref, k)
    stats_ref[...] = stats


def bound_blocks(chunks, tile, packed_refs, environ_ref, out_ref, diag):
    segment = lax.axis_index("seg")
    start = chunks[0][0]

    @pl.when(segment == 0)
    def _():
        for w in range(sum(count for _, count in chunks)):
            out_ref[:, w * tile : (w + 1) * tile] = environ_ref[
                (start + w) * tile : (start + w + 1) * tile, :
            ]

    @pl.when(segment != 0)
    def _():
        for (first, count), ref in zip(chunks, packed_refs):

            def write(w, block, base=first - start):
                out_ref[:, (base + w) * tile : (base + w + 1) * tile] = block.astype(BF16)

            unpack_into(count, tile, reader(ref), write, diag)


def open_kernel(width, tile, environ_ref, *refs):
    chunks = chunks_of(width)[:-1]
    packed_refs, (*product_refs, bound_ref, image_ref, diag) = refs[: len(chunks)], refs[len(chunks) :]
    bound_blocks(chunks, tile, packed_refs, environ_ref, bound_ref, diag)
    rows = bound_ref.shape[1]
    for group, product_ref in enumerate(product_refs):
        image_ref[group] = jnp.dot(bound_ref[...], product_ref[:rows, :], preferred_element_type=F32)


def lanczos_kernel(
    width, tile, dims_ref, packed_ref, environ_ref, early_ref, image_ref, own_ref, next_ref, after_ref,
    start_a, start_b, norm_a, norm_b, product_a, product_b, basis_ref, stats_ref,
    late_s, product_s, diag,
):
    states = len(CHARGES)
    sector = lax.axis_index("sec")
    last = chunks_of(width)[-1:]
    bound_blocks(last, tile, [packed_ref], environ_ref, late_s, diag)
    rows, columns = live_limits(dims_ref, sector)
    row, lane = iotas((tile, tile))
    rights = [own_ref.at[0], next_ref.at[0], next_ref.at[1], after_ref.at[0]]
    stats = norm_a[...] + norm_b[...]
    starts = (start_a, start_b)
    split = last[0][0] * tile
    betas = [None] * states
    for j in range(LANCZOS):
        for group, members in enumerate(GROUPS):
            if j == 0:
                source = (product_a, product_b)[group]
                images = image_ref[group]
            else:
                source = product_s.at[group]
                for k, p in enumerate(members):
                    field = basis_ref[j - 1, p].astype(BF16)
                    right_products(width, tile, field, rights[p], source, k)
                images = jnp.dot(early_ref[...], source[:split, :], preferred_element_type=F32)
            images = images + jnp.dot(late_s[...], source[split:, :], preferred_element_type=F32)
            for k, p in enumerate(members):
                live = (row < rows) & (lane < columns[p])
                image = jnp.where(live, images[:, k * tile : (k + 1) * tile], 0.0)
                vector = starts[group][k] if j == 0 else basis_ref[j - 1, p]
                alpha = total(vector * image)
                image = image - alpha * vector
                if j > 0:
                    before = starts[group][k] if j == 1 else basis_ref[j - 2, p]
                    image = image - betas[p] * before
                following, beta = scaled(image)
                basis_ref[j, p] = following
                betas[p] = beta
                stats = put(stats, 1 + 2 * j, sector * states + p, alpha)
                stats = put(stats, 2 + 2 * j, sector * states + p, beta)
    stats_ref[...] = stats


def finish_kernel(entries, stats_ref, start_a, start_b, basis_ref, vector_ref, table_ref):
    states = len(CHARGES)
    sector = lax.axis_index("sec")
    stats = stats_ref[0]
    for q in range(1, stats_ref.shape[0]):
        stats = stats + stats_ref[q]
    alphas = [stats[1 + 2 * j : 2 + 2 * j, :] for j in range(LANCZOS)]
    betas = [stats[2 + 2 * j : 3 + 2 * j, :] for j in range(LANCZOS)]

    def mean(left, right):
        products = left[0] * right[0]
        for x, y in zip(left[1:], right[1:]):
            products = products + x * y
        return jnp.sum(products, axis=1, keepdims=True) / entries

    start = [stats[0:1, :]]
    vector = [start[0] / jnp.sqrt(mean(start, start) + 1e-06)]
    previous = []
    beta = jnp.zeros((1, 1), F32)
    table_row, table_column = iotas(table_ref.shape)
    table = jnp.zeros(table_ref.shape, F32)
    for j in range(LANCZOS):
        image = []
        for k in range(j + 2):
            term = None
            if k > 0:
                term = betas[k - 1] * vector[k - 1]
            if k <= j:
                more = alphas[k] * vector[k]
                term = more if term is None else term + more
            if k + 1 <= j:
                term = term + betas[k] * vector[k + 1]
            image.append(term)
        alpha = mean(vector, image[: j + 1])
        for k in range(j + 1):
            image[k] = image[k] - alpha * vector[k]
        for k in range(j):
            image[k] = image[k] - beta * previous[k]
        beta = jnp.sqrt(mean(image, image) + 1e-06)
        previous = vector
        vector = [value / beta for value in image]
        table = jnp.where((table_row == 0) & (table_column == j), alpha, table)
        table = jnp.where((table_row == 1) & (table_column == j), beta, table)
    table_ref[...] = table
    lane = lax.broadcasted_iota(jnp.int32, (1, stats.shape[1]), 1)
    starts = {p: ref[k] for members, ref in zip(GROUPS, (start_a, start_b)) for k, p in enumerate(members)}
    for p in range(states):
        value = None
        here = lane == sector * states + p
        for k in range(LANCZOS + 1):
            weight = jnp.sum(jnp.where(here, vector[k], 0.0), axis=1, keepdims=True)
            term = weight * (starts[p] if k == 0 else basis_ref[k - 1, p])
            value = term if value is None else value + term
        vector_ref[p] = value


def smem():
    return pl.BlockSpec(memory_space=pltpu.SMEM)


def vmem():
    return pl.BlockSpec(memory_space=pltpu.VMEM)


def call(name, kernel, scalars, arrays, outs, scratch, limit, micros):
    many = isinstance(outs, (tuple, list))
    return pl.pallas_call(
        kernel,
        out_shape=outs,
        in_specs=[smem()] * len(scalars) + [vmem()] * len(arrays),
        out_specs=[vmem()] * len(outs) if many else vmem(),
        scratch_shapes=scratch,
        compiler_params=pltpu.CompilerParams(vmem_limit_bytes=limit * MIB),
        name=name,
        cost_estimate=pl.CostEstimate(
            flops=int(micros * 1.1e9), bytes_accessed=0, transcendentals=0
        ),
    )(*scalars, *arrays)


def shift_by(count, steps):
    return [(source, (source + steps) % count) for source in range(count)]


def gathered(value, axis):
    count = lax.axis_size(axis)
    return lax.all_to_all(jnp.broadcast_to(value, (count,) + value.shape), axis, 0, 0)


def on_device(left_env, right_env, site_tensors, mpo, boundary_mpo, guess, sector_dims):
    width, tile = left_env.shape[2], left_env.shape[-1]
    half = tile // 2
    wide = padded(width)
    states = len(CHARGES)
    sector_count = sector_dims.shape[0]
    sectors = lax.axis_size("sec")
    segments = lax.axis_size("seg")
    prows = packed_rows(width, tile)
    drows = prows - width * half
    packed = jax.ShapeDtypeStruct((prows, tile), BF16)
    parts = chunks_of(width)

    def packed_parts(dtype):
        return [jax.ShapeDtypeStruct((packed_rows(count, tile), tile), dtype) for _, count in parts]

    def mixed(count):
        return jax.ShapeDtypeStruct((count, tile, width * tile), BF16)

    environ = left_env.reshape(width * tile, tile)
    right = right_env.reshape(width * tile, tile)
    site = site_tensors[0, 0, :, 0]
    site_weights = jnp.transpose(mpo[0, 0], (0, 2, 1)).reshape(width * states, width)
    bound_weights = jnp.transpose(boundary_mpo[0], (0, 2, 1)).reshape(width * states, width)

    sector = lax.axis_index("sec")
    swap = [(q, q ^ 1) for q in range(sectors)]
    up_two = shift_by(sectors, 2)
    down_two = shift_by(sectors, -2)
    onward = shift_by(segments, 1)
    diag = pltpu.VMEM((drows, tile), F32)

    def mix_scratch(count):
        return [
            pltpu.VMEM((tile, tile), F32),
            pltpu.VMEM((count, packed_height(width), 2 * wide), BF16),
            pltpu.VMEM((wide * (tile + 8), tile), F32),
            pltpu.VMEM((count, wide * (tile + 8), tile), F32),
        ]

    right_packed = call(
        "pack_right", functools.partial(pack_kernel, width, tile), [], [right], packed,
        [diag], 6, 1,
    )
    right_far = lax.ppermute(right_packed, "sec", down_two)
    far_environ = lax.ppermute(environ, "sec", swap)
    far_site = lax.ppermute(site, "sec", swap)
    fold_scratch = [
        pltpu.VMEM((tile, 3 * tile), BF16),
        pltpu.VMEM((3, tile, tile), BF16),
        pltpu.VMEM((tile, tile), F32),
        pltpu.VMEM((3, packed_height(width), 2 * wide), BF16),
        pltpu.VMEM((3, width // 2 * tile, 2 * tile), BF16),
        pltpu.VMEM((3, wide * (half + 8), tile), F32),
        pltpu.VMEM((3, drows, tile), F32),
        pltpu.VMEM((wide * (half + 8), tile), F32),
        pltpu.VMEM((drows, tile), F32),
    ]
    outgoing = call(
        "fold_up", functools.partial(fold_kernel, width, tile, True),
        [sector_dims], [environ, site, far_environ, far_site, site_weights], packed_parts(BF16),
        fold_scratch, 20, 12,
    )
    early_arrived = lax.ppermute(outgoing[0], "sec", up_two)
    far_environ, outgoing = lax.optimization_barrier((far_environ, outgoing))
    kept = call(
        "fold_own", functools.partial(fold_kernel, width, tile, False),
        [sector_dims], [environ, site, far_environ, far_site, site_weights], packed_parts(F32),
        fold_scratch, 20, 0.1,
    )
    kept, middle_outgoing = lax.optimization_barrier((kept, outgoing[1]))
    middle_arrived = lax.ppermute(middle_outgoing, "sec", up_two)
    kept, right = lax.optimization_barrier((kept, right))
    own_mixed = call(
        "mix_own", functools.partial(mix_own_kernel, width, tile), [], [right, bound_weights],
        mixed(1), mix_scratch(1), 12, 1,
    )
    own_mixed, right_far, late_outgoing = lax.optimization_barrier((own_mixed, right_far, outgoing[2]))
    late_arrived = lax.ppermute(late_outgoing, "sec", up_two)
    passed_on = jnp.where(sector + 2 < sectors, right_far, jnp.zeros_like(right_far))
    passed_on = jnp.where(lax.rem(sector, 2) == 0, passed_on, right_packed)
    right_near = lax.ppermute(passed_on, "sec", swap)

    def carried(stays, comes):
        return (stays + jnp.where(sector >= 2, comes.astype(F32), 0.0)).astype(BF16)

    early = carried(kept[0], early_arrived)
    early_bound = lax.ppermute(early, "seg", onward)
    early, right_far = lax.optimization_barrier((early, right_far))
    after_mixed = call(
        "mix_after", functools.partial(mix_after_kernel, width, tile), [],
        [right_far, bound_weights], mixed(1), mix_scratch(1) + [diag], 12, 2,
    )
    def head(members, rights):
        return call(
            "head", functools.partial(head_kernel, members, width, tile),
            [sector_dims], [guess[0, :, 0]] + rights,
            (
                jax.ShapeDtypeStruct((2, tile, tile), F32),
                jax.ShapeDtypeStruct((16, 128), F32),
                jax.ShapeDtypeStruct((width * tile, 2 * tile), BF16),
            ),
            [], 9, 0.5,
        )

    start_a, norms_a, products_a = head(GROUPS[0], [own_mixed, after_mixed])
    middle_arrived, products_a = lax.optimization_barrier((middle_arrived, products_a))
    middle = carried(kept[1], middle_arrived)
    middle_bound = lax.ppermute(middle, "seg", onward)
    middle, right_near = lax.optimization_barrier((middle, right_near))
    next_mixed = call(
        "mix_next", functools.partial(mix_next_kernel, width, tile), [],
        [right_near, bound_weights], mixed(2), mix_scratch(2) + [diag], 16, 3,
    )
    start_b, norms_b, products_b = head(GROUPS[1], [next_mixed])
    late_arrived, products_b = lax.optimization_barrier((late_arrived, products_b))
    late = carried(kept[2], late_arrived)
    late_bound = lax.ppermute(late, "seg", onward)
    new_env = call(
        "unpack_env", functools.partial(unpack_kernel, width, tile), [], [early, middle, late],
        jax.ShapeDtypeStruct((width * tile, tile), BF16), [diag], 6, 2,
    )
    middle_bound, new_env = lax.optimization_barrier((middle_bound, new_env))
    bound, image = call(
        "open", functools.partial(open_kernel, width, tile), [],
        [environ, early_bound, middle_bound, products_a, products_b],
        (
            jax.ShapeDtypeStruct((tile, parts[-1][0] * tile), BF16),
            jax.ShapeDtypeStruct((len(GROUPS), tile, 2 * tile), F32),
        ),
        [diag], 12, 1,
    )
    late_bound, bound = lax.optimization_barrier((late_bound, bound))
    basis, stats = call(
        "lanczos", functools.partial(lanczos_kernel, width, tile),
        [sector_dims],
        [late_bound, environ, bound, image, own_mixed, next_mixed, after_mixed, start_a, start_b,
         norms_a, norms_b, products_a, products_b],
        (
            jax.ShapeDtypeStruct((LANCZOS, states, tile, tile), F32),
            jax.ShapeDtypeStruct((16, 128), F32),
        ),
        [
            pltpu.VMEM((tile, parts[-1][1] * tile), BF16),
            pltpu.VMEM((len(GROUPS), width * tile, 2 * tile), BF16),
            diag,
        ],
        22, 12,
    )
    stats = gathered(stats, "sec")
    entries = float(states * sector_count * tile * tile)
    vector, table = call(
        "finish", functools.partial(finish_kernel, entries), [], [stats, start_a, start_b, basis],
        (
            jax.ShapeDtypeStruct((states, tile, tile), F32),
            jax.ShapeDtypeStruct((2, LANCZOS), F32),
        ),
        [], 6, 2,
    )
    return new_env.reshape(left_env.shape), vector[None, :, None], jnp.transpose(table)[None]


def solution(mesh):
    placed = (
        P("seg", "sec", None, None, None),
        P("seg", "sec", None, None, None),
        P("seg", None, None, "sec", None, None),
        P("seg", None, None, None, None),
        P("seg", None, None, None),
        P("seg", None, "sec", None, None),
        P(),
    )
    return jax.shard_map(
        on_device,
        mesh=mesh,
        in_specs=placed,
        out_specs=(
            P("seg", "sec", None, None, None),
            P("seg", None, "sec", None, None),
            P("seg", None, None),
        ),
        check_vma=False,
    )
```

```python
import functools

import jax
import jax.numpy as jnp
from jax import lax
from jax.experimental import pallas as pl
from jax.experimental.pallas import tpu as pltpu
from jax.sharding import PartitionSpec as P

LANCZOS = 4
CHARGES = (0, 1, 1, 2)
GROUPS = ((0, 3), (1, 2))
F32 = jnp.float32
BF16 = jnp.bfloat16
MIB = 1024 * 1024


def padded(count):
    return -(-count // 8) * 8


def packed_height(count):
    return -(-count // 16) * 16


def packed_rows(count, tile):
    return count * tile // 2 + packed_height(count)


def chunks_of(width):
    one = width // 6 * 2
    two = (width - one) // 4 * 2
    return (0, one), (one, two), (one + two, width - one - two)


def iotas(shape):
    return lax.broadcasted_iota(jnp.int32, shape, 0), lax.broadcasted_iota(jnp.int32, shape, 1)


def pack_block(block):
    tile = block.shape[0]
    half = tile // 2
    top, low = block[:half], block[half:]
    row, lane = iotas((half, tile))
    turned = pltpu.roll(low, half, 1)
    folded = jnp.where((lane < half) & (row > lane), turned, top)
    diagonal = jnp.sum(jnp.where(lane == row + half, low, 0.0), axis=0, keepdims=True)
    return folded, diagonal


def unpack_block(folded, diagonal):
    half, tile = folded.shape
    row, lane = iotas((half, tile))
    rolled = pltpu.roll(folded, half, 1)
    turned = jnp.transpose(jnp.concatenate([folded, rolled], axis=0))
    top = jnp.where((lane < half) & (row > lane), turned[:half], folded)
    low = jnp.where((lane >= half) & (row > lane - half), rolled, turned[half:])
    low = jnp.where(lane == row + half, diagonal, low)
    return jnp.concatenate([top, low], axis=0)


def partner_of(sector):
    return sector + 1 - 2 * lax.rem(sector, 2)


def live_limits(dims_ref, sector):
    count = dims_ref.shape[0]
    rows = dims_ref[sector]
    columns = []
    for charge in CHARGES:
        target = sector + charge
        columns.append(jnp.where(target < count, dims_ref[jnp.minimum(target, count - 1)], 0))
    return rows, columns


def weight_rows(weight_ref, width, p, square, turned):
    wide = padded(width)
    square[...] = jnp.zeros_like(square)
    square[:width, :width] = weight_ref[pl.ds(p, width, stride=len(CHARGES)), :]
    value = square[...]
    if turned:
        value = jnp.transpose(value)
    high = value.astype(BF16).astype(F32)
    joined = (high + pltpu.roll(value - high, wide, 1)).astype(BF16)
    return joined[: packed_height(width), : 2 * wide]


def doubled(value):
    return jnp.concatenate([value, value], axis=0).astype(BF16)


def pack_kernel(width, tile, source_ref, out_ref, diag):
    half = tile // 2
    diag[...] = jnp.zeros_like(diag)
    for w in range(width):
        folded, diagonal = pack_block(source_ref[w * tile : (w + 1) * tile, :].astype(F32))
        out_ref[w * half : (w + 1) * half, :] = folded.astype(BF16)
        diag[w : w + 1, :] = diagonal
    out_ref[width * half :, :] = diag[...].astype(BF16)


def unpack_into(count, tile, read, write, diag):
    half = tile // 2
    size = packed_height(count)
    diag[:size, :] = read(count * half, size)
    for w in range(count):
        write(w, unpack_block(read(w * half, half), diag[w : w + 1, :]))


def reader(ref):
    return lambda at, size: ref[at : at + size, :].astype(F32)


def unpack_kernel(width, tile, *refs):
    *part_refs, out_ref, diag = refs
    for (first, count), ref in zip(chunks_of(width), part_refs):

        def write(w, block, first=first):
            out_ref[(first + w) * tile : (first + w + 1) * tile, :] = block.astype(BF16)

        unpack_into(count, tile, reader(ref), write, diag)


def fold_kernel(
    width, tile, travels, dims_ref, environ_ref, site_ref, far_environ_ref, far_site_ref, weight_ref, *refs
):
    part_refs = refs[: len(chunks_of(width))]
    joined_s, turned_s, square_s, weight_s, half_s, packed_s, diag_s, sums_s, diag_sums_s = refs[
        len(part_refs) :
    ]
    half = tile // 2
    pitch = half + 8
    wide = padded(width)
    sector = lax.axis_index("sec")
    partner = partner_of(sector)
    row, lane = iotas((tile, tile))

    def run(own_state, with_partner):
        rows, columns = live_limits(dims_ref, sector)
        live = (row < rows) & (lane < columns[own_state])
        sites = [jnp.where(live, site_ref[own_state].astype(F32), 0.0)]
        states = [own_state]
        if with_partner:
            rows, columns = live_limits(dims_ref, partner)
            for k in range(2):
                live = (row < rows) & (lane < columns[k + 1])
                sites.append(jnp.where(live, far_site_ref[k + 1].astype(F32), 0.0))
                states.append(k + 1)
        parts = len(states)
        for n in range(parts):
            joined_s[:, n * tile : (n + 1) * tile] = sites[n].astype(BF16)
            turned_s[n] = jnp.transpose(sites[n]).astype(BF16)
            weight_s[n] = weight_rows(weight_ref, width, states[n], square_s, True)
            packed_s[n, width * pitch :, :] = jnp.zeros(((wide - width) * pitch, tile), F32)
            diag_s[n] = jnp.zeros_like(diag_s[n])

        for pair in range(width // 2):
            at = slice(pair * tile, (pair + 1) * tile)
            for k in range(2):
                here = slice((pair * 2 + k) * tile, (pair * 2 + k + 1) * tile)
                blocks = [
                    jnp.dot(environ_ref[here, :], joined_s[:, :tile], preferred_element_type=F32)
                ]
                if with_partner:
                    both = jnp.dot(
                        far_environ_ref[here, :], joined_s[:, tile:], preferred_element_type=F32
                    )
                    blocks += [both[:, :tile], both[:, tile:]]
                for n in range(parts):
                    half_s[n, at, k * tile : (k + 1) * tile] = blocks[n].astype(BF16)
            for n in range(parts):
                both = jnp.dot(turned_s[n], half_s[n, at, :], preferred_element_type=F32)
                for k in range(2):
                    w = pair * 2 + k
                    folded, diagonal = pack_block(both[:, k * tile : (k + 1) * tile])
                    packed_s[n, w * pitch : w * pitch + half, :] = folded
                    diag_s[n, w : w + 1, :] = diagonal

        def mixed(inputs):
            value = None
            for n in range(parts):
                term = jnp.dot(weight_s[n], doubled(inputs[n]), preferred_element_type=F32)
                value = term if value is None else value + term
            return value[:wide]

        for at in range(0, half, 2):
            value = mixed([
                jnp.concatenate(
                    [packed_s[n, pl.ds(at + k, wide, stride=pitch), :] for k in range(2)], axis=1
                )
                for n in range(parts)
            ])
            for k in range(2):
                sums_s[pl.ds(at + k, wide, stride=pitch), :] = value[:, k * tile : (k + 1) * tile]
        diag_sums_s[...] = jnp.zeros_like(diag_sums_s)
        diag_sums_s[:wide, :] = mixed([diag_s[n, :wide] for n in range(parts)])
        for (first, count), ref in zip(chunks_of(width), part_refs):
            for w in range(count):
                at = (first + w) * pitch
                ref[w * half : (w + 1) * half, :] = sums_s[at : at + half, :].astype(ref.dtype)
            rows = packed_height(count)
            ref[count * half :, :] = diag_sums_s[first : first + rows, :].astype(ref.dtype)

    even = lax.rem(sector, 2) == 0
    own_state = len(CHARGES) - 1 if travels else 0

    @pl.when(even)
    def _():
        run(own_state, travels)

    @pl.when(jnp.logical_not(even))
    def _():
        run(own_state, not travels)


def mix_into(width, tile, weights, wide_s, sums_s, out_ref):
    wide = padded(width)
    pitch = tile + 8
    wide_s[width * pitch :, :] = jnp.zeros_like(wide_s[width * pitch :, :])

    for at in range(0, tile, 2):
        value = doubled(
            jnp.concatenate(
                [wide_s[pl.ds(at + k, wide, stride=pitch), :] for k in range(2)], axis=1
            )
        )
        for index, weight in enumerate(weights):
            mixed = jnp.dot(weight[...], value, preferred_element_type=F32)[:wide]
            for k in range(2):
                sums_s[index, pl.ds(at + k, wide, stride=pitch), :] = mixed[:, k * tile : (k + 1) * tile]
    for index in range(len(weights)):
        for w in range(width):
            out_ref[index, :, w * tile : (w + 1) * tile] = sums_s[
                index, w * pitch : w * pitch + tile, :
            ].astype(BF16)


def unpack_wide(width, tile, read, wide_s, diag):
    def write(w, block):
        wide_s[w * (tile + 8) : w * (tile + 8) + tile, :] = block

    unpack_into(width, tile, read, write, diag)


def copy_wide(width, tile, source_ref, wide_s):
    for w in range(width):
        at = w * (tile + 8)
        wide_s[at : at + tile, :] = source_ref[w * tile : (w + 1) * tile, :].astype(F32)


def mix_own_kernel(width, tile, source_ref, weight_ref, out_ref, square_s, weight_s, wide_s, sums_s):
    weight_s[0] = weight_rows(weight_ref, width, 0, square_s, False)
    copy_wide(width, tile, source_ref, wide_s)
    mix_into(width, tile, [weight_s.at[0]], wide_s, sums_s, out_ref)


def mix_next_kernel(
    width, tile, near_ref, weight_ref, out_ref, square_s, weight_s, wide_s, sums_s, diag
):
    for k in range(2):
        weight_s[k] = weight_rows(weight_ref, width, k + 1, square_s, False)
    unpack_wide(width, tile, reader(near_ref), wide_s, diag)
    mix_into(width, tile, [weight_s.at[k] for k in range(2)], wide_s, sums_s, out_ref)


def mix_after_kernel(
    width, tile, far_ref, weight_ref, out_ref, square_s, weight_s, wide_s, sums_s, diag
):
    weight_s[0] = weight_rows(weight_ref, width, 3, square_s, False)
    inside = lax.axis_index("sec") + 2 < lax.axis_size("sec")

    def read(at, size):
        return jnp.where(inside, far_ref[at : at + size, :].astype(F32), 0.0)

    unpack_wide(width, tile, read, wide_s, diag)
    mix_into(width, tile, [weight_s.at[0]], wide_s, sums_s, out_ref)


def total(value):
    return jnp.sum(jnp.sum(value, axis=0, keepdims=True), axis=1, keepdims=True)


def put(stats, kind, lane_at, value):
    row, lane = iotas(stats.shape)
    return jnp.where((row == kind) & (lane == lane_at), value, stats)


def scaled(value):
    square = total(value * value)
    inverse = jnp.where(square > 0.0, lax.rsqrt(square), 0.0)
    return value * inverse, square * inverse


def right_products(width, tile, field, right_ref, out_ref, k):
    lanes = slice(k * tile, (k + 1) * tile)
    for pair in range(width // 2):
        at = pair * 2 * tile
        both = jnp.dot(field, right_ref[:, at : at + 2 * tile], preferred_element_type=F32).astype(BF16)
        for n in range(2):
            out_ref[at + n * tile : at + (n + 1) * tile, lanes] = both[:, n * tile : (n + 1) * tile]


def head_kernel(members, width, tile, dims_ref, guess_ref, *refs):
    *right_refs, vector_ref, stats_ref, product_ref = refs
    rights = [ref.at[n] for ref in right_refs for n in range(ref.shape[0])]
    sector = lax.axis_index("sec")
    rows, columns = live_limits(dims_ref, sector)
    row, lane = iotas((tile, tile))
    stats = jnp.zeros(stats_ref.shape, F32)
    for k, p in enumerate(members):
        live = (row < rows) & (lane < columns[p])
        vector, norm = scaled(jnp.where(live, guess_ref[p], 0.0))
        vector_ref[k] = vector
        stats = put(stats, 0, sector * len(CHARGES) + p, norm)
        right_products(width, tile, vector.astype(BF16), rights[k], product_ref, k)
    stats_ref[...] = stats


def bound_blocks(chunks, tile, packed_refs, environ_ref, out_ref, diag):
    segment = lax.axis_index("seg")
    start = chunks[0][0]

    @pl.when(segment == 0)
    def _():
        for w in range(sum(count for _, count in chunks)):
            out_ref[:, w * tile : (w + 1) * tile] = environ_ref[
                (start + w) * tile : (start + w + 1) * tile, :
            ]

    @pl.when(segment != 0)
    def _():
        for (first, count), ref in zip(chunks, packed_refs):

            def write(w, block, base=first - start):
                out_ref[:, (base + w) * tile : (base + w + 1) * tile] = block.astype(BF16)

            unpack_into(count, tile, reader(ref), write, diag)


def open_kernel(width, tile, environ_ref, *refs):
    chunks = chunks_of(width)[:-1]
    packed_refs, (*product_refs, bound_ref, image_ref, diag) = refs[: len(chunks)], refs[len(chunks) :]
    bound_blocks(chunks, tile, packed_refs, environ_ref, bound_ref, diag)
    rows = bound_ref.shape[1]
    for group, product_ref in enumerate(product_refs):
        image_ref[group] = jnp.dot(bound_ref[...], product_ref[:rows, :], preferred_element_type=F32)


def lanczos_kernel(
    width, tile, dims_ref, packed_ref, environ_ref, early_ref, image_ref, own_ref, next_ref, after_ref,
    start_a, start_b, norm_a, norm_b, product_a, product_b, basis_ref, stats_ref,
    late_s, product_s, diag,
):
    states = len(CHARGES)
    sector = lax.axis_index("sec")
    last = chunks_of(width)[-1:]
    bound_blocks(last, tile, [packed_ref], environ_ref, late_s, diag)
    rows, columns = live_limits(dims_ref, sector)
    row, lane = iotas((tile, tile))
    rights = [own_ref.at[0], next_ref.at[0], next_ref.at[1], after_ref.at[0]]
    stats = norm_a[...] + norm_b[...]
    starts = (start_a, start_b)
    split = last[0][0] * tile
    betas = [None] * states
    for j in range(LANCZOS):
        for group, members in enumerate(GROUPS):
            if j == 0:
                source = (product_a, product_b)[group]
                images = image_ref[group]
            else:
                source = product_s.at[group]
                for k, p in enumerate(members):
                    field = basis_ref[j - 1, p].astype(BF16)
                    right_products(width, tile, field, rights[p], source, k)
                images = jnp.dot(early_ref[...], source[:split, :], preferred_element_type=F32)
            images = images + jnp.dot(late_s[...], source[split:, :], preferred_element_type=F32)
            for k, p in enumerate(members):
                live = (row < rows) & (lane < columns[p])
                image = jnp.where(live, images[:, k * tile : (k + 1) * tile], 0.0)
                vector = starts[group][k] if j == 0 else basis_ref[j - 1, p]
                alpha = total(vector * image)
                image = image - alpha * vector
                if j > 0:
                    before = starts[group][k] if j == 1 else basis_ref[j - 2, p]
                    image = image - betas[p] * before
                following, beta = scaled(image)
                basis_ref[j, p] = following
                betas[p] = beta
                stats = put(stats, 1 + 2 * j, sector * states + p, alpha)
                stats = put(stats, 2 + 2 * j, sector * states + p, beta)
    stats_ref[...] = stats


def finish_kernel(entries, start_a, start_b, basis_ref, *refs):
    states = len(CHARGES)
    sector = lax.axis_index("sec")
    *share_refs, vector_ref, table_ref = refs
    stats = share_refs[0][...]
    for ref in share_refs[1:]:
        stats = stats + ref[...]
    alphas = [stats[1 + 2 * j : 2 + 2 * j, :] for j in range(LANCZOS)]
    betas = [stats[2 + 2 * j : 3 + 2 * j, :] for j in range(LANCZOS)]

    def mean(left, right):
        products = left[0] * right[0]
        for x, y in zip(left[1:], right[1:]):
            products = products + x * y
        return jnp.sum(products, axis=1, keepdims=True) / entries

    start = [stats[0:1, :]]
    vector = [start[0] / jnp.sqrt(mean(start, start) + 1e-06)]
    previous = []
    beta = jnp.zeros((1, 1), F32)
    table_row, table_column = iotas(table_ref.shape)
    table = jnp.zeros(table_ref.shape, F32)
    for j in range(LANCZOS):
        image = []
        for k in range(j + 2):
            term = None
            if k > 0:
                term = betas[k - 1] * vector[k - 1]
            if k <= j:
                more = alphas[k] * vector[k]
                term = more if term is None else term + more
            if k + 1 <= j:
                term = term + betas[k] * vector[k + 1]
            image.append(term)
        alpha = mean(vector, image[: j + 1])
        for k in range(j + 1):
            image[k] = image[k] - alpha * vector[k]
        for k in range(j):
            image[k] = image[k] - beta * previous[k]
        beta = jnp.sqrt(mean(image, image) + 1e-06)
        previous = vector
        vector = [value / beta for value in image]
        table = jnp.where((table_row == 0) & (table_column == j), alpha, table)
        table = jnp.where((table_row == 1) & (table_column == j), beta, table)
    table_ref[...] = table
    lane = lax.broadcasted_iota(jnp.int32, (1, stats.shape[1]), 1)
    starts = {p: ref[k] for members, ref in zip(GROUPS, (start_a, start_b)) for k, p in enumerate(members)}
    for p in range(states):
        value = None
        here = lane == sector * states + p
        for k in range(LANCZOS + 1):
            weight = jnp.sum(jnp.where(here, vector[k], 0.0), axis=1, keepdims=True)
            term = weight * (starts[p] if k == 0 else basis_ref[k - 1, p])
            value = term if value is None else value + term
        vector_ref[p] = value


def smem():
    return pl.BlockSpec(memory_space=pltpu.SMEM)


def vmem():
    return pl.BlockSpec(memory_space=pltpu.VMEM)


def call(name, kernel, scalars, arrays, outs, scratch, limit, micros):
    many = isinstance(outs, (tuple, list))
    return pl.pallas_call(
        kernel,
        out_shape=outs,
        in_specs=[smem()] * len(scalars) + [vmem()] * len(arrays),
        out_specs=[vmem()] * len(outs) if many else vmem(),
        scratch_shapes=scratch,
        compiler_params=pltpu.CompilerParams(vmem_limit_bytes=limit * MIB),
        name=name,
        cost_estimate=pl.CostEstimate(
            flops=int(micros * 1.1e9), bytes_accessed=0, transcendentals=0
        ),
    )(*scalars, *arrays)


def shift_by(count, steps):
    return [(source, (source + steps) % count) for source in range(count)]


def shares(value, axis):
    count = lax.axis_size(axis)
    value = value + lax.ppermute(value, axis, [(q, q ^ 1) for q in range(count)])
    return [value] + [
        lax.ppermute(value, axis, shift_by(count, steps)) for steps in range(2, count, 2)
    ]


def on_device(left_env, right_env, site_tensors, mpo, boundary_mpo, guess, sector_dims):
    width, tile = left_env.shape[2], left_env.shape[-1]
    half = tile // 2
    wide = padded(width)
    states = len(CHARGES)
    sector_count = sector_dims.shape[0]
    sectors = lax.axis_size("sec")
    segments = lax.axis_size("seg")
    prows = packed_rows(width, tile)
    drows = prows - width * half
    packed = jax.ShapeDtypeStruct((prows, tile), BF16)
    parts = chunks_of(width)

    def packed_parts(dtype):
        return [jax.ShapeDtypeStruct((packed_rows(count, tile), tile), dtype) for _, count in parts]

    def mixed(count):
        return jax.ShapeDtypeStruct((count, tile, width * tile), BF16)

    environ = left_env.reshape(width * tile, tile)
    right = right_env.reshape(width * tile, tile)
    site = site_tensors[0, 0, :, 0]
    site_weights = jnp.transpose(mpo[0, 0], (0, 2, 1)).reshape(width * states, width)
    bound_weights = jnp.transpose(boundary_mpo[0], (0, 2, 1)).reshape(width * states, width)

    sector = lax.axis_index("sec")
    swap = [(q, q ^ 1) for q in range(sectors)]
    up_two = shift_by(sectors, 2)
    down_two = shift_by(sectors, -2)
    onward = shift_by(segments, 1)
    diag = pltpu.VMEM((drows, tile), F32)

    def mix_scratch(count):
        return [
            pltpu.VMEM((tile, tile), F32),
            pltpu.VMEM((count, packed_height(width), 2 * wide), BF16),
            pltpu.VMEM((wide * (tile + 8), tile), F32),
            pltpu.VMEM((count, wide * (tile + 8), tile), F32),
        ]

    right_packed = call(
        "pack_right", functools.partial(pack_kernel, width, tile), [], [right], packed,
        [diag], 6, 1,
    )
    right_far = lax.ppermute(right_packed, "sec", down_two)
    far_environ = lax.ppermute(environ, "sec", swap)
    far_site = lax.ppermute(site, "sec", swap)
    fold_scratch = [
        pltpu.VMEM((tile, 3 * tile), BF16),
        pltpu.VMEM((3, tile, tile), BF16),
        pltpu.VMEM((tile, tile), F32),
        pltpu.VMEM((3, packed_height(width), 2 * wide), BF16),
        pltpu.VMEM((3, width // 2 * tile, 2 * tile), BF16),
        pltpu.VMEM((3, wide * (half + 8), tile), F32),
        pltpu.VMEM((3, drows, tile), F32),
        pltpu.VMEM((wide * (half + 8), tile), F32),
        pltpu.VMEM((drows, tile), F32),
    ]
    outgoing = call(
        "fold_up", functools.partial(fold_kernel, width, tile, True),
        [sector_dims], [environ, site, far_environ, far_site, site_weights], packed_parts(BF16),
        fold_scratch, 20, 12,
    )
    early_arrived = lax.ppermute(outgoing[0], "sec", up_two)
    far_environ, outgoing = lax.optimization_barrier((far_environ, outgoing))
    kept = call(
        "fold_own", functools.partial(fold_kernel, width, tile, False),
        [sector_dims], [environ, site, far_environ, far_site, site_weights], packed_parts(F32),
        fold_scratch, 20, 0.1,
    )
    kept, middle_outgoing = lax.optimization_barrier((kept, outgoing[1]))
    middle_arrived = lax.ppermute(middle_outgoing, "sec", up_two)
    kept, right = lax.optimization_barrier((kept, right))
    own_mixed = call(
        "mix_own", functools.partial(mix_own_kernel, width, tile), [], [right, bound_weights],
        mixed(1), mix_scratch(1), 12, 1,
    )
    own_mixed, right_far, late_outgoing = lax.optimization_barrier((own_mixed, right_far, outgoing[2]))
    late_arrived = lax.ppermute(late_outgoing, "sec", up_two)
    passed_on = jnp.where(sector + 2 < sectors, right_far, jnp.zeros_like(right_far))
    passed_on = jnp.where(lax.rem(sector, 2) == 0, passed_on, right_packed)
    right_near = lax.ppermute(passed_on, "sec", swap)

    def carried(stays, comes):
        return (stays + jnp.where(sector >= 2, comes.astype(F32), 0.0)).astype(BF16)

    early = carried(kept[0], early_arrived)
    early_bound = lax.ppermute(early, "seg", onward)
    early, right_far = lax.optimization_barrier((early, right_far))
    after_mixed = call(
        "mix_after", functools.partial(mix_after_kernel, width, tile), [],
        [right_far, bound_weights], mixed(1), mix_scratch(1) + [diag], 12, 2,
    )
    def head(members, rights):
        return call(
            "head", functools.partial(head_kernel, members, width, tile),
            [sector_dims], [guess[0, :, 0]] + rights,
            (
                jax.ShapeDtypeStruct((2, tile, tile), F32),
                jax.ShapeDtypeStruct((16, 128), F32),
                jax.ShapeDtypeStruct((width * tile, 2 * tile), BF16),
            ),
            [], 9, 0.5,
        )

    middle_arrived, after_mixed = lax.optimization_barrier((middle_arrived, after_mixed))
    middle = carried(kept[1], middle_arrived)
    middle_bound = lax.ppermute(middle, "seg", onward)
    middle, right_near, after_mixed = lax.optimization_barrier((middle, right_near, after_mixed))
    start_a, norms_a, products_a = head(GROUPS[0], [own_mixed, after_mixed])
    next_mixed = call(
        "mix_next", functools.partial(mix_next_kernel, width, tile), [],
        [right_near, bound_weights], mixed(2), mix_scratch(2) + [diag], 16, 3,
    )
    late_arrived, next_mixed, products_a = lax.optimization_barrier(
        (late_arrived, next_mixed, products_a)
    )
    late = carried(kept[2], late_arrived)
    late_bound = lax.ppermute(late, "seg", onward)
    late, next_mixed = lax.optimization_barrier((late, next_mixed))
    start_b, norms_b, products_b = head(GROUPS[1], [next_mixed])
    new_env = call(
        "unpack_env", functools.partial(unpack_kernel, width, tile), [], [early, middle, late],
        jax.ShapeDtypeStruct((width * tile, tile), BF16), [diag], 6, 2,
    )
    middle_bound, new_env = lax.optimization_barrier((middle_bound, new_env))
    bound, image = call(
        "open", functools.partial(open_kernel, width, tile), [],
        [environ, early_bound, middle_bound, products_a, products_b],
        (
            jax.ShapeDtypeStruct((tile, parts[-1][0] * tile), BF16),
            jax.ShapeDtypeStruct((len(GROUPS), tile, 2 * tile), F32),
        ),
        [diag], 12, 1,
    )
    late_bound, bound = lax.optimization_barrier((late_bound, bound))
    basis, stats = call(
        "lanczos", functools.partial(lanczos_kernel, width, tile),
        [sector_dims],
        [late_bound, environ, bound, image, own_mixed, next_mixed, after_mixed, start_a, start_b,
         norms_a, norms_b, products_a, products_b],
        (
            jax.ShapeDtypeStruct((LANCZOS, states, tile, tile), F32),
            jax.ShapeDtypeStruct((16, 128), F32),
        ),
        [
            pltpu.VMEM((tile, parts[-1][1] * tile), BF16),
            pltpu.VMEM((len(GROUPS), width * tile, 2 * tile), BF16),
            diag,
        ],
        22, 12,
    )
    stats = shares(stats, "sec")
    entries = float(states * sector_count * tile * tile)
    vector, table = call(
        "finish", functools.partial(finish_kernel, entries), [], [start_a, start_b, basis] + stats,
        (
            jax.ShapeDtypeStruct((states, tile, tile), F32),
            jax.ShapeDtypeStruct((2, LANCZOS), F32),
        ),
        [], 6, 2,
    )
    return new_env.reshape(left_env.shape), vector[None, :, None], jnp.transpose(table)[None]


def solution(mesh):
    placed = (
        P("seg", "sec", None, None, None),
        P("seg", "sec", None, None, None),
        P("seg", None, None, "sec", None, None),
        P("seg", None, None, None, None),
        P("seg", None, None, None),
        P("seg", None, "sec", None, None),
        P(),
    )
    return jax.shard_map(
        on_device,
        mesh=mesh,
        in_specs=placed,
        out_specs=(
            P("seg", "sec", None, None, None),
            P("seg", None, "sec", None, None),
            P("seg", None, None),
        ),
        check_vma=False,
    )
```

```python
import functools

import jax
import jax.numpy as jnp
from jax import lax
from jax.experimental import pallas as pl
from jax.experimental.pallas import tpu as pltpu
from jax.sharding import PartitionSpec as P

LANCZOS = 4
CHARGES = (0, 1, 1, 2)
GROUPS = ((0, 3), (1, 2))
F32 = jnp.float32
BF16 = jnp.bfloat16
MIB = 1024 * 1024


def padded(count):
    return -(-count // 8) * 8


def packed_height(count):
    return -(-count // 16) * 16


def packed_rows(count, tile):
    return count * tile // 2 + packed_height(count)


def chunks_of(width):
    one = width // 6 * 2
    two = (width - one) // 4 * 2
    return (0, one), (one, two), (one + two, width - one - two)


def iotas(shape):
    return lax.broadcasted_iota(jnp.int32, shape, 0), lax.broadcasted_iota(jnp.int32, shape, 1)


def pack_block(block):
    tile = block.shape[0]
    half = tile // 2
    top, low = block[:half], block[half:]
    row, lane = iotas((half, tile))
    turned = pltpu.roll(low, half, 1)
    folded = jnp.where((lane < half) & (row > lane), turned, top)
    diagonal = jnp.sum(jnp.where(lane == row + half, low, 0.0), axis=0, keepdims=True)
    return folded, diagonal


def unpack_block(folded, diagonal):
    half, tile = folded.shape
    row, lane = iotas((half, tile))
    rolled = pltpu.roll(folded, half, 1)
    turned = jnp.transpose(jnp.concatenate([folded, rolled], axis=0))
    top = jnp.where((lane < half) & (row > lane), turned[:half], folded)
    low = jnp.where((lane >= half) & (row > lane - half), rolled, turned[half:])
    low = jnp.where(lane == row + half, diagonal, low)
    return jnp.concatenate([top, low], axis=0)


def partner_of(sector):
    return sector + 1 - 2 * lax.rem(sector, 2)


def live_limits(dims_ref, sector):
    count = dims_ref.shape[0]
    rows = dims_ref[sector]
    columns = []
    for charge in CHARGES:
        target = sector + charge
        columns.append(jnp.where(target < count, dims_ref[jnp.minimum(target, count - 1)], 0))
    return rows, columns


def weight_rows(weight_ref, width, p, square, turned):
    wide = padded(width)
    square[...] = jnp.zeros_like(square)
    square[:width, :width] = weight_ref[pl.ds(p, width, stride=len(CHARGES)), :]
    value = square[...]
    if turned:
        value = jnp.transpose(value)
    high = value.astype(BF16).astype(F32)
    joined = (high + pltpu.roll(value - high, wide, 1)).astype(BF16)
    return joined[: packed_height(width), : 2 * wide]


def doubled(value):
    return jnp.concatenate([value, value], axis=0).astype(BF16)


def pack_kernel(width, tile, source_ref, out_ref, diag):
    half = tile // 2
    diag[...] = jnp.zeros_like(diag)
    for w in range(width):
        folded, diagonal = pack_block(source_ref[w * tile : (w + 1) * tile, :].astype(F32))
        out_ref[w * half : (w + 1) * half, :] = folded.astype(BF16)
        diag[w : w + 1, :] = diagonal
    out_ref[width * half :, :] = diag[...].astype(BF16)


def unpack_into(count, tile, read, write, diag):
    half = tile // 2
    size = packed_height(count)
    diag[:size, :] = read(count * half, size)
    for w in range(count):
        write(w, unpack_block(read(w * half, half), diag[w : w + 1, :]))


def reader(ref):
    return lambda at, size: ref[at : at + size, :].astype(F32)


def unpack_kernel(width, tile, *refs):
    *part_refs, out_ref, diag = refs
    for (first, count), ref in zip(chunks_of(width), part_refs):

        def write(w, block, first=first):
            out_ref[(first + w) * tile : (first + w + 1) * tile, :] = block.astype(BF16)

        unpack_into(count, tile, reader(ref), write, diag)


def fold_kernel(
    width, tile, travels, dims_ref, environ_ref, site_ref, far_environ_ref, far_site_ref, weight_ref, *refs
):
    part_refs = refs[: len(chunks_of(width))]
    joined_s, turned_s, square_s, weight_s, half_s, packed_s, diag_s, sums_s, diag_sums_s = refs[
        len(part_refs) :
    ]
    half = tile // 2
    pitch = half + 8
    wide = padded(width)
    sector = lax.axis_index("sec")
    partner = partner_of(sector)
    row, lane = iotas((tile, tile))

    def run(own_state, with_partner):
        rows, columns = live_limits(dims_ref, sector)
        live = (row < rows) & (lane < columns[own_state])
        sites = [jnp.where(live, site_ref[own_state].astype(F32), 0.0)]
        states = [own_state]
        if with_partner:
            rows, columns = live_limits(dims_ref, partner)
            for k in range(2):
                live = (row < rows) & (lane < columns[k + 1])
                sites.append(jnp.where(live, far_site_ref[k + 1].astype(F32), 0.0))
                states.append(k + 1)
        parts = len(states)
        for n in range(parts):
            joined_s[:, n * tile : (n + 1) * tile] = sites[n].astype(BF16)
            turned_s[n] = jnp.transpose(sites[n]).astype(BF16)
            weight_s[n] = weight_rows(weight_ref, width, states[n], square_s, True)
            packed_s[n, width * pitch :, :] = jnp.zeros(((wide - width) * pitch, tile), F32)
            diag_s[n] = jnp.zeros_like(diag_s[n])

        for pair in range(width // 2):
            at = slice(pair * tile, (pair + 1) * tile)
            for k in range(2):
                here = slice((pair * 2 + k) * tile, (pair * 2 + k + 1) * tile)
                blocks = [
                    jnp.dot(environ_ref[here, :], joined_s[:, :tile], preferred_element_type=F32)
                ]
                if with_partner:
                    both = jnp.dot(
                        far_environ_ref[here, :], joined_s[:, tile:], preferred_element_type=F32
                    )
                    blocks += [both[:, :tile], both[:, tile:]]
                for n in range(parts):
                    half_s[n, at, k * tile : (k + 1) * tile] = blocks[n].astype(BF16)
            for n in range(parts):
                both = jnp.dot(turned_s[n], half_s[n, at, :], preferred_element_type=F32)
                for k in range(2):
                    w = pair * 2 + k
                    folded, diagonal = pack_block(both[:, k * tile : (k + 1) * tile])
                    packed_s[n, w * pitch : w * pitch + half, :] = folded
                    diag_s[n, w : w + 1, :] = diagonal

        def mixed(inputs):
            value = None
            for n in range(parts):
                term = jnp.dot(weight_s[n], doubled(inputs[n]), preferred_element_type=F32)
                value = term if value is None else value + term
            return value[:wide]

        for at in range(0, half, 2):
            value = mixed([
                jnp.concatenate(
                    [packed_s[n, pl.ds(at + k, wide, stride=pitch), :] for k in range(2)], axis=1
                )
                for n in range(parts)
            ])
            for k in range(2):
                sums_s[pl.ds(at + k, wide, stride=pitch), :] = value[:, k * tile : (k + 1) * tile]
        diag_sums_s[...] = jnp.zeros_like(diag_sums_s)
        diag_sums_s[:wide, :] = mixed([diag_s[n, :wide] for n in range(parts)])
        for (first, count), ref in zip(chunks_of(width), part_refs):
            for w in range(count):
                at = (first + w) * pitch
                ref[w * half : (w + 1) * half, :] = sums_s[at : at + half, :].astype(ref.dtype)
            rows = packed_height(count)
            ref[count * half :, :] = diag_sums_s[first : first + rows, :].astype(ref.dtype)

    even = lax.rem(sector, 2) == 0
    own_state = len(CHARGES) - 1 if travels else 0

    @pl.when(even)
    def _():
        run(own_state, travels)

    @pl.when(jnp.logical_not(even))
    def _():
        run(own_state, not travels)


def mix_into(width, tile, weights, wide_s, sums_s, out_ref):
    wide = padded(width)
    pitch = tile + 8
    wide_s[width * pitch :, :] = jnp.zeros_like(wide_s[width * pitch :, :])

    for at in range(0, tile, 2):
        value = doubled(
            jnp.concatenate(
                [wide_s[pl.ds(at + k, wide, stride=pitch), :] for k in range(2)], axis=1
            )
        )
        for index, weight in enumerate(weights):
            mixed = jnp.dot(weight[...], value, preferred_element_type=F32)[:wide]
            for k in range(2):
                sums_s[index, pl.ds(at + k, wide, stride=pitch), :] = mixed[:, k * tile : (k + 1) * tile]
    for index in range(len(weights)):
        for w in range(width):
            out_ref[index, :, w * tile : (w + 1) * tile] = sums_s[
                index, w * pitch : w * pitch + tile, :
            ].astype(BF16)


def unpack_wide(width, tile, read, wide_s, diag):
    def write(w, block):
        wide_s[w * (tile + 8) : w * (tile + 8) + tile, :] = block

    unpack_into(width, tile, read, write, diag)


def copy_wide(width, tile, source_ref, wide_s):
    for w in range(width):
        at = w * (tile + 8)
        wide_s[at : at + tile, :] = source_ref[w * tile : (w + 1) * tile, :].astype(F32)


def mix_own_kernel(width, tile, source_ref, weight_ref, out_ref, square_s, weight_s, wide_s, sums_s):
    weight_s[0] = weight_rows(weight_ref, width, 0, square_s, False)
    copy_wide(width, tile, source_ref, wide_s)
    mix_into(width, tile, [weight_s.at[0]], wide_s, sums_s, out_ref)


def mix_next_kernel(
    width, tile, near_ref, weight_ref, out_ref, square_s, weight_s, wide_s, sums_s, diag
):
    for k in range(2):
        weight_s[k] = weight_rows(weight_ref, width, k + 1, square_s, False)
    unpack_wide(width, tile, reader(near_ref), wide_s, diag)
    mix_into(width, tile, [weight_s.at[k] for k in range(2)], wide_s, sums_s, out_ref)


def mix_after_kernel(
    width, tile, far_ref, weight_ref, out_ref, square_s, weight_s, wide_s, sums_s, diag
):
    weight_s[0] = weight_rows(weight_ref, width, 3, square_s, False)
    inside = lax.axis_index("sec") + 2 < lax.axis_size("sec")

    def read(at, size):
        return jnp.where(inside, far_ref[at : at + size, :].astype(F32), 0.0)

    unpack_wide(width, tile, read, wide_s, diag)
    mix_into(width, tile, [weight_s.at[0]], wide_s, sums_s, out_ref)


def total(value):
    return jnp.sum(jnp.sum(value, axis=0, keepdims=True), axis=1, keepdims=True)


def put(stats, kind, lane_at, value):
    row, lane = iotas(stats.shape)
    return jnp.where((row == kind) & (lane == lane_at), value, stats)


def scaled(value):
    square = total(value * value)
    inverse = jnp.where(square > 0.0, lax.rsqrt(square), 0.0)
    return value * inverse, square * inverse


def right_products(width, tile, field, right_ref, out_ref, k):
    lanes = slice(k * tile, (k + 1) * tile)
    for pair in range(width // 2):
        at = pair * 2 * tile
        both = jnp.dot(field, right_ref[:, at : at + 2 * tile], preferred_element_type=F32).astype(BF16)
        for n in range(2):
            out_ref[at + n * tile : at + (n + 1) * tile, lanes] = both[:, n * tile : (n + 1) * tile]


def head_kernel(members, width, tile, dims_ref, guess_ref, *refs):
    *right_refs, vector_ref, stats_ref, product_ref = refs
    rights = [ref.at[n] for ref in right_refs for n in range(ref.shape[0])]
    sector = lax.axis_index("sec")
    rows, columns = live_limits(dims_ref, sector)
    row, lane = iotas((tile, tile))
    stats = jnp.zeros(stats_ref.shape, F32)
    for k, p in enumerate(members):
        live = (row < rows) & (lane < columns[p])
        vector, norm = scaled(jnp.where(live, guess_ref[p], 0.0))
        vector_ref[k] = vector
        stats = put(stats, 0, sector * len(CHARGES) + p, norm)
        right_products(width, tile, vector.astype(BF16), rights[k], product_ref, k)
    stats_ref[...] = stats


def bound_blocks(chunks, tile, packed_refs, environ_ref, out_ref, diag):
    segment = lax.axis_index("seg")
    start = chunks[0][0]

    @pl.when(segment == 0)
    def _():
        for w in range(sum(count for _, count in chunks)):
            out_ref[:, w * tile : (w + 1) * tile] = environ_ref[
                (start + w) * tile : (start + w + 1) * tile, :
            ]

    @pl.when(segment != 0)
    def _():
        for (first, count), ref in zip(chunks, packed_refs):

            def write(w, block, base=first - start):
                out_ref[:, (base + w) * tile : (base + w + 1) * tile] = block.astype(BF16)

            unpack_into(count, tile, reader(ref), write, diag)


def open_kernel(width, tile, environ_ref, *refs):
    chunks = chunks_of(width)[:-1]
    packed_refs, (*product_refs, bound_ref, image_ref, diag) = refs[: len(chunks)], refs[len(chunks) :]
    bound_blocks(chunks, tile, packed_refs, environ_ref, bound_ref, diag)
    rows = bound_ref.shape[1]
    for group, product_ref in enumerate(product_refs):
        image_ref[group] = jnp.dot(bound_ref[...], product_ref[:rows, :], preferred_element_type=F32)


def lanczos_kernel(
    width, tile, dims_ref, packed_ref, environ_ref, early_ref, image_ref, own_ref, next_ref, after_ref,
    start_a, start_b, norm_a, norm_b, product_a, product_b, basis_ref, stats_ref,
    late_s, product_s, diag,
):
    states = len(CHARGES)
    sector = lax.axis_index("sec")
    last = chunks_of(width)[-1:]
    bound_blocks(last, tile, [packed_ref], environ_ref, late_s, diag)
    rows, columns = live_limits(dims_ref, sector)
    row, lane = iotas((tile, tile))
    rights = [own_ref.at[0], next_ref.at[0], next_ref.at[1], after_ref.at[0]]
    stats = norm_a[...] + norm_b[...]
    starts = (start_a, start_b)
    split = last[0][0] * tile
    betas = [None] * states
    for j in range(LANCZOS):
        for group, members in enumerate(GROUPS):
            if j == 0:
                source = (product_a, product_b)[group]
                images = image_ref[group]
            else:
                source = product_s.at[group]
                for k, p in enumerate(members):
                    field = basis_ref[j - 1, p].astype(BF16)
                    right_products(width, tile, field, rights[p], source, k)
                images = jnp.dot(early_ref[...], source[:split, :], preferred_element_type=F32)
            images = images + jnp.dot(late_s[...], source[split:, :], preferred_element_type=F32)
            for k, p in enumerate(members):
                live = (row < rows) & (lane < columns[p])
                image = jnp.where(live, images[:, k * tile : (k + 1) * tile], 0.0)
                vector = starts[group][k] if j == 0 else basis_ref[j - 1, p]
                alpha = total(vector * image)
                image = image - alpha * vector
                if j > 0:
                    before = starts[group][k] if j == 1 else basis_ref[j - 2, p]
                    image = image - betas[p] * before
                following, beta = scaled(image)
                basis_ref[j, p] = following
                betas[p] = beta
                stats = put(stats, 1 + 2 * j, sector * states + p, alpha)
                stats = put(stats, 2 + 2 * j, sector * states + p, beta)
    stats_ref[...] = stats


def finish_kernel(
    entries, stats_ref, start_a, start_b, basis_ref, vector_ref, table_ref
):
    states = len(CHARGES)
    sector = lax.axis_index("sec")
    stats = stats_ref[0]
    for q in range(1, stats_ref.shape[0]):
        stats = stats + stats_ref[q]
    alphas = [stats[1 + 2 * j : 2 + 2 * j, :] for j in range(LANCZOS)]
    betas = [stats[2 + 2 * j : 3 + 2 * j, :] for j in range(LANCZOS)]

    def mean(left, right):
        products = left[0] * right[0]
        for x, y in zip(left[1:], right[1:]):
            products = products + x * y
        return jnp.sum(products, axis=1, keepdims=True) / entries

    def applied(vector):
        count = len(vector)
        image = []
        for k in range(count + 1):
            terms = []
            if k > 0:
                terms.append(betas[k - 1] * vector[k - 1])
            if k < count:
                terms.append(alphas[k] * vector[k])
            if k + 1 < count:
                terms.append(betas[k] * vector[k + 1])
            image.append(sum(terms[1:], terms[0]))
        return image

    residual = [stats[0:1, :]]
    previous = []
    table_row, table_column = iotas(table_ref.shape)
    table = jnp.zeros(table_ref.shape, F32)
    for j in range(LANCZOS):
        image = applied(residual)
        square = mean(residual, residual) + 1e-06
        alpha = mean(residual, image[: j + 1]) / square
        norm = jnp.sqrt(square)
        vector = [value / norm for value in residual]
        residual = [value / norm for value in image]
        for k in range(j + 1):
            residual[k] = residual[k] - alpha * vector[k]
        for k in range(j):
            residual[k] = residual[k] - norm * previous[k]
        previous = vector
        if j > 0:
            table = jnp.where((table_row == 1) & (table_column == j - 1), norm, table)
        table = jnp.where((table_row == 0) & (table_column == j), alpha, table)
    norm = jnp.sqrt(mean(residual, residual) + 1e-06)
    vector = [value / norm for value in residual]
    table = jnp.where((table_row == 1) & (table_column == LANCZOS - 1), norm, table)
    table_ref[...] = table
    lane = lax.broadcasted_iota(jnp.int32, (1, stats.shape[1]), 1)
    starts = {p: ref[k] for members, ref in zip(GROUPS, (start_a, start_b)) for k, p in enumerate(members)}
    for p in range(states):
        value = None
        here = lane == sector * states + p
        for k in range(LANCZOS + 1):
            weight = jnp.sum(jnp.where(here, vector[k], 0.0), axis=1, keepdims=True)
            term = weight * (starts[p] if k == 0 else basis_ref[k - 1, p])
            value = term if value is None else value + term
        vector_ref[p] = value


def smem():
    return pl.BlockSpec(memory_space=pltpu.SMEM)


def vmem():
    return pl.BlockSpec(memory_space=pltpu.VMEM)


def call(name, kernel, scalars, arrays, outs, scratch, limit, micros):
    many = isinstance(outs, (tuple, list))
    return pl.pallas_call(
        kernel,
        out_shape=outs,
        in_specs=[smem()] * len(scalars) + [vmem()] * len(arrays),
        out_specs=[vmem()] * len(outs) if many else vmem(),
        scratch_shapes=scratch,
        compiler_params=pltpu.CompilerParams(vmem_limit_bytes=limit * MIB),
        name=name,
        cost_estimate=pl.CostEstimate(
            flops=int(micros * 1.1e9), bytes_accessed=0, transcendentals=0
        ),
    )(*scalars, *arrays)


def shift_by(count, steps):
    return [(source, (source + steps) % count) for source in range(count)]


def gathered(value, axis):
    count = lax.axis_size(axis)
    return lax.all_to_all(jnp.broadcast_to(value, (count,) + value.shape), axis, 0, 0)


def on_device(left_env, right_env, site_tensors, mpo, boundary_mpo, guess, sector_dims):
    width, tile = left_env.shape[2], left_env.shape[-1]
    half = tile // 2
    wide = padded(width)
    states = len(CHARGES)
    sector_count = sector_dims.shape[0]
    sectors = lax.axis_size("sec")
    segments = lax.axis_size("seg")
    prows = packed_rows(width, tile)
    drows = prows - width * half
    packed = jax.ShapeDtypeStruct((prows, tile), BF16)
    parts = chunks_of(width)

    def packed_parts(dtype):
        return [jax.ShapeDtypeStruct((packed_rows(count, tile), tile), dtype) for _, count in parts]

    def mixed(count):
        return jax.ShapeDtypeStruct((count, tile, width * tile), BF16)

    environ = left_env.reshape(width * tile, tile)
    right = right_env.reshape(width * tile, tile)
    site = site_tensors[0, 0, :, 0]
    site_weights = jnp.transpose(mpo[0, 0], (0, 2, 1)).reshape(width * states, width)
    bound_weights = jnp.transpose(boundary_mpo[0], (0, 2, 1)).reshape(width * states, width)

    sector = lax.axis_index("sec")
    swap = [(q, q ^ 1) for q in range(sectors)]
    up_two = shift_by(sectors, 2)
    down_two = shift_by(sectors, -2)
    onward = shift_by(segments, 1)
    diag = pltpu.VMEM((drows, tile), F32)

    def mix_scratch(count):
        return [
            pltpu.VMEM((tile, tile), F32),
            pltpu.VMEM((count, packed_height(width), 2 * wide), BF16),
            pltpu.VMEM((wide * (tile + 8), tile), F32),
            pltpu.VMEM((count, wide * (tile + 8), tile), F32),
        ]

    right_packed = call(
        "pack_right", functools.partial(pack_kernel, width, tile), [], [right], packed,
        [diag], 6, 1,
    )
    right_far = lax.ppermute(right_packed, "sec", down_two)
    far_environ = lax.ppermute(environ, "sec", swap)
    far_site = lax.ppermute(site, "sec", swap)
    fold_scratch = [
        pltpu.VMEM((tile, 3 * tile), BF16),
        pltpu.VMEM((3, tile, tile), BF16),
        pltpu.VMEM((tile, tile), F32),
        pltpu.VMEM((3, packed_height(width), 2 * wide), BF16),
        pltpu.VMEM((3, width // 2 * tile, 2 * tile), BF16),
        pltpu.VMEM((3, wide * (half + 8), tile), F32),
        pltpu.VMEM((3, drows, tile), F32),
        pltpu.VMEM((wide * (half + 8), tile), F32),
        pltpu.VMEM((drows, tile), F32),
    ]
    outgoing = call(
        "fold_up", functools.partial(fold_kernel, width, tile, True),
        [sector_dims], [environ, site, far_environ, far_site, site_weights], packed_parts(BF16),
        fold_scratch, 20, 12,
    )
    early_arrived = lax.ppermute(outgoing[0], "sec", up_two)
    far_environ, outgoing = lax.optimization_barrier((far_environ, outgoing))
    kept = call(
        "fold_own", functools.partial(fold_kernel, width, tile, False),
        [sector_dims], [environ, site, far_environ, far_site, site_weights], packed_parts(F32),
        fold_scratch, 20, 0.1,
    )
    kept, middle_outgoing = lax.optimization_barrier((kept, outgoing[1]))
    middle_arrived = lax.ppermute(middle_outgoing, "sec", up_two)
    kept, right = lax.optimization_barrier((kept, right))
    own_mixed = call(
        "mix_own", functools.partial(mix_own_kernel, width, tile), [], [right, bound_weights],
        mixed(1), mix_scratch(1), 12, 1,
    )
    own_mixed, right_far, late_outgoing = lax.optimization_barrier((own_mixed, right_far, outgoing[2]))
    late_arrived = lax.ppermute(late_outgoing, "sec", up_two)
    passed_on = jnp.where(sector + 2 < sectors, right_far, jnp.zeros_like(right_far))
    passed_on = jnp.where(lax.rem(sector, 2) == 0, passed_on, right_packed)
    right_near = lax.ppermute(passed_on, "sec", swap)

    def carried(stays, comes):
        return (stays + jnp.where(sector >= 2, comes.astype(F32), 0.0)).astype(BF16)

    early = carried(kept[0], early_arrived)
    early_bound = lax.ppermute(early, "seg", onward)
    early, right_far = lax.optimization_barrier((early, right_far))
    after_mixed = call(
        "mix_after", functools.partial(mix_after_kernel, width, tile), [],
        [right_far, bound_weights], mixed(1), mix_scratch(1) + [diag], 12, 2,
    )
    def head(members, rights):
        return call(
            "head", functools.partial(head_kernel, members, width, tile),
            [sector_dims], [guess[0, :, 0]] + rights,
            (
                jax.ShapeDtypeStruct((2, tile, tile), F32),
                jax.ShapeDtypeStruct((16, 128), F32),
                jax.ShapeDtypeStruct((width * tile, 2 * tile), BF16),
            ),
            [], 9, 0.5,
        )

    middle_arrived, after_mixed = lax.optimization_barrier((middle_arrived, after_mixed))
    middle = carried(kept[1], middle_arrived)
    middle_bound = lax.ppermute(middle, "seg", onward)
    middle, right_near = lax.optimization_barrier((middle, right_near))
    next_mixed = call(
        "mix_next", functools.partial(mix_next_kernel, width, tile), [],
        [right_near, bound_weights], mixed(2), mix_scratch(2) + [diag], 16, 3,
    )
    late_arrived, next_mixed = lax.optimization_barrier((late_arrived, next_mixed))
    late = carried(kept[2], late_arrived)
    late_bound = lax.ppermute(late, "seg", onward)
    late, next_mixed, after_mixed = lax.optimization_barrier((late, next_mixed, after_mixed))
    start_a, norms_a, products_a = head(GROUPS[0], [own_mixed, after_mixed])
    start_b, norms_b, products_b = head(GROUPS[1], [next_mixed])
    new_env = call(
        "unpack_env", functools.partial(unpack_kernel, width, tile), [], [early, middle, late],
        jax.ShapeDtypeStruct((width * tile, tile), BF16), [diag], 6, 2,
    )
    middle_bound, new_env = lax.optimization_barrier((middle_bound, new_env))
    bound, image = call(
        "open", functools.partial(open_kernel, width, tile), [],
        [environ, early_bound, middle_bound, products_a, products_b],
        (
            jax.ShapeDtypeStruct((tile, parts[-1][0] * tile), BF16),
            jax.ShapeDtypeStruct((len(GROUPS), tile, 2 * tile), F32),
        ),
        [diag], 12, 1,
    )
    late_bound, bound = lax.optimization_barrier((late_bound, bound))
    basis, stats = call(
        "lanczos", functools.partial(lanczos_kernel, width, tile),
        [sector_dims],
        [late_bound, environ, bound, image, own_mixed, next_mixed, after_mixed, start_a, start_b,
         norms_a, norms_b, products_a, products_b],
        (
            jax.ShapeDtypeStruct((LANCZOS, states, tile, tile), F32),
            jax.ShapeDtypeStruct((16, 128), F32),
        ),
        [
            pltpu.VMEM((tile, parts[-1][1] * tile), BF16),
            pltpu.VMEM((len(GROUPS), width * tile, 2 * tile), BF16),
            diag,
        ],
        22, 12,
    )
    stats = gathered(stats, "sec")
    entries = float(states * sector_count * tile * tile)
    vector, table = call(
        "finish", functools.partial(finish_kernel, entries), [], [stats, start_a, start_b, basis],
        (
            jax.ShapeDtypeStruct((states, tile, tile), F32),
            jax.ShapeDtypeStruct((2, LANCZOS), F32),
        ),
        [], 6, 2,
    )
    return new_env.reshape(left_env.shape), vector[None, :, None], jnp.transpose(table)[None]


def solution(mesh):
    placed = (
        P("seg", "sec", None, None, None),
        P("seg", "sec", None, None, None),
        P("seg", None, None, "sec", None, None),
        P("seg", None, None, None, None),
        P("seg", None, None, None),
        P("seg", None, "sec", None, None),
        P(),
    )
    return jax.shard_map(
        on_device,
        mesh=mesh,
        in_specs=placed,
        out_specs=(
            P("seg", "sec", None, None, None),
            P("seg", None, "sec", None, None),
            P("seg", None, None),
        ),
        check_vma=False,
    )
```

```python
import functools

import jax
import jax.numpy as jnp
from jax import lax
from jax.experimental import pallas as pl
from jax.experimental.pallas import tpu as pltpu
from jax.sharding import PartitionSpec as P

LANCZOS = 4
CHARGES = (0, 1, 1, 2)
GROUPS = ((0, 3), (1, 2))
F32 = jnp.float32
BF16 = jnp.bfloat16
MIB = 1024 * 1024


def padded(count):
    return -(-count // 8) * 8


def packed_height(count):
    return -(-count // 16) * 16


def packed_rows(count, tile):
    return count * tile // 2 + packed_height(count)


def chunks_of(width):
    side = width // 6 * 2
    middle = width - 2 * side
    return (0, side), (side, middle), (side + middle, side)


def iotas(shape):
    return lax.broadcasted_iota(jnp.int32, shape, 0), lax.broadcasted_iota(jnp.int32, shape, 1)


def pack_block(block):
    tile = block.shape[0]
    half = tile // 2
    top, low = block[:half], block[half:]
    row, lane = iotas((half, tile))
    turned = pltpu.roll(low, half, 1)
    folded = jnp.where((lane < half) & (row > lane), turned, top)
    diagonal = jnp.sum(jnp.where(lane == row + half, low, 0.0), axis=0, keepdims=True)
    return folded, diagonal


def unpack_block(folded, diagonal):
    half, tile = folded.shape
    row, lane = iotas((half, tile))
    rolled = pltpu.roll(folded, half, 1)
    turned = jnp.transpose(jnp.concatenate([folded, rolled], axis=0))
    top = jnp.where((lane < half) & (row > lane), turned[:half], folded)
    low = jnp.where((lane >= half) & (row > lane - half), rolled, turned[half:])
    low = jnp.where(lane == row + half, diagonal, low)
    return jnp.concatenate([top, low], axis=0)


def partner_of(sector):
    return sector + 1 - 2 * lax.rem(sector, 2)


def live_limits(dims_ref, sector):
    count = dims_ref.shape[0]
    rows = dims_ref[sector]
    columns = []
    for charge in CHARGES:
        target = sector + charge
        columns.append(jnp.where(target < count, dims_ref[jnp.minimum(target, count - 1)], 0))
    return rows, columns


def weight_rows(weight_ref, width, p, square, turned):
    wide = padded(width)
    square[...] = jnp.zeros_like(square)
    square[:width, :width] = weight_ref[pl.ds(p, width, stride=len(CHARGES)), :]
    value = square[...]
    if turned:
        value = jnp.transpose(value)
    high = value.astype(BF16).astype(F32)
    joined = (high + pltpu.roll(value - high, wide, 1)).astype(BF16)
    return joined[: packed_height(width), : 2 * wide]


def doubled(value):
    return jnp.concatenate([value, value], axis=0).astype(BF16)


def pack_kernel(width, tile, source_ref, out_ref, diag):
    half = tile // 2
    diag[...] = jnp.zeros_like(diag)
    for w in range(width):
        folded, diagonal = pack_block(source_ref[w * tile : (w + 1) * tile, :].astype(F32))
        out_ref[w * half : (w + 1) * half, :] = folded.astype(BF16)
        diag[w : w + 1, :] = diagonal
    out_ref[width * half :, :] = diag[...].astype(BF16)


def unpack_into(count, tile, read, write, diag):
    half = tile // 2
    size = packed_height(count)
    diag[:size, :] = read(count * half, size)
    for w in range(count):
        write(w, unpack_block(read(w * half, half), diag[w : w + 1, :]))


def reader(ref):
    return lambda at, size: ref[at : at + size, :].astype(F32)


def fold_kernel(
    width, tile, travels, dims_ref, environ_ref, site_ref, far_environ_ref, far_site_ref, weight_ref, *refs
):
    part_refs = refs[: len(chunks_of(width))]
    joined_s, turned_s, square_s, weight_s, half_s, packed_s, diag_s, sums_s, diag_sums_s = refs[
        len(part_refs) :
    ]
    half = tile // 2
    pitch = half + 8
    wide = padded(width)
    sector = lax.axis_index("sec")
    partner = partner_of(sector)
    row, lane = iotas((tile, tile))

    def run(own_state, with_partner):
        rows, columns = live_limits(dims_ref, sector)
        live = (row < rows) & (lane < columns[own_state])
        sites = [jnp.where(live, site_ref[own_state].astype(F32), 0.0)]
        states = [own_state]
        if with_partner:
            rows, columns = live_limits(dims_ref, partner)
            for k in range(2):
                live = (row < rows) & (lane < columns[k + 1])
                sites.append(jnp.where(live, far_site_ref[k + 1].astype(F32), 0.0))
                states.append(k + 1)
        parts = len(states)
        for n in range(parts):
            joined_s[:, n * tile : (n + 1) * tile] = sites[n].astype(BF16)
            turned_s[n] = jnp.transpose(sites[n]).astype(BF16)
            weight_s[n] = weight_rows(weight_ref, width, states[n], square_s, True)
            packed_s[n, width * pitch :, :] = jnp.zeros(((wide - width) * pitch, tile), F32)
            diag_s[n] = jnp.zeros_like(diag_s[n])

        for pair in range(width // 2):
            at = slice(pair * tile, (pair + 1) * tile)
            for k in range(2):
                here = slice((pair * 2 + k) * tile, (pair * 2 + k + 1) * tile)
                blocks = [
                    jnp.dot(environ_ref[here, :], joined_s[:, :tile], preferred_element_type=F32)
                ]
                if with_partner:
                    both = jnp.dot(
                        far_environ_ref[here, :], joined_s[:, tile:], preferred_element_type=F32
                    )
                    blocks += [both[:, :tile], both[:, tile:]]
                for n in range(parts):
                    half_s[n, at, k * tile : (k + 1) * tile] = blocks[n].astype(BF16)
            for n in range(parts):
                both = jnp.dot(turned_s[n], half_s[n, at, :], preferred_element_type=F32)
                for k in range(2):
                    w = pair * 2 + k
                    folded, diagonal = pack_block(both[:, k * tile : (k + 1) * tile])
                    packed_s[n, w * pitch : w * pitch + half, :] = folded
                    diag_s[n, w : w + 1, :] = diagonal

        def mixed(inputs):
            value = None
            for n in range(parts):
                term = jnp.dot(weight_s[n], doubled(inputs[n]), preferred_element_type=F32)
                value = term if value is None else value + term
            return value[:wide]

        for at in range(0, half, 2):
            value = mixed([
                jnp.concatenate(
                    [packed_s[n, pl.ds(at + k, wide, stride=pitch), :] for k in range(2)], axis=1
                )
                for n in range(parts)
            ])
            for k in range(2):
                sums_s[pl.ds(at + k, wide, stride=pitch), :] = value[:, k * tile : (k + 1) * tile]
        diag_sums_s[...] = jnp.zeros_like(diag_sums_s)
        diag_sums_s[:wide, :] = mixed([diag_s[n, :wide] for n in range(parts)])
        for (first, count), ref in zip(chunks_of(width), part_refs):
            for w in range(count):
                at = (first + w) * pitch
                ref[w * half : (w + 1) * half, :] = sums_s[at : at + half, :].astype(ref.dtype)
            rows = packed_height(count)
            ref[count * half :, :] = diag_sums_s[first : first + rows, :].astype(ref.dtype)

    even = lax.rem(sector, 2) == 0
    own_state = len(CHARGES) - 1 if travels else 0

    @pl.when(even)
    def _():
        run(own_state, travels)

    @pl.when(jnp.logical_not(even))
    def _():
        run(own_state, not travels)


def mix_into(width, tile, weights, wide_s, sums_s, out_ref):
    wide = padded(width)
    pitch = tile + 8
    wide_s[width * pitch :, :] = jnp.zeros_like(wide_s[width * pitch :, :])

    for at in range(0, tile, 2):
        value = doubled(
            jnp.concatenate(
                [wide_s[pl.ds(at + k, wide, stride=pitch), :] for k in range(2)], axis=1
            )
        )
        for index, weight in enumerate(weights):
            mixed = jnp.dot(weight[...], value, preferred_element_type=F32)[:wide]
            for k in range(2):
                sums_s[index, pl.ds(at + k, wide, stride=pitch), :] = mixed[:, k * tile : (k + 1) * tile]
    for index in range(len(weights)):
        for w in range(width):
            out_ref[index, :, w * tile : (w + 1) * tile] = sums_s[
                index, w * pitch : w * pitch + tile, :
            ].astype(BF16)


def unpack_wide(width, tile, read, wide_s, diag):
    def write(w, block):
        wide_s[w * (tile + 8) : w * (tile + 8) + tile, :] = block

    unpack_into(width, tile, read, write, diag)


def copy_wide(width, tile, source_ref, wide_s):
    for w in range(width):
        at = w * (tile + 8)
        wide_s[at : at + tile, :] = source_ref[w * tile : (w + 1) * tile, :].astype(F32)


def mix_own_kernel(width, tile, source_ref, weight_ref, out_ref, square_s, weight_s, wide_s, sums_s):
    weight_s[0] = weight_rows(weight_ref, width, 0, square_s, False)
    copy_wide(width, tile, source_ref, wide_s)
    mix_into(width, tile, [weight_s.at[0]], wide_s, sums_s, out_ref)


def mix_next_kernel(
    width, tile, near_ref, weight_ref, out_ref, square_s, weight_s, wide_s, sums_s, diag
):
    for k in range(2):
        weight_s[k] = weight_rows(weight_ref, width, k + 1, square_s, False)
    unpack_wide(width, tile, reader(near_ref), wide_s, diag)
    mix_into(width, tile, [weight_s.at[k] for k in range(2)], wide_s, sums_s, out_ref)


def mix_after_kernel(
    width, tile, far_ref, weight_ref, out_ref, square_s, weight_s, wide_s, sums_s, diag
):
    weight_s[0] = weight_rows(weight_ref, width, 3, square_s, False)
    inside = lax.axis_index("sec") + 2 < lax.axis_size("sec")

    def read(at, size):
        return jnp.where(inside, far_ref[at : at + size, :].astype(F32), 0.0)

    unpack_wide(width, tile, read, wide_s, diag)
    mix_into(width, tile, [weight_s.at[0]], wide_s, sums_s, out_ref)


def total(value):
    return jnp.sum(jnp.sum(value, axis=0, keepdims=True), axis=1, keepdims=True)


def put(stats, kind, lane_at, value):
    row, lane = iotas(stats.shape)
    return jnp.where((row == kind) & (lane == lane_at), value, stats)


def scaled(value):
    square = total(value * value)
    inverse = jnp.where(square > 0.0, lax.rsqrt(square), 0.0)
    return value * inverse, square * inverse


def right_products(width, tile, field, right_ref, out_ref, k, beside=None):
    lanes = slice(k * tile, (k + 1) * tile)
    for pair in range(width // 2):
        if beside is not None:
            beside(pair)
        at = pair * 2 * tile
        both = jnp.dot(field, right_ref[:, at : at + 2 * tile], preferred_element_type=F32).astype(BF16)
        for n in range(2):
            out_ref[at + n * tile : at + (n + 1) * tile, lanes] = both[:, n * tile : (n + 1) * tile]


def head_kernel(members, width, tile, dims_ref, guess_ref, *refs):
    *right_refs, vector_ref, stats_ref, product_ref = refs
    rights = [ref.at[n] for ref in right_refs for n in range(ref.shape[0])]
    sector = lax.axis_index("sec")
    rows, columns = live_limits(dims_ref, sector)
    row, lane = iotas((tile, tile))
    stats = jnp.zeros(stats_ref.shape, F32)
    for k, p in enumerate(members):
        live = (row < rows) & (lane < columns[p])
        vector, norm = scaled(jnp.where(live, guess_ref[p], 0.0))
        vector_ref[k] = vector
        stats = put(stats, 0, sector * len(CHARGES) + p, norm)
        right_products(width, tile, vector.astype(BF16), rights[k], product_ref, k)
    stats_ref[...] = stats


def bound_blocks(chunks, tile, packed_refs, environ_ref, out_ref, diag):
    segment = lax.axis_index("seg")
    start = chunks[0][0]

    @pl.when(segment == 0)
    def _():
        for w in range(sum(count for _, count in chunks)):
            out_ref[:, w * tile : (w + 1) * tile] = environ_ref[
                (start + w) * tile : (start + w + 1) * tile, :
            ]

    @pl.when(segment != 0)
    def _():
        for (first, count), ref in zip(chunks, packed_refs):

            def write(w, block, base=first - start):
                out_ref[:, (base + w) * tile : (base + w + 1) * tile] = block.astype(BF16)

            unpack_into(count, tile, reader(ref), write, diag)


def open_kernel(width, tile, environ_ref, *refs):
    chunks = chunks_of(width)[:-1]
    packed_refs, (*product_refs, bound_ref, image_ref, diag) = refs[: len(chunks)], refs[len(chunks) :]
    bound_blocks(chunks, tile, packed_refs, environ_ref, bound_ref, diag)
    rows = bound_ref.shape[1]
    for group, product_ref in enumerate(product_refs):
        image_ref[group] = jnp.dot(bound_ref[...], product_ref[:rows, :], preferred_element_type=F32)


def lanczos_kernel(
    width, tile, dims_ref, packed_ref, environ_ref, early_ref, image_ref, own_ref, next_ref, after_ref,
    start_a, start_b, norm_a, norm_b, product_a, product_b, *refs
):
    *fresh_refs, basis_ref, stats_ref, env_ref, late_s, product_s, env_s, diag, env_diag, sem = refs
    states = len(CHARGES)
    sector = lax.axis_index("sec")
    last = chunks_of(width)[-1:]
    bound_blocks(last, tile, [packed_ref], environ_ref, late_s, diag)
    rows, columns = live_limits(dims_ref, sector)
    row, lane = iotas((tile, tile))
    rights = [own_ref.at[0], next_ref.at[0], next_ref.at[1], after_ref.at[0]]
    stats = norm_a[...] + norm_b[...]
    starts = (start_a, start_b)
    half = tile // 2
    places = [
        (ref, w, first + w)
        for (first, count), ref in zip(chunks_of(width), fresh_refs)
        for w in range(count)
    ]
    for (first, count), ref in zip(chunks_of(width), fresh_refs):
        env_diag[first : first + count, :] = ref[count * half :, :].astype(F32)[:count]
    copy = pltpu.make_async_copy(env_s, env_ref, sem)

    def unpack_one(n):
        ref, w, to = places[n]
        folded = ref[w * half : (w + 1) * half, :].astype(F32)
        env_s[to * tile : (to + 1) * tile, :] = unpack_block(
            folded, env_diag[to : to + 1, :]
        ).astype(BF16)

    split = last[0][0] * tile
    betas = [None] * states
    for j in range(LANCZOS):
        for group, members in enumerate(GROUPS):
            if j == 0:
                source = (product_a, product_b)[group]
                images = image_ref[group]
            else:
                source = product_s.at[group]
                for k, p in enumerate(members):
                    field = basis_ref[j - 1, p].astype(BF16)
                    beside = None
                    if j == 1 and k == 0:

                        def beside(pair, base=group * width // 2):
                            unpack_one(base + pair)

                    right_products(width, tile, field, rights[p], source, k, beside)
                if j == 1 and group + 1 == len(GROUPS):
                    copy.start()
                images = jnp.dot(early_ref[...], source[:split, :], preferred_element_type=F32)
            images = images + jnp.dot(late_s[...], source[split:, :], preferred_element_type=F32)
            for k, p in enumerate(members):
                live = (row < rows) & (lane < columns[p])
                image = jnp.where(live, images[:, k * tile : (k + 1) * tile], 0.0)
                vector = starts[group][k] if j == 0 else basis_ref[j - 1, p]
                alpha = total(vector * image)
                image = image - alpha * vector
                if j > 0:
                    before = starts[group][k] if j == 1 else basis_ref[j - 2, p]
                    image = image - betas[p] * before
                following, beta = scaled(image)
                basis_ref[j, p] = following
                betas[p] = beta
                stats = put(stats, 1 + 2 * j, sector * states + p, alpha)
                stats = put(stats, 2 + 2 * j, sector * states + p, beta)
    stats_ref[...] = stats
    copy.wait()


def finish_kernel(
    entries, stats_ref, start_a, start_b, basis_ref, vector_ref, table_ref
):
    states = len(CHARGES)
    sector = lax.axis_index("sec")
    stats = stats_ref[0]
    for q in range(1, stats_ref.shape[0]):
        stats = stats + stats_ref[q]
    alphas = [stats[1 + 2 * j : 2 + 2 * j, :] for j in range(LANCZOS)]
    betas = [stats[2 + 2 * j : 3 + 2 * j, :] for j in range(LANCZOS)]

    def mean(left, right):
        products = left[0] * right[0]
        for x, y in zip(left[1:], right[1:]):
            products = products + x * y
        return jnp.sum(products, axis=1, keepdims=True) / entries

    def applied(vector):
        count = len(vector)
        image = []
        for k in range(count + 1):
            terms = []
            if k > 0:
                terms.append(betas[k - 1] * vector[k - 1])
            if k < count:
                terms.append(alphas[k] * vector[k])
            if k + 1 < count:
                terms.append(betas[k] * vector[k + 1])
            image.append(sum(terms[1:], terms[0]))
        return image

    residual = [stats[0:1, :]]
    previous = []
    table_row, table_column = iotas(table_ref.shape)
    table = jnp.zeros(table_ref.shape, F32)
    for j in range(LANCZOS):
        image = applied(residual)
        square = mean(residual, residual) + 1e-06
        alpha = mean(residual, image[: j + 1]) / square
        norm = jnp.sqrt(square)
        vector = [value / norm for value in residual]
        residual = [value / norm for value in image]
        for k in range(j + 1):
            residual[k] = residual[k] - alpha * vector[k]
        for k in range(j):
            residual[k] = residual[k] - norm * previous[k]
        previous = vector
        if j > 0:
            table = jnp.where((table_row == 1) & (table_column == j - 1), norm, table)
        table = jnp.where((table_row == 0) & (table_column == j), alpha, table)
    norm = jnp.sqrt(mean(residual, residual) + 1e-06)
    vector = [value / norm for value in residual]
    table = jnp.where((table_row == 1) & (table_column == LANCZOS - 1), norm, table)
    table_ref[...] = table
    lane = lax.broadcasted_iota(jnp.int32, (1, stats.shape[1]), 1)
    starts = {p: ref[k] for members, ref in zip(GROUPS, (start_a, start_b)) for k, p in enumerate(members)}
    for p in range(states):
        value = None
        here = lane == sector * states + p
        for k in range(LANCZOS + 1):
            weight = jnp.sum(jnp.where(here, vector[k], 0.0), axis=1, keepdims=True)
            term = weight * (starts[p] if k == 0 else basis_ref[k - 1, p])
            value = term if value is None else value + term
        vector_ref[p] = value


def smem():
    return pl.BlockSpec(memory_space=pltpu.SMEM)


def vmem():
    return pl.BlockSpec(memory_space=pltpu.VMEM)


def call(name, kernel, scalars, arrays, outs, scratch, limit, micros, out_specs=None):
    many = isinstance(outs, (tuple, list))
    return pl.pallas_call(
        kernel,
        out_shape=outs,
        in_specs=[smem()] * len(scalars) + [vmem()] * len(arrays),
        out_specs=out_specs or ([vmem()] * len(outs) if many else vmem()),
        scratch_shapes=scratch,
        compiler_params=pltpu.CompilerParams(vmem_limit_bytes=limit * MIB),
        name=name,
        cost_estimate=pl.CostEstimate(
            flops=int(micros * 1.1e9), bytes_accessed=0, transcendentals=0
        ),
    )(*scalars, *arrays)


def shift_by(count, steps):
    return [(source, (source + steps) % count) for source in range(count)]


def gathered(value, axis):
    count = lax.axis_size(axis)
    return lax.all_to_all(jnp.broadcast_to(value, (count,) + value.shape), axis, 0, 0)


def on_device(left_env, right_env, site_tensors, mpo, boundary_mpo, guess, sector_dims):
    width, tile = left_env.shape[2], left_env.shape[-1]
    half = tile // 2
    wide = padded(width)
    states = len(CHARGES)
    sector_count = sector_dims.shape[0]
    sectors = lax.axis_size("sec")
    segments = lax.axis_size("seg")
    prows = packed_rows(width, tile)
    drows = prows - width * half
    packed = jax.ShapeDtypeStruct((prows, tile), BF16)
    parts = chunks_of(width)

    def packed_parts(dtype):
        return [jax.ShapeDtypeStruct((packed_rows(count, tile), tile), dtype) for _, count in parts]

    def mixed(count):
        return jax.ShapeDtypeStruct((count, tile, width * tile), BF16)

    environ = left_env.reshape(width * tile, tile)
    right = right_env.reshape(width * tile, tile)
    site = site_tensors[0, 0, :, 0]
    site_weights = jnp.transpose(mpo[0, 0], (0, 2, 1)).reshape(width * states, width)
    bound_weights = jnp.transpose(boundary_mpo[0], (0, 2, 1)).reshape(width * states, width)

    sector = lax.axis_index("sec")
    swap = [(q, q ^ 1) for q in range(sectors)]
    up_two = shift_by(sectors, 2)
    down_two = shift_by(sectors, -2)
    onward = shift_by(segments, 1)
    diag = pltpu.VMEM((drows, tile), F32)

    def mix_scratch(count):
        return [
            pltpu.VMEM((tile, tile), F32),
            pltpu.VMEM((count, packed_height(width), 2 * wide), BF16),
            pltpu.VMEM((wide * (tile + 8), tile), F32),
            pltpu.VMEM((count, wide * (tile + 8), tile), F32),
        ]

    right_packed = call(
        "pack_right", functools.partial(pack_kernel, width, tile), [], [right], packed,
        [diag], 6, 1,
    )
    right_far = lax.ppermute(right_packed, "sec", down_two)
    far_environ = lax.ppermute(environ, "sec", swap)
    far_site = lax.ppermute(site, "sec", swap)
    fold_scratch = [
        pltpu.VMEM((tile, 3 * tile), BF16),
        pltpu.VMEM((3, tile, tile), BF16),
        pltpu.VMEM((tile, tile), F32),
        pltpu.VMEM((3, packed_height(width), 2 * wide), BF16),
        pltpu.VMEM((3, width // 2 * tile, 2 * tile), BF16),
        pltpu.VMEM((3, wide * (half + 8), tile), F32),
        pltpu.VMEM((3, drows, tile), F32),
        pltpu.VMEM((wide * (half + 8), tile), F32),
        pltpu.VMEM((drows, tile), F32),
    ]
    outgoing = call(
        "fold_up", functools.partial(fold_kernel, width, tile, True),
        [sector_dims], [environ, site, far_environ, far_site, site_weights], packed_parts(BF16),
        fold_scratch, 20, 12,
    )
    early_arrived = lax.ppermute(outgoing[0], "sec", up_two)
    far_environ, outgoing = lax.optimization_barrier((far_environ, outgoing))
    kept = call(
        "fold_own", functools.partial(fold_kernel, width, tile, False),
        [sector_dims], [environ, site, far_environ, far_site, site_weights], packed_parts(F32),
        fold_scratch, 20, 0.1,
    )
    kept, middle_outgoing = lax.optimization_barrier((kept, outgoing[1]))
    middle_arrived = lax.ppermute(middle_outgoing, "sec", up_two)
    kept, right = lax.optimization_barrier((kept, right))
    own_mixed = call(
        "mix_own", functools.partial(mix_own_kernel, width, tile), [], [right, bound_weights],
        mixed(1), mix_scratch(1), 12, 1,
    )
    own_mixed, right_far, late_outgoing = lax.optimization_barrier((own_mixed, right_far, outgoing[2]))
    late_arrived = lax.ppermute(late_outgoing, "sec", up_two)
    passed_on = jnp.where(sector + 2 < sectors, right_far, jnp.zeros_like(right_far))
    passed_on = jnp.where(lax.rem(sector, 2) == 0, passed_on, right_packed)
    right_near = lax.ppermute(passed_on, "sec", swap)

    def carried(stays, comes):
        return (stays + jnp.where(sector >= 2, comes.astype(F32), 0.0)).astype(BF16)

    early = carried(kept[0], early_arrived)
    early_bound = lax.ppermute(early, "seg", onward)
    early, right_far = lax.optimization_barrier((early, right_far))
    after_mixed = call(
        "mix_after", functools.partial(mix_after_kernel, width, tile), [],
        [right_far, bound_weights], mixed(1), mix_scratch(1) + [diag], 12, 2,
    )
    def head(members, rights):
        return call(
            "head", functools.partial(head_kernel, members, width, tile),
            [sector_dims], [guess[0, :, 0]] + rights,
            (
                jax.ShapeDtypeStruct((2, tile, tile), F32),
                jax.ShapeDtypeStruct((16, 128), F32),
                jax.ShapeDtypeStruct((width * tile, 2 * tile), BF16),
            ),
            [], 9, 0.5,
        )

    start_a, norms_a, products_a = head(GROUPS[0], [own_mixed, after_mixed])
    middle_arrived, products_a = lax.optimization_barrier((middle_arrived, products_a))
    middle = carried(kept[1], middle_arrived)
    middle_bound = lax.ppermute(middle, "seg", onward)
    middle, late_arrived = lax.optimization_barrier((middle, late_arrived))
    late = carried(kept[2], late_arrived)
    late_bound = lax.ppermute(late, "seg", onward)
    late, right_near = lax.optimization_barrier((late, right_near))
    next_mixed = call(
        "mix_next", functools.partial(mix_next_kernel, width, tile), [],
        [right_near, bound_weights], mixed(2), mix_scratch(2) + [diag], 16, 3,
    )
    start_b, norms_b, products_b = head(GROUPS[1], [next_mixed])
    middle_bound, products_b = lax.optimization_barrier((middle_bound, products_b))
    bound, image = call(
        "open", functools.partial(open_kernel, width, tile), [],
        [environ, early_bound, middle_bound, products_a, products_b],
        (
            jax.ShapeDtypeStruct((tile, parts[-1][0] * tile), BF16),
            jax.ShapeDtypeStruct((len(GROUPS), tile, 2 * tile), F32),
        ),
        [diag], 12, 1,
    )
    late_bound, bound = lax.optimization_barrier((late_bound, bound))
    basis, stats, new_env = call(
        "lanczos", functools.partial(lanczos_kernel, width, tile),
        [sector_dims],
        [late_bound, environ, bound, image, own_mixed, next_mixed, after_mixed, start_a, start_b,
         norms_a, norms_b, products_a, products_b, early, middle, late],
        (
            jax.ShapeDtypeStruct((LANCZOS, states, tile, tile), F32),
            jax.ShapeDtypeStruct((16, 128), F32),
            jax.ShapeDtypeStruct((width * tile, tile), BF16),
        ),
        [
            pltpu.VMEM((tile, parts[-1][1] * tile), BF16),
            pltpu.VMEM((len(GROUPS), width * tile, 2 * tile), BF16),
            pltpu.VMEM((width * tile, tile), BF16),
            diag,
            diag,
            pltpu.SemaphoreType.DMA,
        ],
        24, 12, [vmem(), vmem(), pl.BlockSpec(memory_space=pltpu.HBM)],
    )
    stats = gathered(stats, "sec")
    entries = float(states * sector_count * tile * tile)
    vector, table = call(
        "finish", functools.partial(finish_kernel, entries), [], [stats, start_a, start_b, basis],
        (
            jax.ShapeDtypeStruct((states, tile, tile), F32),
            jax.ShapeDtypeStruct((2, LANCZOS), F32),
        ),
        [], 6, 2,
    )
    return new_env.reshape(left_env.shape), vector[None, :, None], jnp.transpose(table)[None]


def solution(mesh):
    placed = (
        P("seg", "sec", None, None, None),
        P("seg", "sec", None, None, None),
        P("seg", None, None, "sec", None, None),
        P("seg", None, None, None, None),
        P("seg", None, None, None),
        P("seg", None, "sec", None, None),
        P(),
    )
    return jax.shard_map(
        on_device,
        mesh=mesh,
        in_specs=placed,
        out_specs=(
            P("seg", "sec", None, None, None),
            P("seg", None, "sec", None, None),
            P("seg", None, None),
        ),
        check_vma=False,
    )
```

```python
import functools

import jax
import jax.numpy as jnp
from jax import lax
from jax.experimental import pallas as pl
from jax.experimental.pallas import tpu as pltpu
from jax.sharding import PartitionSpec as P

LANCZOS = 4
CHARGES = (0, 1, 1, 2)
GROUPS = ((0, 3), (1, 2))
F32 = jnp.float32
BF16 = jnp.bfloat16
MIB = 1024 * 1024


def padded(count):
    return -(-count // 8) * 8


def packed_height(count):
    return -(-count // 16) * 16


def packed_rows(count, tile):
    return count * tile // 2 + packed_height(count)


def chunks_of(width):
    side = width // 6 * 2
    return (0, side), (side, side), (2 * side, width - 2 * side)


def iotas(shape):
    return lax.broadcasted_iota(jnp.int32, shape, 0), lax.broadcasted_iota(jnp.int32, shape, 1)


def pack_block(block):
    tile = block.shape[0]
    half = tile // 2
    top, low = block[:half], block[half:]
    row, lane = iotas((half, tile))
    turned = pltpu.roll(low, half, 1)
    folded = jnp.where((lane < half) & (row > lane), turned, top)
    diagonal = jnp.sum(jnp.where(lane == row + half, low, 0.0), axis=0, keepdims=True)
    return folded, diagonal


def unpack_block(folded, diagonal):
    half, tile = folded.shape
    row, lane = iotas((half, tile))
    rolled = pltpu.roll(folded, half, 1)
    turned = jnp.transpose(jnp.concatenate([folded, rolled], axis=0).astype(BF16)).astype(F32)
    top = jnp.where((lane < half) & (row > lane), turned[:half], folded)
    low = jnp.where((lane >= half) & (row > lane - half), rolled, turned[half:])
    low = jnp.where(lane == row + half, diagonal, low)
    return jnp.concatenate([top, low], axis=0)


def partner_of(sector):
    return sector + 1 - 2 * lax.rem(sector, 2)


def live_limits(dims_ref, sector):
    count = dims_ref.shape[0]
    rows = dims_ref[sector]
    columns = []
    for charge in CHARGES:
        target = sector + charge
        columns.append(jnp.where(target < count, dims_ref[jnp.minimum(target, count - 1)], 0))
    return rows, columns


def weight_rows(weight_ref, width, p, square, turned):
    wide = padded(width)
    square[...] = jnp.zeros_like(square)
    square[:width, :width] = weight_ref[pl.ds(p, width, stride=len(CHARGES)), :]
    value = square[...]
    if turned:
        value = jnp.transpose(value)
    high = value.astype(BF16).astype(F32)
    joined = (high + pltpu.roll(value - high, wide, 1)).astype(BF16)
    return joined[: packed_height(width), : 2 * wide]


def doubled(value):
    return jnp.concatenate([value, value], axis=0).astype(BF16)


def pack_kernel(width, tile, source_ref, out_ref, diag):
    half = tile // 2
    diag[...] = jnp.zeros_like(diag)
    for w in range(width):
        folded, diagonal = pack_block(source_ref[w * tile : (w + 1) * tile, :].astype(F32))
        out_ref[w * half : (w + 1) * half, :] = folded.astype(BF16)
        diag[w : w + 1, :] = diagonal
    out_ref[width * half :, :] = diag[...].astype(BF16)


def unpack_into(count, tile, read, write, diag):
    half = tile // 2
    size = packed_height(count)
    diag[:size, :] = read(count * half, size)
    for w in range(count):
        write(w, unpack_block(read(w * half, half), diag[w : w + 1, :]))


def reader(ref):
    return lambda at, size: ref[at : at + size, :].astype(F32)


def unpack_kernel(width, tile, *refs):
    *part_refs, out_ref, diag = refs
    for (first, count), ref in zip(chunks_of(width), part_refs):

        def write(w, block, first=first):
            out_ref[(first + w) * tile : (first + w + 1) * tile, :] = block.astype(BF16)

        unpack_into(count, tile, reader(ref), write, diag)


def fold_kernel(
    width, tile, travels, dims_ref, environ_ref, site_ref, far_environ_ref, far_site_ref, weight_ref, *refs
):
    part_refs = refs[: len(chunks_of(width))]
    joined_s, turned_s, square_s, weight_s, half_s, packed_s, diag_s, sums_s, diag_sums_s = refs[
        len(part_refs) :
    ]
    half = tile // 2
    pitch = half + 8
    wide = padded(width)
    sector = lax.axis_index("sec")
    partner = partner_of(sector)
    row, lane = iotas((tile, tile))

    def run(own_state, with_partner):
        rows, columns = live_limits(dims_ref, sector)
        live = (row < rows) & (lane < columns[own_state])
        sites = [jnp.where(live, site_ref[own_state].astype(F32), 0.0)]
        states = [own_state]
        if with_partner:
            rows, columns = live_limits(dims_ref, partner)
            for k in range(2):
                live = (row < rows) & (lane < columns[k + 1])
                sites.append(jnp.where(live, far_site_ref[k + 1].astype(F32), 0.0))
                states.append(k + 1)
        parts = len(states)
        for n in range(parts):
            joined_s[:, n * tile : (n + 1) * tile] = sites[n].astype(BF16)
            turned_s[n] = jnp.transpose(sites[n]).astype(BF16)
            weight_s[n] = weight_rows(weight_ref, width, states[n], square_s, True)
            packed_s[n, width * pitch :, :] = jnp.zeros(((wide - width) * pitch, tile), F32)
            diag_s[n] = jnp.zeros_like(diag_s[n])

        for pair in range(width // 2):
            at = slice(pair * tile, (pair + 1) * tile)
            for k in range(2):
                here = slice((pair * 2 + k) * tile, (pair * 2 + k + 1) * tile)
                blocks = [
                    jnp.dot(environ_ref[here, :], joined_s[:, :tile], preferred_element_type=F32)
                ]
                if with_partner:
                    both = jnp.dot(
                        far_environ_ref[here, :], joined_s[:, tile:], preferred_element_type=F32
                    )
                    blocks += [both[:, :tile], both[:, tile:]]
                for n in range(parts):
                    half_s[n, at, k * tile : (k + 1) * tile] = blocks[n].astype(BF16)
            for n in range(parts):
                both = jnp.dot(turned_s[n], half_s[n, at, :], preferred_element_type=F32)
                for k in range(2):
                    w = pair * 2 + k
                    folded, diagonal = pack_block(both[:, k * tile : (k + 1) * tile])
                    packed_s[n, w * pitch : w * pitch + half, :] = folded
                    diag_s[n, w : w + 1, :] = diagonal

        def mixed(inputs):
            value = None
            for n in range(parts):
                term = jnp.dot(weight_s[n], doubled(inputs[n]), preferred_element_type=F32)
                value = term if value is None else value + term
            return value[:wide]

        for at in range(0, half, 2):
            value = mixed([
                jnp.concatenate(
                    [packed_s[n, pl.ds(at + k, wide, stride=pitch), :] for k in range(2)], axis=1
                )
                for n in range(parts)
            ])
            for k in range(2):
                sums_s[pl.ds(at + k, wide, stride=pitch), :] = value[:, k * tile : (k + 1) * tile]
        diag_sums_s[...] = jnp.zeros_like(diag_sums_s)
        diag_sums_s[:wide, :] = mixed([diag_s[n, :wide] for n in range(parts)])
        for (first, count), ref in zip(chunks_of(width), part_refs):
            for w in range(count):
                at = (first + w) * pitch
                ref[w * half : (w + 1) * half, :] = sums_s[at : at + half, :].astype(ref.dtype)
            rows = packed_height(count)
            ref[count * half :, :] = diag_sums_s[first : first + rows, :].astype(ref.dtype)

    even = lax.rem(sector, 2) == 0
    own_state = len(CHARGES) - 1 if travels else 0

    @pl.when(even)
    def _():
        run(own_state, travels)

    @pl.when(jnp.logical_not(even))
    def _():
        run(own_state, not travels)


def mix_into(width, tile, weights, wide_s, sums_s, out_ref):
    wide = padded(width)
    pitch = tile + 8
    wide_s[width * pitch :, :] = jnp.zeros_like(wide_s[width * pitch :, :])

    for at in range(0, tile, 2):
        value = doubled(
            jnp.concatenate(
                [wide_s[pl.ds(at + k, wide, stride=pitch), :] for k in range(2)], axis=1
            )
        )
        for index, weight in enumerate(weights):
            mixed = jnp.dot(weight[...], value, preferred_element_type=F32)[:wide]
            for k in range(2):
                sums_s[index, pl.ds(at + k, wide, stride=pitch), :] = mixed[:, k * tile : (k + 1) * tile]
    for index in range(len(weights)):
        for w in range(width):
            out_ref[index, :, w * tile : (w + 1) * tile] = sums_s[
                index, w * pitch : w * pitch + tile, :
            ].astype(BF16)


def unpack_wide(width, tile, read, wide_s, diag):
    def write(w, block):
        wide_s[w * (tile + 8) : w * (tile + 8) + tile, :] = block

    unpack_into(width, tile, read, write, diag)


def copy_wide(width, tile, source_ref, wide_s):
    for w in range(width):
        at = w * (tile + 8)
        wide_s[at : at + tile, :] = source_ref[w * tile : (w + 1) * tile, :].astype(F32)


def mix_own_kernel(width, tile, source_ref, weight_ref, out_ref, square_s, weight_s, wide_s, sums_s):
    weight_s[0] = weight_rows(weight_ref, width, 0, square_s, False)
    copy_wide(width, tile, source_ref, wide_s)
    mix_into(width, tile, [weight_s.at[0]], wide_s, sums_s, out_ref)


def mix_next_kernel(
    width, tile, near_ref, weight_ref, out_ref, square_s, weight_s, wide_s, sums_s, diag
):
    for k in range(2):
        weight_s[k] = weight_rows(weight_ref, width, k + 1, square_s, False)
    unpack_wide(width, tile, reader(near_ref), wide_s, diag)
    mix_into(width, tile, [weight_s.at[k] for k in range(2)], wide_s, sums_s, out_ref)


def mix_after_kernel(
    width, tile, far_ref, weight_ref, out_ref, square_s, weight_s, wide_s, sums_s, diag
):
    weight_s[0] = weight_rows(weight_ref, width, 3, square_s, False)
    inside = lax.axis_index("sec") + 2 < lax.axis_size("sec")

    def read(at, size):
        return jnp.where(inside, far_ref[at : at + size, :].astype(F32), 0.0)

    unpack_wide(width, tile, read, wide_s, diag)
    mix_into(width, tile, [weight_s.at[0]], wide_s, sums_s, out_ref)


def total(value):
    return jnp.sum(jnp.sum(value, axis=0, keepdims=True), axis=1, keepdims=True)


def put(stats, kind, lane_at, value):
    row, lane = iotas(stats.shape)
    return jnp.where((row == kind) & (lane == lane_at), value, stats)


def scaled(value):
    square = total(value * value)
    inverse = jnp.where(square > 0.0, lax.rsqrt(square), 0.0)
    return value * inverse, square * inverse


def right_products(width, tile, field, right_ref, out_ref, k):
    lanes = slice(k * tile, (k + 1) * tile)
    for pair in range(width // 2):
        at = pair * 2 * tile
        both = jnp.dot(field, right_ref[:, at : at + 2 * tile], preferred_element_type=F32).astype(BF16)
        for n in range(2):
            out_ref[at + n * tile : at + (n + 1) * tile, lanes] = both[:, n * tile : (n + 1) * tile]


def head_kernel(
    width, tile, dims_ref, guess_ref, own_ref, next_ref, after_ref,
    start_a, start_b, stats_ref, product_a, product_b,
):
    rights = [own_ref.at[0], next_ref.at[0], next_ref.at[1], after_ref.at[0]]
    sector = lax.axis_index("sec")
    rows, columns = live_limits(dims_ref, sector)
    row, lane = iotas((tile, tile))
    stats = jnp.zeros(stats_ref.shape, F32)
    for members, start_ref, product_ref in zip(GROUPS, (start_a, start_b), (product_a, product_b)):
        for k, p in enumerate(members):
            live = (row < rows) & (lane < columns[p])
            vector, norm = scaled(jnp.where(live, guess_ref[p], 0.0))
            start_ref[k] = vector
            stats = put(stats, 0, sector * len(CHARGES) + p, norm)
            right_products(width, tile, vector.astype(BF16), rights[p], product_ref, k)
    stats_ref[...] = stats


def bound_blocks(chunks, tile, packed_refs, environ_ref, out_ref, diag):
    segment = lax.axis_index("seg")
    start = chunks[0][0]

    @pl.when(segment == 0)
    def _():
        for w in range(sum(count for _, count in chunks)):
            out_ref[:, w * tile : (w + 1) * tile] = environ_ref[
                (start + w) * tile : (start + w + 1) * tile, :
            ]

    @pl.when(segment != 0)
    def _():
        for (first, count), ref in zip(chunks, packed_refs):

            def write(w, block, base=first - start):
                out_ref[:, (base + w) * tile : (base + w + 1) * tile] = block.astype(BF16)

            unpack_into(count, tile, reader(ref), write, diag)


def open_kernel(width, tile, environ_ref, *refs):
    chunks = chunks_of(width)[:-1]
    packed_refs, (*product_refs, bound_ref, image_ref, diag) = refs[: len(chunks)], refs[len(chunks) :]
    bound_blocks(chunks, tile, packed_refs, environ_ref, bound_ref, diag)
    rows = bound_ref.shape[1]
    for group, product_ref in enumerate(product_refs):
        image_ref[group] = jnp.dot(bound_ref[...], product_ref[:rows, :], preferred_element_type=F32)


def lanczos_kernel(
    width, tile, dims_ref, packed_ref, environ_ref, early_ref, image_ref, own_ref, next_ref, after_ref,
    start_a, start_b, norm_ref, product_a, product_b, basis_ref, stats_ref,
    late_s, product_s, diag,
):
    states = len(CHARGES)
    sector = lax.axis_index("sec")
    last = chunks_of(width)[-1:]
    bound_blocks(last, tile, [packed_ref], environ_ref, late_s, diag)
    rows, columns = live_limits(dims_ref, sector)
    row, lane = iotas((tile, tile))
    rights = [own_ref.at[0], next_ref.at[0], next_ref.at[1], after_ref.at[0]]
    stats = norm_ref[...]
    starts = (start_a, start_b)
    split = last[0][0] * tile
    betas = [None] * states
    for j in range(LANCZOS):
        for group, members in enumerate(GROUPS):
            if j == 0:
                source = (product_a, product_b)[group]
                images = image_ref[group]
            else:
                source = product_s.at[group]
                for k, p in enumerate(members):
                    field = basis_ref[j - 1, p].astype(BF16)
                    right_products(width, tile, field, rights[p], source, k)
                images = jnp.dot(early_ref[...], source[:split, :], preferred_element_type=F32)
            images = images + jnp.dot(late_s[...], source[split:, :], preferred_element_type=F32)
            for k, p in enumerate(members):
                live = (row < rows) & (lane < columns[p])
                image = jnp.where(live, images[:, k * tile : (k + 1) * tile], 0.0)
                vector = starts[group][k] if j == 0 else basis_ref[j - 1, p]
                alpha = total(vector * image)
                image = image - alpha * vector
                if j > 0:
                    before = starts[group][k] if j == 1 else basis_ref[j - 2, p]
                    image = image - betas[p] * before
                following, beta = scaled(image)
                basis_ref[j, p] = following
                betas[p] = beta
                stats = put(stats, 1 + 2 * j, sector * states + p, alpha)
                stats = put(stats, 2 + 2 * j, sector * states + p, beta)
    stats_ref[...] = stats


def finish_kernel(
    entries, stats_ref, start_a, start_b, basis_ref, vector_ref, table_ref
):
    states = len(CHARGES)
    sector = lax.axis_index("sec")
    stats = stats_ref[0]
    for q in range(1, stats_ref.shape[0]):
        stats = stats + stats_ref[q]
    alphas = [stats[1 + 2 * j : 2 + 2 * j, :] for j in range(LANCZOS)]
    betas = [stats[2 + 2 * j : 3 + 2 * j, :] for j in range(LANCZOS)]

    def mean(left, right):
        products = left[0] * right[0]
        for x, y in zip(left[1:], right[1:]):
            products = products + x * y
        return jnp.sum(products, axis=1, keepdims=True) / entries

    def applied(vector):
        count = len(vector)
        image = []
        for k in range(count + 1):
            terms = []
            if k > 0:
                terms.append(betas[k - 1] * vector[k - 1])
            if k < count:
                terms.append(alphas[k] * vector[k])
            if k + 1 < count:
                terms.append(betas[k] * vector[k + 1])
            image.append(sum(terms[1:], terms[0]))
        return image

    residual = [stats[0:1, :]]
    previous = []
    table_row, table_column = iotas(table_ref.shape)
    table = jnp.zeros(table_ref.shape, F32)
    for j in range(LANCZOS):
        image = applied(residual)
        square = mean(residual, residual) + 1e-06
        alpha = mean(residual, image[: j + 1]) / square
        norm = jnp.sqrt(square)
        vector = [value / norm for value in residual]
        residual = [value / norm for value in image]
        for k in range(j + 1):
            residual[k] = residual[k] - alpha * vector[k]
        for k in range(j):
            residual[k] = residual[k] - norm * previous[k]
        previous = vector
        if j > 0:
            table = jnp.where((table_row == 1) & (table_column == j - 1), norm, table)
        table = jnp.where((table_row == 0) & (table_column == j), alpha, table)
    norm = jnp.sqrt(mean(residual, residual) + 1e-06)
    vector = [value / norm for value in residual]
    table = jnp.where((table_row == 1) & (table_column == LANCZOS - 1), norm, table)
    table_ref[...] = table
    lane = lax.broadcasted_iota(jnp.int32, (1, stats.shape[1]), 1)
    starts = {p: ref[k] for members, ref in zip(GROUPS, (start_a, start_b)) for k, p in enumerate(members)}
    for p in range(states):
        value = None
        here = lane == sector * states + p
        for k in range(LANCZOS + 1):
            weight = jnp.sum(jnp.where(here, vector[k], 0.0), axis=1, keepdims=True)
            term = weight * (starts[p] if k == 0 else basis_ref[k - 1, p])
            value = term if value is None else value + term
        vector_ref[p] = value


def smem():
    return pl.BlockSpec(memory_space=pltpu.SMEM)


def vmem():
    return pl.BlockSpec(memory_space=pltpu.VMEM)


def call(name, kernel, scalars, arrays, outs, scratch, limit, micros):
    many = isinstance(outs, (tuple, list))
    return pl.pallas_call(
        kernel,
        out_shape=outs,
        in_specs=[smem()] * len(scalars) + [vmem()] * len(arrays),
        out_specs=[vmem()] * len(outs) if many else vmem(),
        scratch_shapes=scratch,
        compiler_params=pltpu.CompilerParams(vmem_limit_bytes=limit * MIB),
        name=name,
        cost_estimate=pl.CostEstimate(
            flops=int(micros * 1.1e9), bytes_accessed=0, transcendentals=0
        ),
    )(*scalars, *arrays)


def shift_by(count, steps):
    return [(source, (source + steps) % count) for source in range(count)]


def gathered(value, axis):
    count = lax.axis_size(axis)
    return lax.all_to_all(jnp.broadcast_to(value, (count,) + value.shape), axis, 0, 0)


def on_device(left_env, right_env, site_tensors, mpo, boundary_mpo, guess, sector_dims):
    width, tile = left_env.shape[2], left_env.shape[-1]
    half = tile // 2
    wide = padded(width)
    states = len(CHARGES)
    sector_count = sector_dims.shape[0]
    sectors = lax.axis_size("sec")
    segments = lax.axis_size("seg")
    prows = packed_rows(width, tile)
    drows = prows - width * half
    packed = jax.ShapeDtypeStruct((prows, tile), BF16)
    parts = chunks_of(width)

    def packed_parts(dtype):
        return [jax.ShapeDtypeStruct((packed_rows(count, tile), tile), dtype) for _, count in parts]

    def mixed(count):
        return jax.ShapeDtypeStruct((count, tile, width * tile), BF16)

    environ = left_env.reshape(width * tile, tile)
    right = right_env.reshape(width * tile, tile)
    site = site_tensors[0, 0, :, 0]
    site_weights = jnp.transpose(mpo[0, 0], (0, 2, 1)).reshape(width * states, width)
    bound_weights = jnp.transpose(boundary_mpo[0], (0, 2, 1)).reshape(width * states, width)

    sector = lax.axis_index("sec")
    swap = [(q, q ^ 1) for q in range(sectors)]
    up_two = shift_by(sectors, 2)
    down_two = shift_by(sectors, -2)
    onward = shift_by(segments, 1)
    diag = pltpu.VMEM((drows, tile), F32)

    def mix_scratch(count):
        return [
            pltpu.VMEM((tile, tile), F32),
            pltpu.VMEM((count, packed_height(width), 2 * wide), BF16),
            pltpu.VMEM((wide * (tile + 8), tile), F32),
            pltpu.VMEM((count, wide * (tile + 8), tile), F32),
        ]

    right_packed = call(
        "pack_right", functools.partial(pack_kernel, width, tile), [], [right], packed,
        [diag], 6, 1,
    )
    right_far = lax.ppermute(right_packed, "sec", down_two)
    far_environ = lax.ppermute(environ, "sec", swap)
    far_site = lax.ppermute(site, "sec", swap)
    fold_scratch = [
        pltpu.VMEM((tile, 3 * tile), BF16),
        pltpu.VMEM((3, tile, tile), BF16),
        pltpu.VMEM((tile, tile), F32),
        pltpu.VMEM((3, packed_height(width), 2 * wide), BF16),
        pltpu.VMEM((3, width // 2 * tile, 2 * tile), BF16),
        pltpu.VMEM((3, wide * (half + 8), tile), F32),
        pltpu.VMEM((3, drows, tile), F32),
        pltpu.VMEM((wide * (half + 8), tile), F32),
        pltpu.VMEM((drows, tile), F32),
    ]
    outgoing = call(
        "fold_up", functools.partial(fold_kernel, width, tile, True),
        [sector_dims], [environ, site, far_environ, far_site, site_weights], packed_parts(BF16),
        fold_scratch, 20, 12,
    )
    early_arrived = lax.ppermute(outgoing[0], "sec", up_two)
    far_environ, outgoing = lax.optimization_barrier((far_environ, outgoing))
    kept = call(
        "fold_own", functools.partial(fold_kernel, width, tile, False),
        [sector_dims], [environ, site, far_environ, far_site, site_weights], packed_parts(F32),
        fold_scratch, 20, 0.1,
    )
    kept, middle_outgoing = lax.optimization_barrier((kept, outgoing[1]))
    middle_arrived = lax.ppermute(middle_outgoing, "sec", up_two)
    kept, right = lax.optimization_barrier((kept, right))
    own_mixed = call(
        "mix_own", functools.partial(mix_own_kernel, width, tile), [], [right, bound_weights],
        mixed(1), mix_scratch(1), 12, 1,
    )
    own_mixed, right_far, late_outgoing = lax.optimization_barrier((own_mixed, right_far, outgoing[2]))
    late_arrived = lax.ppermute(late_outgoing, "sec", up_two)
    passed_on = jnp.where(sector + 2 < sectors, right_far, jnp.zeros_like(right_far))
    passed_on = jnp.where(lax.rem(sector, 2) == 0, passed_on, right_packed)
    right_near = lax.ppermute(passed_on, "sec", swap)

    def carried(stays, comes):
        return (stays + jnp.where(sector >= 2, comes.astype(F32), 0.0)).astype(BF16)

    early = carried(kept[0], early_arrived)
    early_bound = lax.ppermute(early, "seg", onward)
    early, right_far = lax.optimization_barrier((early, right_far))
    after_mixed = call(
        "mix_after", functools.partial(mix_after_kernel, width, tile), [],
        [right_far, bound_weights], mixed(1), mix_scratch(1) + [diag], 12, 2,
    )
    middle_arrived, after_mixed = lax.optimization_barrier((middle_arrived, after_mixed))
    middle = carried(kept[1], middle_arrived)
    middle_bound = lax.ppermute(middle, "seg", onward)
    middle, right_near = lax.optimization_barrier((middle, right_near))
    next_mixed = call(
        "mix_next", functools.partial(mix_next_kernel, width, tile), [],
        [right_near, bound_weights], mixed(2), mix_scratch(2) + [diag], 16, 3,
    )
    late_arrived, next_mixed = lax.optimization_barrier((late_arrived, next_mixed))
    late = carried(kept[2], late_arrived)
    late_bound = lax.ppermute(late, "seg", onward)
    late, next_mixed, after_mixed = lax.optimization_barrier((late, next_mixed, after_mixed))
    start_a, start_b, norms, products_a, products_b = call(
        "head", functools.partial(head_kernel, width, tile),
        [sector_dims], [guess[0, :, 0], own_mixed, next_mixed, after_mixed],
        [jax.ShapeDtypeStruct((2, tile, tile), F32)] * 2
        + [jax.ShapeDtypeStruct((16, 128), F32)]
        + [jax.ShapeDtypeStruct((width * tile, 2 * tile), BF16)] * 2,
        [], 14, 0.2,
    )
    new_env = call(
        "unpack_env", functools.partial(unpack_kernel, width, tile), [], [early, middle, late],
        jax.ShapeDtypeStruct((width * tile, tile), BF16), [diag], 6, 2,
    )
    middle_bound, new_env = lax.optimization_barrier((middle_bound, new_env))
    bound, image = call(
        "open", functools.partial(open_kernel, width, tile), [],
        [environ, early_bound, middle_bound, products_a, products_b],
        (
            jax.ShapeDtypeStruct((tile, parts[-1][0] * tile), BF16),
            jax.ShapeDtypeStruct((len(GROUPS), tile, 2 * tile), F32),
        ),
        [diag], 12, 1,
    )
    late_bound, bound = lax.optimization_barrier((late_bound, bound))
    basis, stats = call(
        "lanczos", functools.partial(lanczos_kernel, width, tile),
        [sector_dims],
        [late_bound, environ, bound, image, own_mixed, next_mixed, after_mixed, start_a, start_b,
         norms, products_a, products_b],
        (
            jax.ShapeDtypeStruct((LANCZOS, states, tile, tile), F32),
            jax.ShapeDtypeStruct((16, 128), F32),
        ),
        [
            pltpu.VMEM((tile, parts[-1][1] * tile), BF16),
            pltpu.VMEM((len(GROUPS), width * tile, 2 * tile), BF16),
            diag,
        ],
        22, 12,
    )
    stats = gathered(stats, "sec")
    entries = float(states * sector_count * tile * tile)
    vector, table = call(
        "finish", functools.partial(finish_kernel, entries), [], [stats, start_a, start_b, basis],
        (
            jax.ShapeDtypeStruct((states, tile, tile), F32),
            jax.ShapeDtypeStruct((2, LANCZOS), F32),
        ),
        [], 6, 2,
    )
    return new_env.reshape(left_env.shape), vector[None, :, None], jnp.transpose(table)[None]


def solution(mesh):
    placed = (
        P("seg", "sec", None, None, None),
        P("seg", "sec", None, None, None),
        P("seg", None, None, "sec", None, None),
        P("seg", None, None, None, None),
        P("seg", None, None, None),
        P("seg", None, "sec", None, None),
        P(),
    )
    return jax.shard_map(
        on_device,
        mesh=mesh,
        in_specs=placed,
        out_specs=(
            P("seg", "sec", None, None, None),
            P("seg", None, "sec", None, None),
            P("seg", None, None),
        ),
        check_vma=False,
    )
```

```python
import functools

import jax
import jax.numpy as jnp
from jax import lax
from jax.experimental import pallas as pl
from jax.experimental.pallas import tpu as pltpu
from jax.sharding import PartitionSpec as P

LANCZOS = 4
CHARGES = (0, 1, 1, 2)
GROUPS = ((0, 3), (1, 2))
F32 = jnp.float32
BF16 = jnp.bfloat16
MIB = 1024 * 1024


def padded(count):
    return -(-count // 8) * 8


def packed_height(count):
    return -(-count // 16) * 16


def packed_rows(count, tile):
    return count * tile // 2 + packed_height(count)


def chunks_of(width):
    one = width // 6 * 2
    two = (width - one) // 4 * 2
    return (0, one), (one, two), (one + two, width - one - two)


def iotas(shape):
    return lax.broadcasted_iota(jnp.int32, shape, 0), lax.broadcasted_iota(jnp.int32, shape, 1)


def pack_block(block):
    tile = block.shape[0]
    half = tile // 2
    top, low = block[:half], block[half:]
    row, lane = iotas((half, tile))
    turned = pltpu.roll(low, half, 1)
    folded = jnp.where((lane < half) & (row > lane), turned, top)
    diagonal = jnp.sum(jnp.where(lane == row + half, low, 0.0), axis=0, keepdims=True)
    return folded, diagonal


def unpack_block(folded, diagonal, kind=BF16):
    half, tile = folded.shape
    row, lane = iotas((half, tile))
    rolled = pltpu.roll(folded, half, 1)
    turned = jnp.transpose(jnp.concatenate([folded, rolled], axis=0).astype(kind)).astype(F32)
    top = jnp.where((lane < half) & (row > lane), turned[:half], folded)
    low = jnp.where((lane >= half) & (row > lane - half), rolled, turned[half:])
    low = jnp.where(lane == row + half, diagonal, low)
    return jnp.concatenate([top, low], axis=0)


def partner_of(sector):
    return sector + 1 - 2 * lax.rem(sector, 2)


def live_limits(dims_ref, sector):
    count = dims_ref.shape[0]
    rows = dims_ref[sector]
    columns = []
    for charge in CHARGES:
        target = sector + charge
        columns.append(jnp.where(target < count, dims_ref[jnp.minimum(target, count - 1)], 0))
    return rows, columns


def weight_rows(weight_ref, width, p, square, turned):
    wide = padded(width)
    square[...] = jnp.zeros_like(square)
    square[:width, :width] = weight_ref[pl.ds(p, width, stride=len(CHARGES)), :]
    value = square[...]
    if turned:
        value = jnp.transpose(value)
    high = value.astype(BF16).astype(F32)
    joined = (high + pltpu.roll(value - high, wide, 1)).astype(BF16)
    return joined[: packed_height(width), : 2 * wide]


def doubled(value):
    return jnp.concatenate([value, value], axis=0).astype(BF16)


def pack_kernel(width, tile, source_ref, out_ref, diag):
    half = tile // 2
    diag[...] = jnp.zeros_like(diag)
    for w in range(width):
        folded, diagonal = pack_block(source_ref[w * tile : (w + 1) * tile, :].astype(F32))
        out_ref[w * half : (w + 1) * half, :] = folded.astype(BF16)
        diag[w : w + 1, :] = diagonal
    out_ref[width * half :, :] = diag[...].astype(BF16)


def unpack_into(count, tile, read, write, diag, kind=BF16):
    half = tile // 2
    size = packed_height(count)
    diag[:size, :] = read(count * half, size)
    for w in range(count):
        write(w, unpack_block(read(w * half, half), diag[w : w + 1, :], kind))


def reader(ref):
    return lambda at, size: ref[at : at + size, :].astype(F32)


def unpack_kernel(width, tile, *refs):
    *part_refs, out_ref, diag = refs
    for (first, count), ref in zip(chunks_of(width), part_refs):

        def write(w, block, first=first):
            out_ref[(first + w) * tile : (first + w + 1) * tile, :] = block.astype(BF16)

        unpack_into(count, tile, reader(ref), write, diag, F32)


def fold_kernel(
    width, tile, travels, dims_ref, environ_ref, site_ref, far_environ_ref, far_site_ref, weight_ref, *refs
):
    part_refs = refs[: len(chunks_of(width))]
    joined_s, turned_s, square_s, weight_s, half_s, packed_s, diag_s, sums_s, diag_sums_s = refs[
        len(part_refs) :
    ]
    half = tile // 2
    pitch = half + 8
    wide = padded(width)
    sector = lax.axis_index("sec")
    partner = partner_of(sector)
    row, lane = iotas((tile, tile))

    def run(own_state, with_partner):
        rows, columns = live_limits(dims_ref, sector)
        live = (row < rows) & (lane < columns[own_state])
        sites = [jnp.where(live, site_ref[own_state].astype(F32), 0.0)]
        states = [own_state]
        if with_partner:
            rows, columns = live_limits(dims_ref, partner)
            for k in range(2):
                live = (row < rows) & (lane < columns[k + 1])
                sites.append(jnp.where(live, far_site_ref[k + 1].astype(F32), 0.0))
                states.append(k + 1)
        parts = len(states)
        for n in range(parts):
            joined_s[:, n * tile : (n + 1) * tile] = sites[n].astype(BF16)
            turned_s[n] = jnp.transpose(sites[n]).astype(BF16)
            weight_s[n] = weight_rows(weight_ref, width, states[n], square_s, True)
            packed_s[n, width * pitch :, :] = jnp.zeros(((wide - width) * pitch, tile), F32)
            diag_s[n] = jnp.zeros_like(diag_s[n])

        for pair in range(width // 2):
            at = slice(pair * tile, (pair + 1) * tile)
            for k in range(2):
                here = slice((pair * 2 + k) * tile, (pair * 2 + k + 1) * tile)
                blocks = [
                    jnp.dot(environ_ref[here, :], joined_s[:, :tile], preferred_element_type=F32)
                ]
                if with_partner:
                    both = jnp.dot(
                        far_environ_ref[here, :], joined_s[:, tile:], preferred_element_type=F32
                    )
                    blocks += [both[:, :tile], both[:, tile:]]
                for n in range(parts):
                    half_s[n, at, k * tile : (k + 1) * tile] = blocks[n].astype(BF16)
            for n in range(parts):
                both = jnp.dot(turned_s[n], half_s[n, at, :], preferred_element_type=F32)
                for k in range(2):
                    w = pair * 2 + k
                    folded, diagonal = pack_block(both[:, k * tile : (k + 1) * tile])
                    packed_s[n, w * pitch : w * pitch + half, :] = folded
                    diag_s[n, w : w + 1, :] = diagonal

        def mixed(inputs):
            value = None
            for n in range(parts):
                term = jnp.dot(weight_s[n], doubled(inputs[n]), preferred_element_type=F32)
                value = term if value is None else value + term
            return value[:wide]

        for at in range(0, half, 2):
            value = mixed([
                jnp.concatenate(
                    [packed_s[n, pl.ds(at + k, wide, stride=pitch), :] for k in range(2)], axis=1
                )
                for n in range(parts)
            ])
            for k in range(2):
                sums_s[pl.ds(at + k, wide, stride=pitch), :] = value[:, k * tile : (k + 1) * tile]
        diag_sums_s[...] = jnp.zeros_like(diag_sums_s)
        diag_sums_s[:wide, :] = mixed([diag_s[n, :wide] for n in range(parts)])
        for (first, count), ref in zip(chunks_of(width), part_refs):
            for w in range(count):
                at = (first + w) * pitch
                ref[w * half : (w + 1) * half, :] = sums_s[at : at + half, :].astype(ref.dtype)
            rows = packed_height(count)
            ref[count * half :, :] = diag_sums_s[first : first + rows, :].astype(ref.dtype)

    even = lax.rem(sector, 2) == 0
    own_state = len(CHARGES) - 1 if travels else 0

    @pl.when(even)
    def _():
        run(own_state, travels)

    @pl.when(jnp.logical_not(even))
    def _():
        run(own_state, not travels)


def mix_into(width, tile, weights, wide_s, sums_s, out_ref):
    wide = padded(width)
    pitch = tile + 8
    wide_s[width * pitch :, :] = jnp.zeros_like(wide_s[width * pitch :, :])

    for at in range(0, tile, 2):
        value = doubled(
            jnp.concatenate(
                [wide_s[pl.ds(at + k, wide, stride=pitch), :] for k in range(2)], axis=1
            )
        )
        for index, weight in enumerate(weights):
            mixed = jnp.dot(weight[...], value, preferred_element_type=F32)[:wide]
            for k in range(2):
                sums_s[index, pl.ds(at + k, wide, stride=pitch), :] = mixed[:, k * tile : (k + 1) * tile]
    for index in range(len(weights)):
        for w in range(width):
            out_ref[index, :, w * tile : (w + 1) * tile] = sums_s[
                index, w * pitch : w * pitch + tile, :
            ].astype(BF16)


def unpack_wide(width, tile, read, wide_s, diag):
    def write(w, block):
        wide_s[w * (tile + 8) : w * (tile + 8) + tile, :] = block

    unpack_into(width, tile, read, write, diag)


def copy_wide(width, tile, source_ref, wide_s):
    for w in range(width):
        at = w * (tile + 8)
        wide_s[at : at + tile, :] = source_ref[w * tile : (w + 1) * tile, :].astype(F32)


def mix_own_kernel(width, tile, source_ref, weight_ref, out_ref, square_s, weight_s, wide_s, sums_s):
    weight_s[0] = weight_rows(weight_ref, width, 0, square_s, False)
    copy_wide(width, tile, source_ref, wide_s)
    mix_into(width, tile, [weight_s.at[0]], wide_s, sums_s, out_ref)


def mix_next_kernel(
    width, tile, near_ref, weight_ref, out_ref, square_s, weight_s, wide_s, sums_s, diag
):
    for k in range(2):
        weight_s[k] = weight_rows(weight_ref, width, k + 1, square_s, False)
    unpack_wide(width, tile, reader(near_ref), wide_s, diag)
    mix_into(width, tile, [weight_s.at[k] for k in range(2)], wide_s, sums_s, out_ref)


def mix_after_kernel(
    width, tile, far_ref, weight_ref, out_ref, square_s, weight_s, wide_s, sums_s, diag
):
    weight_s[0] = weight_rows(weight_ref, width, 3, square_s, False)
    inside = lax.axis_index("sec") + 2 < lax.axis_size("sec")

    def read(at, size):
        return jnp.where(inside, far_ref[at : at + size, :].astype(F32), 0.0)

    unpack_wide(width, tile, read, wide_s, diag)
    mix_into(width, tile, [weight_s.at[0]], wide_s, sums_s, out_ref)


def total(value):
    return jnp.sum(jnp.sum(value, axis=0, keepdims=True), axis=1, keepdims=True)


def put(stats, kind, lane_at, value):
    row, lane = iotas(stats.shape)
    return jnp.where((row == kind) & (lane == lane_at), value, stats)


def scaled(value):
    square = total(value * value)
    inverse = jnp.where(square > 0.0, lax.rsqrt(square), 0.0)
    return value * inverse, square * inverse


def right_products(width, tile, field, right_ref, out_ref, k):
    lanes = slice(k * tile, (k + 1) * tile)
    for pair in range(width // 2):
        at = pair * 2 * tile
        both = jnp.dot(field, right_ref[:, at : at + 2 * tile], preferred_element_type=F32).astype(BF16)
        for n in range(2):
            out_ref[at + n * tile : at + (n + 1) * tile, lanes] = both[:, n * tile : (n + 1) * tile]


def head_kernel(
    width, tile, dims_ref, guess_ref, own_ref, next_ref, after_ref,
    start_a, start_b, stats_ref, product_a, product_b,
):
    rights = [own_ref.at[0], next_ref.at[0], next_ref.at[1], after_ref.at[0]]
    sector = lax.axis_index("sec")
    rows, columns = live_limits(dims_ref, sector)
    row, lane = iotas((tile, tile))
    stats = jnp.zeros(stats_ref.shape, F32)
    for members, start_ref, product_ref in zip(GROUPS, (start_a, start_b), (product_a, product_b)):
        for k, p in enumerate(members):
            live = (row < rows) & (lane < columns[p])
            vector, norm = scaled(jnp.where(live, guess_ref[p], 0.0))
            start_ref[k] = vector
            stats = put(stats, 0, sector * len(CHARGES) + p, norm)
            right_products(width, tile, vector.astype(BF16), rights[p], product_ref, k)
    stats_ref[...] = stats


def bound_blocks(chunks, tile, packed_refs, environ_ref, out_ref, diag):
    segment = lax.axis_index("seg")
    start = chunks[0][0]

    @pl.when(segment == 0)
    def _():
        for w in range(sum(count for _, count in chunks)):
            out_ref[:, w * tile : (w + 1) * tile] = environ_ref[
                (start + w) * tile : (start + w + 1) * tile, :
            ]

    @pl.when(segment != 0)
    def _():
        for (first, count), ref in zip(chunks, packed_refs):

            def write(w, block, base=first - start):
                out_ref[:, (base + w) * tile : (base + w + 1) * tile] = block.astype(BF16)

            unpack_into(count, tile, reader(ref), write, diag)


def open_kernel(width, tile, environ_ref, *refs):
    chunks = chunks_of(width)[:-1]
    packed_refs, (*product_refs, bound_ref, image_ref, diag) = refs[: len(chunks)], refs[len(chunks) :]
    bound_blocks(chunks, tile, packed_refs, environ_ref, bound_ref, diag)
    rows = bound_ref.shape[1]
    for group, product_ref in enumerate(product_refs):
        image_ref[group] = jnp.dot(bound_ref[...], product_ref[:rows, :], preferred_element_type=F32)


def lanczos_kernel(
    width, tile, dims_ref, packed_ref, environ_ref, early_ref, image_ref, own_ref, next_ref, after_ref,
    start_a, start_b, norm_ref, product_a, product_b, basis_ref, stats_ref,
    late_s, product_s, diag,
):
    states = len(CHARGES)
    sector = lax.axis_index("sec")
    last = chunks_of(width)[-1:]
    bound_blocks(last, tile, [packed_ref], environ_ref, late_s, diag)
    rows, columns = live_limits(dims_ref, sector)
    row, lane = iotas((tile, tile))
    rights = [own_ref.at[0], next_ref.at[0], next_ref.at[1], after_ref.at[0]]
    stats = norm_ref[...]
    starts = (start_a, start_b)
    split = last[0][0] * tile
    betas = [None] * states
    for j in range(LANCZOS):
        for group, members in enumerate(GROUPS):
            if j == 0:
                source = (product_a, product_b)[group]
                images = image_ref[group]
            else:
                source = product_s.at[group]
                for k, p in enumerate(members):
                    field = basis_ref[j - 1, p].astype(BF16)
                    right_products(width, tile, field, rights[p], source, k)
                images = jnp.dot(early_ref[...], source[:split, :], preferred_element_type=F32)
            images = images + jnp.dot(late_s[...], source[split:, :], preferred_element_type=F32)
            for k, p in enumerate(members):
                live = (row < rows) & (lane < columns[p])
                image = jnp.where(live, images[:, k * tile : (k + 1) * tile], 0.0)
                vector = starts[group][k] if j == 0 else basis_ref[j - 1, p]
                alpha = total(vector * image)
                image = image - alpha * vector
                if j > 0:
                    before = starts[group][k] if j == 1 else basis_ref[j - 2, p]
                    image = image - betas[p] * before
                following, beta = scaled(image)
                basis_ref[j, p] = following
                betas[p] = beta
                stats = put(stats, 1 + 2 * j, sector * states + p, alpha)
                stats = put(stats, 2 + 2 * j, sector * states + p, beta)
    stats_ref[...] = stats


def finish_kernel(
    entries, stats_ref, start_a, start_b, basis_ref, vector_ref, table_ref
):
    states = len(CHARGES)
    sector = lax.axis_index("sec")
    stats = stats_ref[0]
    for q in range(1, stats_ref.shape[0]):
        stats = stats + stats_ref[q]
    alphas = [stats[1 + 2 * j : 2 + 2 * j, :] for j in range(LANCZOS)]
    betas = [stats[2 + 2 * j : 3 + 2 * j, :] for j in range(LANCZOS)]

    def mean(left, right):
        products = left[0] * right[0]
        for x, y in zip(left[1:], right[1:]):
            products = products + x * y
        return jnp.sum(products, axis=1, keepdims=True) / entries

    def applied(vector):
        count = len(vector)
        image = []
        for k in range(count + 1):
            terms = []
            if k > 0:
                terms.append(betas[k - 1] * vector[k - 1])
            if k < count:
                terms.append(alphas[k] * vector[k])
            if k + 1 < count:
                terms.append(betas[k] * vector[k + 1])
            image.append(sum(terms[1:], terms[0]))
        return image

    residual = [stats[0:1, :]]
    previous = []
    table_row, table_column = iotas(table_ref.shape)
    table = jnp.zeros(table_ref.shape, F32)
    for j in range(LANCZOS):
        image = applied(residual)
        square = mean(residual, residual) + 1e-06
        alpha = mean(residual, image[: j + 1]) / square
        norm = jnp.sqrt(square)
        vector = [value / norm for value in residual]
        residual = [value / norm for value in image]
        for k in range(j + 1):
            residual[k] = residual[k] - alpha * vector[k]
        for k in range(j):
            residual[k] = residual[k] - norm * previous[k]
        previous = vector
        if j > 0:
            table = jnp.where((table_row == 1) & (table_column == j - 1), norm, table)
        table = jnp.where((table_row == 0) & (table_column == j), alpha, table)
    norm = jnp.sqrt(mean(residual, residual) + 1e-06)
    vector = [value / norm for value in residual]
    table = jnp.where((table_row == 1) & (table_column == LANCZOS - 1), norm, table)
    table_ref[...] = table
    lane = lax.broadcasted_iota(jnp.int32, (1, stats.shape[1]), 1)
    starts = {p: ref[k] for members, ref in zip(GROUPS, (start_a, start_b)) for k, p in enumerate(members)}
    for p in range(states):
        value = None
        here = lane == sector * states + p
        for k in range(LANCZOS + 1):
            weight = jnp.sum(jnp.where(here, vector[k], 0.0), axis=1, keepdims=True)
            term = weight * (starts[p] if k == 0 else basis_ref[k - 1, p])
            value = term if value is None else value + term
        vector_ref[p] = value


def smem():
    return pl.BlockSpec(memory_space=pltpu.SMEM)


def vmem():
    return pl.BlockSpec(memory_space=pltpu.VMEM)


def call(name, kernel, scalars, arrays, outs, scratch, limit, micros):
    many = isinstance(outs, (tuple, list))
    return pl.pallas_call(
        kernel,
        out_shape=outs,
        in_specs=[smem()] * len(scalars) + [vmem()] * len(arrays),
        out_specs=[vmem()] * len(outs) if many else vmem(),
        scratch_shapes=scratch,
        compiler_params=pltpu.CompilerParams(vmem_limit_bytes=limit * MIB),
        name=name,
        cost_estimate=pl.CostEstimate(
            flops=int(micros * 1.1e9), bytes_accessed=0, transcendentals=0
        ),
    )(*scalars, *arrays)


def shift_by(count, steps):
    return [(source, (source + steps) % count) for source in range(count)]


def gathered(value, axis):
    count = lax.axis_size(axis)
    return lax.all_to_all(jnp.broadcast_to(value, (count,) + value.shape), axis, 0, 0)


def on_device(left_env, right_env, site_tensors, mpo, boundary_mpo, guess, sector_dims):
    width, tile = left_env.shape[2], left_env.shape[-1]
    half = tile // 2
    wide = padded(width)
    states = len(CHARGES)
    sector_count = sector_dims.shape[0]
    sectors = lax.axis_size("sec")
    segments = lax.axis_size("seg")
    prows = packed_rows(width, tile)
    drows = prows - width * half
    packed = jax.ShapeDtypeStruct((prows, tile), BF16)
    parts = chunks_of(width)

    def packed_parts(dtype):
        return [jax.ShapeDtypeStruct((packed_rows(count, tile), tile), dtype) for _, count in parts]

    def mixed(count):
        return jax.ShapeDtypeStruct((count, tile, width * tile), BF16)

    environ = left_env.reshape(width * tile, tile)
    right = right_env.reshape(width * tile, tile)
    site = site_tensors[0, 0, :, 0]
    site_weights = jnp.transpose(mpo[0, 0], (0, 2, 1)).reshape(width * states, width)
    bound_weights = jnp.transpose(boundary_mpo[0], (0, 2, 1)).reshape(width * states, width)

    sector = lax.axis_index("sec")
    swap = [(q, q ^ 1) for q in range(sectors)]
    up_two = shift_by(sectors, 2)
    down_two = shift_by(sectors, -2)
    onward = shift_by(segments, 1)
    diag = pltpu.VMEM((drows, tile), F32)

    def mix_scratch(count):
        return [
            pltpu.VMEM((tile, tile), F32),
            pltpu.VMEM((count, packed_height(width), 2 * wide), BF16),
            pltpu.VMEM((wide * (tile + 8), tile), F32),
            pltpu.VMEM((count, wide * (tile + 8), tile), F32),
        ]

    right_packed = call(
        "pack_right", functools.partial(pack_kernel, width, tile), [], [right], packed,
        [diag], 6, 1,
    )
    right_far = lax.ppermute(right_packed, "sec", down_two)
    far_environ = lax.ppermute(environ, "sec", swap)
    far_site = lax.ppermute(site, "sec", swap)
    fold_scratch = [
        pltpu.VMEM((tile, 3 * tile), BF16),
        pltpu.VMEM((3, tile, tile), BF16),
        pltpu.VMEM((tile, tile), F32),
        pltpu.VMEM((3, packed_height(width), 2 * wide), BF16),
        pltpu.VMEM((3, width // 2 * tile, 2 * tile), BF16),
        pltpu.VMEM((3, wide * (half + 8), tile), F32),
        pltpu.VMEM((3, drows, tile), F32),
        pltpu.VMEM((wide * (half + 8), tile), F32),
        pltpu.VMEM((drows, tile), F32),
    ]
    outgoing = call(
        "fold_up", functools.partial(fold_kernel, width, tile, True),
        [sector_dims], [environ, site, far_environ, far_site, site_weights], packed_parts(BF16),
        fold_scratch, 20, 12,
    )
    early_arrived = lax.ppermute(outgoing[0], "sec", up_two)
    far_environ, outgoing = lax.optimization_barrier((far_environ, outgoing))
    kept = call(
        "fold_own", functools.partial(fold_kernel, width, tile, False),
        [sector_dims], [environ, site, far_environ, far_site, site_weights], packed_parts(F32),
        fold_scratch, 20, 0.1,
    )
    kept, middle_outgoing = lax.optimization_barrier((kept, outgoing[1]))
    middle_arrived = lax.ppermute(middle_outgoing, "sec", up_two)
    kept, right = lax.optimization_barrier((kept, right))
    own_mixed = call(
        "mix_own", functools.partial(mix_own_kernel, width, tile), [], [right, bound_weights],
        mixed(1), mix_scratch(1), 12, 1,
    )
    own_mixed, right_far, late_outgoing = lax.optimization_barrier((own_mixed, right_far, outgoing[2]))
    late_arrived = lax.ppermute(late_outgoing, "sec", up_two)
    passed_on = jnp.where(sector + 2 < sectors, right_far, jnp.zeros_like(right_far))
    passed_on = jnp.where(lax.rem(sector, 2) == 0, passed_on, right_packed)
    right_near = lax.ppermute(passed_on, "sec", swap)

    def carried(stays, comes):
        return (stays + jnp.where(sector >= 2, comes.astype(F32), 0.0)).astype(BF16)

    early = carried(kept[0], early_arrived)
    early_bound = lax.ppermute(early, "seg", onward)
    early, right_far = lax.optimization_barrier((early, right_far))
    after_mixed = call(
        "mix_after", functools.partial(mix_after_kernel, width, tile), [],
        [right_far, bound_weights], mixed(1), mix_scratch(1) + [diag], 12, 2,
    )
    middle_arrived, after_mixed = lax.optimization_barrier((middle_arrived, after_mixed))
    middle = carried(kept[1], middle_arrived)
    middle_bound = lax.ppermute(middle, "seg", onward)
    middle, right_near = lax.optimization_barrier((middle, right_near))
    next_mixed = call(
        "mix_next", functools.partial(mix_next_kernel, width, tile), [],
        [right_near, bound_weights], mixed(2), mix_scratch(2) + [diag], 16, 3,
    )
    late_arrived, next_mixed = lax.optimization_barrier((late_arrived, next_mixed))
    late = carried(kept[2], late_arrived)
    late_bound = lax.ppermute(late, "seg", onward[:-1])
    late, next_mixed, after_mixed = lax.optimization_barrier((late, next_mixed, after_mixed))
    start_a, start_b, norms, products_a, products_b = call(
        "head", functools.partial(head_kernel, width, tile),
        [sector_dims], [guess[0, :, 0], own_mixed, next_mixed, after_mixed],
        [jax.ShapeDtypeStruct((2, tile, tile), F32)] * 2
        + [jax.ShapeDtypeStruct((16, 128), F32)]
        + [jax.ShapeDtypeStruct((width * tile, 2 * tile), BF16)] * 2,
        [], 14, 0.2,
    )
    new_env = call(
        "unpack_env", functools.partial(unpack_kernel, width, tile), [], [early, middle, late],
        jax.ShapeDtypeStruct((width * tile, tile), BF16), [diag], 6, 2,
    )
    middle_bound, new_env = lax.optimization_barrier((middle_bound, new_env))
    bound, image = call(
        "open", functools.partial(open_kernel, width, tile), [],
        [environ, early_bound, middle_bound, products_a, products_b],
        (
            jax.ShapeDtypeStruct((tile, parts[-1][0] * tile), BF16),
            jax.ShapeDtypeStruct((len(GROUPS), tile, 2 * tile), F32),
        ),
        [diag], 12, 1,
    )
    late_bound, bound = lax.optimization_barrier((late_bound, bound))
    basis, stats = call(
        "lanczos", functools.partial(lanczos_kernel, width, tile),
        [sector_dims],
        [late_bound, environ, bound, image, own_mixed, next_mixed, after_mixed, start_a, start_b,
         norms, products_a, products_b],
        (
            jax.ShapeDtypeStruct((LANCZOS, states, tile, tile), F32),
            jax.ShapeDtypeStruct((16, 128), F32),
        ),
        [
            pltpu.VMEM((tile, parts[-1][1] * tile), BF16),
            pltpu.VMEM((len(GROUPS), width * tile, 2 * tile), BF16),
            diag,
        ],
        22, 12,
    )
    stats = gathered(stats, "sec")
    entries = float(states * sector_count * tile * tile)
    vector, table = call(
        "finish", functools.partial(finish_kernel, entries), [], [stats, start_a, start_b, basis],
        (
            jax.ShapeDtypeStruct((states, tile, tile), F32),
            jax.ShapeDtypeStruct((2, LANCZOS), F32),
        ),
        [], 6, 2,
    )
    return new_env.reshape(left_env.shape), vector[None, :, None], jnp.transpose(table)[None]


def solution(mesh):
    placed = (
        P("seg", "sec", None, None, None),
        P("seg", "sec", None, None, None),
        P("seg", None, None, "sec", None, None),
        P("seg", None, None, None, None),
        P("seg", None, None, None),
        P("seg", None, "sec", None, None),
        P(),
    )
    return jax.shard_map(
        on_device,
        mesh=mesh,
        in_specs=placed,
        out_specs=(
            P("seg", "sec", None, None, None),
            P("seg", None, "sec", None, None),
            P("seg", None, None),
        ),
        check_vma=False,
    )
```

```python
import functools

import jax
import jax.numpy as jnp
from jax import lax
from jax.experimental import pallas as pl
from jax.experimental.pallas import tpu as pltpu
from jax.sharding import PartitionSpec as P

LANCZOS = 4
CHARGES = (0, 1, 1, 2)
GROUPS = ((0, 3), (1, 2))
F32 = jnp.float32
BF16 = jnp.bfloat16
MIB = 1024 * 1024


def padded(count):
    return -(-count // 8) * 8


def packed_height(count):
    return -(-count // 16) * 16


def packed_rows(count, tile):
    return count * tile // 2 + packed_height(count)


def chunks_of(width):
    one = width // 6 * 2
    two = (width - one) // 4 * 2
    return (0, one), (one, two), (one + two, width - one - two)


def iotas(shape):
    return lax.broadcasted_iota(jnp.int32, shape, 0), lax.broadcasted_iota(jnp.int32, shape, 1)


def pack_block(block):
    tile = block.shape[0]
    half = tile // 2
    top, low = block[:half], block[half:]
    row, lane = iotas((half, tile))
    turned = pltpu.roll(low, half, 1)
    folded = jnp.where((lane < half) & (row > lane), turned, top)
    diagonal = jnp.sum(jnp.where(lane == row + half, low, 0.0), axis=0, keepdims=True)
    return folded, diagonal


def unpack_block(folded, diagonal):
    half, tile = folded.shape
    row, lane = iotas((half, tile))
    rolled = pltpu.roll(folded, half, 1)
    turned = jnp.transpose(jnp.concatenate([folded, rolled], axis=0))
    top = jnp.where((lane < half) & (row > lane), turned[:half], folded)
    low = jnp.where((lane >= half) & (row > lane - half), rolled, turned[half:])
    low = jnp.where(lane == row + half, diagonal, low)
    return jnp.concatenate([top, low], axis=0)


def partner_of(sector):
    return sector + 1 - 2 * lax.rem(sector, 2)


def live_limits(dims_ref, sector):
    count = dims_ref.shape[0]
    rows = dims_ref[sector]
    columns = []
    for charge in CHARGES:
        target = sector + charge
        columns.append(jnp.where(target < count, dims_ref[jnp.minimum(target, count - 1)], 0))
    return rows, columns


def weight_rows(weight_ref, width, p, square, turned):
    wide = padded(width)
    square[...] = jnp.zeros_like(square)
    square[:width, :width] = weight_ref[pl.ds(p, width, stride=len(CHARGES)), :]
    value = square[...]
    if turned:
        value = jnp.transpose(value)
    high = value.astype(BF16).astype(F32)
    joined = (high + pltpu.roll(value - high, wide, 1)).astype(BF16)
    return joined[: packed_height(width), : 2 * wide]


def doubled(value):
    return jnp.concatenate([value, value], axis=0).astype(BF16)


def pack_kernel(width, tile, source_ref, weight_ref, out_ref, kept_ref, diag):
    half = tile // 2
    kept_ref[...] = weight_ref[...]
    diag[...] = jnp.zeros_like(diag)
    for w in range(width):
        folded, diagonal = pack_block(source_ref[w * tile : (w + 1) * tile, :].astype(F32))
        out_ref[w * half : (w + 1) * half, :] = folded.astype(BF16)
        diag[w : w + 1, :] = diagonal
    out_ref[width * half :, :] = diag[...].astype(BF16)


def unpack_into(count, tile, read, write, diag):
    half = tile // 2
    size = packed_height(count)
    diag[:size, :] = read(count * half, size)
    for w in range(count):
        write(w, unpack_block(read(w * half, half), diag[w : w + 1, :]))


def reader(ref):
    return lambda at, size: ref[at : at + size, :].astype(F32)


def unpack_kernel(width, tile, *refs):
    *part_refs, out_ref, diag = refs
    for (first, count), ref in zip(chunks_of(width), part_refs):

        def write(w, block, first=first):
            out_ref[(first + w) * tile : (first + w + 1) * tile, :] = block.astype(BF16)

        unpack_into(count, tile, reader(ref), write, diag)


def fold_kernel(
    width, tile, travels, dims_ref, environ_ref, site_ref, far_environ_ref, far_site_ref, weight_ref, *refs
):
    part_refs = refs[: len(chunks_of(width))]
    joined_s, turned_s, square_s, weight_s, half_s, packed_s, diag_s, sums_s, diag_sums_s = refs[
        len(part_refs) :
    ]
    half = tile // 2
    pitch = half + 8
    wide = padded(width)
    sector = lax.axis_index("sec")
    partner = partner_of(sector)
    row, lane = iotas((tile, tile))

    def run(own_state, with_partner):
        rows, columns = live_limits(dims_ref, sector)
        live = (row < rows) & (lane < columns[own_state])
        sites = [jnp.where(live, site_ref[own_state].astype(F32), 0.0)]
        states = [own_state]
        if with_partner:
            rows, columns = live_limits(dims_ref, partner)
            for k in range(2):
                live = (row < rows) & (lane < columns[k + 1])
                sites.append(jnp.where(live, far_site_ref[k + 1].astype(F32), 0.0))
                states.append(k + 1)
        parts = len(states)
        for n in range(parts):
            joined_s[:, n * tile : (n + 1) * tile] = sites[n].astype(BF16)
            turned_s[n] = jnp.transpose(sites[n]).astype(BF16)
            weight_s[n] = weight_rows(weight_ref, width, states[n], square_s, True)
            packed_s[n, width * pitch :, :] = jnp.zeros(((wide - width) * pitch, tile), F32)
            diag_s[n] = jnp.zeros_like(diag_s[n])

        for pair in range(width // 2):
            at = slice(pair * tile, (pair + 1) * tile)
            for k in range(2):
                here = slice((pair * 2 + k) * tile, (pair * 2 + k + 1) * tile)
                blocks = [
                    jnp.dot(environ_ref[here, :], joined_s[:, :tile], preferred_element_type=F32)
                ]
                if with_partner:
                    both = jnp.dot(
                        far_environ_ref[here, :], joined_s[:, tile:], preferred_element_type=F32
                    )
                    blocks += [both[:, :tile], both[:, tile:]]
                for n in range(parts):
                    half_s[n, at, k * tile : (k + 1) * tile] = blocks[n].astype(BF16)
            for n in range(parts):
                both = jnp.dot(turned_s[n], half_s[n, at, :], preferred_element_type=F32)
                for k in range(2):
                    w = pair * 2 + k
                    folded, diagonal = pack_block(both[:, k * tile : (k + 1) * tile])
                    packed_s[n, w * pitch : w * pitch + half, :] = folded
                    diag_s[n, w : w + 1, :] = diagonal

        def mixed(inputs):
            value = None
            for n in range(parts):
                term = jnp.dot(weight_s[n], doubled(inputs[n]), preferred_element_type=F32)
                value = term if value is None else value + term
            return value[:wide]

        for at in range(0, half, 2):
            value = mixed([
                jnp.concatenate(
                    [packed_s[n, pl.ds(at + k, wide, stride=pitch), :] for k in range(2)], axis=1
                )
                for n in range(parts)
            ])
            for k in range(2):
                sums_s[pl.ds(at + k, wide, stride=pitch), :] = value[:, k * tile : (k + 1) * tile]
        diag_sums_s[...] = jnp.zeros_like(diag_sums_s)
        diag_sums_s[:wide, :] = mixed([diag_s[n, :wide] for n in range(parts)])
        for (first, count), ref in zip(chunks_of(width), part_refs):
            for w in range(count):
                at = (first + w) * pitch
                ref[w * half : (w + 1) * half, :] = sums_s[at : at + half, :].astype(ref.dtype)
            rows = packed_height(count)
            ref[count * half :, :] = diag_sums_s[first : first + rows, :].astype(ref.dtype)

    even = lax.rem(sector, 2) == 0
    own_state = len(CHARGES) - 1 if travels else 0

    @pl.when(even)
    def _():
        run(own_state, travels)

    @pl.when(jnp.logical_not(even))
    def _():
        run(own_state, not travels)


def mix_into(width, tile, weights, wide_s, sums_s, out_ref):
    wide = padded(width)
    pitch = tile + 8
    wide_s[width * pitch :, :] = jnp.zeros_like(wide_s[width * pitch :, :])

    for at in range(0, tile, 2):
        value = doubled(
            jnp.concatenate(
                [wide_s[pl.ds(at + k, wide, stride=pitch), :] for k in range(2)], axis=1
            )
        )
        for index, weight in enumerate(weights):
            mixed = jnp.dot(weight[...], value, preferred_element_type=F32)[:wide]
            for k in range(2):
                sums_s[index, pl.ds(at + k, wide, stride=pitch), :] = mixed[:, k * tile : (k + 1) * tile]
    for index in range(len(weights)):
        for w in range(width):
            out_ref[index, :, w * tile : (w + 1) * tile] = sums_s[
                index, w * pitch : w * pitch + tile, :
            ].astype(BF16)


def unpack_wide(width, tile, read, wide_s, diag):
    def write(w, block):
        wide_s[w * (tile + 8) : w * (tile + 8) + tile, :] = block

    unpack_into(width, tile, read, write, diag)


def copy_wide(width, tile, source_ref, wide_s):
    for w in range(width):
        at = w * (tile + 8)
        wide_s[at : at + tile, :] = source_ref[w * tile : (w + 1) * tile, :].astype(F32)


def mix_own_kernel(width, tile, source_ref, weight_ref, out_ref, square_s, weight_s, wide_s, sums_s):
    weight_s[0] = weight_rows(weight_ref, width, 0, square_s, False)
    copy_wide(width, tile, source_ref, wide_s)
    mix_into(width, tile, [weight_s.at[0]], wide_s, sums_s, out_ref)


def mix_next_kernel(
    width, tile, near_ref, weight_ref, out_ref, square_s, weight_s, wide_s, sums_s, diag
):
    for k in range(2):
        weight_s[k] = weight_rows(weight_ref, width, k + 1, square_s, False)
    unpack_wide(width, tile, reader(near_ref), wide_s, diag)
    mix_into(width, tile, [weight_s.at[k] for k in range(2)], wide_s, sums_s, out_ref)


def mix_after_kernel(
    width, tile, far_ref, weight_ref, out_ref, square_s, weight_s, wide_s, sums_s, diag
):
    weight_s[0] = weight_rows(weight_ref, width, 3, square_s, False)
    inside = lax.axis_index("sec") + 2 < lax.axis_size("sec")

    def read(at, size):
        return jnp.where(inside, far_ref[at : at + size, :].astype(F32), 0.0)

    unpack_wide(width, tile, read, wide_s, diag)
    mix_into(width, tile, [weight_s.at[0]], wide_s, sums_s, out_ref)


def total(value):
    return jnp.sum(jnp.sum(value, axis=0, keepdims=True), axis=1, keepdims=True)


def put(stats, kind, lane_at, value):
    row, lane = iotas(stats.shape)
    return jnp.where((row == kind) & (lane == lane_at), value, stats)


def scaled(value):
    square = total(value * value)
    inverse = jnp.where(square > 0.0, lax.rsqrt(square), 0.0)
    return value * inverse, square * inverse


def right_products(width, tile, field, right_ref, out_ref, k):
    lanes = slice(k * tile, (k + 1) * tile)
    for pair in range(width // 2):
        at = pair * 2 * tile
        both = jnp.dot(field, right_ref[:, at : at + 2 * tile], preferred_element_type=F32).astype(BF16)
        for n in range(2):
            out_ref[at + n * tile : at + (n + 1) * tile, lanes] = both[:, n * tile : (n + 1) * tile]


def head_kernel(
    width, tile, dims_ref, guess_ref, own_ref, next_ref, after_ref,
    start_a, start_b, stats_ref, product_a, product_b,
):
    rights = [own_ref.at[0], next_ref.at[0], next_ref.at[1], after_ref.at[0]]
    sector = lax.axis_index("sec")
    rows, columns = live_limits(dims_ref, sector)
    row, lane = iotas((tile, tile))
    stats = jnp.zeros(stats_ref.shape, F32)
    for members, start_ref, product_ref in zip(GROUPS, (start_a, start_b), (product_a, product_b)):
        for k, p in enumerate(members):
            live = (row < rows) & (lane < columns[p])
            vector, norm = scaled(jnp.where(live, guess_ref[p], 0.0))
            start_ref[k] = vector
            stats = put(stats, 0, sector * len(CHARGES) + p, norm)
            right_products(width, tile, vector.astype(BF16), rights[p], product_ref, k)
    stats_ref[...] = stats


def bound_blocks(chunks, tile, packed_refs, environ_ref, out_ref, diag):
    segment = lax.axis_index("seg")
    start = chunks[0][0]

    @pl.when(segment == 0)
    def _():
        for w in range(sum(count for _, count in chunks)):
            out_ref[:, w * tile : (w + 1) * tile] = environ_ref[
                (start + w) * tile : (start + w + 1) * tile, :
            ]

    @pl.when(segment != 0)
    def _():
        for (first, count), ref in zip(chunks, packed_refs):

            def write(w, block, base=first - start):
                out_ref[:, (base + w) * tile : (base + w + 1) * tile] = block.astype(BF16)

            unpack_into(count, tile, reader(ref), write, diag)


def open_kernel(width, tile, environ_ref, *refs):
    chunks = chunks_of(width)[:-1]
    packed_refs, (*product_refs, bound_ref, image_ref, diag) = refs[: len(chunks)], refs[len(chunks) :]
    bound_blocks(chunks, tile, packed_refs, environ_ref, bound_ref, diag)
    rows = bound_ref.shape[1]
    for group, product_ref in enumerate(product_refs):
        image_ref[group] = jnp.dot(bound_ref[...], product_ref[:rows, :], preferred_element_type=F32)


def lanczos_kernel(
    width, tile, dims_ref, packed_ref, environ_ref, early_ref, image_ref, own_ref, next_ref, after_ref,
    start_a, start_b, norm_ref, product_a, product_b, basis_ref, stats_ref,
    late_s, product_s, diag,
):
    states = len(CHARGES)
    sector = lax.axis_index("sec")
    last = chunks_of(width)[-1:]
    bound_blocks(last, tile, [packed_ref], environ_ref, late_s, diag)
    rows, columns = live_limits(dims_ref, sector)
    row, lane = iotas((tile, tile))
    rights = [own_ref.at[0], next_ref.at[0], next_ref.at[1], after_ref.at[0]]
    stats = norm_ref[...]
    starts = (start_a, start_b)
    split = last[0][0] * tile
    betas = [None] * states
    for j in range(LANCZOS):
        for group, members in enumerate(GROUPS):
            if j == 0:
                source = (product_a, product_b)[group]
                images = image_ref[group]
            else:
                source = product_s.at[group]
                for k, p in enumerate(members):
                    field = basis_ref[j - 1, p].astype(BF16)
                    right_products(width, tile, field, rights[p], source, k)
                images = jnp.dot(early_ref[...], source[:split, :], preferred_element_type=F32)
            images = images + jnp.dot(late_s[...], source[split:, :], preferred_element_type=F32)
            for k, p in enumerate(members):
                live = (row < rows) & (lane < columns[p])
                image = jnp.where(live, images[:, k * tile : (k + 1) * tile], 0.0)
                vector = starts[group][k] if j == 0 else basis_ref[j - 1, p]
                alpha = total(vector * image)
                image = image - alpha * vector
                if j > 0:
                    before = starts[group][k] if j == 1 else basis_ref[j - 2, p]
                    image = image - betas[p] * before
                following, beta = scaled(image)
                basis_ref[j, p] = following
                betas[p] = beta
                stats = put(stats, 1 + 2 * j, sector * states + p, alpha)
                stats = put(stats, 2 + 2 * j, sector * states + p, beta)
    stats_ref[...] = stats


def finish_kernel(
    entries, stats_ref, start_a, start_b, basis_ref, vector_ref, table_ref
):
    states = len(CHARGES)
    sector = lax.axis_index("sec")
    stats = stats_ref[0]
    for q in range(1, stats_ref.shape[0]):
        stats = stats + stats_ref[q]
    alphas = [stats[1 + 2 * j : 2 + 2 * j, :] for j in range(LANCZOS)]
    betas = [stats[2 + 2 * j : 3 + 2 * j, :] for j in range(LANCZOS)]

    def mean(left, right):
        products = left[0] * right[0]
        for x, y in zip(left[1:], right[1:]):
            products = products + x * y
        return jnp.sum(products, axis=1, keepdims=True) / entries

    def applied(vector):
        count = len(vector)
        image = []
        for k in range(count + 1):
            terms = []
            if k > 0:
                terms.append(betas[k - 1] * vector[k - 1])
            if k < count:
                terms.append(alphas[k] * vector[k])
            if k + 1 < count:
                terms.append(betas[k] * vector[k + 1])
            image.append(sum(terms[1:], terms[0]))
        return image

    residual = [stats[0:1, :]]
    previous = []
    table_row, table_column = iotas(table_ref.shape)
    table = jnp.zeros(table_ref.shape, F32)
    for j in range(LANCZOS):
        image = applied(residual)
        square = mean(residual, residual) + 1e-06
        alpha = mean(residual, image[: j + 1]) / square
        norm = jnp.sqrt(square)
        vector = [value / norm for value in residual]
        residual = [value / norm for value in image]
        for k in range(j + 1):
            residual[k] = residual[k] - alpha * vector[k]
        for k in range(j):
            residual[k] = residual[k] - norm * previous[k]
        previous = vector
        if j > 0:
            table = jnp.where((table_row == 1) & (table_column == j - 1), norm, table)
        table = jnp.where((table_row == 0) & (table_column == j), alpha, table)
    norm = jnp.sqrt(mean(residual, residual) + 1e-06)
    vector = [value / norm for value in residual]
    table = jnp.where((table_row == 1) & (table_column == LANCZOS - 1), norm, table)
    table_ref[...] = table
    lane = lax.broadcasted_iota(jnp.int32, (1, stats.shape[1]), 1)
    starts = {p: ref[k] for members, ref in zip(GROUPS, (start_a, start_b)) for k, p in enumerate(members)}
    for p in range(states):
        value = None
        here = lane == sector * states + p
        for k in range(LANCZOS + 1):
            weight = jnp.sum(jnp.where(here, vector[k], 0.0), axis=1, keepdims=True)
            term = weight * (starts[p] if k == 0 else basis_ref[k - 1, p])
            value = term if value is None else value + term
        vector_ref[p] = value


def smem():
    return pl.BlockSpec(memory_space=pltpu.SMEM)


def vmem():
    return pl.BlockSpec(memory_space=pltpu.VMEM)


def call(name, kernel, scalars, arrays, outs, scratch, limit, micros):
    many = isinstance(outs, (tuple, list))
    return pl.pallas_call(
        kernel,
        out_shape=outs,
        in_specs=[smem()] * len(scalars) + [vmem()] * len(arrays),
        out_specs=[vmem()] * len(outs) if many else vmem(),
        scratch_shapes=scratch,
        compiler_params=pltpu.CompilerParams(vmem_limit_bytes=limit * MIB),
        name=name,
        cost_estimate=pl.CostEstimate(
            flops=int(micros * 1.1e9), bytes_accessed=0, transcendentals=0
        ),
    )(*scalars, *arrays)


def shift_by(count, steps):
    return [(source, (source + steps) % count) for source in range(count)]


def gathered(value, axis):
    count = lax.axis_size(axis)
    return lax.all_to_all(jnp.broadcast_to(value, (count,) + value.shape), axis, 0, 0)


def on_device(left_env, right_env, site_tensors, mpo, boundary_mpo, guess, sector_dims):
    width, tile = left_env.shape[2], left_env.shape[-1]
    half = tile // 2
    wide = padded(width)
    states = len(CHARGES)
    sector_count = sector_dims.shape[0]
    sectors = lax.axis_size("sec")
    segments = lax.axis_size("seg")
    prows = packed_rows(width, tile)
    drows = prows - width * half
    packed = jax.ShapeDtypeStruct((prows, tile), BF16)
    parts = chunks_of(width)

    def packed_parts(dtype):
        return [jax.ShapeDtypeStruct((packed_rows(count, tile), tile), dtype) for _, count in parts]

    def mixed(count):
        return jax.ShapeDtypeStruct((count, tile, width * tile), BF16)

    environ = left_env.reshape(width * tile, tile)
    right = right_env.reshape(width * tile, tile)
    site = site_tensors[0, 0, :, 0]
    site_weights = jnp.transpose(mpo[0, 0], (0, 2, 1)).reshape(width * states, width)
    bound_weights = jnp.transpose(boundary_mpo[0], (0, 2, 1)).reshape(width * states, width)

    sector = lax.axis_index("sec")
    swap = [(q, q ^ 1) for q in range(sectors)]
    up_two = shift_by(sectors, 2)
    down_two = shift_by(sectors, -2)
    onward = shift_by(segments, 1)
    diag = pltpu.VMEM((drows, tile), F32)

    def mix_scratch(count):
        return [
            pltpu.VMEM((tile, tile), F32),
            pltpu.VMEM((count, packed_height(width), 2 * wide), BF16),
            pltpu.VMEM((wide * (tile + 8), tile), F32),
            pltpu.VMEM((count, wide * (tile + 8), tile), F32),
        ]

    right_packed, site_weights = call(
        "pack_right", functools.partial(pack_kernel, width, tile), [], [right, site_weights],
        (packed, jax.ShapeDtypeStruct(site_weights.shape, F32)), [diag], 6, 1,
    )
    right_far = lax.ppermute(right_packed, "sec", down_two)
    far_environ = lax.ppermute(environ, "sec", swap)
    far_site = lax.ppermute(site, "sec", swap)
    fold_scratch = [
        pltpu.VMEM((tile, 3 * tile), BF16),
        pltpu.VMEM((3, tile, tile), BF16),
        pltpu.VMEM((tile, tile), F32),
        pltpu.VMEM((3, packed_height(width), 2 * wide), BF16),
        pltpu.VMEM((3, width // 2 * tile, 2 * tile), BF16),
        pltpu.VMEM((3, wide * (half + 8), tile), F32),
        pltpu.VMEM((3, drows, tile), F32),
        pltpu.VMEM((wide * (half + 8), tile), F32),
        pltpu.VMEM((drows, tile), F32),
    ]
    outgoing = call(
        "fold_up", functools.partial(fold_kernel, width, tile, True),
        [sector_dims], [environ, site, far_environ, far_site, site_weights], packed_parts(BF16),
        fold_scratch, 20, 12,
    )
    early_arrived = lax.ppermute(outgoing[0], "sec", up_two)
    far_environ, outgoing = lax.optimization_barrier((far_environ, outgoing))
    kept = call(
        "fold_own", functools.partial(fold_kernel, width, tile, False),
        [sector_dims], [environ, site, far_environ, far_site, site_weights], packed_parts(F32),
        fold_scratch, 20, 0.1,
    )
    kept, middle_outgoing = lax.optimization_barrier((kept, outgoing[1]))
    middle_arrived = lax.ppermute(middle_outgoing, "sec", up_two)
    kept, right = lax.optimization_barrier((kept, right))
    own_mixed = call(
        "mix_own", functools.partial(mix_own_kernel, width, tile), [], [right, bound_weights],
        mixed(1), mix_scratch(1), 12, 1,
    )
    own_mixed, right_far, late_outgoing = lax.optimization_barrier((own_mixed, right_far, outgoing[2]))
    late_arrived = lax.ppermute(late_outgoing, "sec", up_two)
    passed_on = jnp.where(sector + 2 < sectors, right_far, jnp.zeros_like(right_far))
    passed_on = jnp.where(lax.rem(sector, 2) == 0, passed_on, right_packed)
    right_near = lax.ppermute(passed_on, "sec", swap)

    def carried(stays, comes):
        return (stays + jnp.where(sector >= 2, comes.astype(F32), 0.0)).astype(BF16)

    early = carried(kept[0], early_arrived)
    early_bound = lax.ppermute(early, "seg", onward)
    early, right_far = lax.optimization_barrier((early, right_far))
    after_mixed = call(
        "mix_after", functools.partial(mix_after_kernel, width, tile), [],
        [right_far, bound_weights], mixed(1), mix_scratch(1) + [diag], 12, 2,
    )
    middle_arrived, after_mixed = lax.optimization_barrier((middle_arrived, after_mixed))
    middle = carried(kept[1], middle_arrived)
    middle_bound = lax.ppermute(middle, "seg", onward)
    middle, right_near = lax.optimization_barrier((middle, right_near))
    next_mixed = call(
        "mix_next", functools.partial(mix_next_kernel, width, tile), [],
        [right_near, bound_weights], mixed(2), mix_scratch(2) + [diag], 16, 3,
    )
    late_arrived, next_mixed = lax.optimization_barrier((late_arrived, next_mixed))
    late = carried(kept[2], late_arrived)
    late_bound = lax.ppermute(late, "seg", onward)
    late, next_mixed, after_mixed = lax.optimization_barrier((late, next_mixed, after_mixed))
    start_a, start_b, norms, products_a, products_b = call(
        "head", functools.partial(head_kernel, width, tile),
        [sector_dims], [guess[0, :, 0], own_mixed, next_mixed, after_mixed],
        [jax.ShapeDtypeStruct((2, tile, tile), F32)] * 2
        + [jax.ShapeDtypeStruct((16, 128), F32)]
        + [jax.ShapeDtypeStruct((width * tile, 2 * tile), BF16)] * 2,
        [], 14, 0.2,
    )
    new_env = call(
        "unpack_env", functools.partial(unpack_kernel, width, tile), [], [early, middle, late],
        jax.ShapeDtypeStruct((width * tile, tile), BF16), [diag], 6, 2,
    )
    middle_bound, new_env = lax.optimization_barrier((middle_bound, new_env))
    bound, image = call(
        "open", functools.partial(open_kernel, width, tile), [],
        [environ, early_bound, middle_bound, products_a, products_b],
        (
            jax.ShapeDtypeStruct((tile, parts[-1][0] * tile), BF16),
            jax.ShapeDtypeStruct((len(GROUPS), tile, 2 * tile), F32),
        ),
        [diag], 12, 1,
    )
    late_bound, bound = lax.optimization_barrier((late_bound, bound))
    basis, stats = call(
        "lanczos", functools.partial(lanczos_kernel, width, tile),
        [sector_dims],
        [late_bound, environ, bound, image, own_mixed, next_mixed, after_mixed, start_a, start_b,
         norms, products_a, products_b],
        (
            jax.ShapeDtypeStruct((LANCZOS, states, tile, tile), F32),
            jax.ShapeDtypeStruct((16, 128), F32),
        ),
        [
            pltpu.VMEM((tile, parts[-1][1] * tile), BF16),
            pltpu.VMEM((len(GROUPS), width * tile, 2 * tile), BF16),
            diag,
        ],
        22, 12,
    )
    stats = gathered(stats, "sec")
    entries = float(states * sector_count * tile * tile)
    vector, table = call(
        "finish", functools.partial(finish_kernel, entries), [], [stats, start_a, start_b, basis],
        (
            jax.ShapeDtypeStruct((states, tile, tile), F32),
            jax.ShapeDtypeStruct((2, LANCZOS), F32),
        ),
        [], 6, 2,
    )
    return new_env.reshape(left_env.shape), vector[None, :, None], jnp.transpose(table)[None]


def solution(mesh):
    placed = (
        P("seg", "sec", None, None, None),
        P("seg", "sec", None, None, None),
        P("seg", None, None, "sec", None, None),
        P("seg", None, None, None, None),
        P("seg", None, None, None),
        P("seg", None, "sec", None, None),
        P(),
    )
    return jax.shard_map(
        on_device,
        mesh=mesh,
        in_specs=placed,
        out_specs=(
            P("seg", "sec", None, None, None),
            P("seg", None, "sec", None, None),
            P("seg", None, None),
        ),
        check_vma=False,
    )
```

```python
import functools

import jax
import jax.numpy as jnp
from jax import lax
from jax.experimental import pallas as pl
from jax.experimental.pallas import tpu as pltpu
from jax.sharding import PartitionSpec as P

LANCZOS = 4
CHARGES = (0, 1, 1, 2)
GROUPS = ((0, 3), (1, 2))
F32 = jnp.float32
BF16 = jnp.bfloat16
MIB = 1024 * 1024


def padded(count):
    return -(-count // 8) * 8


def packed_height(count):
    return -(-count // 16) * 16


def packed_rows(count, tile):
    return count * tile // 2 + packed_height(count)


def chunks_of(width):
    one = width // 6 * 2
    two = (width - one) // 4 * 2
    return (0, one), (one, two), (one + two, width - one - two)


def iotas(shape):
    return lax.broadcasted_iota(jnp.int32, shape, 0), lax.broadcasted_iota(jnp.int32, shape, 1)


def pack_block(block):
    tile = block.shape[0]
    half = tile // 2
    top, low = block[:half], block[half:]
    row, lane = iotas((half, tile))
    turned = pltpu.roll(low, half, 1)
    folded = jnp.where((lane < half) & (row > lane), turned, top)
    diagonal = jnp.sum(jnp.where(lane == row + half, low, 0.0), axis=0, keepdims=True)
    return folded, diagonal


def unpack_block(folded, diagonal):
    half, tile = folded.shape
    row, lane = iotas((half, tile))
    rolled = pltpu.roll(folded, half, 1)
    turned = jnp.transpose(jnp.concatenate([folded, rolled], axis=0))
    top = jnp.where((lane < half) & (row > lane), turned[:half], folded)
    low = jnp.where((lane >= half) & (row > lane - half), rolled, turned[half:])
    low = jnp.where(lane == row + half, diagonal, low)
    return jnp.concatenate([top, low], axis=0)


def partner_of(sector):
    return sector + 1 - 2 * lax.rem(sector, 2)


def live_limits(dims_ref, sector):
    count = dims_ref.shape[0]
    rows = dims_ref[sector]
    columns = []
    for charge in CHARGES:
        target = sector + charge
        columns.append(jnp.where(target < count, dims_ref[jnp.minimum(target, count - 1)], 0))
    return rows, columns


def weight_rows(weight_ref, width, p, square, turned):
    wide = padded(width)
    square[...] = jnp.zeros_like(square)
    square[:width, :width] = weight_ref[pl.ds(p, width, stride=len(CHARGES)), :]
    value = square[...]
    if turned:
        value = jnp.transpose(value)
    high = value.astype(BF16).astype(F32)
    joined = (high + pltpu.roll(value - high, wide, 1)).astype(BF16)
    return joined[: packed_height(width), : 2 * wide]


def doubled(value):
    return jnp.concatenate([value, value], axis=0).astype(BF16)


def pack_kernel(width, tile, source_ref, out_ref, diag):
    half = tile // 2
    diag[...] = jnp.zeros_like(diag)
    for w in range(width):
        folded, diagonal = pack_block(source_ref[w * tile : (w + 1) * tile, :].astype(F32))
        out_ref[w * half : (w + 1) * half, :] = folded.astype(BF16)
        diag[w : w + 1, :] = diagonal
    out_ref[width * half :, :] = diag[...].astype(BF16)


def unpack_into(count, tile, read, write, diag):
    half = tile // 2
    size = packed_height(count)
    diag[:size, :] = read(count * half, size)
    for w in range(count):
        write(w, unpack_block(read(w * half, half), diag[w : w + 1, :]))


def reader(ref):
    return lambda at, size: ref[at : at + size, :].astype(F32)


def unpack_kernel(width, tile, *refs):
    *part_refs, out_ref, diag = refs
    for (first, count), ref in zip(chunks_of(width), part_refs):

        def write(w, block, first=first):
            out_ref[(first + w) * tile : (first + w + 1) * tile, :] = block.astype(BF16)

        unpack_into(count, tile, reader(ref), write, diag)


def fold_kernel(
    width, tile, travels, dims_ref, environ_ref, site_ref, far_environ_ref, far_site_ref, weight_ref, *refs
):
    part_refs = refs[: len(chunks_of(width))]
    joined_s, turned_s, square_s, weight_s, half_s, packed_s, diag_s, sums_s, diag_sums_s = refs[
        len(part_refs) :
    ]
    half = tile // 2
    pitch = half + 8
    wide = padded(width)
    sector = lax.axis_index("sec")
    partner = partner_of(sector)
    row, lane = iotas((tile, tile))

    def run(own_state, with_partner):
        rows, columns = live_limits(dims_ref, sector)
        live = (row < rows) & (lane < columns[own_state])
        sites = [jnp.where(live, site_ref[own_state].astype(F32), 0.0)]
        states = [own_state]
        if with_partner:
            rows, columns = live_limits(dims_ref, partner)
            for k in range(2):
                live = (row < rows) & (lane < columns[k + 1])
                sites.append(jnp.where(live, far_site_ref[k + 1].astype(F32), 0.0))
                states.append(k + 1)
        parts = len(states)
        for n in range(parts):
            joined_s[:, n * tile : (n + 1) * tile] = sites[n].astype(BF16)
            turned_s[n] = jnp.transpose(sites[n]).astype(BF16)
            weight_s[n] = weight_rows(weight_ref, width, states[n], square_s, True)
            packed_s[n, width * pitch :, :] = jnp.zeros(((wide - width) * pitch, tile), F32)
            diag_s[n] = jnp.zeros_like(diag_s[n])

        for pair in range(width // 2):
            at = slice(pair * tile, (pair + 1) * tile)
            for k in range(2):
                here = slice((pair * 2 + k) * tile, (pair * 2 + k + 1) * tile)
                blocks = [
                    jnp.dot(environ_ref[here, :], joined_s[:, :tile], preferred_element_type=F32)
                ]
                if with_partner:
                    both = jnp.dot(
                        far_environ_ref[here, :], joined_s[:, tile:], preferred_element_type=F32
                    )
                    blocks += [both[:, :tile], both[:, tile:]]
                for n in range(parts):
                    half_s[n, at, k * tile : (k + 1) * tile] = blocks[n].astype(BF16)
            for n in range(parts):
                both = jnp.dot(turned_s[n], half_s[n, at, :], preferred_element_type=F32)
                for k in range(2):
                    w = pair * 2 + k
                    folded, diagonal = pack_block(both[:, k * tile : (k + 1) * tile])
                    packed_s[n, w * pitch : w * pitch + half, :] = folded
                    diag_s[n, w : w + 1, :] = diagonal

        def mixed(inputs):
            value = None
            for n in range(parts):
                term = jnp.dot(weight_s[n], doubled(inputs[n]), preferred_element_type=F32)
                value = term if value is None else value + term
            return value[:wide]

        for at in range(0, half, 2):
            value = mixed([
                jnp.concatenate(
                    [packed_s[n, pl.ds(at + k, wide, stride=pitch), :] for k in range(2)], axis=1
                )
                for n in range(parts)
            ])
            for k in range(2):
                sums_s[pl.ds(at + k, wide, stride=pitch), :] = value[:, k * tile : (k + 1) * tile]
        diag_sums_s[...] = jnp.zeros_like(diag_sums_s)
        diag_sums_s[:wide, :] = mixed([diag_s[n, :wide] for n in range(parts)])
        for (first, count), ref in zip(chunks_of(width), part_refs):
            for w in range(count):
                at = (first + w) * pitch
                ref[w * half : (w + 1) * half, :] = sums_s[at : at + half, :].astype(ref.dtype)
            rows = packed_height(count)
            ref[count * half :, :] = diag_sums_s[first : first + rows, :].astype(ref.dtype)

    even = lax.rem(sector, 2) == 0
    own_state = len(CHARGES) - 1 if travels else 0

    @pl.when(even)
    def _():
        run(own_state, travels)

    @pl.when(jnp.logical_not(even))
    def _():
        run(own_state, not travels)


def mix_into(width, tile, weights, wide_s, sums_s, out_ref):
    wide = padded(width)
    pitch = tile + 8
    wide_s[width * pitch :, :] = jnp.zeros_like(wide_s[width * pitch :, :])

    for at in range(0, tile, 2):
        value = doubled(
            jnp.concatenate(
                [wide_s[pl.ds(at + k, wide, stride=pitch), :] for k in range(2)], axis=1
            )
        )
        for index, weight in enumerate(weights):
            mixed = jnp.dot(weight[...], value, preferred_element_type=F32)[:wide]
            for k in range(2):
                sums_s[index, pl.ds(at + k, wide, stride=pitch), :] = mixed[:, k * tile : (k + 1) * tile]
    for index in range(len(weights)):
        for w in range(width):
            out_ref[index, :, w * tile : (w + 1) * tile] = sums_s[
                index, w * pitch : w * pitch + tile, :
            ].astype(BF16)


def unpack_wide(width, tile, read, wide_s, diag):
    def write(w, block):
        wide_s[w * (tile + 8) : w * (tile + 8) + tile, :] = block

    unpack_into(width, tile, read, write, diag)


def copy_wide(width, tile, source_ref, wide_s):
    for w in range(width):
        at = w * (tile + 8)
        wide_s[at : at + tile, :] = source_ref[w * tile : (w + 1) * tile, :].astype(F32)


def mix_own_kernel(width, tile, source_ref, weight_ref, out_ref, square_s, weight_s, wide_s, sums_s):
    weight_s[0] = weight_rows(weight_ref, width, 0, square_s, False)
    copy_wide(width, tile, source_ref, wide_s)
    mix_into(width, tile, [weight_s.at[0]], wide_s, sums_s, out_ref)


def mix_next_kernel(
    width, tile, near_ref, weight_ref, out_ref, square_s, weight_s, wide_s, sums_s, diag
):
    for k in range(2):
        weight_s[k] = weight_rows(weight_ref, width, k + 1, square_s, False)
    unpack_wide(width, tile, reader(near_ref), wide_s, diag)
    mix_into(width, tile, [weight_s.at[k] for k in range(2)], wide_s, sums_s, out_ref)


def mix_after_kernel(
    width, tile, far_ref, weight_ref, out_ref, square_s, weight_s, wide_s, sums_s, diag
):
    weight_s[0] = weight_rows(weight_ref, width, 3, square_s, False)
    inside = lax.axis_index("sec") + 2 < lax.axis_size("sec")

    def read(at, size):
        return jnp.where(inside, far_ref[at : at + size, :].astype(F32), 0.0)

    unpack_wide(width, tile, read, wide_s, diag)
    mix_into(width, tile, [weight_s.at[0]], wide_s, sums_s, out_ref)


def total(value):
    return jnp.sum(jnp.sum(value, axis=0, keepdims=True), axis=1, keepdims=True)


def put(stats, kind, lane_at, value):
    row, lane = iotas(stats.shape)
    return jnp.where((row == kind) & (lane == lane_at), value, stats)


def scaled(value):
    square = total(value * value)
    inverse = jnp.where(square > 0.0, lax.rsqrt(square), 0.0)
    return value * inverse, square * inverse


def right_products(width, tile, field, right_ref, out_ref, k):
    lanes = slice(k * tile, (k + 1) * tile)
    for pair in range(width // 2):
        at = pair * 2 * tile
        both = jnp.dot(field, right_ref[:, at : at + 2 * tile], preferred_element_type=F32).astype(BF16)
        for n in range(2):
            out_ref[at + n * tile : at + (n + 1) * tile, lanes] = both[:, n * tile : (n + 1) * tile]


def head_kernel(
    width, tile, dims_ref, guess_ref, own_ref, next_ref, after_ref,
    start_a, start_b, stats_ref, product_a, product_b,
):
    rights = [own_ref.at[0], next_ref.at[0], next_ref.at[1], after_ref.at[0]]
    sector = lax.axis_index("sec")
    rows, columns = live_limits(dims_ref, sector)
    row, lane = iotas((tile, tile))
    stats = jnp.zeros(stats_ref.shape, F32)
    for members, start_ref, product_ref in zip(GROUPS, (start_a, start_b), (product_a, product_b)):
        for k, p in enumerate(members):
            live = (row < rows) & (lane < columns[p])
            vector, norm = scaled(jnp.where(live, guess_ref[p], 0.0))
            start_ref[k] = vector
            stats = put(stats, 0, sector * len(CHARGES) + p, norm)
            right_products(width, tile, vector.astype(BF16), rights[p], product_ref, k)
    stats_ref[...] = stats


def bound_blocks(chunks, tile, packed_refs, environ_ref, out_ref, diag):
    segment = lax.axis_index("seg")
    start = chunks[0][0]

    @pl.when(segment == 0)
    def _():
        for w in range(sum(count for _, count in chunks)):
            out_ref[:, w * tile : (w + 1) * tile] = environ_ref[
                (start + w) * tile : (start + w + 1) * tile, :
            ]

    @pl.when(segment != 0)
    def _():
        for (first, count), ref in zip(chunks, packed_refs):

            def write(w, block, base=first - start):
                out_ref[:, (base + w) * tile : (base + w + 1) * tile] = block.astype(BF16)

            unpack_into(count, tile, reader(ref), write, diag)


def open_kernel(
    width, tile, dims_ref, environ_ref, early_in, middle_in, own_ref, next_ref, after_ref,
    start_a, start_b, norm_ref, product_a, product_b,
    bound_ref, image_ref, basis_ref, stats_ref, late_s, product_s, diag,
):
    chunks = chunks_of(width)
    bound_blocks(chunks[:-1], tile, (early_in, middle_in), environ_ref, bound_ref, diag)
    rows = bound_ref.shape[1]
    for group, product_ref in enumerate((product_a, product_b)):
        image_ref[group] = jnp.dot(bound_ref[...], product_ref[:rows, :], preferred_element_type=F32)

    @pl.when(lax.axis_index("seg") == 0)
    def _():
        first, count = chunks[-1]
        for w in range(count):
            late_s[:, w * tile : (w + 1) * tile] = environ_ref[
                (first + w) * tile : (first + w + 1) * tile, :
            ]
        lanczos_steps(
            width, tile, dims_ref, bound_ref, late_s, image_ref, own_ref, next_ref, after_ref,
            start_a, start_b, norm_ref, product_a, product_b, basis_ref, stats_ref, product_s,
        )


def lanczos_kernel(
    width, tile, dims_ref, packed_ref, early_ref, image_ref, own_ref, next_ref, after_ref,
    start_a, start_b, norm_ref, product_a, product_b, basis_in, stats_in, basis_ref, stats_ref,
    late_s, product_s, diag,
):
    segment = lax.axis_index("seg")

    @pl.when(segment == 0)
    def _():
        basis_ref[...] = basis_in[...]
        stats_ref[...] = stats_in[...]

    @pl.when(segment != 0)
    def _():
        def write(w, block):
            late_s[:, w * tile : (w + 1) * tile] = block.astype(BF16)

        unpack_into(chunks_of(width)[-1][1], tile, reader(packed_ref), write, diag)
        lanczos_steps(
            width, tile, dims_ref, early_ref, late_s, image_ref, own_ref, next_ref, after_ref,
            start_a, start_b, norm_ref, product_a, product_b, basis_ref, stats_ref, product_s,
        )


def lanczos_steps(
    width, tile, dims_ref, early_ref, late_s, image_ref, own_ref, next_ref, after_ref,
    start_a, start_b, norm_ref, product_a, product_b, basis_ref, stats_ref, product_s,
):
    states = len(CHARGES)
    sector = lax.axis_index("sec")
    last = chunks_of(width)[-1:]
    rows, columns = live_limits(dims_ref, sector)
    row, lane = iotas((tile, tile))
    rights = [own_ref.at[0], next_ref.at[0], next_ref.at[1], after_ref.at[0]]
    stats = norm_ref[...]
    starts = (start_a, start_b)
    split = last[0][0] * tile
    betas = [None] * states
    for j in range(LANCZOS):
        for group, members in enumerate(GROUPS):
            if j == 0:
                source = (product_a, product_b)[group]
                images = image_ref[group]
            else:
                source = product_s.at[group]
                for k, p in enumerate(members):
                    field = basis_ref[j - 1, p].astype(BF16)
                    right_products(width, tile, field, rights[p], source, k)
                images = jnp.dot(early_ref[...], source[:split, :], preferred_element_type=F32)
            images = images + jnp.dot(late_s[...], source[split:, :], preferred_element_type=F32)
            for k, p in enumerate(members):
                live = (row < rows) & (lane < columns[p])
                image = jnp.where(live, images[:, k * tile : (k + 1) * tile], 0.0)
                vector = starts[group][k] if j == 0 else basis_ref[j - 1, p]
                alpha = total(vector * image)
                image = image - alpha * vector
                if j > 0:
                    before = starts[group][k] if j == 1 else basis_ref[j - 2, p]
                    image = image - betas[p] * before
                following, beta = scaled(image)
                basis_ref[j, p] = following
                betas[p] = beta
                stats = put(stats, 1 + 2 * j, sector * states + p, alpha)
                stats = put(stats, 2 + 2 * j, sector * states + p, beta)
    stats_ref[...] = stats


def finish_kernel(
    entries, stats_ref, start_a, start_b, basis_ref, vector_ref, table_ref
):
    states = len(CHARGES)
    sector = lax.axis_index("sec")
    stats = stats_ref[0]
    for q in range(1, stats_ref.shape[0]):
        stats = stats + stats_ref[q]
    alphas = [stats[1 + 2 * j : 2 + 2 * j, :] for j in range(LANCZOS)]
    betas = [stats[2 + 2 * j : 3 + 2 * j, :] for j in range(LANCZOS)]

    def mean(left, right):
        products = left[0] * right[0]
        for x, y in zip(left[1:], right[1:]):
            products = products + x * y
        return jnp.sum(products, axis=1, keepdims=True) / entries

    def applied(vector):
        count = len(vector)
        image = []
        for k in range(count + 1):
            terms = []
            if k > 0:
                terms.append(betas[k - 1] * vector[k - 1])
            if k < count:
                terms.append(alphas[k] * vector[k])
            if k + 1 < count:
                terms.append(betas[k] * vector[k + 1])
            image.append(sum(terms[1:], terms[0]))
        return image

    residual = [stats[0:1, :]]
    previous = []
    table_row, table_column = iotas(table_ref.shape)
    table = jnp.zeros(table_ref.shape, F32)
    for j in range(LANCZOS):
        image = applied(residual)
        square = mean(residual, residual) + 1e-06
        alpha = mean(residual, image[: j + 1]) / square
        norm = jnp.sqrt(square)
        vector = [value / norm for value in residual]
        residual = [value / norm for value in image]
        for k in range(j + 1):
            residual[k] = residual[k] - alpha * vector[k]
        for k in range(j):
            residual[k] = residual[k] - norm * previous[k]
        previous = vector
        if j > 0:
            table = jnp.where((table_row == 1) & (table_column == j - 1), norm, table)
        table = jnp.where((table_row == 0) & (table_column == j), alpha, table)
    norm = jnp.sqrt(mean(residual, residual) + 1e-06)
    vector = [value / norm for value in residual]
    table = jnp.where((table_row == 1) & (table_column == LANCZOS - 1), norm, table)
    table_ref[...] = table
    lane = lax.broadcasted_iota(jnp.int32, (1, stats.shape[1]), 1)
    starts = {p: ref[k] for members, ref in zip(GROUPS, (start_a, start_b)) for k, p in enumerate(members)}
    for p in range(states):
        value = None
        here = lane == sector * states + p
        for k in range(LANCZOS + 1):
            weight = jnp.sum(jnp.where(here, vector[k], 0.0), axis=1, keepdims=True)
            term = weight * (starts[p] if k == 0 else basis_ref[k - 1, p])
            value = term if value is None else value + term
        vector_ref[p] = value


def smem():
    return pl.BlockSpec(memory_space=pltpu.SMEM)


def vmem():
    return pl.BlockSpec(memory_space=pltpu.VMEM)


def call(name, kernel, scalars, arrays, outs, scratch, limit, micros):
    many = isinstance(outs, (tuple, list))
    return pl.pallas_call(
        kernel,
        out_shape=outs,
        in_specs=[smem()] * len(scalars) + [vmem()] * len(arrays),
        out_specs=[vmem()] * len(outs) if many else vmem(),
        scratch_shapes=scratch,
        compiler_params=pltpu.CompilerParams(vmem_limit_bytes=limit * MIB),
        name=name,
        cost_estimate=pl.CostEstimate(
            flops=int(micros * 1.1e9), bytes_accessed=0, transcendentals=0
        ),
    )(*scalars, *arrays)


def shift_by(count, steps):
    return [(source, (source + steps) % count) for source in range(count)]


def gathered(value, axis):
    count = lax.axis_size(axis)
    return lax.all_to_all(jnp.broadcast_to(value, (count,) + value.shape), axis, 0, 0)


def on_device(left_env, right_env, site_tensors, mpo, boundary_mpo, guess, sector_dims):
    width, tile = left_env.shape[2], left_env.shape[-1]
    half = tile // 2
    wide = padded(width)
    states = len(CHARGES)
    sector_count = sector_dims.shape[0]
    sectors = lax.axis_size("sec")
    segments = lax.axis_size("seg")
    prows = packed_rows(width, tile)
    drows = prows - width * half
    packed = jax.ShapeDtypeStruct((prows, tile), BF16)
    parts = chunks_of(width)

    def packed_parts(dtype):
        return [jax.ShapeDtypeStruct((packed_rows(count, tile), tile), dtype) for _, count in parts]

    def mixed(count):
        return jax.ShapeDtypeStruct((count, tile, width * tile), BF16)

    environ = left_env.reshape(width * tile, tile)
    right = right_env.reshape(width * tile, tile)
    site = site_tensors[0, 0, :, 0]
    site_weights = jnp.transpose(mpo[0, 0], (0, 2, 1)).reshape(width * states, width)
    bound_weights = jnp.transpose(boundary_mpo[0], (0, 2, 1)).reshape(width * states, width)

    sector = lax.axis_index("sec")
    swap = [(q, q ^ 1) for q in range(sectors)]
    up_two = shift_by(sectors, 2)
    down_two = shift_by(sectors, -2)
    onward = shift_by(segments, 1)
    diag = pltpu.VMEM((drows, tile), F32)

    def mix_scratch(count):
        return [
            pltpu.VMEM((tile, tile), F32),
            pltpu.VMEM((count, packed_height(width), 2 * wide), BF16),
            pltpu.VMEM((wide * (tile + 8), tile), F32),
            pltpu.VMEM((count, wide * (tile + 8), tile), F32),
        ]

    right_packed = call(
        "pack_right", functools.partial(pack_kernel, width, tile), [], [right], packed,
        [diag], 6, 1,
    )
    right_far = lax.ppermute(right_packed, "sec", down_two)
    far_environ = lax.ppermute(environ, "sec", swap)
    far_site = lax.ppermute(site, "sec", swap)
    fold_scratch = [
        pltpu.VMEM((tile, 3 * tile), BF16),
        pltpu.VMEM((3, tile, tile), BF16),
        pltpu.VMEM((tile, tile), F32),
        pltpu.VMEM((3, packed_height(width), 2 * wide), BF16),
        pltpu.VMEM((3, width // 2 * tile, 2 * tile), BF16),
        pltpu.VMEM((3, wide * (half + 8), tile), F32),
        pltpu.VMEM((3, drows, tile), F32),
        pltpu.VMEM((wide * (half + 8), tile), F32),
        pltpu.VMEM((drows, tile), F32),
    ]
    outgoing = call(
        "fold_up", functools.partial(fold_kernel, width, tile, True),
        [sector_dims], [environ, site, far_environ, far_site, site_weights], packed_parts(BF16),
        fold_scratch, 20, 12,
    )
    early_arrived = lax.ppermute(outgoing[0], "sec", up_two)
    far_environ, outgoing = lax.optimization_barrier((far_environ, outgoing))
    kept = call(
        "fold_own", functools.partial(fold_kernel, width, tile, False),
        [sector_dims], [environ, site, far_environ, far_site, site_weights], packed_parts(F32),
        fold_scratch, 20, 0.1,
    )
    kept, middle_outgoing = lax.optimization_barrier((kept, outgoing[1]))
    middle_arrived = lax.ppermute(middle_outgoing, "sec", up_two)
    kept, right = lax.optimization_barrier((kept, right))
    own_mixed = call(
        "mix_own", functools.partial(mix_own_kernel, width, tile), [], [right, bound_weights],
        mixed(1), mix_scratch(1), 12, 1,
    )
    own_mixed, right_far, late_outgoing = lax.optimization_barrier((own_mixed, right_far, outgoing[2]))
    late_arrived = lax.ppermute(late_outgoing, "sec", up_two)
    passed_on = jnp.where(sector + 2 < sectors, right_far, jnp.zeros_like(right_far))
    passed_on = jnp.where(lax.rem(sector, 2) == 0, passed_on, right_packed)
    right_near = lax.ppermute(passed_on, "sec", swap)

    def carried(stays, comes):
        return (stays + jnp.where(sector >= 2, comes.astype(F32), 0.0)).astype(BF16)

    early = carried(kept[0], early_arrived)
    early_bound = lax.ppermute(early, "seg", onward)
    early, right_far = lax.optimization_barrier((early, right_far))
    after_mixed = call(
        "mix_after", functools.partial(mix_after_kernel, width, tile), [],
        [right_far, bound_weights], mixed(1), mix_scratch(1) + [diag], 12, 2,
    )
    middle_arrived, after_mixed = lax.optimization_barrier((middle_arrived, after_mixed))
    middle = carried(kept[1], middle_arrived)
    middle_bound = lax.ppermute(middle, "seg", onward)
    middle, right_near = lax.optimization_barrier((middle, right_near))
    next_mixed = call(
        "mix_next", functools.partial(mix_next_kernel, width, tile), [],
        [right_near, bound_weights], mixed(2), mix_scratch(2) + [diag], 16, 3,
    )
    late_arrived, next_mixed = lax.optimization_barrier((late_arrived, next_mixed))
    late = carried(kept[2], late_arrived)
    late_bound = lax.ppermute(late, "seg", onward)
    late, next_mixed, after_mixed = lax.optimization_barrier((late, next_mixed, after_mixed))
    start_a, start_b, norms, products_a, products_b = call(
        "head", functools.partial(head_kernel, width, tile),
        [sector_dims], [guess[0, :, 0], own_mixed, next_mixed, after_mixed],
        [jax.ShapeDtypeStruct((2, tile, tile), F32)] * 2
        + [jax.ShapeDtypeStruct((16, 128), F32)]
        + [jax.ShapeDtypeStruct((width * tile, 2 * tile), BF16)] * 2,
        [], 14, 0.2,
    )
    new_env = call(
        "unpack_env", functools.partial(unpack_kernel, width, tile), [], [early, middle, late],
        jax.ShapeDtypeStruct((width * tile, tile), BF16), [diag], 6, 2,
    )
    middle_bound, new_env = lax.optimization_barrier((middle_bound, new_env))
    steps = [own_mixed, next_mixed, after_mixed, start_a, start_b, norms, products_a, products_b]
    results = [
        jax.ShapeDtypeStruct((LANCZOS, states, tile, tile), F32),
        jax.ShapeDtypeStruct((16, 128), F32),
    ]
    steps_scratch = [
        pltpu.VMEM((tile, parts[-1][1] * tile), BF16),
        pltpu.VMEM((len(GROUPS), width * tile, 2 * tile), BF16),
        diag,
    ]
    bound, image, basis, stats = call(
        "open", functools.partial(open_kernel, width, tile),
        [sector_dims], [environ, early_bound, middle_bound] + steps,
        [
            jax.ShapeDtypeStruct((tile, parts[-1][0] * tile), BF16),
            jax.ShapeDtypeStruct((len(GROUPS), tile, 2 * tile), F32),
        ]
        + results,
        steps_scratch, 24, 1,
    )
    late_bound, bound = lax.optimization_barrier((late_bound, bound))
    basis, stats = call(
        "lanczos", functools.partial(lanczos_kernel, width, tile),
        [sector_dims], [late_bound, bound, image] + steps + [basis, stats], results,
        steps_scratch, 24, 12,
    )
    stats = gathered(stats, "sec")
    entries = float(states * sector_count * tile * tile)
    vector, table = call(
        "finish", functools.partial(finish_kernel, entries), [], [stats, start_a, start_b, basis],
        (
            jax.ShapeDtypeStruct((states, tile, tile), F32),
            jax.ShapeDtypeStruct((2, LANCZOS), F32),
        ),
        [], 6, 2,
    )
    return new_env.reshape(left_env.shape), vector[None, :, None], jnp.transpose(table)[None]


def solution(mesh):
    placed = (
        P("seg", "sec", None, None, None),
        P("seg", "sec", None, None, None),
        P("seg", None, None, "sec", None, None),
        P("seg", None, None, None, None),
        P("seg", None, None, None),
        P("seg", None, "sec", None, None),
        P(),
    )
    return jax.shard_map(
        on_device,
        mesh=mesh,
        in_specs=placed,
        out_specs=(
            P("seg", "sec", None, None, None),
            P("seg", None, "sec", None, None),
            P("seg", None, None),
        ),
        check_vma=False,
    )
```

```python
import functools

import jax
import jax.numpy as jnp
from jax import lax
from jax.experimental import pallas as pl
from jax.experimental.pallas import tpu as pltpu
from jax.sharding import PartitionSpec as P

LANCZOS = 4
CHARGES = (0, 1, 1, 2)
GROUPS = ((0, 3), (1, 2))
F32 = jnp.float32
BF16 = jnp.bfloat16
MIB = 1024 * 1024


def padded(count):
    return -(-count // 8) * 8


def packed_height(count):
    return -(-count // 16) * 16


def packed_rows(count, tile):
    return count * tile // 2 + packed_height(count)


def chunks_of(width):
    one = width // 6 * 2
    two = (width - one) // 4 * 2
    return (0, one), (one, two), (one + two, width - one - two)


def iotas(shape):
    return lax.broadcasted_iota(jnp.int32, shape, 0), lax.broadcasted_iota(jnp.int32, shape, 1)


def pack_block(block):
    tile = block.shape[0]
    half = tile // 2
    top, low = block[:half], block[half:]
    row, lane = iotas((half, tile))
    turned = pltpu.roll(low, half, 1)
    folded = jnp.where((lane < half) & (row > lane), turned, top)
    diagonal = jnp.sum(jnp.where(lane == row + half, low, 0.0), axis=0, keepdims=True)
    return folded, diagonal


def unpack_block(folded, diagonal):
    half, tile = folded.shape
    row, lane = iotas((half, tile))
    rolled = pltpu.roll(folded, half, 1)
    turned = jnp.transpose(jnp.concatenate([folded, rolled], axis=0))
    top = jnp.where((lane < half) & (row > lane), turned[:half], folded)
    low = jnp.where((lane >= half) & (row > lane - half), rolled, turned[half:])
    low = jnp.where(lane == row + half, diagonal, low)
    return jnp.concatenate([top, low], axis=0)


def partner_of(sector):
    return sector + 1 - 2 * lax.rem(sector, 2)


def live_limits(dims_ref, sector):
    count = dims_ref.shape[0]
    rows = dims_ref[sector]
    columns = []
    for charge in CHARGES:
        target = sector + charge
        columns.append(jnp.where(target < count, dims_ref[jnp.minimum(target, count - 1)], 0))
    return rows, columns


def weight_rows(weight_ref, width, p, square, turned):
    wide = padded(width)
    square[...] = jnp.zeros_like(square)
    square[:width, :width] = weight_ref[pl.ds(p, width, stride=len(CHARGES)), :]
    value = square[...]
    if turned:
        value = jnp.transpose(value)
    high = value.astype(BF16).astype(F32)
    joined = (high + pltpu.roll(value - high, wide, 1)).astype(BF16)
    return joined[: packed_height(width), : 2 * wide]


def doubled(value):
    return jnp.concatenate([value, value], axis=0).astype(BF16)


def pack_kernel(width, tile, source_ref, out_ref, diag):
    half = tile // 2
    diag[...] = jnp.zeros_like(diag)
    for w in range(width):
        folded, diagonal = pack_block(source_ref[w * tile : (w + 1) * tile, :].astype(F32))
        out_ref[w * half : (w + 1) * half, :] = folded.astype(BF16)
        diag[w : w + 1, :] = diagonal
    out_ref[width * half :, :] = diag[...].astype(BF16)


def unpack_into(count, tile, read, write, diag):
    half = tile // 2
    size = packed_height(count)
    diag[:size, :] = read(count * half, size)
    for w in range(count):
        write(w, unpack_block(read(w * half, half), diag[w : w + 1, :]))


def reader(ref):
    return lambda at, size: ref[at : at + size, :].astype(F32)


def unpack_kernel(width, tile, *refs):
    *part_refs, out_ref, diag = refs
    for (first, count), ref in zip(chunks_of(width), part_refs):

        def write(w, block, first=first):
            out_ref[(first + w) * tile : (first + w + 1) * tile, :] = block.astype(BF16)

        unpack_into(count, tile, reader(ref), write, diag)


def fold_kernel(
    width, tile, travels, dims_ref, environ_ref, site_ref, far_environ_ref, far_site_ref, weight_ref, *refs
):
    part_refs = refs[: len(chunks_of(width))]
    joined_s, turned_s, square_s, weight_s, half_s, packed_s, diag_s, sums_s, diag_sums_s = refs[
        len(part_refs) :
    ]
    half = tile // 2
    pitch = half + 8
    wide = padded(width)
    sector = lax.axis_index("sec")
    partner = partner_of(sector)
    row, lane = iotas((tile, tile))

    def run(own_state, with_partner):
        rows, columns = live_limits(dims_ref, sector)
        live = (row < rows) & (lane < columns[own_state])
        sites = [jnp.where(live, site_ref[own_state].astype(F32), 0.0)]
        states = [own_state]
        if with_partner:
            rows, columns = live_limits(dims_ref, partner)
            for k in range(2):
                live = (row < rows) & (lane < columns[k + 1])
                sites.append(jnp.where(live, far_site_ref[k + 1].astype(F32), 0.0))
                states.append(k + 1)
        parts = len(states)
        for n in range(parts):
            joined_s[:, n * tile : (n + 1) * tile] = sites[n].astype(BF16)
            turned_s[n] = jnp.transpose(sites[n]).astype(BF16)
            weight_s[n] = weight_rows(weight_ref, width, states[n], square_s, True)
            packed_s[n, width * pitch :, :] = jnp.zeros(((wide - width) * pitch, tile), F32)
            diag_s[n] = jnp.zeros_like(diag_s[n])

        for pair in range(width // 2):
            at = slice(pair * tile, (pair + 1) * tile)
            for k in range(2):
                here = slice((pair * 2 + k) * tile, (pair * 2 + k + 1) * tile)
                blocks = [
                    jnp.dot(environ_ref[here, :], joined_s[:, :tile], preferred_element_type=F32)
                ]
                if with_partner:
                    both = jnp.dot(
                        far_environ_ref[here, :], joined_s[:, tile:], preferred_element_type=F32
                    )
                    blocks += [both[:, :tile], both[:, tile:]]
                for n in range(parts):
                    half_s[n, at, k * tile : (k + 1) * tile] = blocks[n].astype(BF16)
            for n in range(parts):
                both = jnp.dot(turned_s[n], half_s[n, at, :], preferred_element_type=F32)
                for k in range(2):
                    w = pair * 2 + k
                    folded, diagonal = pack_block(both[:, k * tile : (k + 1) * tile])
                    packed_s[n, w * pitch : w * pitch + half, :] = folded
                    diag_s[n, w : w + 1, :] = diagonal

        def mixed(inputs):
            value = None
            for n in range(parts):
                term = jnp.dot(weight_s[n], doubled(inputs[n]), preferred_element_type=F32)
                value = term if value is None else value + term
            return value[:wide]

        for at in range(0, half, 2):
            value = mixed([
                jnp.concatenate(
                    [packed_s[n, pl.ds(at + k, wide, stride=pitch), :] for k in range(2)], axis=1
                )
                for n in range(parts)
            ])
            for k in range(2):
                sums_s[pl.ds(at + k, wide, stride=pitch), :] = value[:, k * tile : (k + 1) * tile]
        diag_sums_s[...] = jnp.zeros_like(diag_sums_s)
        diag_sums_s[:wide, :] = mixed([diag_s[n, :wide] for n in range(parts)])
        for (first, count), ref in zip(chunks_of(width), part_refs):
            for w in range(count):
                at = (first + w) * pitch
                ref[w * half : (w + 1) * half, :] = sums_s[at : at + half, :].astype(ref.dtype)
            rows = packed_height(count)
            ref[count * half :, :] = diag_sums_s[first : first + rows, :].astype(ref.dtype)

    even = lax.rem(sector, 2) == 0
    own_state = len(CHARGES) - 1 if travels else 0

    @pl.when(even)
    def _():
        run(own_state, travels)

    @pl.when(jnp.logical_not(even))
    def _():
        run(own_state, not travels)


def mix_into(width, tile, weights, wide_s, sums_s, out_ref):
    wide = padded(width)
    pitch = tile + 8
    wide_s[width * pitch :, :] = jnp.zeros_like(wide_s[width * pitch :, :])

    for at in range(0, tile, 2):
        value = doubled(
            jnp.concatenate(
                [wide_s[pl.ds(at + k, wide, stride=pitch), :] for k in range(2)], axis=1
            )
        )
        for index, weight in enumerate(weights):
            mixed = jnp.dot(weight[...], value, preferred_element_type=F32)[:wide]
            for k in range(2):
                sums_s[index, pl.ds(at + k, wide, stride=pitch), :] = mixed[:, k * tile : (k + 1) * tile]
    for index in range(len(weights)):
        for w in range(width):
            out_ref[index, :, w * tile : (w + 1) * tile] = sums_s[
                index, w * pitch : w * pitch + tile, :
            ].astype(BF16)


def unpack_wide(width, tile, read, wide_s, diag):
    def write(w, block):
        wide_s[w * (tile + 8) : w * (tile + 8) + tile, :] = block

    unpack_into(width, tile, read, write, diag)


def copy_wide(width, tile, source_ref, wide_s):
    for w in range(width):
        at = w * (tile + 8)
        wide_s[at : at + tile, :] = source_ref[w * tile : (w + 1) * tile, :].astype(F32)


def mix_own_kernel(width, tile, source_ref, weight_ref, out_ref, square_s, weight_s, wide_s, sums_s):
    weight_s[0] = weight_rows(weight_ref, width, 0, square_s, False)
    copy_wide(width, tile, source_ref, wide_s)
    mix_into(width, tile, [weight_s.at[0]], wide_s, sums_s, out_ref)


def mix_next_kernel(
    width, tile, near_ref, weight_ref, out_ref, square_s, weight_s, wide_s, sums_s, diag
):
    for k in range(2):
        weight_s[k] = weight_rows(weight_ref, width, k + 1, square_s, False)
    unpack_wide(width, tile, reader(near_ref), wide_s, diag)
    mix_into(width, tile, [weight_s.at[k] for k in range(2)], wide_s, sums_s, out_ref)


def mix_after_kernel(
    width, tile, far_ref, weight_ref, out_ref, square_s, weight_s, wide_s, sums_s, diag
):
    weight_s[0] = weight_rows(weight_ref, width, 3, square_s, False)
    inside = lax.axis_index("sec") + 2 < lax.axis_size("sec")

    def read(at, size):
        return jnp.where(inside, far_ref[at : at + size, :].astype(F32), 0.0)

    unpack_wide(width, tile, read, wide_s, diag)
    mix_into(width, tile, [weight_s.at[0]], wide_s, sums_s, out_ref)


def total(value):
    return jnp.sum(jnp.sum(value, axis=0, keepdims=True), axis=1, keepdims=True)


def put(stats, kind, lane_at, value):
    row, lane = iotas(stats.shape)
    return jnp.where((row == kind) & (lane == lane_at), value, stats)


def scaled(value):
    square = total(value * value)
    inverse = jnp.where(square > 0.0, lax.rsqrt(square), 0.0)
    return value * inverse, square * inverse


def right_products(width, tile, field, right_ref, out_ref, k):
    lanes = slice(k * tile, (k + 1) * tile)
    for pair in range(width // 2):
        at = pair * 2 * tile
        both = jnp.dot(field, right_ref[:, at : at + 2 * tile], preferred_element_type=F32).astype(BF16)
        for n in range(2):
            out_ref[at + n * tile : at + (n + 1) * tile, lanes] = both[:, n * tile : (n + 1) * tile]


def head_kernel(
    width, tile, dims_ref, guess_ref, own_ref, next_ref, after_ref,
    start_a, start_b, stats_ref, product_a, product_b,
):
    rights = [own_ref.at[0], next_ref.at[0], next_ref.at[1], after_ref.at[0]]
    sector = lax.axis_index("sec")
    rows, columns = live_limits(dims_ref, sector)
    row, lane = iotas((tile, tile))
    stats = jnp.zeros(stats_ref.shape, F32)
    for members, start_ref, product_ref in zip(GROUPS, (start_a, start_b), (product_a, product_b)):
        for k, p in enumerate(members):
            live = (row < rows) & (lane < columns[p])
            vector, norm = scaled(jnp.where(live, guess_ref[p], 0.0))
            start_ref[k] = vector
            stats = put(stats, 0, sector * len(CHARGES) + p, norm)
            right_products(width, tile, vector.astype(BF16), rights[p], product_ref, k)
    stats_ref[...] = stats


def bound_blocks(chunks, tile, packed_refs, environ_ref, out_ref, diag):
    segment = lax.axis_index("seg")
    start = chunks[0][0]

    @pl.when(segment == 0)
    def _():
        for w in range(sum(count for _, count in chunks)):
            out_ref[:, w * tile : (w + 1) * tile] = environ_ref[
                (start + w) * tile : (start + w + 1) * tile, :
            ]

    @pl.when(segment != 0)
    def _():
        for (first, count), ref in zip(chunks, packed_refs):

            def write(w, block, base=first - start):
                out_ref[:, (base + w) * tile : (base + w + 1) * tile] = block.astype(BF16)

            unpack_into(count, tile, reader(ref), write, diag)


def open_kernel(
    width, tile, dims_ref, environ_ref, early_in, middle_in, own_ref, next_ref, after_ref,
    start_a, start_b, norm_ref, product_a, product_b,
    bound_ref, image_ref, basis_ref, stats_ref, late_s, product_s, diag,
):
    chunks = chunks_of(width)
    bound_blocks(chunks[:-1], tile, (early_in, middle_in), environ_ref, bound_ref, diag)
    rows = bound_ref.shape[1]
    for group, product_ref in enumerate((product_a, product_b)):
        image_ref[group] = jnp.dot(bound_ref[...], product_ref[:rows, :], preferred_element_type=F32)

    @pl.when(lax.axis_index("seg") == 0)
    def _():
        first, count = chunks[-1]
        for w in range(count):
            late_s[:, w * tile : (w + 1) * tile] = environ_ref[
                (first + w) * tile : (first + w + 1) * tile, :
            ]
        lanczos_steps(
            width, tile, dims_ref, bound_ref, late_s, image_ref, own_ref, next_ref, after_ref,
            start_a, start_b, norm_ref, product_a, product_b, basis_ref, stats_ref, product_s,
        )


def lanczos_kernel(
    width, tile, dims_ref, packed_ref, early_ref, image_ref, own_ref, next_ref, after_ref,
    start_a, start_b, norm_ref, product_a, product_b, stats_in, basis_ref, stats_ref,
    late_s, product_s, diag,
):
    segment = lax.axis_index("seg")

    @pl.when(segment == 0)
    def _():
        stats_ref[...] = stats_in[...]

    @pl.when(segment != 0)
    def _():
        def write(w, block):
            late_s[:, w * tile : (w + 1) * tile] = block.astype(BF16)

        unpack_into(chunks_of(width)[-1][1], tile, reader(packed_ref), write, diag)
        lanczos_steps(
            width, tile, dims_ref, early_ref, late_s, image_ref, own_ref, next_ref, after_ref,
            start_a, start_b, norm_ref, product_a, product_b, basis_ref, stats_ref, product_s,
        )


def lanczos_steps(
    width, tile, dims_ref, early_ref, late_s, image_ref, own_ref, next_ref, after_ref,
    start_a, start_b, norm_ref, product_a, product_b, basis_ref, stats_ref, product_s,
):
    states = len(CHARGES)
    sector = lax.axis_index("sec")
    last = chunks_of(width)[-1:]
    rows, columns = live_limits(dims_ref, sector)
    row, lane = iotas((tile, tile))
    rights = [own_ref.at[0], next_ref.at[0], next_ref.at[1], after_ref.at[0]]
    stats = norm_ref[...]
    starts = (start_a, start_b)
    split = last[0][0] * tile
    betas = [None] * states
    for j in range(LANCZOS):
        for group, members in enumerate(GROUPS):
            if j == 0:
                source = (product_a, product_b)[group]
                images = image_ref[group]
            else:
                source = product_s.at[group]
                for k, p in enumerate(members):
                    field = basis_ref[j - 1, p].astype(BF16)
                    right_products(width, tile, field, rights[p], source, k)
                images = jnp.dot(early_ref[...], source[:split, :], preferred_element_type=F32)
            images = images + jnp.dot(late_s[...], source[split:, :], preferred_element_type=F32)
            for k, p in enumerate(members):
                live = (row < rows) & (lane < columns[p])
                image = jnp.where(live, images[:, k * tile : (k + 1) * tile], 0.0)
                vector = starts[group][k] if j == 0 else basis_ref[j - 1, p]
                alpha = total(vector * image)
                image = image - alpha * vector
                if j > 0:
                    before = starts[group][k] if j == 1 else basis_ref[j - 2, p]
                    image = image - betas[p] * before
                following, beta = scaled(image)
                basis_ref[j, p] = following
                betas[p] = beta
                stats = put(stats, 1 + 2 * j, sector * states + p, alpha)
                stats = put(stats, 2 + 2 * j, sector * states + p, beta)
    stats_ref[...] = stats


def finish_kernel(
    entries, stats_ref, start_a, start_b, first_basis_ref, basis_ref, vector_ref, table_ref
):
    states = len(CHARGES)
    sector = lax.axis_index("sec")
    stats = stats_ref[0]
    for q in range(1, stats_ref.shape[0]):
        stats = stats + stats_ref[q]
    alphas = [stats[1 + 2 * j : 2 + 2 * j, :] for j in range(LANCZOS)]
    betas = [stats[2 + 2 * j : 3 + 2 * j, :] for j in range(LANCZOS)]

    def mean(left, right):
        products = left[0] * right[0]
        for x, y in zip(left[1:], right[1:]):
            products = products + x * y
        return jnp.sum(products, axis=1, keepdims=True) / entries

    def applied(vector):
        count = len(vector)
        image = []
        for k in range(count + 1):
            terms = []
            if k > 0:
                terms.append(betas[k - 1] * vector[k - 1])
            if k < count:
                terms.append(alphas[k] * vector[k])
            if k + 1 < count:
                terms.append(betas[k] * vector[k + 1])
            image.append(sum(terms[1:], terms[0]))
        return image

    residual = [stats[0:1, :]]
    previous = []
    table_row, table_column = iotas(table_ref.shape)
    table = jnp.zeros(table_ref.shape, F32)
    for j in range(LANCZOS):
        image = applied(residual)
        square = mean(residual, residual) + 1e-06
        alpha = mean(residual, image[: j + 1]) / square
        norm = jnp.sqrt(square)
        vector = [value / norm for value in residual]
        residual = [value / norm for value in image]
        for k in range(j + 1):
            residual[k] = residual[k] - alpha * vector[k]
        for k in range(j):
            residual[k] = residual[k] - norm * previous[k]
        previous = vector
        if j > 0:
            table = jnp.where((table_row == 1) & (table_column == j - 1), norm, table)
        table = jnp.where((table_row == 0) & (table_column == j), alpha, table)
    norm = jnp.sqrt(mean(residual, residual) + 1e-06)
    vector = [value / norm for value in residual]
    table = jnp.where((table_row == 1) & (table_column == LANCZOS - 1), norm, table)
    table_ref[...] = table
    lane = lax.broadcasted_iota(jnp.int32, (1, stats.shape[1]), 1)
    starts = {p: ref[k] for members, ref in zip(GROUPS, (start_a, start_b)) for k, p in enumerate(members)}
    weights = {}
    for p in range(states):
        here = lane == sector * states + p
        for k in range(LANCZOS + 1):
            weights[p, k] = jnp.sum(jnp.where(here, vector[k], 0.0), axis=1, keepdims=True)

    def write(source):
        for p in range(states):
            value = weights[p, 0] * starts[p]
            for k in range(1, LANCZOS + 1):
                value = value + weights[p, k] * source[k - 1, p]
            vector_ref[p] = value

    segment = lax.axis_index("seg")

    @pl.when(segment == 0)
    def _():
        write(first_basis_ref)

    @pl.when(segment != 0)
    def _():
        write(basis_ref)


def smem():
    return pl.BlockSpec(memory_space=pltpu.SMEM)


def vmem():
    return pl.BlockSpec(memory_space=pltpu.VMEM)


def call(name, kernel, scalars, arrays, outs, scratch, limit, micros):
    many = isinstance(outs, (tuple, list))
    return pl.pallas_call(
        kernel,
        out_shape=outs,
        in_specs=[smem()] * len(scalars) + [vmem()] * len(arrays),
        out_specs=[vmem()] * len(outs) if many else vmem(),
        scratch_shapes=scratch,
        compiler_params=pltpu.CompilerParams(vmem_limit_bytes=limit * MIB),
        name=name,
        cost_estimate=pl.CostEstimate(
            flops=int(micros * 1.1e9), bytes_accessed=0, transcendentals=0
        ),
    )(*scalars, *arrays)


def shift_by(count, steps):
    return [(source, (source + steps) % count) for source in range(count)]


def gathered(value, axis):
    count = lax.axis_size(axis)
    return lax.all_to_all(jnp.broadcast_to(value, (count,) + value.shape), axis, 0, 0)


def on_device(left_env, right_env, site_tensors, mpo, boundary_mpo, guess, sector_dims):
    width, tile = left_env.shape[2], left_env.shape[-1]
    half = tile // 2
    wide = padded(width)
    states = len(CHARGES)
    sector_count = sector_dims.shape[0]
    sectors = lax.axis_size("sec")
    segments = lax.axis_size("seg")
    prows = packed_rows(width, tile)
    drows = prows - width * half
    packed = jax.ShapeDtypeStruct((prows, tile), BF16)
    parts = chunks_of(width)

    def packed_parts(dtype):
        return [jax.ShapeDtypeStruct((packed_rows(count, tile), tile), dtype) for _, count in parts]

    def mixed(count):
        return jax.ShapeDtypeStruct((count, tile, width * tile), BF16)

    environ = left_env.reshape(width * tile, tile)
    right = right_env.reshape(width * tile, tile)
    site = site_tensors[0, 0, :, 0]
    site_weights = jnp.transpose(mpo[0, 0], (0, 2, 1)).reshape(width * states, width)
    bound_weights = jnp.transpose(boundary_mpo[0], (0, 2, 1)).reshape(width * states, width)

    sector = lax.axis_index("sec")
    swap = [(q, q ^ 1) for q in range(sectors)]
    up_two = shift_by(sectors, 2)
    down_two = shift_by(sectors, -2)
    onward = shift_by(segments, 1)
    diag = pltpu.VMEM((drows, tile), F32)

    def mix_scratch(count):
        return [
            pltpu.VMEM((tile, tile), F32),
            pltpu.VMEM((count, packed_height(width), 2 * wide), BF16),
            pltpu.VMEM((wide * (tile + 8), tile), F32),
            pltpu.VMEM((count, wide * (tile + 8), tile), F32),
        ]

    right_packed = call(
        "pack_right", functools.partial(pack_kernel, width, tile), [], [right], packed,
        [diag], 6, 1,
    )
    right_far = lax.ppermute(right_packed, "sec", down_two)
    far_environ = lax.ppermute(environ, "sec", swap)
    far_site = lax.ppermute(site, "sec", swap)
    fold_scratch = [
        pltpu.VMEM((tile, 3 * tile), BF16),
        pltpu.VMEM((3, tile, tile), BF16),
        pltpu.VMEM((tile, tile), F32),
        pltpu.VMEM((3, packed_height(width), 2 * wide), BF16),
        pltpu.VMEM((3, width // 2 * tile, 2 * tile), BF16),
        pltpu.VMEM((3, wide * (half + 8), tile), F32),
        pltpu.VMEM((3, drows, tile), F32),
        pltpu.VMEM((wide * (half + 8), tile), F32),
        pltpu.VMEM((drows, tile), F32),
    ]
    outgoing = call(
        "fold_up", functools.partial(fold_kernel, width, tile, True),
        [sector_dims], [environ, site, far_environ, far_site, site_weights], packed_parts(BF16),
        fold_scratch, 20, 12,
    )
    early_arrived = lax.ppermute(outgoing[0], "sec", up_two)
    far_environ, outgoing = lax.optimization_barrier((far_environ, outgoing))
    kept = call(
        "fold_own", functools.partial(fold_kernel, width, tile, False),
        [sector_dims], [environ, site, far_environ, far_site, site_weights], packed_parts(F32),
        fold_scratch, 20, 0.1,
    )
    kept, middle_outgoing = lax.optimization_barrier((kept, outgoing[1]))
    middle_arrived = lax.ppermute(middle_outgoing, "sec", up_two)
    kept, right = lax.optimization_barrier((kept, right))
    own_mixed = call(
        "mix_own", functools.partial(mix_own_kernel, width, tile), [], [right, bound_weights],
        mixed(1), mix_scratch(1), 12, 1,
    )
    own_mixed, right_far, late_outgoing = lax.optimization_barrier((own_mixed, right_far, outgoing[2]))
    late_arrived = lax.ppermute(late_outgoing, "sec", up_two)
    passed_on = jnp.where(sector + 2 < sectors, right_far, jnp.zeros_like(right_far))
    passed_on = jnp.where(lax.rem(sector, 2) == 0, passed_on, right_packed)
    right_near = lax.ppermute(passed_on, "sec", swap)

    def carried(stays, comes):
        return (stays + jnp.where(sector >= 2, comes.astype(F32), 0.0)).astype(BF16)

    early = carried(kept[0], early_arrived)
    early_bound = lax.ppermute(early, "seg", onward)
    early, right_far = lax.optimization_barrier((early, right_far))
    after_mixed = call(
        "mix_after", functools.partial(mix_after_kernel, width, tile), [],
        [right_far, bound_weights], mixed(1), mix_scratch(1) + [diag], 12, 2,
    )
    middle_arrived, after_mixed = lax.optimization_barrier((middle_arrived, after_mixed))
    middle = carried(kept[1], middle_arrived)
    middle_bound = lax.ppermute(middle, "seg", onward)
    middle, right_near = lax.optimization_barrier((middle, right_near))
    next_mixed = call(
        "mix_next", functools.partial(mix_next_kernel, width, tile), [],
        [right_near, bound_weights], mixed(2), mix_scratch(2) + [diag], 16, 3,
    )
    late_arrived, next_mixed = lax.optimization_barrier((late_arrived, next_mixed))
    late = carried(kept[2], late_arrived)
    late_bound = lax.ppermute(late, "seg", onward)
    late, next_mixed, after_mixed = lax.optimization_barrier((late, next_mixed, after_mixed))
    start_a, start_b, norms, products_a, products_b = call(
        "head", functools.partial(head_kernel, width, tile),
        [sector_dims], [guess[0, :, 0], own_mixed, next_mixed, after_mixed],
        [jax.ShapeDtypeStruct((2, tile, tile), F32)] * 2
        + [jax.ShapeDtypeStruct((16, 128), F32)]
        + [jax.ShapeDtypeStruct((width * tile, 2 * tile), BF16)] * 2,
        [], 14, 0.2,
    )
    new_env = call(
        "unpack_env", functools.partial(unpack_kernel, width, tile), [], [early, middle, late],
        jax.ShapeDtypeStruct((width * tile, tile), BF16), [diag], 6, 2,
    )
    middle_bound, new_env = lax.optimization_barrier((middle_bound, new_env))
    steps = [own_mixed, next_mixed, after_mixed, start_a, start_b, norms, products_a, products_b]
    results = [
        jax.ShapeDtypeStruct((LANCZOS, states, tile, tile), F32),
        jax.ShapeDtypeStruct((16, 128), F32),
    ]
    steps_scratch = [
        pltpu.VMEM((tile, parts[-1][1] * tile), BF16),
        pltpu.VMEM((len(GROUPS), width * tile, 2 * tile), BF16),
        diag,
    ]
    bound, image, basis, stats = call(
        "open", functools.partial(open_kernel, width, tile),
        [sector_dims], [environ, early_bound, middle_bound] + steps,
        [
            jax.ShapeDtypeStruct((tile, parts[-1][0] * tile), BF16),
            jax.ShapeDtypeStruct((len(GROUPS), tile, 2 * tile), F32),
        ]
        + results,
        steps_scratch, 24, 1,
    )
    late_bound, bound = lax.optimization_barrier((late_bound, bound))
    first_basis = basis
    basis, stats = call(
        "lanczos", functools.partial(lanczos_kernel, width, tile),
        [sector_dims], [late_bound, bound, image] + steps + [stats], results,
        steps_scratch, 24, 12,
    )
    stats = gathered(stats, "sec")
    entries = float(states * sector_count * tile * tile)
    vector, table = call(
        "finish", functools.partial(finish_kernel, entries), [], [stats, start_a, start_b, first_basis, basis],
        (
            jax.ShapeDtypeStruct((states, tile, tile), F32),
            jax.ShapeDtypeStruct((2, LANCZOS), F32),
        ),
        [], 6, 2,
    )
    return new_env.reshape(left_env.shape), vector[None, :, None], jnp.transpose(table)[None]


def solution(mesh):
    placed = (
        P("seg", "sec", None, None, None),
        P("seg", "sec", None, None, None),
        P("seg", None, None, "sec", None, None),
        P("seg", None, None, None, None),
        P("seg", None, None, None),
        P("seg", None, "sec", None, None),
        P(),
    )
    return jax.shard_map(
        on_device,
        mesh=mesh,
        in_specs=placed,
        out_specs=(
            P("seg", "sec", None, None, None),
            P("seg", None, "sec", None, None),
            P("seg", None, None),
        ),
        check_vma=False,
    )
```
